256 devices in a mesh: dp: 8 (over y, core), tower: 2 (over z_hi), tensor: 16 (over z_lo, x).
Axes of the slice: x: 4, y: 4, z: 8 (z_hi: 2, z_lo: 4; z = z_hi * 4 + z_lo), core: 2. Of those that a mesh axis runs over, the one named last changes fastest.
Arguments:
- q_act: bfloat16 [24576, 1536], P(('dp', 'tower', 'tensor')), may hold values from -6 to 6
- q_norm_gain: bfloat16 [1536], replicated, may hold values from 0.099609375 to 1.8984375
- q_gate: bfloat16 [1536, 8960], P(None, 'tensor'), may hold values from -0.15625 to 0.15625
- q_up: bfloat16 [1536, 8960], P(None, 'tensor'), may hold values from -0.15625 to 0.15625
- q_down: bfloat16 [8960, 1536], P('tensor'), may hold values from -0.125 to 0.125
- q_final_gain: bfloat16 [1536], replicated, may hold values from 0.099609375 to 1.8984375
- projection: bfloat16 [1536, 768], replicated, may hold values from -1 to 1
- i_act: bfloat16 [8192, 768], P(('dp', 'tower', 'tensor')), may hold values from -6 to 6
- i_norm_gain: bfloat16 [768], replicated, may hold values from 0.099609375 to 1.8984375
- i_gate: bfloat16 [768, 3072], P(None, ('tower', 'tensor')), may hold values from -0.21875 to 0.21875
- i_up: bfloat16 [768, 3072], P(None, ('tower', 'tensor')), may hold values from -0.21875 to 0.21875
- i_down: bfloat16 [3072, 768], P(('tower', 'tensor')), may hold values from -0.109375 to 0.109375
- i_final_gain: bfloat16 [768], replicated, may hold values from 0.099609375 to 1.8984375
- ranks: int32 [16, 16], replicated, may hold values from 0 to 15, each once within a row
- positive: int32 [16], replicated, may hold values from 0 to 15
Outputs:
- loss_value: float32 [], replicated
- q_grad: float32 [8960, 1536], P('tensor', ('dp', 'tower'))
- i_grad: float32 [3072, 768], P(('tower', 'tensor'), 'dp')
The draws below stay inside these ranges and needn't reach their ends.
Inputs may be any that keep to these rules, and one draw needn't show every extreme that they name: Each row of ranks holds every rank 0 to 15 once.
All inputs are finite; a program needn't handle non-finite values.
Results may differ from the reference program's by a relative error of at most 0.0012.
Values may be sent and summed in bfloat16 or wider, within the bound.
A program may use at most 128 MiB of HBM per device.

```python
import math
import jax
import jax.numpy as jnp
from jax import lax

DQ = 1536
FFQ = 8960
DI = 768
FFI = 3072
QLEN = 1536
ILEN = 512
QUERIES = 16
ITEMS = 16


def common_parts(key):
    center_key, sign_key = jax.random.split(key)
    centers = jnp.clip(jax.random.normal(center_key, (ITEMS, DI), jnp.float32), -4.0, 4.0)
    sign_flips = (jax.random.randint(sign_key, (DQ,), 0, 2) * 2 - 1).astype(jnp.float32)
    return (centers, sign_flips)


def draw_q_act(key, part):
    centers, sign_flips = common_parts(key)
    key = jax.random.fold_in(key, 11)
    noise_key, pick_key, size_key, flip_key = jax.random.split(key, 4)
    row_count = QUERIES * QLEN
    chosen_items = jax.random.randint(pick_key, (row_count,), 0, ITEMS)
    tiled_center = centers[:, jnp.arange(DQ) % DI] * sign_flips[None, :]
    row_center = tiled_center[chosen_items]
    magnitude = jax.random.uniform(size_key, (row_count, 1), jnp.float32, 0.6, 2.0)
    row_sign = (jax.random.randint(flip_key, (row_count, 1), 0, 2) * 2 - 1).astype(jnp.float32)
    base_noise = jnp.clip(jax.random.normal(noise_key, (row_count, DQ), jnp.float32), -6.0, 6.0)
    values = jnp.clip(base_noise + magnitude * row_sign * row_center, -6.0, 6.0)
    return values.astype(jnp.bfloat16)


def draw_i_act(key, part):
    centers, sign_flips = common_parts(key)
    key = jax.random.fold_in(key, 12)
    row_count = ITEMS * ILEN
    owner_item = jnp.arange(row_count) // ILEN
    base_noise = jnp.clip(jax.random.normal(key, (row_count, DI), jnp.float32), -6.0, 6.0)
    values = jnp.clip(base_noise + centers[owner_item], -6.0, 6.0)
    return values.astype(jnp.bfloat16)


def draw_projection(key, part):
    centers, sign_flips = common_parts(key)
    key = jax.random.fold_in(key, 13)
    spread_noise = jnp.clip(jax.random.normal(key, (DQ, DI), jnp.float32), -4.0, 4.0) * (1.0 / math.sqrt(DQ))
    row_index = jnp.arange(DQ) % DI
    col_index = jnp.arange(DI)
    on_diagonal = row_index[:, None] == col_index[None, :]
    values = jnp.where(on_diagonal, sign_flips[:, None], spread_noise)
    return values.astype(jnp.bfloat16)


def plant(entries, key, smallest, largest):
    longest = entries.shape.index(max(entries.shape))
    spots = []
    for shift in (0, 1):
        where = [jax.random.randint(jax.random.fold_in(key, axis), (), 0, length) for axis, length in enumerate(entries.shape)]
        where[longest] = (where[longest] + shift) % entries.shape[longest]
        spots.append(tuple(where))
    return entries.at[spots[0]].set(smallest).at[spots[1]].set(largest)


def block_levels(own_key, extent, pieces, smallest, top_value):
    loudness, own = 1.0, jax.random.fold_in(own_key, 6)
    for dim, shards_of in pieces:
        heights = jnp.exp(jax.random.uniform(jax.random.fold_in(own, dim), (shards_of,), jnp.float32, smallest / len(pieces), top_value / len(pieces)))
        loudness = loudness * jnp.repeat(heights, extent[dim] // shards_of).reshape([-1 if axis == dim else 1 for axis in range(len(extent))])
    return loudness


def gaussian(key, shape, width, most, shards=(), held_as=jnp.bfloat16):
    drawn = jax.random.normal(key, shape, jnp.float32) * width
    if len(shards) > 0:
        drawn = block_levels(key, shape, shards, -0.22, 0.18) * drawn
    return jnp.clip(drawn, min=-most, max=most).astype(held_as)


def setup_inputs(seed: int = 0) -> dict:
    arg_keys = jax.random.split(jax.random.key(seed), 16)
    q_act = draw_q_act(jax.random.fold_in(arg_keys[15], 71), 0)
    q_norm_gain = jnp.clip(1.0 + 0.18 * jax.random.normal(arg_keys[1], (DQ,), jnp.float32), 0.099609375, 1.8984375).astype(jnp.bfloat16)
    q_gate = gaussian(arg_keys[2], (DQ, FFQ), DQ ** -0.5, 0.15625, ((1, 16),))
    q_up = gaussian(arg_keys[3], (DQ, FFQ), DQ ** -0.5, 0.15625, ((1, 16),))
    q_down = gaussian(arg_keys[4], (FFQ, DQ), (FFQ // 4) ** -0.5, 0.125, ((0, 16),))
    q_final_gain = jnp.clip(1.0 + 0.18 * jax.random.normal(arg_keys[5], (DQ,), jnp.float32), 0.099609375, 1.8984375).astype(jnp.bfloat16)
    projection = draw_projection(jax.random.fold_in(arg_keys[15], 71), 0)
    i_act = draw_i_act(jax.random.fold_in(arg_keys[15], 71), 0)
    i_norm_gain = jnp.clip(1.0 + 0.18 * jax.random.normal(arg_keys[8], (DI,), jnp.float32), 0.099609375, 1.8984375).astype(jnp.bfloat16)
    i_gate = gaussian(arg_keys[9], (DI, FFI), DI ** -0.5, 0.21875, ((1, 32),))
    i_up = gaussian(arg_keys[10], (DI, FFI), DI ** -0.5, 0.21875, ((1, 32),))
    i_down = gaussian(arg_keys[11], (FFI, DI), FFI ** -0.5, 0.109375, ((0, 32),))
    i_final_gain = jnp.clip(1.0 + 0.18 * jax.random.normal(arg_keys[12], (DI,), jnp.float32), 0.099609375, 1.8984375).astype(jnp.bfloat16)
    ranks = jax.vmap(lambda own: jax.random.permutation(own, ITEMS))(jax.random.split(arg_keys[13], QUERIES)).reshape((QUERIES, ITEMS)).astype(jnp.int32)
    positive = plant(jax.random.randint(arg_keys[14], (QUERIES,), 0, ITEMS), jax.random.fold_in(arg_keys[14], 1), 0, ITEMS - 1).astype(jnp.int32)
    return {"q_act": q_act, "q_norm_gain": q_norm_gain, "q_gate": q_gate, "q_up": q_up, "q_down": q_down, "q_final_gain": q_final_gain, "projection": projection, "i_act": i_act, "i_norm_gain": i_norm_gain, "i_gate": i_gate, "i_up": i_up, "i_down": i_down, "i_final_gain": i_final_gain, "ranks": ranks, "positive": positive}


EPS = 1e-06
TAU = 0.05
TEACH = 2.0
LOSS_SCALE = 64.0
HIGH = lax.Precision.HIGHEST

def rms_scale(values):
    return lax.rsqrt(lax.optimization_barrier(jnp.mean(values * values, axis=-1, keepdims=True)) + EPS)

def tower_forward(activ, norm_gain, gate_w, up_w, down_w, final_gain):
    values = activ.astype(jnp.float32)
    normed = (values * rms_scale(values) * norm_gain.astype(jnp.float32)).astype(jnp.bfloat16)
    gate_val = jnp.dot(normed, gate_w, preferred_element_type=jnp.float32)
    up_val = jnp.dot(normed, up_w, preferred_element_type=jnp.float32)
    hidden = (jax.nn.silu(gate_val) * up_val).astype(jnp.bfloat16)
    mlp_out = jnp.dot(hidden, down_w, preferred_element_type=jnp.float32)
    resid = values + mlp_out
    scales = rms_scale(resid)
    pooled = lax.optimization_barrier(jnp.mean(resid * scales * final_gain.astype(jnp.float32), axis=0))
    return (hidden, resid, scales, pooled)

def unit_norm(vec):
    scales = lax.rsqrt(lax.optimization_barrier(jnp.sum(vec * vec, axis=-1, keepdims=True)) + EPS)
    return (vec * scales, scales)

def unit_back(vec, scales, upstream):
    inner = lax.optimization_barrier(jnp.sum(vec * upstream, axis=-1, keepdims=True))
    return scales * upstream - vec * (scales * scales * scales) * inner

def grad_rows(resid, scales, gain, upstream):
    along = gain.astype(jnp.float32) * upstream
    inner = lax.optimization_barrier(jnp.mean(along * resid, axis=-1, keepdims=True))
    return (scales * along - resid * (scales * scales * scales) * inner).astype(jnp.bfloat16)

def contrast(query_hat, item_hat, ranks, positive):
    logits = jnp.dot(query_hat, item_hat.T, precision=HIGH) / TAU
    shifted = logits - 1.0 / TAU
    log_student = shifted - jnp.log(lax.optimization_barrier(jnp.sum(jnp.exp(shifted), axis=1, keepdims=True)))
    teach = -ranks.astype(jnp.float32) / TEACH
    log_teacher = teach - jnp.log(lax.optimization_barrier(jnp.sum(jnp.exp(teach), axis=1, keepdims=True)))
    teacher = jnp.exp(log_teacher)
    columns = lax.broadcasted_iota(jnp.int32, logits.shape, 1)
    onehot = (columns == positive.astype(jnp.int32)[:, None]).astype(jnp.float32)
    per_row = lax.optimization_barrier(jnp.sum(teacher * (log_teacher - log_student) - onehot * log_student, axis=1))
    slopes = 2.0 * jnp.exp(log_student) - onehot - teacher
    return (per_row, slopes)

def reference(q_act, q_norm_gain, q_gate, q_up, q_down, q_final_gain, projection, i_act, i_norm_gain, i_gate, i_up, i_down, i_final_gain, ranks, positive):
    query_seq = q_act.reshape(QUERIES, QLEN, DQ)
    item_seq = i_act.reshape(ITEMS, ILEN, DI)

    def query_forward(activ):
        return tower_forward(activ, q_norm_gain, q_gate, q_up, q_down, q_final_gain)

    def item_forward(activ):
        return tower_forward(activ, i_norm_gain, i_gate, i_up, i_down, i_final_gain)
    query_h, query_resid, query_scale, query_pooled = lax.map(query_forward, query_seq)
    item_h, item_resid, item_scale, item_pooled = lax.map(item_forward, item_seq)
    proj_f = projection.astype(jnp.float32)
    query_e = jnp.dot(query_pooled, proj_f, precision=HIGH)
    query_hat, query_norm = unit_norm(query_e)
    item_hat, item_norm = unit_norm(item_pooled)
    per_row, slopes = contrast(query_hat, item_hat, ranks, positive)
    loss_value = jnp.mean(per_row)
    weights = slopes * (LOSS_SCALE / (TAU * QUERIES))
    query_grad_hat = jnp.dot(weights, item_hat, precision=HIGH)
    item_grad_hat = jnp.dot(weights.T, query_hat, precision=HIGH)
    query_up_vec = jnp.dot(unit_back(query_e, query_norm, query_grad_hat), proj_f.T, precision=HIGH) / QLEN
    item_up_vec = unit_back(item_pooled, item_norm, item_grad_hat) / ILEN

    def query_add(total, inputs):
        hidden, resid, scales, upstream = inputs
        grad_res = grad_rows(resid, scales, q_final_gain, upstream[None, :])
        return (total + jnp.dot(hidden.T, grad_res, preferred_element_type=jnp.float32), None)

    def item_add(total, inputs):
        hidden, resid, scales, upstream = inputs
        grad_res = grad_rows(resid, scales, i_final_gain, upstream[None, :])
        return (total + jnp.dot(hidden.T, grad_res, preferred_element_type=jnp.float32), None)
    q_grad, _ = lax.scan(query_add, jnp.zeros((FFQ, DQ), jnp.float32), (query_h, query_resid, query_scale, query_up_vec))
    i_grad, _ = lax.scan(item_add, jnp.zeros((FFI, DI), jnp.float32), (item_h, item_resid, item_scale, item_up_vec))
    return (loss_value, q_grad, i_grad)
```

```python
import functools

import jax
import jax.numpy as jnp
from jax import lax
from jax.experimental import pallas as pl
from jax.experimental.pallas import tpu as pltpu
from jax.sharding import PartitionSpec as P

QLEN = 1536
ILEN = 512
EPS = 1e-06
TAU = 0.05
TEACH = 2.0
LOSS_SCALE = 64.0
HIGH = lax.Precision.HIGHEST
MESH = pl.DeviceIdType.MESH
F32 = jnp.float32
BF16 = jnp.bfloat16

X = 4
ZL = 4
ZR = 8
VMEM_LIMIT = 60 * 1024 * 1024


def rms_scale(values):
    return lax.rsqrt(jnp.mean(values * values, axis=-1, keepdims=True) + EPS)


def dot(left, right, dims=((1,), (0,)), precision=None):
    return lax.dot_general(
        left, right, (dims, ((), ())), preferred_element_type=F32, precision=precision
    )


def remote(src, dst, send, recv, where):
    return pltpu.make_async_remote_copy(
        src_ref=src, dst_ref=dst, send_sem=send, recv_sem=recv, device_id=where, device_id_type=MESH
    )


class Place:
    def __init__(self):
        self.t = lax.axis_index("tensor")
        self.w = lax.axis_index("tower")
        self.a = self.t // X
        self.b = self.t % X
        self.z = self.w * ZL + self.a
        self.bp = (self.b + 1) % X
        self.bm = (self.b + X - 1) % X
        self.bo = (self.b + 2) % X
        self.xp = {"tensor": self.a * X + self.bp}
        self.xm = {"tensor": self.a * X + self.bm}
        self.zp = self.ring(1)
        self.zm = self.ring(ZR - 1)

    def ring(self, step):
        z = (self.z + step) % ZR
        return {"tower": z // ZL, "tensor": (z % ZL) * X + self.b}

    def column(self, row):
        return {"tensor": row * X + self.b}

    def order(self, j):
        near = jnp.minimum(self.a, ZL - 1 - self.a)
        swapped = jnp.where(j == 0, 1, jnp.where(j == 1, 0, j))
        row = jnp.where(near == 1, swapped, j)
        return jnp.where(self.a >= 2, ZL - 1 - row, row)


def rows_of(ref, first, count, unit):
    return ref.at[pl.ds(pl.multiple_of(first, unit), count), :]


class RowGather:
    def __init__(self, place, buf, rows, send, recv):
        self.p, self.buf, self.n, self.send, self.recv = place, buf, rows, send, recv

    def block(self, s, b):
        return rows_of(self.buf, (s * X + b) * self.n, self.n, self.n)

    def half(self, s, b, h):
        n = self.n // 2
        return rows_of(self.buf, (s * X + b) * self.n + h * n, n, n)

    def up(self, s):
        ref = self.block(s, self.p.b)
        where = self.p.column(jnp.minimum(self.p.a + 1, ZL - 1))
        return remote(ref, ref, self.send.at[0, s], self.recv.at[0, s], where)

    def down(self, s):
        ref = self.block(s, self.p.b)
        where = self.p.column(jnp.maximum(self.p.a - 1, 0))
        return remote(ref, ref, self.send.at[1, s], self.recv.at[0, s], where)

    def right(self, s):
        ref = self.block(s, self.p.b)
        return remote(ref, ref, self.send.at[2, s], self.recv.at[1, s], self.p.xp)

    def left(self, s):
        ref = self.block(s, self.p.b)
        return remote(ref, ref, self.send.at[3, s], self.recv.at[2, s], self.p.xm)

    def half_right(self, s):
        ref = self.half(s, self.p.bm, 0)
        return remote(ref, ref, self.send.at[4, s], self.recv.at[3, s], self.p.xp)

    def half_left(self, s):
        ref = self.half(s, self.p.bp, 1)
        return remote(ref, ref, self.send.at[5, s], self.recv.at[4, s], self.p.xm)

    def goes_up(self, s):
        return (s <= self.p.a) & (self.p.a < ZL - 1)

    def goes_down(self, s):
        return (s >= self.p.a) & (self.p.a > 0)

    def take_z(self, s):
        @pl.when(s != self.p.a)
        def _():
            self.up(s).wait_recv()

        @pl.when(self.goes_up(s))
        def _():
            self.up(s).start()

        @pl.when(self.goes_down(s))
        def _():
            self.down(s).start()

        self.right(s).start()
        self.left(s).start()

    def take_x(self, s):
        ref = self.block(s, self.p.bm)
        remote(ref, ref, self.send.at[2, s], self.recv.at[1, s], self.p.xm).wait_recv()
        self.half_right(s).start()
        ref = self.block(s, self.p.bp)
        remote(ref, ref, self.send.at[3, s], self.recv.at[2, s], self.p.xp).wait_recv()
        self.half_left(s).start()

    def take_halves(self, s):
        ref = self.half(s, self.p.bo, 0)
        remote(ref, ref, self.send.at[4, s], self.recv.at[3, s], self.p.xm).wait_recv()
        ref = self.half(s, self.p.bo, 1)
        remote(ref, ref, self.send.at[5, s], self.recv.at[4, s], self.p.xp).wait_recv()

    def drain(self):
        def each(s, _):
            @pl.when(self.goes_up(s))
            def _():
                self.up(s).wait_send()

            @pl.when(self.goes_down(s))
            def _():
                self.down(s).wait_send()

            self.right(s).wait_send()
            self.left(s).wait_send()
            self.half_right(s).wait_send()
            self.half_left(s).wait_send()
            return 0

        lax.fori_loop(0, ZL, each, 0)


class RingGather:
    def __init__(self, place, buf, rows, send, recv):
        self.p, self.buf, self.n, self.send, self.recv = place, buf, rows, send, recv

    def ref(self, z, hop, upward):
        z = (z + 2 * ZR) % ZR
        if hop < 4:
            return rows_of(self.buf, z * self.n, self.n, self.n)
        n = self.n // 2
        return rows_of(self.buf, z * self.n + (0 if upward else n), n, n)

    def copies(self, hop):
        up = self.ref(self.p.z - hop + 1, hop, True)
        down = self.ref(self.p.z + hop - 1, hop, False)
        return (
            remote(up, up, self.send.at[0, hop - 1], self.recv.at[0, hop - 1], self.p.zp),
            remote(down, down, self.send.at[1, hop - 1], self.recv.at[1, hop - 1], self.p.zm),
        )

    def start(self, hop):
        for copy in self.copies(hop):
            copy.start()

    def take(self, hop):
        up = self.ref(self.p.z - hop, hop, True)
        down = self.ref(self.p.z + hop, hop, False)
        remote(up, up, self.send.at[0, hop - 1], self.recv.at[0, hop - 1], self.p.zm).wait_recv()
        remote(down, down, self.send.at[1, hop - 1], self.recv.at[1, hop - 1], self.p.zp).wait_recv()

    def drain(self):
        for hop in range(1, 5):
            for copy in self.copies(hop):
                copy.wait_send()


class RingSum:
    def __init__(self, place, buf, land, rows, send, recv):
        self.p, self.buf, self.land = place, buf, land
        self.n, self.send, self.recv = rows, send, recv

    def part(self, z, half):
        z = (z + 2 * ZR) % ZR
        if half is None:
            return rows_of(self.buf, z * self.n, self.n, self.n)
        n = self.n // 2
        return rows_of(self.buf, z * self.n + half * n, n, n)

    def slot(self, way, hop):
        if hop == 1:
            return self.land.at[way, 0, pl.ds(0, self.n // 2), :]
        return self.land.at[way, hop - 1]

    def copies(self, hop):
        half = (0, 1) if hop == 1 else (None, None)
        up = self.part(self.p.z + 5 - hop, half[0])
        down = self.part(self.p.z - 5 + hop, half[1])
        return (
            remote(up, self.slot(0, hop), self.send.at[0, hop - 1], self.recv.at[0, hop - 1], self.p.zp),
            remote(down, self.slot(1, hop), self.send.at[1, hop - 1], self.recv.at[1, hop - 1], self.p.zm),
        )

    def start(self, hop):
        for copy in self.copies(hop):
            copy.start()

    def take(self, hop):
        for copy in self.copies(hop):
            copy.wait_recv()

    def add(self, hop):
        half = (0, 1) if hop == 1 else (None, None)
        for way, z in ((0, self.p.z + 4 - hop), (1, self.p.z - 4 + hop)):
            ref = self.part(z, half[way])
            ref[...] = (ref[...].astype(F32) + self.slot(way, hop)[...].astype(F32)).astype(BF16)

    def drain(self):
        for hop in range(1, 5):
            for copy in self.copies(hop):
                copy.wait_send()


def normed_rows(act, gain):
    values = act.astype(F32)
    return (values * rms_scale(values) * gain).astype(BF16)


def gated(gate_val, up_val):
    return (jax.nn.silu(gate_val) * up_val).astype(BF16)


def at_step(i, step):
    return pl.when(i == step)


def forward_kernel(
    qa, qg, gate, up, down, ia, ig, iw,
    hq, hi, qr, ir,
    nq, pm, r1, r2, zs, zin, acc, ni, wi, ip, land,
    gs, gr, ss, sr, ws, wr, ias, iar, irs, irr,
):
    p = Place()
    n = qa.shape[0]
    m = ia.shape[0]
    k = iw.shape[1]
    group = X * n
    h = n // 2

    barrier = pltpu.get_barrier_semaphore()
    for where in (p.xp, p.xm, p.zp, p.zm):
        pl.semaphore_signal(barrier, inc=1, device_id=where, device_id_type=MESH)
    for step in range(1, ZL):
        pl.semaphore_signal(
            barrier, inc=1, device_id=p.column((p.a + step) % ZL), device_id_type=MESH
        )
    nq[pl.ds(pl.multiple_of(p.t * n, n), n), :] = normed_rows(qa[...], qg[...])
    ni[pl.ds(pl.multiple_of(p.z * m, m), m), :] = normed_rows(ia[...], ig[...])
    wi[:, pl.ds(pl.multiple_of(p.b * k, k), k), :] = iw[...]
    pl.semaphore_wait(barrier, 4 + ZL - 1)

    rows = RowGather(p, nq, n, gs, gr)
    items = RingGather(p, ni, m, ias, iar)
    isum = RingSum(p, ip, land, m, irs, irr)

    def wref(b):
        return wi.at[:, pl.ds(pl.multiple_of(b * k, k), k), :]

    def whalf(b, part):
        return wi.at[:, pl.ds(pl.multiple_of(b * k + part * (k // 2), k // 2), k // 2), :]

    def w_copy(ref, index, where):
        return remote(ref, ref, ws.at[index], wr.at[index], where)

    def block(s, b):
        return rows_of(pm, (s * X + b) * n, n, n)

    def half(s, b, part):
        return rows_of(pm, (s * X + b) * n + part * h, h, h)

    def first_right(s):
        return remote(half(s, p.bo, 0), r1.at[0, s], ss.at[0, s], sr.at[0, s], p.xp)

    def first_left(s):
        return remote(half(s, p.bo, 1), r1.at[1, s], ss.at[1, s], sr.at[1, s], p.xm)

    def second_right(s):
        return remote(block(s, p.bp), r2.at[0, s], ss.at[2, s], sr.at[2, s], p.xp)

    def second_left(s):
        return remote(block(s, p.bm), r2.at[1, s], ss.at[3, s], sr.at[3, s], p.xm)

    def to_owner(s):
        return remote(zs.at[s], zin.at[p.a], ss.at[4, s], sr.at[4, p.a], p.column(s))

    def product(s):
        here = pl.ds(pl.multiple_of(s * group, group), group)
        left = nq[here, :]
        hidden = gated(dot(left, gate[...]), dot(left, up[...]))
        hq[here, :] = hidden
        pm[here, :] = dot(hidden, down[...]).astype(BF16)

    def step(i, _):
        @pl.when(i < ZL)
        def _():
            rows.take_z(p.order(i))

        @at_step(i, 1)
        def _():
            w_copy(wref(p.b), 0, p.xp).start()
            w_copy(wref(p.b), 1, p.xm).start()

        @pl.when((i >= 1) & (i <= ZL))
        def _():
            rows.take_x(p.order(i - 1))

        for hop in range(1, 5):

            @at_step(i, hop - 1)
            def _():
                if hop > 1:
                    items.take(hop - 1)
                items.start(hop)

        @at_step(i, 3)
        def _():
            w_copy(wref(p.bm), 0, p.xm).wait_recv()
            w_copy(whalf(p.bm, 0), 2, p.xp).start()
            w_copy(wref(p.bp), 1, p.xp).wait_recv()
            w_copy(whalf(p.bp, 1), 3, p.xm).start()

        @pl.when((i >= 2) & (i <= ZL + 1))
        def _():
            s = p.order(i - 2)
            rows.take_halves(s)
            product(s)
            first_right(s).start()
            first_left(s).start()

        @pl.when((i >= 3) & (i <= ZL + 2))
        def _():
            s = p.order(i - 3)
            first_right(s).wait_recv()
            ref = half(s, p.bp, 0)
            ref[...] = (ref[...].astype(F32) + r1[0, s].astype(F32)).astype(BF16)
            second_right(s).start()
            first_left(s).wait_recv()
            ref = half(s, p.bm, 1)
            ref[...] = (ref[...].astype(F32) + r1[1, s].astype(F32)).astype(BF16)
            second_left(s).start()

        @at_step(i, 4)
        def _():
            items.take(4)
            w_copy(whalf(p.bo, 0), 2, p.xm).wait_recv()
            w_copy(whalf(p.bo, 1), 3, p.xp).wait_recv()
            left = ni[...]
            hidden = gated(dot(left, wi[0], ((1,), (1,))), dot(left, wi[1], ((1,), (1,))))
            hi[...] = hidden
            ip[...] = dot(hidden, wi[2]).astype(BF16)
            isum.start(1)

        for hop in range(1, 4):

            @at_step(i, 4 + hop)
            def _():
                isum.take(hop)
                isum.add(hop)
                isum.start(hop + 1)

        @pl.when(i >= 4)
        def _():
            s = p.order(i - 4)
            second_right(s).wait_recv()
            second_left(s).wait_recv()
            total = block(s, p.b)[...].astype(F32) + r2[0, s].astype(F32) + r2[1, s].astype(F32)

            @pl.when(s == p.a)
            def _():
                acc[...] = total

            @pl.when(s != p.a)
            def _():
                zs[s] = total.astype(BF16)
                to_owner(s).start()

        return 0

    lax.fori_loop(0, 2 * ZL, step, 0)

    isum.take(4)
    own = ip[pl.ds(pl.multiple_of(p.z * m, m), m), :].astype(F32)
    ir[...] = ia[...].astype(F32) + (own + land[0, 3].astype(F32) + land[1, 3].astype(F32))

    def collect(step, _):
        s = (p.a + step) % ZL
        remote(zs.at[s], zin.at[s], ss.at[4, s], sr.at[4, s], p.column(s)).wait_recv()
        acc[...] += zin[s].astype(F32)
        return 0

    lax.fori_loop(1, ZL, collect, 0)
    qr[...] = qa[...].astype(F32) + acc[...]

    rows.drain()
    items.drain()
    isum.drain()
    w_copy(wref(p.b), 0, p.xp).wait_send()
    w_copy(wref(p.b), 1, p.xm).wait_send()
    w_copy(whalf(p.bm, 0), 2, p.xp).wait_send()
    w_copy(whalf(p.bp, 1), 3, p.xm).wait_send()

    def drain(s, _):
        first_right(s).wait_send()
        first_left(s).wait_send()
        second_right(s).wait_send()
        second_left(s).wait_send()

        @pl.when(s != p.a)
        def _():
            to_owner(s).wait_send()

        return 0

    lax.fori_loop(0, ZL, drain, 0)


def forward(qa, qg, gate, up, down, ia, ig, iw):
    n, dq = qa.shape
    m, di = ia.shape
    k = iw.shape[1]
    all_q = X * ZL * n
    all_i = ZR * m
    dma = pltpu.SemaphoreType.DMA
    return pl.pallas_call(
        forward_kernel,
        out_shape=(
            jax.ShapeDtypeStruct((all_q, gate.shape[1]), BF16),
            jax.ShapeDtypeStruct((all_i, X * k), BF16),
            jax.ShapeDtypeStruct((n, dq), F32),
            jax.ShapeDtypeStruct((m, di), F32),
        ),
        in_specs=[pl.BlockSpec(memory_space=pltpu.VMEM)] * 8,
        out_specs=[pl.BlockSpec(memory_space=pltpu.VMEM)] * 4,
        scratch_shapes=[
            pltpu.VMEM((all_q, dq), BF16),
            pltpu.VMEM((all_q, dq), BF16),
            pltpu.VMEM((2, ZL, n // 2, dq), BF16),
            pltpu.VMEM((2, ZL, n, dq), BF16),
            pltpu.VMEM((ZL, n, dq), BF16),
            pltpu.VMEM((ZL, n, dq), BF16),
            pltpu.VMEM((n, dq), F32),
            pltpu.VMEM((all_i, di), BF16),
            pltpu.VMEM((3, X * k, di), BF16),
            pltpu.VMEM((all_i, di), BF16),
            pltpu.VMEM((2, 4, m, di), BF16),
            dma((6, ZL)),
            dma((5, ZL)),
            dma((5, ZL)),
            dma((5, ZL)),
            dma((4,)),
            dma((4,)),
            dma((2, 4)),
            dma((2, 4)),
            dma((2, 4)),
            dma((2, 4)),
        ],
        compiler_params=pltpu.CompilerParams(
            collective_id=0, has_side_effects=True, vmem_limit_bytes=VMEM_LIMIT
        ),
        name="towers_forward",
    )(qa, qg, gate, up, down, ia, ig, iw)


def split_rows(row):
    high = row.astype(BF16).astype(F32)
    rest = row - high
    mid = rest.astype(BF16).astype(F32)
    low = rest - mid
    index = lax.broadcasted_iota(jnp.int32, (8, row.shape[1]), 0)
    out = jnp.where(index == 0, high, jnp.where(index == 1, mid, jnp.where(index == 2, low, 0.0)))
    return out.astype(BF16)


def unit_scale(vec):
    return lax.rsqrt(jnp.sum(vec * vec, axis=-1, keepdims=True) + EPS)


def unit_back(vec, scales, upstream):
    inner = jnp.sum(vec * upstream, axis=-1, keepdims=True)
    return scales * upstream - vec * (scales * scales * scales) * inner


def contrast(query_hat, item_hat, ranks, positive):
    logits = dot(query_hat, item_hat, ((1,), (1,)), HIGH) / TAU
    shifted = logits - 1.0 / TAU
    log_student = shifted - jnp.log(jnp.sum(jnp.exp(shifted), axis=1, keepdims=True))
    teach = -ranks.astype(F32) / TEACH
    log_teacher = teach - jnp.log(jnp.sum(jnp.exp(teach), axis=1, keepdims=True))
    teacher = jnp.exp(log_teacher)
    columns = lax.broadcasted_iota(jnp.int32, logits.shape, 1)
    onehot = (columns == positive).astype(F32)
    per_row = jnp.sum(
        teacher * (log_teacher - log_student) - onehot * log_student, axis=1, keepdims=True
    )
    slopes = 2.0 * jnp.exp(log_student) - onehot - teacher
    return (per_row, slopes)


def grad_rows(resid, scales, gain, upstream):
    along = gain * upstream
    inner = jnp.mean(along * resid, axis=-1, keepdims=True)
    return (scales * along - resid * (scales * scales * scales) * inner).astype(BF16)


def backward_kernel(
    qr, ir, qf, if_, hq, hi, proj, ranks, positive,
    loss, gq, gi,
    sums, hats, nq, ni,
    s1, r1, s2, r2, gs, gr, ias, iar,
):
    p = Place()
    n, dq = qr.shape
    m, di = ir.shape
    group = X * n
    parts = X * ZL
    own = lax.axis_index("dp") * 2 + p.w
    count = hats.shape[0]

    def member(step):
        return {"tensor": (p.t + step) % parts}

    def replica(step):
        other = (own + step) % count
        return {"dp": other // 2, "tower": other % 2}

    barrier = pltpu.get_barrier_semaphore()

    def greet(step, _):
        pl.semaphore_signal(barrier, inc=1, device_id=member(step), device_id_type=MESH)
        return 0

    def greet_replica(step, _):
        pl.semaphore_signal(barrier, inc=1, device_id=replica(step), device_id_type=MESH)
        return 0

    lax.fori_loop(1, parts, greet, 0)
    lax.fori_loop(1, count, greet_replica, 0)
    for where in (p.zp, p.zm):
        pl.semaphore_signal(barrier, inc=1, device_id=where, device_id_type=MESH)

    q_resid, i_resid = qr[...], ir[...]
    q_scale, i_scale = rms_scale(q_resid), rms_scale(i_resid)
    sums[p.t, :, :dq] = jnp.sum(q_resid * q_scale * qf[...], axis=0, keepdims=True)
    sums[p.t, :, dq:] = jnp.sum(i_resid * i_scale * if_[...], axis=0, keepdims=True)
    pl.semaphore_wait(barrier, parts + count)

    def spread(step, _):
        remote(sums.at[p.t], sums.at[p.t], s1.at[step], r1.at[p.t], member(step)).start()
        return 0

    def gathered(step, _):
        other = (p.t + step) % parts
        remote(sums.at[p.t], sums.at[other], s1.at[step], r1.at[other], member(step)).wait()
        return 0

    lax.fori_loop(1, parts, spread, 0)
    lax.fori_loop(1, parts, gathered, 0)
    total = sums[0]
    for slot in range(1, parts):
        total = total + sums[slot]
    q_pooled = total[:, :dq] / QLEN
    i_pooled = total[:, dq:] / ILEN
    q_e = jnp.sum(dot(split_rows(q_pooled), proj[...]), axis=0, keepdims=True)
    q_norm, i_norm = unit_scale(q_e), unit_scale(i_pooled)
    hats[own, :, :di] = q_e * q_norm
    hats[own, :, di:] = i_pooled * i_norm

    def spread_hats(step, _):
        remote(hats.at[own], hats.at[own], s2.at[step], r2.at[own], replica(step)).start()
        return 0

    def gathered_hats(step, _):
        other = (own + step) % count
        remote(hats.at[own], hats.at[other], s2.at[step], r2.at[other], replica(step)).wait()
        return 0

    lax.fori_loop(1, count, spread_hats, 0)
    lax.fori_loop(1, count, gathered_hats, 0)
    index = lax.broadcasted_iota(jnp.int32, (count, 2 * di), 0)
    every = jnp.zeros((count, 2 * di), F32)
    for slot in range(count):
        every = jnp.where(index == slot, hats[slot], every)
    every_query, every_items = every[:, :di], every[:, di:]
    per_row, slopes = contrast(every_query, every_items, ranks[...], positive[...])
    loss[...] = jnp.sum(per_row, axis=0, keepdims=True) / count
    weights = slopes * (LOSS_SCALE / (TAU * count))
    mine = lax.broadcasted_iota(jnp.int32, (count, di), 0) == own
    q_back = jnp.sum(
        jnp.where(mine, dot(weights, every_items, precision=HIGH), 0.0), axis=0, keepdims=True
    )
    column = lax.broadcasted_iota(jnp.int32, (count, count), 1) == own
    i_back = jnp.sum(
        jnp.sum(jnp.where(column, weights, 0.0), axis=1, keepdims=True) * every_query,
        axis=0,
        keepdims=True,
    )
    q_grad_e = unit_back(q_e, q_norm, q_back)
    q_up = jnp.sum(dot(split_rows(q_grad_e), proj[...], ((1,), (1,))), axis=0, keepdims=True) / QLEN
    i_up = unit_back(i_pooled, i_norm, i_back) / ILEN
    nq[pl.ds(pl.multiple_of(p.t * n, n), n), :] = grad_rows(q_resid, q_scale, qf[...], q_up)
    ni[pl.ds(pl.multiple_of(p.z * m, m), m), :] = grad_rows(i_resid, i_scale, if_[...], i_up)

    rows = RowGather(p, nq, n, gs, gr)
    items = RingGather(p, ni, m, ias, iar)
    gq[...] = jnp.zeros_like(gq)

    def step(i, _):
        @pl.when(i < ZL)
        def _():
            rows.take_z(p.order(i))

        for hop in range(1, 5):

            @at_step(i, hop - 1)
            def _():
                if hop > 1:
                    items.take(hop - 1)
                items.start(hop)

        @pl.when((i >= 1) & (i <= ZL))
        def _():
            rows.take_x(p.order(i - 1))

        @at_step(i, 4)
        def _():
            items.take(4)
            gi[...] = dot(hi[...], ni[...], ((0,), (0,)))

        @pl.when(i >= 2)
        def _():
            s = p.order(i - 2)
            rows.take_halves(s)
            here = pl.ds(pl.multiple_of(s * group, group), group)
            gq[...] += dot(hq[here, :], nq[here, :], ((0,), (0,)))

        return 0

    lax.fori_loop(0, ZL + 2, step, 0)
    rows.drain()
    items.drain()


def backward(qr, ir, qf, if_, hq, hi, proj, ranks, positive):
    n, dq = qr.shape
    m, di = ir.shape
    dma = pltpu.SemaphoreType.DMA
    parts = X * ZL
    count = ranks.shape[0]
    return pl.pallas_call(
        backward_kernel,
        out_shape=(
            jax.ShapeDtypeStruct((1, 1), F32),
            jax.ShapeDtypeStruct((hq.shape[1], dq), F32),
            jax.ShapeDtypeStruct((hi.shape[1], di), F32),
        ),
        in_specs=[pl.BlockSpec(memory_space=pltpu.VMEM)] * 9,
        out_specs=[pl.BlockSpec(memory_space=pltpu.VMEM)] * 3,
        scratch_shapes=[
            pltpu.VMEM((parts, 1, dq + di), F32),
            pltpu.VMEM((count, 1, 2 * di), F32),
            pltpu.VMEM((parts * n, dq), BF16),
            pltpu.VMEM((ZR * m, di), BF16),
            dma((parts,)),
            dma((parts,)),
            dma((count,)),
            dma((count,)),
            dma((6, ZL)),
            dma((5, ZL)),
            dma((2, 4)),
            dma((2, 4)),
        ],
        compiler_params=pltpu.CompilerParams(
            collective_id=1, has_side_effects=True, vmem_limit_bytes=VMEM_LIMIT
        ),
        name="towers_backward",
    )(qr, ir, qf, if_, hq, hi, proj, ranks, positive)


def gain_row(gain):
    return gain.astype(F32).reshape(1, -1)


def body(
    q_act,
    q_norm_gain,
    q_gate,
    q_up,
    q_down,
    q_final_gain,
    projection,
    i_act,
    i_norm_gain,
    i_gate,
    i_up,
    i_down,
    i_final_gain,
    ranks,
    positive,
):
    item_w = jnp.stack([i_gate.T, i_up.T, i_down])
    hq, hi, qr, ir = forward(
        q_act, gain_row(q_norm_gain), q_gate, q_up, q_down, i_act, gain_row(i_norm_gain), item_w
    )
    loss, gq, gi = backward(
        qr,
        ir,
        gain_row(q_final_gain),
        gain_row(i_final_gain),
        hq,
        hi,
        projection,
        ranks,
        positive.reshape(-1, 1),
    )
    q_grad = lax.psum_scatter(gq, ("dp", "tower"), scatter_dimension=1, tiled=True)
    i_part = lax.psum_scatter(gi, "dp", scatter_dimension=1, tiled=True)
    groups = [[a * X + b for b in range(X)] for a in range(ZL)]
    i_grad = lax.psum_scatter(
        i_part, "tensor", scatter_dimension=0, tiled=True, axis_index_groups=groups
    )
    return (loss.reshape(()), q_grad, i_grad)


def solution(mesh):
    in_specs = (
        P(("dp", "tower", "tensor"), None),
        P(),
        P(None, "tensor"),
        P(None, "tensor"),
        P("tensor", None),
        P(),
        P(),
        P(("dp", "tower", "tensor"), None),
        P(),
        P(None, ("tower", "tensor")),
        P(None, ("tower", "tensor")),
        P(("tower", "tensor"), None),
        P(),
        P(),
        P(),
    )
    out_specs = (P(), P("tensor", ("dp", "tower")), P(("tower", "tensor"), "dp"))
    return jax.shard_map(body, mesh=mesh, in_specs=in_specs, out_specs=out_specs, check_vma=False)
```

```python
import functools

import jax
import jax.numpy as jnp
from jax import lax
from jax.experimental import pallas as pl
from jax.experimental.pallas import tpu as pltpu
from jax.sharding import PartitionSpec as P

QLEN = 1536
ILEN = 512
EPS = 1e-06
TAU = 0.05
TEACH = 2.0
LOSS_SCALE = 64.0
HIGH = lax.Precision.HIGHEST
MESH = pl.DeviceIdType.MESH
F32 = jnp.float32
BF16 = jnp.bfloat16

X = 4
ZL = 4
ZR = 8
VMEM_LIMIT = 60 * 1024 * 1024


def rms_scale(values):
    return lax.rsqrt(jnp.mean(values * values, axis=-1, keepdims=True) + EPS)


def dot(left, right, dims=((1,), (0,)), precision=None):
    return lax.dot_general(
        left, right, (dims, ((), ())), preferred_element_type=F32, precision=precision
    )


def remote(src, dst, send, recv, where):
    return pltpu.make_async_remote_copy(
        src_ref=src, dst_ref=dst, send_sem=send, recv_sem=recv, device_id=where, device_id_type=MESH
    )


class Place:
    def __init__(self):
        self.t = lax.axis_index("tensor")
        self.w = lax.axis_index("tower")
        self.a = self.t // X
        self.b = self.t % X
        self.z = self.w * ZL + self.a
        self.bp = (self.b + 1) % X
        self.bm = (self.b + X - 1) % X
        self.bo = (self.b + 2) % X
        self.xp = {"tensor": self.a * X + self.bp}
        self.xm = {"tensor": self.a * X + self.bm}
        self.zp = self.ring(1)
        self.zm = self.ring(ZR - 1)

    def ring(self, step):
        z = (self.z + step) % ZR
        return {"tower": z // ZL, "tensor": (z % ZL) * X + self.b}

    def column(self, row):
        return {"tensor": row * X + self.b}

    def order(self, j):
        near = jnp.minimum(self.a, ZL - 1 - self.a)
        swapped = jnp.where(j == 0, 1, jnp.where(j == 1, 0, j))
        row = jnp.where(near == 1, swapped, j)
        return jnp.where(self.a >= 2, ZL - 1 - row, row)


def rows_of(ref, first, count, unit):
    return ref.at[pl.ds(pl.multiple_of(first, unit), count), :]


class RowGather:
    def __init__(self, place, buf, rows, send, recv):
        self.p, self.buf, self.n, self.send, self.recv = place, buf, rows, send, recv

    def block(self, s, b):
        return rows_of(self.buf, (s * X + b) * self.n, self.n, self.n)

    def half(self, s, b, h):
        n = self.n // 2
        return rows_of(self.buf, (s * X + b) * self.n + h * n, n, n)

    def up(self, s):
        ref = self.block(s, self.p.b)
        where = self.p.column(jnp.minimum(self.p.a + 1, ZL - 1))
        return remote(ref, ref, self.send.at[0, s], self.recv.at[0, s], where)

    def down(self, s):
        ref = self.block(s, self.p.b)
        where = self.p.column(jnp.maximum(self.p.a - 1, 0))
        return remote(ref, ref, self.send.at[1, s], self.recv.at[0, s], where)

    def right(self, s):
        ref = self.block(s, self.p.b)
        return remote(ref, ref, self.send.at[2, s], self.recv.at[1, s], self.p.xp)

    def left(self, s):
        ref = self.block(s, self.p.b)
        return remote(ref, ref, self.send.at[3, s], self.recv.at[2, s], self.p.xm)

    def half_right(self, s):
        ref = self.half(s, self.p.bm, 0)
        return remote(ref, ref, self.send.at[4, s], self.recv.at[3, s], self.p.xp)

    def half_left(self, s):
        ref = self.half(s, self.p.bp, 1)
        return remote(ref, ref, self.send.at[5, s], self.recv.at[4, s], self.p.xm)

    def goes_up(self, s):
        return (s <= self.p.a) & (self.p.a < ZL - 1)

    def goes_down(self, s):
        return (s >= self.p.a) & (self.p.a > 0)

    def take_z(self, s):
        @pl.when(s != self.p.a)
        def _():
            self.up(s).wait_recv()

        @pl.when(self.goes_up(s))
        def _():
            self.up(s).start()

        @pl.when(self.goes_down(s))
        def _():
            self.down(s).start()

        self.right(s).start()
        self.left(s).start()

    def take_x(self, s):
        ref = self.block(s, self.p.bm)
        remote(ref, ref, self.send.at[2, s], self.recv.at[1, s], self.p.xm).wait_recv()
        self.half_right(s).start()
        ref = self.block(s, self.p.bp)
        remote(ref, ref, self.send.at[3, s], self.recv.at[2, s], self.p.xp).wait_recv()
        self.half_left(s).start()

    def take_halves(self, s):
        ref = self.half(s, self.p.bo, 0)
        remote(ref, ref, self.send.at[4, s], self.recv.at[3, s], self.p.xm).wait_recv()
        ref = self.half(s, self.p.bo, 1)
        remote(ref, ref, self.send.at[5, s], self.recv.at[4, s], self.p.xp).wait_recv()

    def drain(self):
        def each(s, _):
            @pl.when(self.goes_up(s))
            def _():
                self.up(s).wait_send()

            @pl.when(self.goes_down(s))
            def _():
                self.down(s).wait_send()

            self.right(s).wait_send()
            self.left(s).wait_send()
            self.half_right(s).wait_send()
            self.half_left(s).wait_send()
            return 0

        lax.fori_loop(0, ZL, each, 0)


class RingGather:
    def __init__(self, place, buf, rows, send, recv):
        self.p, self.buf, self.n, self.send, self.recv = place, buf, rows, send, recv

    def ref(self, z, hop, upward):
        z = (z + 2 * ZR) % ZR
        if hop < 4:
            return rows_of(self.buf, z * self.n, self.n, self.n)
        n = self.n // 2
        return rows_of(self.buf, z * self.n + (0 if upward else n), n, n)

    def copies(self, hop):
        up = self.ref(self.p.z - hop + 1, hop, True)
        down = self.ref(self.p.z + hop - 1, hop, False)
        return (
            remote(up, up, self.send.at[0, hop - 1], self.recv.at[0, hop - 1], self.p.zp),
            remote(down, down, self.send.at[1, hop - 1], self.recv.at[1, hop - 1], self.p.zm),
        )

    def start(self, hop):
        for copy in self.copies(hop):
            copy.start()

    def take(self, hop):
        up = self.ref(self.p.z - hop, hop, True)
        down = self.ref(self.p.z + hop, hop, False)
        remote(up, up, self.send.at[0, hop - 1], self.recv.at[0, hop - 1], self.p.zm).wait_recv()
        remote(down, down, self.send.at[1, hop - 1], self.recv.at[1, hop - 1], self.p.zp).wait_recv()

    def drain(self):
        for hop in range(1, 5):
            for copy in self.copies(hop):
                copy.wait_send()


class RingSum:
    def __init__(self, place, buf, land, rows, send, recv):
        self.p, self.buf, self.land = place, buf, land
        self.n, self.send, self.recv = rows, send, recv

    def part(self, z, half):
        z = (z + 2 * ZR) % ZR
        if half is None:
            return rows_of(self.buf, z * self.n, self.n, self.n)
        n = self.n // 2
        return rows_of(self.buf, z * self.n + half * n, n, n)

    def slot(self, way, hop):
        if hop == 1:
            return self.land.at[way, 0, pl.ds(0, self.n // 2), :]
        return self.land.at[way, hop - 1]

    def copies(self, hop):
        half = (0, 1) if hop == 1 else (None, None)
        up = self.part(self.p.z + 5 - hop, half[0])
        down = self.part(self.p.z - 5 + hop, half[1])
        return (
            remote(up, self.slot(0, hop), self.send.at[0, hop - 1], self.recv.at[0, hop - 1], self.p.zp),
            remote(down, self.slot(1, hop), self.send.at[1, hop - 1], self.recv.at[1, hop - 1], self.p.zm),
        )

    def start(self, hop):
        for copy in self.copies(hop):
            copy.start()

    def take(self, hop):
        for copy in self.copies(hop):
            copy.wait_recv()

    def add(self, hop):
        half = (0, 1) if hop == 1 else (None, None)
        for way, z in ((0, self.p.z + 4 - hop), (1, self.p.z - 4 + hop)):
            ref = self.part(z, half[way])
            ref[...] = (ref[...].astype(F32) + self.slot(way, hop)[...].astype(F32)).astype(BF16)

    def drain(self):
        for hop in range(1, 5):
            for copy in self.copies(hop):
                copy.wait_send()


def gain_row(ref):
    return ref[...].astype(F32).reshape(1, -1)


def normed_rows(act, gain):
    values = act.astype(F32)
    return (values * rms_scale(values) * gain).astype(BF16)


def gated(gate_val, up_val):
    return (jax.nn.silu(gate_val) * up_val).astype(BF16)


def at_step(i, step):
    return pl.when(i == step)


def forward_kernel(
    qa, qg, gate_hbm, up_hbm, down_hbm, ia, ig, ig_w, iu_w, id_w,
    hq, hi, qr, ir,
    gate, up, down, nq, pm, r1, r2, zs, zin, acc, ni, wi, ip, land,
    loads, gs, gr, ss, sr, ws, wr, ias, iar, irs, irr,
):
    p = Place()
    n = qa.shape[0]
    m = ia.shape[0]
    k = id_w.shape[0]
    group = X * n
    h = n // 2

    weights = [
        pltpu.make_async_copy(gate_hbm, gate, loads.at[0]),
        pltpu.make_async_copy(up_hbm, up, loads.at[1]),
        pltpu.make_async_copy(down_hbm, down, loads.at[2]),
    ]
    for copy in weights:
        copy.start()
    barrier = pltpu.get_barrier_semaphore()
    for where in (p.xp, p.xm, p.zp, p.zm):
        pl.semaphore_signal(barrier, inc=1, device_id=where, device_id_type=MESH)
    for step in range(1, ZL):
        pl.semaphore_signal(
            barrier, inc=1, device_id=p.column((p.a + step) % ZL), device_id_type=MESH
        )
    nq[pl.ds(pl.multiple_of(p.t * n, n), n), :] = normed_rows(qa[...], gain_row(qg))
    ni[pl.ds(pl.multiple_of(p.z * m, m), m), :] = normed_rows(ia[...], gain_row(ig))
    for index, ref in enumerate((ig_w, iu_w, id_w)):
        wi[index, pl.ds(pl.multiple_of(p.b * k, k), k), :] = ref[...]
    pl.semaphore_wait(barrier, 4 + ZL - 1)

    rows = RowGather(p, nq, n, gs, gr)
    items = RingGather(p, ni, m, ias, iar)
    isum = RingSum(p, ip, land, m, irs, irr)

    def wref(b):
        return wi.at[:, pl.ds(pl.multiple_of(b * k, k), k), :]

    def whalf(b, part):
        return wi.at[:, pl.ds(pl.multiple_of(b * k + part * (k // 2), k // 2), k // 2), :]

    def w_copy(ref, index, where):
        return remote(ref, ref, ws.at[index], wr.at[index], where)

    def block(s, b):
        return rows_of(pm, (s * X + b) * n, n, n)

    def half(s, b, part):
        return rows_of(pm, (s * X + b) * n + part * h, h, h)

    def first_right(s):
        return remote(half(s, p.bo, 0), r1.at[0, s], ss.at[0, s], sr.at[0, s], p.xp)

    def first_left(s):
        return remote(half(s, p.bo, 1), r1.at[1, s], ss.at[1, s], sr.at[1, s], p.xm)

    def second_right(s):
        return remote(block(s, p.bp), r2.at[0, s], ss.at[2, s], sr.at[2, s], p.xp)

    def second_left(s):
        return remote(block(s, p.bm), r2.at[1, s], ss.at[3, s], sr.at[3, s], p.xm)

    def to_owner(s):
        return remote(zs.at[s], zin.at[p.a], ss.at[4, s], sr.at[4, p.a], p.column(s))

    def product(s):
        here = pl.ds(pl.multiple_of(s * group, group), group)
        left = nq[here, :]
        hidden = gated(dot(left, gate[...], ((1,), (1,))), dot(left, up[...], ((1,), (1,))))
        hq[here, :] = hidden
        pm[here, :] = dot(hidden, down[...]).astype(BF16)

    def step(i, _):
        @pl.when(i < ZL)
        def _():
            rows.take_z(p.order(i))

        @at_step(i, 2)
        def _():
            for copy in weights:
                copy.wait()

        @at_step(i, 1)
        def _():
            w_copy(wref(p.b), 0, p.xp).start()
            w_copy(wref(p.b), 1, p.xm).start()

        @pl.when((i >= 1) & (i <= ZL))
        def _():
            rows.take_x(p.order(i - 1))

        for hop in range(1, 5):

            @at_step(i, hop - 1)
            def _():
                if hop > 1:
                    items.take(hop - 1)
                items.start(hop)

        @at_step(i, 3)
        def _():
            w_copy(wref(p.bm), 0, p.xm).wait_recv()
            w_copy(whalf(p.bm, 0), 2, p.xp).start()
            w_copy(wref(p.bp), 1, p.xp).wait_recv()
            w_copy(whalf(p.bp, 1), 3, p.xm).start()

        @pl.when((i >= 2) & (i <= ZL + 1))
        def _():
            s = p.order(i - 2)
            rows.take_halves(s)
            product(s)
            first_right(s).start()
            first_left(s).start()

        @pl.when((i >= 3) & (i <= ZL + 2))
        def _():
            s = p.order(i - 3)
            first_right(s).wait_recv()
            ref = half(s, p.bp, 0)
            ref[...] = (ref[...].astype(F32) + r1[0, s].astype(F32)).astype(BF16)
            second_right(s).start()
            first_left(s).wait_recv()
            ref = half(s, p.bm, 1)
            ref[...] = (ref[...].astype(F32) + r1[1, s].astype(F32)).astype(BF16)
            second_left(s).start()

        @at_step(i, 4)
        def _():
            items.take(4)
            w_copy(whalf(p.bo, 0), 2, p.xm).wait_recv()
            w_copy(whalf(p.bo, 1), 3, p.xp).wait_recv()
            left = ni[...]
            partial = 0.0
            for b in range(X):
                here = slice(b * k, (b + 1) * k)
                gate_val = dot(left, wi[0, here, :], ((1,), (1,)))
                hidden = gated(gate_val, dot(left, wi[1, here, :], ((1,), (1,))))
                hi[b] = hidden
                partial = partial + dot(hidden, wi[2, here, :])
            ip[...] = partial.astype(BF16)
            isum.start(1)

        for hop in range(1, 4):

            @at_step(i, 4 + hop)
            def _():
                isum.take(hop)
                isum.add(hop)
                isum.start(hop + 1)

        @pl.when(i >= 4)
        def _():
            s = p.order(i - 4)
            second_right(s).wait_recv()
            second_left(s).wait_recv()
            total = block(s, p.b)[...].astype(F32) + r2[0, s].astype(F32) + r2[1, s].astype(F32)

            @pl.when(s == p.a)
            def _():
                acc[...] = total

            @pl.when(s != p.a)
            def _():
                zs[s] = total.astype(BF16)
                to_owner(s).start()

        return 0

    lax.fori_loop(0, 2 * ZL, step, 0)

    isum.take(4)
    own = ip[pl.ds(pl.multiple_of(p.z * m, m), m), :].astype(F32)
    ir[...] = ia[...].astype(F32) + (own + land[0, 3].astype(F32) + land[1, 3].astype(F32))

    def collect(step, _):
        s = (p.a + step) % ZL
        remote(zs.at[s], zin.at[s], ss.at[4, s], sr.at[4, s], p.column(s)).wait_recv()
        acc[...] += zin[s].astype(F32)
        return 0

    lax.fori_loop(1, ZL, collect, 0)
    qr[...] = qa[...].astype(F32) + acc[...]

    rows.drain()
    items.drain()
    isum.drain()
    w_copy(wref(p.b), 0, p.xp).wait_send()
    w_copy(wref(p.b), 1, p.xm).wait_send()
    w_copy(whalf(p.bm, 0), 2, p.xp).wait_send()
    w_copy(whalf(p.bp, 1), 3, p.xm).wait_send()

    def drain(s, _):
        first_right(s).wait_send()
        first_left(s).wait_send()
        second_right(s).wait_send()
        second_left(s).wait_send()

        @pl.when(s != p.a)
        def _():
            to_owner(s).wait_send()

        return 0

    lax.fori_loop(0, ZL, drain, 0)


def forward(qa, qg, gate, up, down, ia, ig, ig_w, iu_w, id_w):
    n, dq = qa.shape
    m, di = ia.shape
    k = id_w.shape[0]
    vmem, hbm = pl.BlockSpec(memory_space=pltpu.VMEM), pl.BlockSpec(memory_space=pl.ANY)
    all_q = X * ZL * n
    all_i = ZR * m
    dma = pltpu.SemaphoreType.DMA
    return pl.pallas_call(
        forward_kernel,
        out_shape=(
            jax.ShapeDtypeStruct((all_q, down.shape[0]), BF16),
            jax.ShapeDtypeStruct((X, all_i, k), BF16),
            jax.ShapeDtypeStruct((n, dq), F32),
            jax.ShapeDtypeStruct((m, di), F32),
        ),
        in_specs=[vmem, vmem, hbm, hbm, hbm, vmem, vmem, vmem, vmem, vmem],
        out_specs=[vmem] * 4,
        scratch_shapes=[
            pltpu.VMEM(gate.shape, BF16),
            pltpu.VMEM(up.shape, BF16),
            pltpu.VMEM(down.shape, BF16),
            pltpu.VMEM((all_q, dq), BF16),
            pltpu.VMEM((all_q, dq), BF16),
            pltpu.VMEM((2, ZL, n // 2, dq), BF16),
            pltpu.VMEM((2, ZL, n, dq), BF16),
            pltpu.VMEM((ZL, n, dq), BF16),
            pltpu.VMEM((ZL, n, dq), BF16),
            pltpu.VMEM((n, dq), F32),
            pltpu.VMEM((all_i, di), BF16),
            pltpu.VMEM((3, X * k, di), BF16),
            pltpu.VMEM((all_i, di), BF16),
            pltpu.VMEM((2, 4, m, di), BF16),
            dma((3,)),
            dma((6, ZL)),
            dma((5, ZL)),
            dma((5, ZL)),
            dma((5, ZL)),
            dma((4,)),
            dma((4,)),
            dma((2, 4)),
            dma((2, 4)),
            dma((2, 4)),
            dma((2, 4)),
        ],
        compiler_params=pltpu.CompilerParams(
            collective_id=0, has_side_effects=True, vmem_limit_bytes=VMEM_LIMIT
        ),
        name="towers_forward",
    )(qa, qg, gate, up, down, ia, ig, ig_w, iu_w, id_w)


def split_rows(row):
    high = row.astype(BF16).astype(F32)
    rest = row - high
    mid = rest.astype(BF16).astype(F32)
    low = rest - mid
    index = lax.broadcasted_iota(jnp.int32, (8, row.shape[1]), 0)
    out = jnp.where(index == 0, high, jnp.where(index == 1, mid, jnp.where(index == 2, low, 0.0)))
    return out.astype(BF16)


def unit_scale(vec):
    return lax.rsqrt(jnp.sum(vec * vec, axis=-1, keepdims=True) + EPS)


def unit_back(vec, scales, upstream):
    inner = jnp.sum(vec * upstream, axis=-1, keepdims=True)
    return scales * upstream - vec * (scales * scales * scales) * inner


def contrast(query_hat, item_hat, ranks, positive):
    logits = dot(query_hat, item_hat, ((1,), (1,)), HIGH) / TAU
    shifted = logits - 1.0 / TAU
    log_student = shifted - jnp.log(jnp.sum(jnp.exp(shifted), axis=1, keepdims=True))
    teach = -ranks.astype(F32) / TEACH
    log_teacher = teach - jnp.log(jnp.sum(jnp.exp(teach), axis=1, keepdims=True))
    teacher = jnp.exp(log_teacher)
    columns = lax.broadcasted_iota(jnp.int32, logits.shape, 1)
    onehot = (columns == positive).astype(F32)
    per_row = jnp.sum(
        teacher * (log_teacher - log_student) - onehot * log_student, axis=1, keepdims=True
    )
    slopes = 2.0 * jnp.exp(log_student) - onehot - teacher
    return (per_row, slopes)


def grad_rows(resid, scales, gain, upstream):
    along = gain * upstream
    inner = jnp.mean(along * resid, axis=-1, keepdims=True)
    return (scales * along - resid * (scales * scales * scales) * inner).astype(BF16)


def backward_kernel(
    qr, ir, qf, if_, hq, hi, proj, ranks, positive,
    loss, q_out, i_out,
    sums, hats, nq, ni, gq, gi, qa, qb1, qb2, qc, ia, ib1, ib2, ic,
    s1, r1, s2, r2, gs, gr, ias, iar, qs, qv, bs, bv,
):
    p = Place()
    n, dq = qr.shape
    m, di = ir.shape
    group = X * n
    parts = X * ZL
    own = lax.axis_index("dp") * 2 + p.w
    count = hats.shape[0]

    def member(step):
        return {"tensor": (p.t + step) % parts}

    def replica(step):
        other = (own + step) % count
        return {"dp": other // 2, "tower": other % 2}

    barrier = pltpu.get_barrier_semaphore()

    def greet(step, _):
        pl.semaphore_signal(barrier, inc=1, device_id=member(step), device_id_type=MESH)
        return 0

    def greet_replica(step, _):
        pl.semaphore_signal(barrier, inc=1, device_id=replica(step), device_id_type=MESH)
        return 0

    lax.fori_loop(1, parts, greet, 0)
    lax.fori_loop(1, count, greet_replica, 0)
    for where in (p.zp, p.zm):
        pl.semaphore_signal(barrier, inc=1, device_id=where, device_id_type=MESH)

    q_gain, i_gain = gain_row(qf), gain_row(if_)
    q_resid, i_resid = qr[...], ir[...]
    q_scale, i_scale = rms_scale(q_resid), rms_scale(i_resid)
    sums[p.t, :, :dq] = jnp.sum(q_resid * q_scale * q_gain, axis=0, keepdims=True)
    sums[p.t, :, dq:] = jnp.sum(i_resid * i_scale * i_gain, axis=0, keepdims=True)
    pl.semaphore_wait(barrier, parts + count)

    def spread(step, _):
        remote(sums.at[p.t], sums.at[p.t], s1.at[step], r1.at[p.t], member(step)).start()
        return 0

    def gathered(step, _):
        other = (p.t + step) % parts
        remote(sums.at[p.t], sums.at[other], s1.at[step], r1.at[other], member(step)).wait()
        return 0

    lax.fori_loop(1, parts, spread, 0)
    lax.fori_loop(1, parts, gathered, 0)
    total = sums[0]
    for slot in range(1, parts):
        total = total + sums[slot]
    q_pooled = total[:, :dq] / QLEN
    i_pooled = total[:, dq:] / ILEN
    q_e = jnp.sum(dot(split_rows(q_pooled), proj[...]), axis=0, keepdims=True)
    q_norm, i_norm = unit_scale(q_e), unit_scale(i_pooled)
    hats[own, :, :di] = q_e * q_norm
    hats[own, :, di:] = i_pooled * i_norm

    def spread_hats(step, _):
        remote(hats.at[own], hats.at[own], s2.at[step], r2.at[own], replica(step)).start()
        return 0

    def gathered_hats(step, _):
        other = (own + step) % count
        remote(hats.at[own], hats.at[other], s2.at[step], r2.at[other], replica(step)).wait()
        return 0

    lax.fori_loop(1, count, spread_hats, 0)
    lax.fori_loop(1, count, gathered_hats, 0)
    index = lax.broadcasted_iota(jnp.int32, (count, 2 * di), 0)
    every = jnp.zeros((count, 2 * di), F32)
    for slot in range(count):
        every = jnp.where(index == slot, hats[slot], every)
    every_query, every_items = every[:, :di], every[:, di:]
    line = lax.broadcasted_iota(jnp.int32, (count, count), 0)
    target = jnp.zeros((count, count), jnp.int32)
    for slot in range(count):
        target = jnp.where(line == slot, positive[slot], target)
    per_row, slopes = contrast(every_query, every_items, ranks[...], target)
    loss[...] = jnp.sum(per_row, axis=0, keepdims=True) / count
    weights = slopes * (LOSS_SCALE / (TAU * count))
    mine = lax.broadcasted_iota(jnp.int32, (count, di), 0) == own
    q_back = jnp.sum(
        jnp.where(mine, dot(weights, every_items, precision=HIGH), 0.0), axis=0, keepdims=True
    )
    column = lax.broadcasted_iota(jnp.int32, (count, count), 1) == own
    i_back = jnp.sum(
        jnp.sum(jnp.where(column, weights, 0.0), axis=1, keepdims=True) * every_query,
        axis=0,
        keepdims=True,
    )
    q_grad_e = unit_back(q_e, q_norm, q_back)
    q_up = jnp.sum(dot(split_rows(q_grad_e), proj[...], ((1,), (1,))), axis=0, keepdims=True) / QLEN
    i_up = unit_back(i_pooled, i_norm, i_back) / ILEN
    nq[pl.ds(pl.multiple_of(p.t * n, n), n), :] = grad_rows(q_resid, q_scale, q_gain, q_up)
    ni[pl.ds(pl.multiple_of(p.z * m, m), m), :] = grad_rows(i_resid, i_scale, i_gain, i_up)

    rows = RowGather(p, nq, n, gs, gr)
    items = RingGather(p, ni, m, ias, iar)
    gq[...] = jnp.zeros_like(gq)

    wide = dq // count
    dp = lax.axis_index("dp")
    y, c = dp // 2, dp % 2
    yp, ym, y2 = (y + 1) % 4, (y + 3) % 4, (y + 2) % 4
    line_y = (y2, yp, ym, y)
    to_core = {"dp": y * 2 + 1 - c}
    to_y = ({"dp": yp * 2 + c}, {"dp": ym * 2 + c})
    to_tower = {"tower": 1 - p.w}

    def q_rows(line_of, core):
        return rows_of(gq, (line_of * 2 + core) * 2 * wide, 2 * wide, wide)

    def q_half(line_of, core, tower):
        return rows_of(gq, ((line_of * 2 + core) * 2 + tower) * wide, wide, wide)

    def q_core(j):
        return remote(q_rows(line_y[j], 1 - c), qa.at[j], qs.at[j], qv.at[j], to_core)

    def q_first(way):
        return remote(q_half(y2, c, way), qb1.at[way], qs.at[4 + way], qv.at[4 + way], to_y[way])

    def q_second(way):
        src = q_rows((yp, ym)[way], c)
        return remote(src, qb2.at[way], qs.at[6 + way], qv.at[6 + way], to_y[way])

    def q_tower_ref():
        return q_half(y, c, 1 - p.w)

    def q_tower():
        return remote(q_tower_ref(), qc, qs.at[8], qv.at[8], to_tower)

    def i_rows(line_of, core):
        first = pl.multiple_of((line_of * 2 + core) * wide, wide)
        return gi.at[:, pl.ds(first, wide), :]

    def i_half(line_of, core, way):
        first = pl.multiple_of((line_of * 2 + core) * wide, wide)
        return gi.at[pl.ds(way * 2, 2), pl.ds(first, wide), :]

    def i_slab(b):
        return gi.at[b, pl.ds(pl.multiple_of((y * 2 + c) * wide, wide), wide), :]

    def i_core(j):
        return remote(i_rows(line_y[j], 1 - c), ia.at[j], bs.at[j], bv.at[j], to_core)

    def i_first(way):
        return remote(i_half(y2, c, way), ib1.at[way], bs.at[4 + way], bv.at[4 + way], to_y[way])

    def i_second(way):
        src = i_rows((yp, ym)[way], c)
        return remote(src, ib2.at[way], bs.at[6 + way], bv.at[6 + way], to_y[way])

    def i_x(hop):
        other = (p.b + hop) % X
        where = {"tensor": p.a * X + other}
        return remote(i_slab(other), ic.at[p.b], bs.at[8 + hop], bv.at[8 + p.b], where)

    def take_i_core():
        for j in range(4):
            i_core(j).wait_recv()
            ref = i_rows(line_y[j], c)
            ref[...] += ia[j]
        i_first(0).start()
        i_first(1).start()

    def step(i, _):
        @pl.when(i < ZL)
        def _():
            rows.take_z(p.order(i))

        for hop in range(1, 5):

            @at_step(i, hop - 1)
            def _():
                if hop > 1:
                    items.take(hop - 1)
                items.start(hop)

        @pl.when((i >= 1) & (i <= ZL))
        def _():
            rows.take_x(p.order(i - 1))

        @at_step(i, 4)
        def _():
            items.take(4)
            for b in range(X):
                gi[b] = dot(ni[...], hi[b], ((0,), (0,)))
            for j in range(4):
                i_core(j).start()

        @at_step(i, 5)
        def _():
            take_i_core()

        @pl.when(i >= 2)
        def _():
            s = p.order(i - 2)
            rows.take_halves(s)
            here = pl.ds(pl.multiple_of(s * group, group), group)
            gq[...] += dot(nq[here, :], hq[here, :], ((0,), (0,)))

        return 0

    lax.fori_loop(0, ZL + 2, step, 0)

    for j in range(4):
        q_core(j).start()
    q_core(0).wait_recv()
    far = q_rows(y2, c)
    far[...] += qa[0]
    q_first(0).start()
    q_first(1).start()
    for way in range(2):
        q_core(1 + way).wait_recv()
        near = q_rows((yp, ym)[way], c)
        near[...] += qa[1 + way]
        q_first(way).wait_recv()
        part = q_half((yp, ym)[way], c, way)
        part[...] += qb1[way]
        q_second(way).start()
    for way in range(2):
        i_first(way).wait_recv()
        part = i_half((yp, ym)[way], c, way)
        part[...] += ib1[way]
        i_second(way).start()
    q_core(3).wait_recv()
    theirs = pl.ds(pl.multiple_of((1 - p.w) * wide, wide), wide)
    ours = pl.ds(pl.multiple_of(p.w * wide, wide), wide)
    for way in range(2):
        q_second(way).wait_recv()
    q_tower_ref()[...] = q_tower_ref()[...] + qa[3, theirs, :] + qb2[0, theirs, :] + qb2[1, theirs, :]
    q_tower().start()
    for way in range(2):
        i_second(way).wait_recv()
    own_i = i_rows(y, c)
    own_i[...] = own_i[...] + ib2[0] + ib2[1]
    for hop in range(1, X):
        i_x(hop).start()
    q_own = q_half(y, c, p.w)[...] + qa[3, ours, :] + qb2[0, ours, :] + qb2[1, ours, :]
    i_own = gi[p.b, pl.ds(pl.multiple_of((y * 2 + c) * wide, wide), wide), :]
    for hop in range(1, X):
        other = (p.b + hop) % X
        remote(i_slab(other), ic.at[other], bs.at[8 + hop], bv.at[8 + other], p.xp).wait_recv()
        i_own = i_own + ic[other]
    i_out[...] = i_own
    q_tower().wait_recv()
    q_out[...] = q_own + qc[...]

    rows.drain()
    items.drain()
    for j in range(4):
        q_core(j).wait_send()
        i_core(j).wait_send()
    for way in range(2):
        q_first(way).wait_send()
        q_second(way).wait_send()
        i_first(way).wait_send()
        i_second(way).wait_send()
    for hop in range(1, X):
        i_x(hop).wait_send()
    q_tower().wait_send()


def backward(qr, ir, qf, if_, hq, hi, proj, ranks, positive):
    n, dq = qr.shape
    m, di = ir.shape
    dma = pltpu.SemaphoreType.DMA
    parts = X * ZL
    count = ranks.shape[0]
    wide = dq // count
    f, k = hq.shape[1], hi.shape[2]
    return pl.pallas_call(
        backward_kernel,
        out_shape=(
            jax.ShapeDtypeStruct((1, 1), F32),
            jax.ShapeDtypeStruct((wide, f), F32),
            jax.ShapeDtypeStruct((wide, k), F32),
        ),
        in_specs=[pl.BlockSpec(memory_space=pltpu.VMEM)] * 8 + [pl.BlockSpec(memory_space=pltpu.SMEM)],
        out_specs=[pl.BlockSpec(memory_space=pltpu.VMEM)] * 3,
        scratch_shapes=[
            pltpu.VMEM((parts, 1, dq + di), F32),
            pltpu.VMEM((count, 1, 2 * di), F32),
            pltpu.VMEM((parts * n, dq), BF16),
            pltpu.VMEM((ZR * m, di), BF16),
            pltpu.VMEM((dq, f), F32),
            pltpu.VMEM((X, di, k), F32),
            pltpu.VMEM((4, 2 * wide, f), F32),
            pltpu.VMEM((2, wide, f), F32),
            pltpu.VMEM((2, 2 * wide, f), F32),
            pltpu.VMEM((wide, f), F32),
            pltpu.VMEM((4, X, wide, k), F32),
            pltpu.VMEM((2, 2, wide, k), F32),
            pltpu.VMEM((2, X, wide, k), F32),
            pltpu.VMEM((X, wide, k), F32),
            dma((parts,)),
            dma((parts,)),
            dma((count,)),
            dma((count,)),
            dma((6, ZL)),
            dma((5, ZL)),
            dma((2, 4)),
            dma((2, 4)),
            dma((9,)),
            dma((9,)),
            dma((12,)),
            dma((12,)),
        ],
        compiler_params=pltpu.CompilerParams(
            collective_id=1, has_side_effects=True, vmem_limit_bytes=VMEM_LIMIT
        ),
        name="towers_backward",
    )(qr, ir, qf, if_, hq, hi, proj, ranks, positive)


def body(
    q_act,
    q_norm_gain,
    q_gate,
    q_up,
    q_down,
    q_final_gain,
    projection,
    i_act,
    i_norm_gain,
    i_gate,
    i_up,
    i_down,
    i_final_gain,
    ranks,
    positive,
):
    hq, hi, qr, ir = forward(
        q_act,
        q_norm_gain,
        q_gate.T,
        q_up.T,
        q_down,
        i_act,
        i_norm_gain,
        i_gate.T,
        i_up.T,
        i_down,
    )
    loss, q_grad, i_grad = backward(
        qr, ir, q_final_gain, i_final_gain, hq, hi, projection, ranks, positive
    )
    return (loss.reshape(()), q_grad.T, i_grad.T)


def solution(mesh):
    in_specs = (
        P(("dp", "tower", "tensor"), None),
        P(),
        P(None, "tensor"),
        P(None, "tensor"),
        P("tensor", None),
        P(),
        P(),
        P(("dp", "tower", "tensor"), None),
        P(),
        P(None, ("tower", "tensor")),
        P(None, ("tower", "tensor")),
        P(("tower", "tensor"), None),
        P(),
        P(),
        P(),
    )
    out_specs = (P(), P("tensor", ("dp", "tower")), P(("tower", "tensor"), "dp"))
    return jax.shard_map(body, mesh=mesh, in_specs=in_specs, out_specs=out_specs, check_vma=False)
```

```python
import functools

import jax
import jax.numpy as jnp
from jax import lax
from jax.experimental import pallas as pl
from jax.experimental.pallas import tpu as pltpu
from jax.sharding import PartitionSpec as P

QLEN = 1536
ILEN = 512
EPS = 1e-06
TAU = 0.05
TEACH = 2.0
LOSS_SCALE = 64.0
HIGH = lax.Precision.HIGHEST
MESH = pl.DeviceIdType.MESH
F32 = jnp.float32
BF16 = jnp.bfloat16

X = 4
ZL = 4
ZR = 8
VMEM_LIMIT = 60 * 1024 * 1024


def rms_scale(values):
    return lax.rsqrt(jnp.mean(values * values, axis=-1, keepdims=True) + EPS)


def dot(left, right, dims=((1,), (0,)), precision=None):
    return lax.dot_general(
        left, right, (dims, ((), ())), preferred_element_type=F32, precision=precision
    )


def remote(src, dst, send, recv, where):
    return pltpu.make_async_remote_copy(
        src_ref=src, dst_ref=dst, send_sem=send, recv_sem=recv, device_id=where, device_id_type=MESH
    )


class Place:
    def __init__(self):
        self.t = lax.axis_index("tensor")
        self.w = lax.axis_index("tower")
        self.a = self.t // X
        self.b = self.t % X
        self.z = self.w * ZL + self.a
        self.bp = (self.b + 1) % X
        self.bm = (self.b + X - 1) % X
        self.bo = (self.b + 2) % X
        self.xp = {"tensor": self.a * X + self.bp}
        self.xm = {"tensor": self.a * X + self.bm}
        self.zp = self.ring(1)
        self.zm = self.ring(ZR - 1)

    def ring(self, step):
        z = (self.z + step) % ZR
        return {"tower": z // ZL, "tensor": (z % ZL) * X + self.b}

    def column(self, row):
        return {"tensor": row * X + self.b}

    def order(self, j):
        near = jnp.minimum(self.a, ZL - 1 - self.a)
        swapped = jnp.where(j == 0, 1, jnp.where(j == 1, 0, j))
        row = jnp.where(near == 1, swapped, j)
        return jnp.where(self.a >= 2, ZL - 1 - row, row)


def rows_of(ref, first, count, unit):
    return ref.at[pl.ds(pl.multiple_of(first, unit), count), :]


class RowGather:
    def __init__(self, place, buf, rows, send, recv):
        self.p, self.buf, self.n, self.send, self.recv = place, buf, rows, send, recv

    def block(self, s, b):
        return rows_of(self.buf, (s * X + b) * self.n, self.n, self.n)

    def half(self, s, b, h):
        n = self.n // 2
        return rows_of(self.buf, (s * X + b) * self.n + h * n, n, n)

    def up(self, s):
        ref = self.block(s, self.p.b)
        where = self.p.column(jnp.minimum(self.p.a + 1, ZL - 1))
        return remote(ref, ref, self.send.at[0, s], self.recv.at[0, s], where)

    def down(self, s):
        ref = self.block(s, self.p.b)
        where = self.p.column(jnp.maximum(self.p.a - 1, 0))
        return remote(ref, ref, self.send.at[1, s], self.recv.at[0, s], where)

    def right(self, s):
        ref = self.block(s, self.p.b)
        return remote(ref, ref, self.send.at[2, s], self.recv.at[1, s], self.p.xp)

    def left(self, s):
        ref = self.block(s, self.p.b)
        return remote(ref, ref, self.send.at[3, s], self.recv.at[2, s], self.p.xm)

    def half_right(self, s):
        ref = self.half(s, self.p.bm, 0)
        return remote(ref, ref, self.send.at[4, s], self.recv.at[3, s], self.p.xp)

    def half_left(self, s):
        ref = self.half(s, self.p.bp, 1)
        return remote(ref, ref, self.send.at[5, s], self.recv.at[4, s], self.p.xm)

    def goes_up(self, s):
        return (s <= self.p.a) & (self.p.a < ZL - 1)

    def goes_down(self, s):
        return (s >= self.p.a) & (self.p.a > 0)

    def take_z(self, s):
        @pl.when(s != self.p.a)
        def _():
            self.up(s).wait_recv()

        @pl.when(self.goes_up(s))
        def _():
            self.up(s).start()

        @pl.when(self.goes_down(s))
        def _():
            self.down(s).start()

        self.right(s).start()
        self.left(s).start()

    def take_x(self, s):
        ref = self.block(s, self.p.bm)
        remote(ref, ref, self.send.at[2, s], self.recv.at[1, s], self.p.xm).wait_recv()
        self.half_right(s).start()
        ref = self.block(s, self.p.bp)
        remote(ref, ref, self.send.at[3, s], self.recv.at[2, s], self.p.xp).wait_recv()
        self.half_left(s).start()

    def take_halves(self, s):
        ref = self.half(s, self.p.bo, 0)
        remote(ref, ref, self.send.at[4, s], self.recv.at[3, s], self.p.xm).wait_recv()
        ref = self.half(s, self.p.bo, 1)
        remote(ref, ref, self.send.at[5, s], self.recv.at[4, s], self.p.xp).wait_recv()

    def drain(self):
        def each(s, _):
            @pl.when(self.goes_up(s))
            def _():
                self.up(s).wait_send()

            @pl.when(self.goes_down(s))
            def _():
                self.down(s).wait_send()

            self.right(s).wait_send()
            self.left(s).wait_send()
            self.half_right(s).wait_send()
            self.half_left(s).wait_send()
            return 0

        lax.fori_loop(0, ZL, each, 0)


class RingGather:
    def __init__(self, place, buf, rows, send, recv):
        self.p, self.buf, self.n, self.send, self.recv = place, buf, rows, send, recv

    def ref(self, z, hop, upward):
        z = (z + 2 * ZR) % ZR
        if hop < 4:
            return rows_of(self.buf, z * self.n, self.n, self.n)
        n = self.n // 2
        return rows_of(self.buf, z * self.n + (0 if upward else n), n, n)

    def copies(self, hop):
        up = self.ref(self.p.z - hop + 1, hop, True)
        down = self.ref(self.p.z + hop - 1, hop, False)
        return (
            remote(up, up, self.send.at[0, hop - 1], self.recv.at[0, hop - 1], self.p.zp),
            remote(down, down, self.send.at[1, hop - 1], self.recv.at[1, hop - 1], self.p.zm),
        )

    def start(self, hop):
        for copy in self.copies(hop):
            copy.start()

    def take(self, hop):
        up = self.ref(self.p.z - hop, hop, True)
        down = self.ref(self.p.z + hop, hop, False)
        remote(up, up, self.send.at[0, hop - 1], self.recv.at[0, hop - 1], self.p.zm).wait_recv()
        remote(down, down, self.send.at[1, hop - 1], self.recv.at[1, hop - 1], self.p.zp).wait_recv()

    def drain(self):
        for hop in range(1, 5):
            for copy in self.copies(hop):
                copy.wait_send()


class RingSum:
    def __init__(self, place, buf, land, rows, send, recv):
        self.p, self.buf, self.land = place, buf, land
        self.n, self.send, self.recv = rows, send, recv

    def part(self, z, half):
        z = (z + 2 * ZR) % ZR
        if half is None:
            return rows_of(self.buf, z * self.n, self.n, self.n)
        n = self.n // 2
        return rows_of(self.buf, z * self.n + half * n, n, n)

    def slot(self, way, hop):
        if hop == 1:
            return self.land.at[way, 0, pl.ds(0, self.n // 2), :]
        return self.land.at[way, hop - 1]

    def copies(self, hop):
        half = (0, 1) if hop == 1 else (None, None)
        up = self.part(self.p.z + 5 - hop, half[0])
        down = self.part(self.p.z - 5 + hop, half[1])
        return (
            remote(up, self.slot(0, hop), self.send.at[0, hop - 1], self.recv.at[0, hop - 1], self.p.zp),
            remote(down, self.slot(1, hop), self.send.at[1, hop - 1], self.recv.at[1, hop - 1], self.p.zm),
        )

    def start(self, hop):
        for copy in self.copies(hop):
            copy.start()

    def take(self, hop):
        for copy in self.copies(hop):
            copy.wait_recv()

    def add(self, hop):
        half = (0, 1) if hop == 1 else (None, None)
        for way, z in ((0, self.p.z + 4 - hop), (1, self.p.z - 4 + hop)):
            ref = self.part(z, half[way])
            ref[...] = (ref[...].astype(F32) + self.slot(way, hop)[...].astype(F32)).astype(BF16)

    def drain(self):
        for hop in range(1, 5):
            for copy in self.copies(hop):
                copy.wait_send()


def gain_row(ref):
    return ref[...].astype(F32).reshape(1, -1)


def normed_rows(act, gain):
    values = act.astype(F32)
    return (values * rms_scale(values) * gain).astype(BF16)


def gated(gate_val, up_val):
    return (jax.nn.silu(gate_val) * up_val).astype(BF16)


def at_step(i, step):
    return pl.when(i == step)


def forward_kernel(
    qa, qg, gate_hbm, up_hbm, down_hbm, ia, ig, ig_w, iu_w, id_w,
    hq, hi, qr, ir,
    w, nq, part, h2, pm, r1, r2, zs, zin, ni, wi, ip, land,
    loads, gs, gr, ss, sr, ws, wr, vs, vr, hs, hr, ias, iar, irs, irr,
):
    p = Place()
    n, dq = qa.shape
    m, di = ia.shape
    f, k = down_hbm.shape[0], id_w.shape[0]
    group = X * n
    h = n // 2
    piece = w.shape[2] // 4
    wide, thin = dq // 2, dq // 4
    dp = lax.axis_index("dp")
    y, c = dp // 2, dp % 2
    yp, ym, y2 = (y + 1) % 4, (y + 3) % 4, (y + 2) % 4
    to_yp, to_ym, to_core = {"dp": yp * 2 + c}, {"dp": ym * 2 + c}, {"dp": y * 2 + 1 - c}
    a2 = (p.a + 2) % ZL
    mate = p.a + 1 - 2 * (p.a % 2)
    to_a2, to_mate = p.column(a2), p.column(mate)

    own_weights = [
        pltpu.make_async_copy(ref, w.at[0, index, pl.ds(0, f), :], loads.at[index])
        for index, ref in enumerate((gate_hbm, up_hbm, down_hbm))
    ]
    for copy in own_weights:
        copy.start()
    barrier = pltpu.get_barrier_semaphore()
    friends = (p.xp, p.xm, p.zp, p.zm, to_a2, to_mate, to_yp, to_ym, to_core)
    for where in friends:
        pl.semaphore_signal(barrier, inc=1, device_id=where, device_id_type=MESH)
    for index in range(3):
        w[0, index, f:, :] = jnp.zeros((w.shape[2] - f, dq), BF16)
    nq[pl.ds(pl.multiple_of(p.b * n, n), n), :] = normed_rows(qa[...], gain_row(qg))
    ni[pl.ds(pl.multiple_of(p.z * m, m), m), :] = normed_rows(ia[...], gain_row(ig))
    for index, ref in enumerate((ig_w, iu_w, id_w)):
        wi[index, pl.ds(pl.multiple_of(p.b * k, k), k), :] = ref[...]
    pl.semaphore_wait(barrier, len(friends))

    rows = RowGather(p, nq, n, gs, gr)
    items = RingGather(p, ni, m, ias, iar)
    isum = RingSum(p, ip, land, m, irs, irr)

    def across():
        return remote(rows.block(0, p.b), rows.block(1, p.b), gs.at[0, 0], gr.at[0, 0], to_a2)

    def wpiece(which, index, line, core):
        first = pl.multiple_of(line * piece, piece)
        return w.at[which, index, pl.ds(first, piece), pl.ds(pl.multiple_of(core * wide, wide), wide)]

    def whalf(index, line, part_of):
        first = pl.multiple_of(line * piece, piece)
        column = pl.multiple_of(c * wide + part_of * thin, thin)
        return w.at[1, index, pl.ds(first, piece), pl.ds(column, thin)]

    def w_send(index, kind):
        here = wpiece(1, index, y, c)
        low, high = wpiece(1, index, ym, c), wpiece(1, index, yp, c)
        src, dst, where = (
            (wpiece(0, index, y, c), here, to_mate),
            (here, here, to_yp),
            (here, here, to_ym),
            (whalf(index, ym, 0), whalf(index, ym, 0), to_yp),
            (whalf(index, yp, 1), whalf(index, yp, 1), to_ym),
            (here, here, to_core),
            (low, low, to_core),
            (high, high, to_core),
            (wpiece(1, index, y2, c), wpiece(1, index, y2, c), to_core),
        )[kind]
        return remote(src, dst, ws.at[kind, index], wr.at[kind, index], where)

    def w_got(index, kind):
        dst = (
            wpiece(1, index, y, c),
            wpiece(1, index, ym, c),
            wpiece(1, index, yp, c),
            whalf(index, y2, 0),
            whalf(index, y2, 1),
            wpiece(1, index, y, 1 - c),
            wpiece(1, index, ym, 1 - c),
            wpiece(1, index, yp, 1 - c),
            wpiece(1, index, y2, 1 - c),
        )[kind]
        remote(dst, dst, ws.at[kind, index], wr.at[kind, index], to_core).wait_recv()

    def w_near(index):
        w_got(index, 0)
        for kind in (1, 2, 5):
            w_send(index, kind).start()

    def w_ring(index):
        w_got(index, 1)
        w_send(index, 3).start()
        w_send(index, 6).start()
        w_got(index, 2)
        w_send(index, 4).start()
        w_send(index, 7).start()

    def w_far(index):
        w_got(index, 3)
        w_got(index, 4)
        w_send(index, 8).start()

    def w_done(index):
        for kind in (5, 6, 7, 8):
            w_got(index, kind)

    def vpiece(b, core):
        column = pl.multiple_of(core * (di // 2), di // 2)
        return wi.at[:, pl.ds(pl.multiple_of(b * k, k), k), pl.ds(column, di // 2)]

    def vhalf(b, part_of):
        first = pl.multiple_of(b * k + part_of * (k // 2), k // 2)
        column = pl.multiple_of(c * (di // 2), di // 2)
        return wi.at[:, pl.ds(first, k // 2), pl.ds(column, di // 2)]

    def v_send(kind):
        ref, where = (
            (vpiece(p.b, c), p.xp),
            (vpiece(p.b, c), p.xm),
            (vhalf(p.bm, 0), p.xp),
            (vhalf(p.bp, 1), p.xm),
            (vpiece(p.bm, c), to_core),
            (vpiece(p.bp, c), to_core),
            (vpiece(p.bo, c), to_core),
        )[kind]
        return remote(ref, ref, vs.at[kind], vr.at[kind], where)

    def v_got(kind):
        ref = (
            vpiece(p.bm, c),
            vpiece(p.bp, c),
            vhalf(p.bo, 0),
            vhalf(p.bo, 1),
            vpiece(p.bm, 1 - c),
            vpiece(p.bp, 1 - c),
            vpiece(p.bo, 1 - c),
        )[kind]
        remote(ref, ref, vs.at[kind], vr.at[kind], to_core).wait_recv()

    def block(j, b):
        return rows_of(pm, (j * X + b) * n, n, n)

    def half(j, b, part_of):
        return rows_of(pm, (j * X + b) * n + part_of * h, h, h)

    def first(j, way):
        src = half(j, p.bo, way)
        return remote(src, r1.at[way, j], ss.at[way, j], sr.at[way, j], (p.xp, p.xm)[way])

    def second(j, way):
        src = block(j, (p.bp, p.bm)[way])
        return remote(src, r2.at[way, j], ss.at[2 + way, j], sr.at[2 + way, j], (p.xp, p.xm)[way])

    def to_owner():
        return remote(zs, zin, ss.at[4, 0], sr.at[4, 0], to_a2)

    def back(j):
        s = (p.a, a2)[j]
        dst = hq.at[pl.ds(pl.multiple_of(s * group, group), group), :]
        return remote(h2.at[j], dst, hs.at[j], hr.at[j], to_mate)

    def back_got(j):
        other = (mate, (mate + 2) % ZL)[j]
        dst = hq.at[pl.ds(pl.multiple_of(other * group, group), group), :]
        remote(h2.at[j], dst, hs.at[j], hr.at[j], to_mate).wait_recv()

    def hidden(which, j):
        left = nq[j * group : (j + 1) * group, :]
        gate_val = dot(left, w[which, 0, :f, :], ((1,), (1,)))
        return gated(gate_val, dot(left, w[which, 1, :f, :], ((1,), (1,))))

    def own_units(j):
        value = hidden(0, j)
        hq[pl.ds(pl.multiple_of((p.a, a2)[j] * group, group), group), :] = value
        part[j] = dot(value, w[0, 2, :f, :])

    def mate_units(j):
        value = hidden(1, j)
        h2[j] = value
        total = part[j] + dot(value, w[1, 2, :f, :])
        pm[j * group : (j + 1) * group, :] = total.astype(BF16)
        first(j, 0).start()
        first(j, 1).start()
        back(j).start()

    def combine(j):
        for way in range(2):
            first(j, way).wait_recv()
            ref = half(j, (p.bp, p.bm)[way], way)
            ref[...] = (ref[...].astype(F32) + r1[way, j].astype(F32)).astype(BF16)
            second(j, way).start()

    def summed(j):
        second(j, 0).wait_recv()
        second(j, 1).wait_recv()
        return block(j, p.b)[...].astype(F32) + r2[0, j].astype(F32) + r2[1, j].astype(F32)

    def item_product():
        left = ni[...]
        partial = 0.0
        for b in range(X):
            here = slice(b * k, (b + 1) * k)
            gate_val = dot(left, wi[0, here, :], ((1,), (1,)))
            value = gated(gate_val, dot(left, wi[1, here, :], ((1,), (1,))))
            hi[b] = value
            partial = partial + dot(value, wi[2, here, :])
        ip[...] = partial.astype(BF16)

    rows.right(0).start()
    rows.left(0).start()
    across().start()
    items.start(1)
    for index in range(3):
        own_weights[index].wait()
        w_send(index, 0).start()
    v_send(0).start()
    v_send(1).start()
    rows.take_x(0)
    w_near(0)
    items.take(1)
    items.start(2)
    remote(rows.block(0, p.b), rows.block(1, p.b), gs.at[0, 0], gr.at[0, 0], to_a2).wait_recv()
    rows.right(1).start()
    rows.left(1).start()
    w_near(1)
    rows.take_halves(0)
    own_units(0)
    w_ring(0)
    w_near(2)
    for kind in range(2):
        v_got(kind)
        v_send(2 + kind).start()
        v_send(4 + kind).start()
    items.take(2)
    items.start(3)
    rows.take_x(1)
    w_far(0)
    w_ring(1)
    rows.take_halves(1)
    items.take(3)
    items.start(4)
    own_units(1)
    w_far(1)
    w_ring(2)
    v_got(2)
    v_got(3)
    v_send(6).start()
    w_far(2)
    for index in range(3):
        w_done(index)
    mate_units(1)
    mate_units(0)
    combine(1)
    items.take(4)
    for kind in (4, 5, 6):
        v_got(kind)
    item_product()
    isum.start(1)
    combine(0)
    isum.take(1)
    isum.add(1)
    isum.start(2)
    zs[...] = summed(1).astype(BF16)
    to_owner().start()
    isum.take(2)
    isum.add(2)
    isum.start(3)
    mlp = summed(0)
    isum.take(3)
    isum.add(3)
    isum.start(4)
    to_owner().wait_recv()
    qr[...] = qa[...].astype(F32) + (mlp + zin[...].astype(F32))
    isum.take(4)
    own = ip[pl.ds(pl.multiple_of(p.z * m, m), m), :].astype(F32)
    ir[...] = ia[...].astype(F32) + (own + land[0, 3].astype(F32) + land[1, 3].astype(F32))

    for j in range(2):
        back_got(j)
        back(j).wait_send()
        for copy in (rows.right(j), rows.left(j), rows.half_right(j), rows.half_left(j)):
            copy.wait_send()
        for way in range(2):
            first(j, way).wait_send()
            second(j, way).wait_send()
    across().wait_send()
    to_owner().wait_send()
    items.drain()
    isum.drain()
    for index in range(3):
        for kind in range(9):
            w_send(index, kind).wait_send()
    for kind in range(7):
        v_send(kind).wait_send()


def forward(qa, qg, gate, up, down, ia, ig, ig_w, iu_w, id_w):
    n, dq = qa.shape
    m, di = ia.shape
    f, k = down.shape[0], id_w.shape[0]
    padded = 64 * ((f + 63) // 64)
    vmem, hbm = pl.BlockSpec(memory_space=pltpu.VMEM), pl.BlockSpec(memory_space=pl.ANY)
    all_i = ZR * m
    group = X * n
    dma = pltpu.SemaphoreType.DMA
    return pl.pallas_call(
        forward_kernel,
        out_shape=(
            jax.ShapeDtypeStruct((ZL * group, f), BF16),
            jax.ShapeDtypeStruct((X, all_i, k), BF16),
            jax.ShapeDtypeStruct((n, dq), F32),
            jax.ShapeDtypeStruct((m, di), F32),
        ),
        in_specs=[vmem, vmem, hbm, hbm, hbm, vmem, vmem, vmem, vmem, vmem],
        out_specs=[vmem] * 4,
        scratch_shapes=[
            pltpu.VMEM((2, 3, padded, dq), BF16),
            pltpu.VMEM((2 * group, dq), BF16),
            pltpu.VMEM((2, group, dq), F32),
            pltpu.VMEM((2, group, f), BF16),
            pltpu.VMEM((2 * group, dq), BF16),
            pltpu.VMEM((2, 2, n // 2, dq), BF16),
            pltpu.VMEM((2, 2, n, dq), BF16),
            pltpu.VMEM((n, dq), BF16),
            pltpu.VMEM((n, dq), BF16),
            pltpu.VMEM((all_i, di), BF16),
            pltpu.VMEM((3, X * k, di), BF16),
            pltpu.VMEM((all_i, di), BF16),
            pltpu.VMEM((2, 4, m, di), BF16),
            dma((3,)),
            dma((6, 2)),
            dma((5, 2)),
            dma((5, 2)),
            dma((5, 2)),
            dma((9, 3)),
            dma((9, 3)),
            dma((7,)),
            dma((7,)),
            dma((2,)),
            dma((2,)),
            dma((2, 4)),
            dma((2, 4)),
            dma((2, 4)),
            dma((2, 4)),
        ],
        compiler_params=pltpu.CompilerParams(
            collective_id=0, has_side_effects=True, vmem_limit_bytes=VMEM_LIMIT
        ),
        name="towers_forward",
    )(qa, qg, gate, up, down, ia, ig, ig_w, iu_w, id_w)


def split_rows(row):
    high = row.astype(BF16).astype(F32)
    rest = row - high
    mid = rest.astype(BF16).astype(F32)
    low = rest - mid
    index = lax.broadcasted_iota(jnp.int32, (8, row.shape[1]), 0)
    out = jnp.where(index == 0, high, jnp.where(index == 1, mid, jnp.where(index == 2, low, 0.0)))
    return out.astype(BF16)


def unit_scale(vec):
    return lax.rsqrt(jnp.sum(vec * vec, axis=-1, keepdims=True) + EPS)


def unit_back(vec, scales, upstream):
    inner = jnp.sum(vec * upstream, axis=-1, keepdims=True)
    return scales * upstream - vec * (scales * scales * scales) * inner


def contrast(query_hat, item_hat, ranks, positive):
    logits = dot(query_hat, item_hat, ((1,), (1,)), HIGH) / TAU
    shifted = logits - 1.0 / TAU
    log_student = shifted - jnp.log(jnp.sum(jnp.exp(shifted), axis=1, keepdims=True))
    teach = -ranks.astype(F32) / TEACH
    log_teacher = teach - jnp.log(jnp.sum(jnp.exp(teach), axis=1, keepdims=True))
    teacher = jnp.exp(log_teacher)
    columns = lax.broadcasted_iota(jnp.int32, logits.shape, 1)
    onehot = (columns == positive).astype(F32)
    per_row = jnp.sum(
        teacher * (log_teacher - log_student) - onehot * log_student, axis=1, keepdims=True
    )
    slopes = 2.0 * jnp.exp(log_student) - onehot - teacher
    return (per_row, slopes)


def grad_rows(resid, scales, gain, upstream):
    along = gain * upstream
    inner = jnp.mean(along * resid, axis=-1, keepdims=True)
    return (scales * along - resid * (scales * scales * scales) * inner).astype(BF16)


def backward_kernel(
    qr, ir, qf, if_, hq, hi, proj, ranks, positive,
    loss, q_out, i_out,
    sums, hats, nq, ni, gq, gi, qa, qb1, qb2, qc, ia, ib1, ib2, ic,
    s1, r1, s2, r2, gs, gr, ias, iar, qs, qv, bs, bv,
):
    p = Place()
    n, dq = qr.shape
    m, di = ir.shape
    group = X * n
    parts = X * ZL
    own = lax.axis_index("dp") * 2 + p.w
    count = hats.shape[0]

    def member(step):
        return {"tensor": (p.t + step) % parts}

    def replica(step):
        other = (own + step) % count
        return {"dp": other // 2, "tower": other % 2}

    barrier = pltpu.get_barrier_semaphore()

    def greet(step, _):
        pl.semaphore_signal(barrier, inc=1, device_id=member(step), device_id_type=MESH)
        return 0

    def greet_replica(step, _):
        pl.semaphore_signal(barrier, inc=1, device_id=replica(step), device_id_type=MESH)
        return 0

    lax.fori_loop(1, parts, greet, 0)
    lax.fori_loop(1, count, greet_replica, 0)
    for where in (p.zp, p.zm):
        pl.semaphore_signal(barrier, inc=1, device_id=where, device_id_type=MESH)

    q_gain, i_gain = gain_row(qf), gain_row(if_)
    q_resid, i_resid = qr[...], ir[...]
    q_scale, i_scale = rms_scale(q_resid), rms_scale(i_resid)
    sums[p.t, :, :dq] = jnp.sum(q_resid * q_scale * q_gain, axis=0, keepdims=True)
    sums[p.t, :, dq:] = jnp.sum(i_resid * i_scale * i_gain, axis=0, keepdims=True)
    pl.semaphore_wait(barrier, parts + count)

    def spread(step, _):
        remote(sums.at[p.t], sums.at[p.t], s1.at[step], r1.at[p.t], member(step)).start()
        return 0

    def gathered(step, _):
        other = (p.t + step) % parts
        remote(sums.at[p.t], sums.at[other], s1.at[step], r1.at[other], member(step)).wait()
        return 0

    lax.fori_loop(1, parts, spread, 0)
    lax.fori_loop(1, parts, gathered, 0)
    total = sums[0]
    for slot in range(1, parts):
        total = total + sums[slot]
    q_pooled = total[:, :dq] / QLEN
    i_pooled = total[:, dq:] / ILEN
    q_e = jnp.sum(dot(split_rows(q_pooled), proj[...]), axis=0, keepdims=True)
    q_norm, i_norm = unit_scale(q_e), unit_scale(i_pooled)
    hats[own, :, :di] = q_e * q_norm
    hats[own, :, di:] = i_pooled * i_norm

    def spread_hats(step, _):
        remote(hats.at[own], hats.at[own], s2.at[step], r2.at[own], replica(step)).start()
        return 0

    def gathered_hats(step, _):
        other = (own + step) % count
        remote(hats.at[own], hats.at[other], s2.at[step], r2.at[other], replica(step)).wait()
        return 0

    lax.fori_loop(1, count, spread_hats, 0)
    lax.fori_loop(1, count, gathered_hats, 0)
    index = lax.broadcasted_iota(jnp.int32, (count, 2 * di), 0)
    every = jnp.zeros((count, 2 * di), F32)
    for slot in range(count):
        every = jnp.where(index == slot, hats[slot], every)
    every_query, every_items = every[:, :di], every[:, di:]
    line = lax.broadcasted_iota(jnp.int32, (count, count), 0)
    target = jnp.zeros((count, count), jnp.int32)
    for slot in range(count):
        target = jnp.where(line == slot, positive[slot], target)
    per_row, slopes = contrast(every_query, every_items, ranks[...], target)
    loss[...] = jnp.sum(per_row, axis=0, keepdims=True) / count
    weights = slopes * (LOSS_SCALE / (TAU * count))
    mine = lax.broadcasted_iota(jnp.int32, (count, di), 0) == own
    q_back = jnp.sum(
        jnp.where(mine, dot(weights, every_items, precision=HIGH), 0.0), axis=0, keepdims=True
    )
    column = lax.broadcasted_iota(jnp.int32, (count, count), 1) == own
    i_back = jnp.sum(
        jnp.sum(jnp.where(column, weights, 0.0), axis=1, keepdims=True) * every_query,
        axis=0,
        keepdims=True,
    )
    q_grad_e = unit_back(q_e, q_norm, q_back)
    q_up = jnp.sum(dot(split_rows(q_grad_e), proj[...], ((1,), (1,))), axis=0, keepdims=True) / QLEN
    i_up = unit_back(i_pooled, i_norm, i_back) / ILEN
    nq[pl.ds(pl.multiple_of(p.t * n, n), n), :] = grad_rows(q_resid, q_scale, q_gain, q_up)
    ni[pl.ds(pl.multiple_of(p.z * m, m), m), :] = grad_rows(i_resid, i_scale, i_gain, i_up)

    rows = RowGather(p, nq, n, gs, gr)
    items = RingGather(p, ni, m, ias, iar)
    gq[...] = jnp.zeros_like(gq)

    wide = dq // count
    dp = lax.axis_index("dp")
    y, c = dp // 2, dp % 2
    yp, ym, y2 = (y + 1) % 4, (y + 3) % 4, (y + 2) % 4
    line_y = (y2, yp, ym, y)
    to_core = {"dp": y * 2 + 1 - c}
    to_y = ({"dp": yp * 2 + c}, {"dp": ym * 2 + c})
    to_tower = {"tower": 1 - p.w}

    def q_rows(line_of, core):
        return rows_of(gq, (line_of * 2 + core) * 2 * wide, 2 * wide, wide)

    def q_half(line_of, core, tower):
        return rows_of(gq, ((line_of * 2 + core) * 2 + tower) * wide, wide, wide)

    def q_core(j):
        return remote(q_rows(line_y[j], 1 - c), qa.at[j], qs.at[j], qv.at[j], to_core)

    def q_first(way):
        return remote(q_half(y2, c, way), qb1.at[way], qs.at[4 + way], qv.at[4 + way], to_y[way])

    def q_second(way):
        src = q_rows((yp, ym)[way], c)
        return remote(src, qb2.at[way], qs.at[6 + way], qv.at[6 + way], to_y[way])

    def q_tower_ref():
        return q_half(y, c, 1 - p.w)

    def q_tower():
        return remote(q_tower_ref(), qc, qs.at[8], qv.at[8], to_tower)

    def i_rows(line_of, core):
        first = pl.multiple_of((line_of * 2 + core) * wide, wide)
        return gi.at[:, pl.ds(first, wide), :]

    def i_half(line_of, core, way):
        first = pl.multiple_of((line_of * 2 + core) * wide, wide)
        return gi.at[pl.ds(way * 2, 2), pl.ds(first, wide), :]

    def i_slab(b):
        return gi.at[b, pl.ds(pl.multiple_of((y * 2 + c) * wide, wide), wide), :]

    def i_core(j):
        return remote(i_rows(line_y[j], 1 - c), ia.at[j], bs.at[j], bv.at[j], to_core)

    def i_first(way):
        return remote(i_half(y2, c, way), ib1.at[way], bs.at[4 + way], bv.at[4 + way], to_y[way])

    def i_second(way):
        src = i_rows((yp, ym)[way], c)
        return remote(src, ib2.at[way], bs.at[6 + way], bv.at[6 + way], to_y[way])

    def i_x(hop):
        other = (p.b + hop) % X
        where = {"tensor": p.a * X + other}
        return remote(i_slab(other), ic.at[p.b], bs.at[8 + hop], bv.at[8 + p.b], where)

    def take_i_core():
        for j in range(4):
            i_core(j).wait_recv()
            ref = i_rows(line_y[j], c)
            ref[...] += ia[j]
        i_first(0).start()
        i_first(1).start()

    def step(i, _):
        @pl.when(i < ZL)
        def _():
            rows.take_z(p.order(i))

        for hop in range(1, 5):

            @at_step(i, hop - 1)
            def _():
                if hop > 1:
                    items.take(hop - 1)
                items.start(hop)

        @pl.when((i >= 1) & (i <= ZL))
        def _():
            rows.take_x(p.order(i - 1))

        @at_step(i, 4)
        def _():
            items.take(4)
            for b in range(X):
                gi[b] = dot(ni[...], hi[b], ((0,), (0,)))
            for j in range(4):
                i_core(j).start()

        @at_step(i, 5)
        def _():
            take_i_core()

        @pl.when(i >= 2)
        def _():
            s = p.order(i - 2)
            rows.take_halves(s)
            here = pl.ds(pl.multiple_of(s * group, group), group)
            gq[...] += dot(nq[here, :], hq[here, :], ((0,), (0,)))

        return 0

    lax.fori_loop(0, ZL + 2, step, 0)

    for j in range(4):
        q_core(j).start()
    q_core(0).wait_recv()
    far = q_rows(y2, c)
    far[...] += qa[0]
    q_first(0).start()
    q_first(1).start()
    for way in range(2):
        q_core(1 + way).wait_recv()
        near = q_rows((yp, ym)[way], c)
        near[...] += qa[1 + way]
        q_first(way).wait_recv()
        part = q_half((yp, ym)[way], c, way)
        part[...] += qb1[way]
        q_second(way).start()
    for way in range(2):
        i_first(way).wait_recv()
        part = i_half((yp, ym)[way], c, way)
        part[...] += ib1[way]
        i_second(way).start()
    q_core(3).wait_recv()
    theirs = pl.ds(pl.multiple_of((1 - p.w) * wide, wide), wide)
    ours = pl.ds(pl.multiple_of(p.w * wide, wide), wide)
    for way in range(2):
        q_second(way).wait_recv()
    q_tower_ref()[...] = q_tower_ref()[...] + qa[3, theirs, :] + qb2[0, theirs, :] + qb2[1, theirs, :]
    q_tower().start()
    for way in range(2):
        i_second(way).wait_recv()
    own_i = i_rows(y, c)
    own_i[...] = own_i[...] + ib2[0] + ib2[1]
    for hop in range(1, X):
        i_x(hop).start()
    q_own = q_half(y, c, p.w)[...] + qa[3, ours, :] + qb2[0, ours, :] + qb2[1, ours, :]
    i_own = gi[p.b, pl.ds(pl.multiple_of((y * 2 + c) * wide, wide), wide), :]
    for hop in range(1, X):
        other = (p.b + hop) % X
        remote(i_slab(other), ic.at[other], bs.at[8 + hop], bv.at[8 + other], p.xp).wait_recv()
        i_own = i_own + ic[other]
    i_out[...] = i_own
    q_tower().wait_recv()
    q_out[...] = q_own + qc[...]

    rows.drain()
    items.drain()
    for j in range(4):
        q_core(j).wait_send()
        i_core(j).wait_send()
    for way in range(2):
        q_first(way).wait_send()
        q_second(way).wait_send()
        i_first(way).wait_send()
        i_second(way).wait_send()
    for hop in range(1, X):
        i_x(hop).wait_send()
    q_tower().wait_send()


def backward(qr, ir, qf, if_, hq, hi, proj, ranks, positive):
    n, dq = qr.shape
    m, di = ir.shape
    dma = pltpu.SemaphoreType.DMA
    parts = X * ZL
    count = ranks.shape[0]
    wide = dq // count
    f, k = hq.shape[1], hi.shape[2]
    return pl.pallas_call(
        backward_kernel,
        out_shape=(
            jax.ShapeDtypeStruct((1, 1), F32),
            jax.ShapeDtypeStruct((wide, f), F32),
            jax.ShapeDtypeStruct((wide, k), F32),
        ),
        in_specs=[pl.BlockSpec(memory_space=pltpu.VMEM)] * 8 + [pl.BlockSpec(memory_space=pltpu.SMEM)],
        out_specs=[pl.BlockSpec(memory_space=pltpu.VMEM)] * 3,
        scratch_shapes=[
            pltpu.VMEM((parts, 1, dq + di), F32),
            pltpu.VMEM((count, 1, 2 * di), F32),
            pltpu.VMEM((parts * n, dq), BF16),
            pltpu.VMEM((ZR * m, di), BF16),
            pltpu.VMEM((dq, f), F32),
            pltpu.VMEM((X, di, k), F32),
            pltpu.VMEM((4, 2 * wide, f), F32),
            pltpu.VMEM((2, wide, f), F32),
            pltpu.VMEM((2, 2 * wide, f), F32),
            pltpu.VMEM((wide, f), F32),
            pltpu.VMEM((4, X, wide, k), F32),
            pltpu.VMEM((2, 2, wide, k), F32),
            pltpu.VMEM((2, X, wide, k), F32),
            pltpu.VMEM((X, wide, k), F32),
            dma((parts,)),
            dma((parts,)),
            dma((count,)),
            dma((count,)),
            dma((6, ZL)),
            dma((5, ZL)),
            dma((2, 4)),
            dma((2, 4)),
            dma((9,)),
            dma((9,)),
            dma((12,)),
            dma((12,)),
        ],
        compiler_params=pltpu.CompilerParams(
            collective_id=1, has_side_effects=True, vmem_limit_bytes=VMEM_LIMIT
        ),
        name="towers_backward",
    )(qr, ir, qf, if_, hq, hi, proj, ranks, positive)


def body(
    q_act,
    q_norm_gain,
    q_gate,
    q_up,
    q_down,
    q_final_gain,
    projection,
    i_act,
    i_norm_gain,
    i_gate,
    i_up,
    i_down,
    i_final_gain,
    ranks,
    positive,
):
    hq, hi, qr, ir = forward(
        q_act,
        q_norm_gain,
        q_gate.T,
        q_up.T,
        q_down,
        i_act,
        i_norm_gain,
        i_gate.T,
        i_up.T,
        i_down,
    )
    loss, q_grad, i_grad = backward(
        qr, ir, q_final_gain, i_final_gain, hq, hi, projection, ranks, positive
    )
    return (loss.reshape(()), q_grad.T, i_grad.T)


def solution(mesh):
    in_specs = (
        P(("dp", "tower", "tensor"), None),
        P(),
        P(None, "tensor"),
        P(None, "tensor"),
        P("tensor", None),
        P(),
        P(),
        P(("dp", "tower", "tensor"), None),
        P(),
        P(None, ("tower", "tensor")),
        P(None, ("tower", "tensor")),
        P(("tower", "tensor"), None),
        P(),
        P(),
        P(),
    )
    out_specs = (P(), P("tensor", ("dp", "tower")), P(("tower", "tensor"), "dp"))
    return jax.shard_map(body, mesh=mesh, in_specs=in_specs, out_specs=out_specs, check_vma=False)
```

```python
import functools

import jax
import jax.numpy as jnp
from jax import lax
from jax.experimental import pallas as pl
from jax.experimental.pallas import tpu as pltpu
from jax.sharding import PartitionSpec as P

QLEN = 1536
ILEN = 512
EPS = 1e-06
TAU = 0.05
TEACH = 2.0
LOSS_SCALE = 64.0
HIGH = lax.Precision.HIGHEST
MESH = pl.DeviceIdType.MESH
F32 = jnp.float32
BF16 = jnp.bfloat16

X = 4
ZL = 4
ZR = 8
VMEM_LIMIT = 60 * 1024 * 1024


def rms_scale(values):
    return lax.rsqrt(jnp.mean(values * values, axis=-1, keepdims=True) + EPS)


def dot(left, right, dims=((1,), (0,)), precision=None):
    return lax.dot_general(
        left, right, (dims, ((), ())), preferred_element_type=F32, precision=precision
    )


def remote(src, dst, send, recv, where):
    return pltpu.make_async_remote_copy(
        src_ref=src, dst_ref=dst, send_sem=send, recv_sem=recv, device_id=where, device_id_type=MESH
    )


class Place:
    def __init__(self):
        self.t = lax.axis_index("tensor")
        self.w = lax.axis_index("tower")
        self.a = self.t // X
        self.b = self.t % X
        self.z = self.w * ZL + self.a
        self.bp = (self.b + 1) % X
        self.bm = (self.b + X - 1) % X
        self.bo = (self.b + 2) % X
        self.xp = {"tensor": self.a * X + self.bp}
        self.xm = {"tensor": self.a * X + self.bm}
        self.zp = self.ring(1)
        self.zm = self.ring(ZR - 1)

    def ring(self, step):
        z = (self.z + step) % ZR
        return {"tower": z // ZL, "tensor": (z % ZL) * X + self.b}

    def column(self, row):
        return {"tensor": row * X + self.b}

    def order(self, j):
        near = jnp.minimum(self.a, ZL - 1 - self.a)
        swapped = jnp.where(j == 0, 1, jnp.where(j == 1, 0, j))
        row = jnp.where(near == 1, swapped, j)
        return jnp.where(self.a >= 2, ZL - 1 - row, row)


def rows_of(ref, first, count, unit):
    return ref.at[pl.ds(pl.multiple_of(first, unit), count), :]


class RowGather:
    def __init__(self, place, buf, rows, send, recv):
        self.p, self.buf, self.n, self.send, self.recv = place, buf, rows, send, recv

    def block(self, s, b):
        return rows_of(self.buf, (s * X + b) * self.n, self.n, self.n)

    def half(self, s, b, h):
        n = self.n // 2
        return rows_of(self.buf, (s * X + b) * self.n + h * n, n, n)

    def up(self, s):
        ref = self.block(s, self.p.b)
        where = self.p.column(jnp.minimum(self.p.a + 1, ZL - 1))
        return remote(ref, ref, self.send.at[0, s], self.recv.at[0, s], where)

    def down(self, s):
        ref = self.block(s, self.p.b)
        where = self.p.column(jnp.maximum(self.p.a - 1, 0))
        return remote(ref, ref, self.send.at[1, s], self.recv.at[0, s], where)

    def right(self, s):
        ref = self.block(s, self.p.b)
        return remote(ref, ref, self.send.at[2, s], self.recv.at[1, s], self.p.xp)

    def left(self, s):
        ref = self.block(s, self.p.b)
        return remote(ref, ref, self.send.at[3, s], self.recv.at[2, s], self.p.xm)

    def half_right(self, s):
        ref = self.half(s, self.p.bm, 0)
        return remote(ref, ref, self.send.at[4, s], self.recv.at[3, s], self.p.xp)

    def half_left(self, s):
        ref = self.half(s, self.p.bp, 1)
        return remote(ref, ref, self.send.at[5, s], self.recv.at[4, s], self.p.xm)

    def goes_up(self, s):
        return (s <= self.p.a) & (self.p.a < ZL - 1)

    def goes_down(self, s):
        return (s >= self.p.a) & (self.p.a > 0)

    def take_z(self, s):
        @pl.when(s != self.p.a)
        def _():
            self.up(s).wait_recv()

        @pl.when(self.goes_up(s))
        def _():
            self.up(s).start()

        @pl.when(self.goes_down(s))
        def _():
            self.down(s).start()

        self.right(s).start()
        self.left(s).start()

    def take_x(self, s):
        ref = self.block(s, self.p.bm)
        remote(ref, ref, self.send.at[2, s], self.recv.at[1, s], self.p.xm).wait_recv()
        self.half_right(s).start()
        ref = self.block(s, self.p.bp)
        remote(ref, ref, self.send.at[3, s], self.recv.at[2, s], self.p.xp).wait_recv()
        self.half_left(s).start()

    def take_halves(self, s):
        ref = self.half(s, self.p.bo, 0)
        remote(ref, ref, self.send.at[4, s], self.recv.at[3, s], self.p.xm).wait_recv()
        ref = self.half(s, self.p.bo, 1)
        remote(ref, ref, self.send.at[5, s], self.recv.at[4, s], self.p.xp).wait_recv()

    def drain(self):
        def each(s, _):
            @pl.when(self.goes_up(s))
            def _():
                self.up(s).wait_send()

            @pl.when(self.goes_down(s))
            def _():
                self.down(s).wait_send()

            self.right(s).wait_send()
            self.left(s).wait_send()
            self.half_right(s).wait_send()
            self.half_left(s).wait_send()
            return 0

        lax.fori_loop(0, ZL, each, 0)


class RingGather:
    def __init__(self, place, buf, rows, send, recv):
        self.p, self.buf, self.n, self.send, self.recv = place, buf, rows, send, recv

    def ref(self, z, hop, upward):
        z = (z + 2 * ZR) % ZR
        if hop < 4:
            return rows_of(self.buf, z * self.n, self.n, self.n)
        n = self.n // 2
        return rows_of(self.buf, z * self.n + (0 if upward else n), n, n)

    def copies(self, hop):
        up = self.ref(self.p.z - hop + 1, hop, True)
        down = self.ref(self.p.z + hop - 1, hop, False)
        return (
            remote(up, up, self.send.at[0, hop - 1], self.recv.at[0, hop - 1], self.p.zp),
            remote(down, down, self.send.at[1, hop - 1], self.recv.at[1, hop - 1], self.p.zm),
        )

    def start(self, hop):
        for copy in self.copies(hop):
            copy.start()

    def take(self, hop):
        up = self.ref(self.p.z - hop, hop, True)
        down = self.ref(self.p.z + hop, hop, False)
        remote(up, up, self.send.at[0, hop - 1], self.recv.at[0, hop - 1], self.p.zm).wait_recv()
        remote(down, down, self.send.at[1, hop - 1], self.recv.at[1, hop - 1], self.p.zp).wait_recv()

    def drain(self):
        for hop in range(1, 5):
            for copy in self.copies(hop):
                copy.wait_send()


class RingSum:
    def __init__(self, place, buf, land, rows, send, recv):
        self.p, self.buf, self.land = place, buf, land
        self.n, self.send, self.recv = rows, send, recv

    def part(self, z, half):
        z = (z + 2 * ZR) % ZR
        if half is None:
            return rows_of(self.buf, z * self.n, self.n, self.n)
        n = self.n // 2
        return rows_of(self.buf, z * self.n + half * n, n, n)

    def slot(self, way, hop):
        if hop == 1:
            return self.land.at[way, 0, pl.ds(0, self.n // 2), :]
        return self.land.at[way, hop - 1]

    def copies(self, hop):
        half = (0, 1) if hop == 1 else (None, None)
        up = self.part(self.p.z + 5 - hop, half[0])
        down = self.part(self.p.z - 5 + hop, half[1])
        return (
            remote(up, self.slot(0, hop), self.send.at[0, hop - 1], self.recv.at[0, hop - 1], self.p.zp),
            remote(down, self.slot(1, hop), self.send.at[1, hop - 1], self.recv.at[1, hop - 1], self.p.zm),
        )

    def start(self, hop):
        for copy in self.copies(hop):
            copy.start()

    def take(self, hop):
        for copy in self.copies(hop):
            copy.wait_recv()

    def add(self, hop):
        half = (0, 1) if hop == 1 else (None, None)
        for way, z in ((0, self.p.z + 4 - hop), (1, self.p.z - 4 + hop)):
            ref = self.part(z, half[way])
            ref[...] = (ref[...].astype(F32) + self.slot(way, hop)[...].astype(F32)).astype(BF16)

    def drain(self):
        for hop in range(1, 5):
            for copy in self.copies(hop):
                copy.wait_send()


def gain_row(ref):
    return ref[...].astype(F32).reshape(1, -1)


def normed_rows(act, gain):
    values = act.astype(F32)
    return (values * rms_scale(values) * gain).astype(BF16)


def gated(gate_val, up_val):
    return (jax.nn.silu(gate_val) * up_val).astype(BF16)


def at_step(i, step):
    return pl.when(i == step)


def forward_kernel(
    qa, qg, gate_hbm, up_hbm, down_hbm, ia, ig, ig_w, iu_w, id_w,
    hq, hi, qr, ir,
    w, nq, part, h2, pm, r1, r2, zs, zin, ni, wi, ip, land,
    loads, gs, gr, ss, sr, ws, wr, vs, vr, hs, hr, ias, iar, irs, irr,
):
    p = Place()
    n, dq = qa.shape
    m, di = ia.shape
    f, k = down_hbm.shape[0], id_w.shape[0]
    group = X * n
    h = n // 2
    piece = w.shape[2] // 4
    wide, thin = dq // 2, dq // 4
    dp = lax.axis_index("dp")
    y, c = dp // 2, dp % 2
    yp, ym, y2 = (y + 1) % 4, (y + 3) % 4, (y + 2) % 4
    to_yp, to_ym, to_core = {"dp": yp * 2 + c}, {"dp": ym * 2 + c}, {"dp": y * 2 + 1 - c}
    a2 = (p.a + 2) % ZL
    mate = p.a + 1 - 2 * (p.a % 2)
    to_a2, to_mate = p.column(a2), p.column(mate)

    own_weights = [
        pltpu.make_async_copy(ref, w.at[0, index, pl.ds(0, f), :], loads.at[index])
        for index, ref in enumerate((gate_hbm, up_hbm, down_hbm))
    ]
    for copy in own_weights:
        copy.start()
    barrier = pltpu.get_barrier_semaphore()
    friends = (p.xp, p.xm, p.zp, p.zm, to_a2, to_mate, to_yp, to_ym, to_core)
    for where in friends:
        pl.semaphore_signal(barrier, inc=1, device_id=where, device_id_type=MESH)
    for index in range(3):
        w[0, index, f:, :] = jnp.zeros((w.shape[2] - f, dq), BF16)
    nq[pl.ds(pl.multiple_of(p.b * n, n), n), :] = normed_rows(qa[...], gain_row(qg))
    ni[pl.ds(pl.multiple_of(p.z * m, m), m), :] = normed_rows(ia[...], gain_row(ig))
    for index, ref in enumerate((ig_w, iu_w, id_w)):
        wi[index, pl.ds(pl.multiple_of(p.b * k, k), k), :] = ref[...]
    pl.semaphore_wait(barrier, len(friends))

    rows = RowGather(p, nq, n, gs, gr)
    items = RingGather(p, ni, m, ias, iar)
    isum = RingSum(p, ip, land, m, irs, irr)

    def across():
        return remote(rows.block(0, p.b), rows.block(1, p.b), gs.at[0, 0], gr.at[0, 0], to_a2)

    def wpiece(which, index, line, core):
        first = pl.multiple_of(line * piece, piece)
        return w.at[which, index, pl.ds(first, piece), pl.ds(pl.multiple_of(core * wide, wide), wide)]

    def whalf(index, line, part_of):
        first = pl.multiple_of(line * piece, piece)
        column = pl.multiple_of(c * wide + part_of * thin, thin)
        return w.at[1, index, pl.ds(first, piece), pl.ds(column, thin)]

    def w_send(index, kind):
        here = wpiece(1, index, y, c)
        low, high = wpiece(1, index, ym, c), wpiece(1, index, yp, c)
        src, dst, where = (
            (wpiece(0, index, y, c), here, to_mate),
            (here, here, to_yp),
            (here, here, to_ym),
            (whalf(index, ym, 0), whalf(index, ym, 0), to_yp),
            (whalf(index, yp, 1), whalf(index, yp, 1), to_ym),
            (here, here, to_core),
            (low, low, to_core),
            (high, high, to_core),
            (wpiece(1, index, y2, c), wpiece(1, index, y2, c), to_core),
        )[kind]
        return remote(src, dst, ws.at[kind, index], wr.at[kind, index], where)

    def w_got(index, kind):
        dst = (
            wpiece(1, index, y, c),
            wpiece(1, index, ym, c),
            wpiece(1, index, yp, c),
            whalf(index, y2, 0),
            whalf(index, y2, 1),
            wpiece(1, index, y, 1 - c),
            wpiece(1, index, ym, 1 - c),
            wpiece(1, index, yp, 1 - c),
            wpiece(1, index, y2, 1 - c),
        )[kind]
        remote(dst, dst, ws.at[kind, index], wr.at[kind, index], to_core).wait_recv()

    def w_near(index):
        w_got(index, 0)
        for kind in (1, 2, 5):
            w_send(index, kind).start()

    def w_ring(index):
        w_got(index, 1)
        w_send(index, 3).start()
        w_send(index, 6).start()
        w_got(index, 2)
        w_send(index, 4).start()
        w_send(index, 7).start()

    def w_far(index):
        w_got(index, 3)
        w_got(index, 4)
        w_send(index, 8).start()

    def w_done(index):
        for kind in (5, 6, 7, 8):
            w_got(index, kind)

    def vpiece(b, core):
        column = pl.multiple_of(core * (di // 2), di // 2)
        return wi.at[:, pl.ds(pl.multiple_of(b * k, k), k), pl.ds(column, di // 2)]

    def vhalf(b, part_of):
        first = pl.multiple_of(b * k + part_of * (k // 2), k // 2)
        column = pl.multiple_of(c * (di // 2), di // 2)
        return wi.at[:, pl.ds(first, k // 2), pl.ds(column, di // 2)]

    def v_send(kind):
        ref, where = (
            (vpiece(p.b, c), p.xp),
            (vpiece(p.b, c), p.xm),
            (vhalf(p.bm, 0), p.xp),
            (vhalf(p.bp, 1), p.xm),
            (vpiece(p.bm, c), to_core),
            (vpiece(p.bp, c), to_core),
            (vpiece(p.bo, c), to_core),
        )[kind]
        return remote(ref, ref, vs.at[kind], vr.at[kind], where)

    def v_got(kind):
        ref = (
            vpiece(p.bm, c),
            vpiece(p.bp, c),
            vhalf(p.bo, 0),
            vhalf(p.bo, 1),
            vpiece(p.bm, 1 - c),
            vpiece(p.bp, 1 - c),
            vpiece(p.bo, 1 - c),
        )[kind]
        remote(ref, ref, vs.at[kind], vr.at[kind], to_core).wait_recv()

    def block(j, b):
        return rows_of(pm, (j * X + b) * n, n, n)

    def half(j, b, part_of):
        return rows_of(pm, (j * X + b) * n + part_of * h, h, h)

    def first(j, way):
        src = half(j, p.bo, way)
        return remote(src, r1.at[way, j], ss.at[way, j], sr.at[way, j], (p.xp, p.xm)[way])

    def second(j, way):
        src = block(j, (p.bp, p.bm)[way])
        return remote(src, r2.at[way, j], ss.at[2 + way, j], sr.at[2 + way, j], (p.xp, p.xm)[way])

    def to_owner():
        return remote(zs, zin, ss.at[4, 0], sr.at[4, 0], to_a2)

    def back(j):
        s = (p.a, a2)[j]
        dst = hq.at[pl.ds(pl.multiple_of(s * group, group), group), :]
        return remote(h2.at[j], dst, hs.at[j], hr.at[j], to_mate)

    def back_got(j):
        other = (mate, (mate + 2) % ZL)[j]
        dst = hq.at[pl.ds(pl.multiple_of(other * group, group), group), :]
        remote(h2.at[j], dst, hs.at[j], hr.at[j], to_mate).wait_recv()

    def hidden(which, j):
        left = nq[j * group : (j + 1) * group, :]
        gate_val = dot(left, w[which, 0, :f, :], ((1,), (1,)))
        return gated(gate_val, dot(left, w[which, 1, :f, :], ((1,), (1,))))

    def own_units(j):
        value = hidden(0, j)
        hq[pl.ds(pl.multiple_of((p.a, a2)[j] * group, group), group), :] = value
        part[j] = dot(value, w[0, 2, :f, :])

    def mate_units(j):
        value = hidden(1, j)
        h2[j] = value
        total = part[j] + dot(value, w[1, 2, :f, :])
        pm[j * group : (j + 1) * group, :] = total.astype(BF16)
        first(j, 0).start()
        first(j, 1).start()
        back(j).start()

    def combine(j):
        for way in range(2):
            first(j, way).wait_recv()
            ref = half(j, (p.bp, p.bm)[way], way)
            ref[...] = (ref[...].astype(F32) + r1[way, j].astype(F32)).astype(BF16)
            second(j, way).start()

    def summed(j):
        second(j, 0).wait_recv()
        second(j, 1).wait_recv()
        return block(j, p.b)[...].astype(F32) + r2[0, j].astype(F32) + r2[1, j].astype(F32)

    def item_product():
        left = ni[...]
        partial = 0.0
        for b in range(X):
            here = slice(b * k, (b + 1) * k)
            gate_val = dot(left, wi[0, here, :], ((1,), (1,)))
            value = gated(gate_val, dot(left, wi[1, here, :], ((1,), (1,))))
            hi[b] = value
            partial = partial + dot(value, wi[2, here, :])
        ip[...] = partial.astype(BF16)

    rows.right(0).start()
    rows.left(0).start()
    across().start()
    items.start(1)
    for index in range(3):
        own_weights[index].wait()
        w_send(index, 0).start()
    v_send(0).start()
    v_send(1).start()
    rows.take_x(0)
    w_near(0)
    items.take(1)
    items.start(2)
    remote(rows.block(0, p.b), rows.block(1, p.b), gs.at[0, 0], gr.at[0, 0], to_a2).wait_recv()
    rows.right(1).start()
    rows.left(1).start()
    w_near(1)
    rows.take_halves(0)
    own_units(0)
    w_ring(0)
    w_near(2)
    for kind in range(2):
        v_got(kind)
        v_send(2 + kind).start()
        v_send(4 + kind).start()
    items.take(2)
    items.start(3)
    rows.take_x(1)
    w_far(0)
    w_ring(1)
    rows.take_halves(1)
    items.take(3)
    items.start(4)
    own_units(1)
    w_far(1)
    w_ring(2)
    v_got(2)
    v_got(3)
    v_send(6).start()
    w_far(2)
    for index in range(3):
        w_done(index)
    mate_units(1)
    mate_units(0)
    combine(1)
    items.take(4)
    for kind in (4, 5, 6):
        v_got(kind)
    item_product()
    isum.start(1)
    combine(0)
    isum.take(1)
    isum.add(1)
    isum.start(2)
    zs[...] = summed(1).astype(BF16)
    to_owner().start()
    isum.take(2)
    isum.add(2)
    isum.start(3)
    mlp = summed(0)
    isum.take(3)
    isum.add(3)
    isum.start(4)
    to_owner().wait_recv()
    qr[...] = qa[...].astype(F32) + (mlp + zin[...].astype(F32))
    isum.take(4)
    own = ip[pl.ds(pl.multiple_of(p.z * m, m), m), :].astype(F32)
    ir[...] = ia[...].astype(F32) + (own + land[0, 3].astype(F32) + land[1, 3].astype(F32))

    for j in range(2):
        back_got(j)
        back(j).wait_send()
        for copy in (rows.right(j), rows.left(j), rows.half_right(j), rows.half_left(j)):
            copy.wait_send()
        for way in range(2):
            first(j, way).wait_send()
            second(j, way).wait_send()
    across().wait_send()
    to_owner().wait_send()
    items.drain()
    isum.drain()
    for index in range(3):
        for kind in range(9):
            w_send(index, kind).wait_send()
    for kind in range(7):
        v_send(kind).wait_send()


def forward(qa, qg, gate, up, down, ia, ig, ig_w, iu_w, id_w):
    n, dq = qa.shape
    m, di = ia.shape
    f, k = down.shape[0], id_w.shape[0]
    padded = 64 * ((f + 63) // 64)
    vmem, hbm = pl.BlockSpec(memory_space=pltpu.VMEM), pl.BlockSpec(memory_space=pl.ANY)
    all_i = ZR * m
    group = X * n
    dma = pltpu.SemaphoreType.DMA
    return pl.pallas_call(
        forward_kernel,
        out_shape=(
            jax.ShapeDtypeStruct((ZL * group, f), BF16),
            jax.ShapeDtypeStruct((X, all_i, k), BF16),
            jax.ShapeDtypeStruct((n, dq), F32),
            jax.ShapeDtypeStruct((m, di), F32),
        ),
        in_specs=[vmem, vmem, hbm, hbm, hbm, vmem, vmem, vmem, vmem, vmem],
        out_specs=[vmem] * 4,
        scratch_shapes=[
            pltpu.VMEM((2, 3, padded, dq), BF16),
            pltpu.VMEM((2 * group, dq), BF16),
            pltpu.VMEM((2, group, dq), F32),
            pltpu.VMEM((2, group, f), BF16),
            pltpu.VMEM((2 * group, dq), BF16),
            pltpu.VMEM((2, 2, n // 2, dq), BF16),
            pltpu.VMEM((2, 2, n, dq), BF16),
            pltpu.VMEM((n, dq), BF16),
            pltpu.VMEM((n, dq), BF16),
            pltpu.VMEM((all_i, di), BF16),
            pltpu.VMEM((3, X * k, di), BF16),
            pltpu.VMEM((all_i, di), BF16),
            pltpu.VMEM((2, 4, m, di), BF16),
            dma((3,)),
            dma((6, 2)),
            dma((5, 2)),
            dma((5, 2)),
            dma((5, 2)),
            dma((9, 3)),
            dma((9, 3)),
            dma((7,)),
            dma((7,)),
            dma((2,)),
            dma((2,)),
            dma((2, 4)),
            dma((2, 4)),
            dma((2, 4)),
            dma((2, 4)),
        ],
        compiler_params=pltpu.CompilerParams(
            collective_id=0, has_side_effects=True, vmem_limit_bytes=VMEM_LIMIT
        ),
        name="towers_forward",
    )(qa, qg, gate, up, down, ia, ig, ig_w, iu_w, id_w)


def split_rows(row):
    high = row.astype(BF16).astype(F32)
    rest = row - high
    mid = rest.astype(BF16).astype(F32)
    low = rest - mid
    index = lax.broadcasted_iota(jnp.int32, (8, row.shape[1]), 0)
    out = jnp.where(index == 0, high, jnp.where(index == 1, mid, jnp.where(index == 2, low, 0.0)))
    return out.astype(BF16)


def unit_scale(vec):
    return lax.rsqrt(jnp.sum(vec * vec, axis=-1, keepdims=True) + EPS)


def unit_back(vec, scales, upstream):
    inner = jnp.sum(vec * upstream, axis=-1, keepdims=True)
    return scales * upstream - vec * (scales * scales * scales) * inner


def contrast(query_hat, item_hat, ranks, positive):
    logits = dot(query_hat, item_hat, ((1,), (1,)), HIGH) / TAU
    shifted = logits - 1.0 / TAU
    log_student = shifted - jnp.log(jnp.sum(jnp.exp(shifted), axis=1, keepdims=True))
    teach = -ranks.astype(F32) / TEACH
    log_teacher = teach - jnp.log(jnp.sum(jnp.exp(teach), axis=1, keepdims=True))
    teacher = jnp.exp(log_teacher)
    columns = lax.broadcasted_iota(jnp.int32, logits.shape, 1)
    onehot = (columns == positive).astype(F32)
    per_row = jnp.sum(
        teacher * (log_teacher - log_student) - onehot * log_student, axis=1, keepdims=True
    )
    slopes = 2.0 * jnp.exp(log_student) - onehot - teacher
    return (per_row, slopes)


def grad_rows(resid, scales, gain, upstream):
    along = gain * upstream
    inner = jnp.mean(along * resid, axis=-1, keepdims=True)
    return (scales * along - resid * (scales * scales * scales) * inner).astype(BF16)


def by_tower(values, parts, tower):
    wide = values.shape[1] // parts
    blocks = [values[:, d * wide : (d + 1) * wide] for d in range(tower, parts, 2)]
    return jnp.concatenate(blocks, axis=1)


def backward_kernel(
    qr, ir, qf, if_, hq, hi, proj, ranks, positive,
    loss, q_out, i_out,
    sums, hats, scal, nq, grad, ni, gq, gi, qa, qb1, qb2, qc, ia, ib1, ib2, ic,
    s1, r1, s2, r2, s3, r3, gs, gr, ias, iar, qs, qv, bs, bv,
):
    p = Place()
    n, dq = qr.shape
    m, di = ir.shape
    group = X * n
    parts = X * ZL
    own = lax.axis_index("dp") * 2 + p.w
    count = hats.shape[0]
    wide = dq // count
    dp = lax.axis_index("dp")
    y, c = dp // 2, dp % 2
    yp, ym, y2 = (y + 1) % 4, (y + 3) % 4, (y + 2) % 4
    line_y = (y2, yp, ym, y)
    to_core = {"dp": y * 2 + 1 - c}
    to_y = ({"dp": yp * 2 + c}, {"dp": ym * 2 + c})
    to_tower = {"tower": 1 - p.w}

    def member(step):
        return {"tensor": (p.t + step) % parts}

    def replica(step):
        other = (own + step) % count
        return {"dp": other // 2, "tower": other % 2}

    barrier = pltpu.get_barrier_semaphore()

    def greet(step, _):
        pl.semaphore_signal(barrier, inc=1, device_id=member(step), device_id_type=MESH)
        return 0

    def greet_replica(step, _):
        pl.semaphore_signal(barrier, inc=1, device_id=replica(step), device_id_type=MESH)
        return 0

    lax.fori_loop(1, parts, greet, 0)
    lax.fori_loop(1, count, greet_replica, 0)
    for where in (p.zp, p.zm):
        pl.semaphore_signal(barrier, inc=1, device_id=where, device_id_type=MESH)

    q_gain, i_gain = gain_row(qf), gain_row(if_)
    q_resid, i_resid = qr[...], ir[...]
    for tower in range(2):
        here = pl.ds(pl.multiple_of(p.t * n, n), n)
        nq[tower, here, :] = by_tower(q_resid, count, tower).astype(BF16)
    q_scale, i_scale = rms_scale(q_resid), rms_scale(i_resid)
    sums[p.t, :, :dq] = jnp.sum(q_resid * q_scale * q_gain, axis=0, keepdims=True)
    sums[p.t, :, dq:] = jnp.sum(i_resid * i_scale * i_gain, axis=0, keepdims=True)
    pl.semaphore_wait(barrier, parts + count)

    rows = [RowGather(p, nq.at[tower], n, gs.at[tower], gr.at[tower]) for tower in range(2)]
    items = RingGather(p, ni, m, ias, iar)

    def spread_members(buf, send, recv):
        def each(step, _):
            remote(buf.at[p.t], buf.at[p.t], send.at[step], recv.at[p.t], member(step)).start()
            return 0

        lax.fori_loop(1, parts, each, 0)

    def await_members(buf, send, recv):
        def each(step, _):
            other = (p.t + step) % parts
            remote(buf.at[p.t], buf.at[other], send.at[step], recv.at[other], member(step)).wait()
            return 0

        lax.fori_loop(1, parts, each, 0)

    def spread_hats(step, _):
        remote(hats.at[own], hats.at[own], s2.at[step], r2.at[own], replica(step)).start()
        return 0

    def gathered_hats(step, _):
        other = (own + step) % count
        remote(hats.at[own], hats.at[other], s2.at[step], r2.at[other], replica(step)).wait()
        return 0

    def q_rows(tower, line_of, core):
        return rows_of(gq.at[tower], (line_of * 2 + core) * wide, wide, wide)

    def q_half(tower, line_of, way):
        first = (line_of * 2 + c) * wide + way * (wide // 2)
        return rows_of(gq.at[tower], first, wide // 2, wide // 2)

    def q_core(tower, j):
        src = q_rows(tower, line_y[j], 1 - c)
        return remote(src, qa.at[tower, j], qs.at[tower, j], qv.at[tower, j], to_core)

    def q_first(tower, way):
        src, dst = q_half(tower, y2, way), qb1.at[tower, way]
        return remote(src, dst, qs.at[tower, 4 + way], qv.at[tower, 4 + way], to_y[way])

    def q_second(tower, way):
        src, dst = q_rows(tower, (yp, ym)[way], c), qb2.at[tower, way]
        return remote(src, dst, qs.at[tower, 6 + way], qv.at[tower, 6 + way], to_y[way])

    def q_tower(tower):
        return remote(q_rows(tower, y, c), qc, qs.at[tower, 8], qv.at[tower, 8], to_tower)

    def q_start(tower):
        for j in range(4):
            q_core(tower, j).start()

    def q_far(tower):
        q_core(tower, 0).wait_recv()
        ref = q_rows(tower, y2, c)
        ref[...] += qa[tower, 0]
        for way in range(2):
            q_first(tower, way).start()

    def q_near(tower):
        for way in range(2):
            q_core(tower, 1 + way).wait_recv()
            ref = q_rows(tower, (yp, ym)[way], c)
            ref[...] += qa[tower, 1 + way]
            q_first(tower, way).wait_recv()
            ref = q_half(tower, (yp, ym)[way], way)
            ref[...] += qb1[tower, way]
            q_second(tower, way).start()

    def q_own(tower):
        q_core(tower, 3).wait_recv()
        for way in range(2):
            q_second(tower, way).wait_recv()
        ref = q_rows(tower, y, c)
        ref[...] = ref[...] + qa[tower, 3] + qb2[tower, 0] + qb2[tower, 1]

        @pl.when(p.w != tower)
        def _():
            q_tower(tower).start()

    def q_finish(tower):
        @pl.when(p.w == tower)
        def _():
            q_tower(tower).wait_recv()
            q_out[...] = q_rows(tower, y, c)[...] + qc[...]

    def i_rows(line_of, core):
        first = pl.multiple_of((line_of * 2 + core) * wide, wide)
        return gi.at[:, pl.ds(first, wide), :]

    def i_half(line_of, way):
        first = pl.multiple_of((line_of * 2 + c) * wide, wide)
        return gi.at[pl.ds(way * 2, 2), pl.ds(first, wide), :]

    def i_slab(b):
        return gi.at[b, pl.ds(pl.multiple_of((y * 2 + c) * wide, wide), wide), :]

    def i_core(j):
        return remote(i_rows(line_y[j], 1 - c), ia.at[j], bs.at[j], bv.at[j], to_core)

    def i_first(way):
        return remote(i_half(y2, way), ib1.at[way], bs.at[4 + way], bv.at[4 + way], to_y[way])

    def i_second(way):
        src = i_rows((yp, ym)[way], c)
        return remote(src, ib2.at[way], bs.at[6 + way], bv.at[6 + way], to_y[way])

    def i_x(hop):
        other = (p.b + hop) % X
        where = {"tensor": p.a * X + other}
        return remote(i_slab(other), ic.at[p.b], bs.at[8 + hop], bv.at[8 + p.b], where)

    def i_product():
        for b in range(X):
            gi[b] = dot(ni[...], hi[b], ((0,), (0,)))
        for j in range(4):
            i_core(j).start()

    def i_far():
        for j in range(4):
            i_core(j).wait_recv()
            ref = i_rows(line_y[j], c)
            ref[...] += ia[j]
        for way in range(2):
            i_first(way).start()

    def i_near():
        for way in range(2):
            i_first(way).wait_recv()
            ref = i_half((yp, ym)[way], way)
            ref[...] += ib1[way]
            i_second(way).start()

    def i_own():
        for way in range(2):
            i_second(way).wait_recv()
        ref = i_rows(y, c)
        ref[...] = ref[...] + ib2[0] + ib2[1]
        for hop in range(1, X):
            i_x(hop).start()

    def i_finish():
        total = i_slab(p.b)[...]
        for hop in range(1, X):
            other = (p.b + hop) % X
            remote(i_slab(other), ic.at[other], bs.at[8 + hop], bv.at[8 + other], p.xp).wait_recv()
            total = total + ic[other]
        i_out[...] = total

    def take_z(g):
        rows[g // ZL].take_z(p.order(g % ZL))

    def take_x(g):
        rows[g // ZL].take_x(p.order(g % ZL))

    def product(g):
        tower = g // ZL
        s = p.order(g % ZL)
        rows[tower].take_halves(s)
        for b in range(X):
            tile = scal[s * X + b]
            columns = jnp.concatenate([tile] * 16, axis=0).T[:n]
            first = pl.multiple_of((s * X + b) * n, n)
            resid = nq[tower, pl.ds(first, n), :].astype(F32)
            value = columns[:, 0:1] * along_of[tower] - resid * columns[:, 1:2]
            grad[b * n : (b + 1) * n, :] = value.astype(BF16)
        here = pl.ds(pl.multiple_of(s * group, group), group)
        value = dot(grad[...], hq[here, :], ((0,), (0,)))
        gq[tower] = value if g % ZL == 0 else gq[tower] + value

    take_z(0)
    spread_members(sums, s1, r1)
    take_z(1)
    take_x(0)
    await_members(sums, s1, r1)
    total = sums[0]
    for slot in range(1, parts):
        total = total + sums[slot]
    q_pooled = total[:, :dq] / QLEN
    i_pooled = total[:, dq:] / ILEN
    q_e = jnp.sum(dot(split_rows(q_pooled), proj[...]), axis=0, keepdims=True)
    q_norm, i_norm = unit_scale(q_e), unit_scale(i_pooled)
    hats[own, :, :di] = q_e * q_norm
    hats[own, :, di:] = i_pooled * i_norm
    lax.fori_loop(1, count, spread_hats, 0)
    take_z(2)
    take_x(1)
    lax.fori_loop(1, count, gathered_hats, 0)
    index = lax.broadcasted_iota(jnp.int32, (count, 2 * di), 0)
    every = jnp.zeros((count, 2 * di), F32)
    for slot in range(count):
        every = jnp.where(index == slot, hats[slot], every)
    every_query, every_items = every[:, :di], every[:, di:]
    line = lax.broadcasted_iota(jnp.int32, (count, count), 0)
    target = jnp.zeros((count, count), jnp.int32)
    for slot in range(count):
        target = jnp.where(line == slot, positive[slot], target)
    per_row, slopes = contrast(every_query, every_items, ranks[...], target)
    loss[...] = jnp.sum(per_row, axis=0, keepdims=True) / count
    weights = slopes * (LOSS_SCALE / (TAU * count))
    mine = lax.broadcasted_iota(jnp.int32, (count, di), 0) == own
    q_back = jnp.sum(
        jnp.where(mine, dot(weights, every_items, precision=HIGH), 0.0), axis=0, keepdims=True
    )
    column = lax.broadcasted_iota(jnp.int32, (count, count), 1) == own
    i_back = jnp.sum(
        jnp.sum(jnp.where(column, weights, 0.0), axis=1, keepdims=True) * every_query,
        axis=0,
        keepdims=True,
    )
    q_grad_e = unit_back(q_e, q_norm, q_back)
    q_up = jnp.sum(dot(split_rows(q_grad_e), proj[...], ((1,), (1,))), axis=0, keepdims=True) / QLEN
    i_up = unit_back(i_pooled, i_norm, i_back) / ILEN
    along = q_gain * q_up
    along_of = [by_tower(along, count, tower) for tower in range(2)]
    inner = jnp.mean(along * q_resid, axis=-1, keepdims=True)
    slope = (q_scale * q_scale * q_scale) * inner
    lane = lax.broadcasted_iota(jnp.int32, (n, 128), 1)
    columns = jnp.where(lane == 0, q_scale, jnp.where(lane == 1, slope, 0.0))
    columns = jnp.concatenate([columns, jnp.zeros((128 - n, 128), F32)], axis=0)
    scal[p.t] = columns.T[:8]
    spread_members(scal, s3, r3)
    ni[pl.ds(pl.multiple_of(p.z * m, m), m), :] = grad_rows(i_resid, i_scale, i_gain, i_up)
    items.start(1)
    take_z(3)
    take_x(2)
    items.take(1)
    items.start(2)
    await_members(scal, s3, r3)
    take_z(4)
    product(0)
    take_x(3)
    items.take(2)
    items.start(3)
    product(1)
    take_z(5)
    take_x(4)
    product(2)
    items.take(3)
    items.start(4)
    take_z(6)
    take_x(5)
    product(3)
    q_start(0)
    take_z(7)
    take_x(6)
    items.take(4)
    i_product()
    q_far(0)
    product(4)
    i_far()
    q_near(0)
    take_x(7)
    product(5)
    i_near()
    product(6)
    q_own(0)
    i_own()
    product(7)
    q_start(1)
    q_far(1)
    i_finish()
    q_near(1)
    q_finish(0)
    q_own(1)
    q_finish(1)

    for tower in range(2):
        rows[tower].drain()
        for j in range(4):
            q_core(tower, j).wait_send()
        for way in range(2):
            q_first(tower, way).wait_send()
            q_second(tower, way).wait_send()

        @pl.when(p.w != tower)
        def _():
            q_tower(tower).wait_send()

    items.drain()
    for j in range(4):
        i_core(j).wait_send()
    for way in range(2):
        i_first(way).wait_send()
        i_second(way).wait_send()
    for hop in range(1, X):
        i_x(hop).wait_send()


def backward(qr, ir, qf, if_, hq, hi, proj, ranks, positive):
    n, dq = qr.shape
    m, di = ir.shape
    dma = pltpu.SemaphoreType.DMA
    parts = X * ZL
    count = ranks.shape[0]
    wide = dq // count
    f, k = hq.shape[1], hi.shape[2]
    return pl.pallas_call(
        backward_kernel,
        out_shape=(
            jax.ShapeDtypeStruct((1, 1), F32),
            jax.ShapeDtypeStruct((wide, f), F32),
            jax.ShapeDtypeStruct((wide, k), F32),
        ),
        in_specs=[pl.BlockSpec(memory_space=pltpu.VMEM)] * 8 + [pl.BlockSpec(memory_space=pltpu.SMEM)],
        out_specs=[pl.BlockSpec(memory_space=pltpu.VMEM)] * 3,
        scratch_shapes=[
            pltpu.VMEM((parts, 1, dq + di), F32),
            pltpu.VMEM((count, 1, 2 * di), F32),
            pltpu.VMEM((parts, 8, 128), F32),
            pltpu.VMEM((2, parts * n, dq // 2), BF16),
            pltpu.VMEM((X * n, dq // 2), BF16),
            pltpu.VMEM((ZR * m, di), BF16),
            pltpu.VMEM((2, dq // 2, f), F32),
            pltpu.VMEM((X, di, k), F32),
            pltpu.VMEM((2, 4, wide, f), F32),
            pltpu.VMEM((2, 2, wide // 2, f), F32),
            pltpu.VMEM((2, 2, wide, f), F32),
            pltpu.VMEM((wide, f), F32),
            pltpu.VMEM((4, X, wide, k), F32),
            pltpu.VMEM((2, 2, wide, k), F32),
            pltpu.VMEM((2, X, wide, k), F32),
            pltpu.VMEM((X, wide, k), F32),
            dma((parts,)),
            dma((parts,)),
            dma((count,)),
            dma((count,)),
            dma((parts,)),
            dma((parts,)),
            dma((2, 6, ZL)),
            dma((2, 5, ZL)),
            dma((2, 4)),
            dma((2, 4)),
            dma((2, 9)),
            dma((2, 9)),
            dma((12,)),
            dma((12,)),
        ],
        compiler_params=pltpu.CompilerParams(
            collective_id=1, has_side_effects=True, vmem_limit_bytes=VMEM_LIMIT
        ),
        name="towers_backward",
    )(qr, ir, qf, if_, hq, hi, proj, ranks, positive)


def body(
    q_act,
    q_norm_gain,
    q_gate,
    q_up,
    q_down,
    q_final_gain,
    projection,
    i_act,
    i_norm_gain,
    i_gate,
    i_up,
    i_down,
    i_final_gain,
    ranks,
    positive,
):
    hq, hi, qr, ir = forward(
        q_act,
        q_norm_gain,
        q_gate.T,
        q_up.T,
        q_down,
        i_act,
        i_norm_gain,
        i_gate.T,
        i_up.T,
        i_down,
    )
    loss, q_grad, i_grad = backward(
        qr, ir, q_final_gain, i_final_gain, hq, hi, projection, ranks, positive
    )
    return (loss.reshape(()), q_grad.T, i_grad.T)


def solution(mesh):
    in_specs = (
        P(("dp", "tower", "tensor"), None),
        P(),
        P(None, "tensor"),
        P(None, "tensor"),
        P("tensor", None),
        P(),
        P(),
        P(("dp", "tower", "tensor"), None),
        P(),
        P(None, ("tower", "tensor")),
        P(None, ("tower", "tensor")),
        P(("tower", "tensor"), None),
        P(),
        P(),
        P(),
    )
    out_specs = (P(), P("tensor", ("dp", "tower")), P(("tower", "tensor"), "dp"))
    return jax.shard_map(body, mesh=mesh, in_specs=in_specs, out_specs=out_specs, check_vma=False)
```

```python
import functools

import jax
import jax.numpy as jnp
from jax import lax
from jax.experimental import pallas as pl
from jax.experimental.pallas import tpu as pltpu
from jax.sharding import PartitionSpec as P

QLEN = 1536
ILEN = 512
EPS = 1e-06
TAU = 0.05
TEACH = 2.0
LOSS_SCALE = 64.0
HIGH = lax.Precision.HIGHEST
MESH = pl.DeviceIdType.MESH
F32 = jnp.float32
BF16 = jnp.bfloat16

X = 4
ZL = 4
ZR = 8
VMEM_LIMIT = 60 * 1024 * 1024


def rms_scale(values):
    return lax.rsqrt(jnp.mean(values * values, axis=-1, keepdims=True) + EPS)


def dot(left, right, dims=((1,), (0,)), precision=None):
    return lax.dot_general(
        left, right, (dims, ((), ())), preferred_element_type=F32, precision=precision
    )


def remote(src, dst, send, recv, where):
    return pltpu.make_async_remote_copy(
        src_ref=src, dst_ref=dst, send_sem=send, recv_sem=recv, device_id=where, device_id_type=MESH
    )


class Place:
    def __init__(self):
        self.t = lax.axis_index("tensor")
        self.w = lax.axis_index("tower")
        self.a = self.t // X
        self.b = self.t % X
        self.z = self.w * ZL + self.a
        self.bp = (self.b + 1) % X
        self.bm = (self.b + X - 1) % X
        self.bo = (self.b + 2) % X
        self.xp = {"tensor": self.a * X + self.bp}
        self.xm = {"tensor": self.a * X + self.bm}
        self.zp = self.ring(1)
        self.zm = self.ring(ZR - 1)

    def ring(self, step):
        z = (self.z + step) % ZR
        return {"tower": z // ZL, "tensor": (z % ZL) * X + self.b}

    def column(self, row):
        return {"tensor": row * X + self.b}

    def order(self, j):
        near = jnp.minimum(self.a, ZL - 1 - self.a)
        swapped = jnp.where(j == 0, 1, jnp.where(j == 1, 0, j))
        row = jnp.where(near == 1, swapped, j)
        return jnp.where(self.a >= 2, ZL - 1 - row, row)


def rows_of(ref, first, count, unit):
    return ref.at[pl.ds(pl.multiple_of(first, unit), count), :]


class RowGather:
    def __init__(self, place, buf, rows, send, recv):
        self.p, self.buf, self.n, self.send, self.recv = place, buf, rows, send, recv

    def block(self, s, b):
        return rows_of(self.buf, (s * X + b) * self.n, self.n, self.n)

    def half(self, s, b, h):
        n = self.n // 2
        return rows_of(self.buf, (s * X + b) * self.n + h * n, n, n)

    def up(self, s):
        ref = self.block(s, self.p.b)
        where = self.p.column(jnp.minimum(self.p.a + 1, ZL - 1))
        return remote(ref, ref, self.send.at[0, s], self.recv.at[0, s], where)

    def down(self, s):
        ref = self.block(s, self.p.b)
        where = self.p.column(jnp.maximum(self.p.a - 1, 0))
        return remote(ref, ref, self.send.at[1, s], self.recv.at[0, s], where)

    def right(self, s):
        ref = self.block(s, self.p.b)
        return remote(ref, ref, self.send.at[2, s], self.recv.at[1, s], self.p.xp)

    def left(self, s):
        ref = self.block(s, self.p.b)
        return remote(ref, ref, self.send.at[3, s], self.recv.at[2, s], self.p.xm)

    def half_right(self, s):
        ref = self.half(s, self.p.bm, 0)
        return remote(ref, ref, self.send.at[4, s], self.recv.at[3, s], self.p.xp)

    def half_left(self, s):
        ref = self.half(s, self.p.bp, 1)
        return remote(ref, ref, self.send.at[5, s], self.recv.at[4, s], self.p.xm)

    def goes_up(self, s):
        return (s <= self.p.a) & (self.p.a < ZL - 1)

    def goes_down(self, s):
        return (s >= self.p.a) & (self.p.a > 0)

    def take_z(self, s):
        @pl.when(s != self.p.a)
        def _():
            self.up(s).wait_recv()

        @pl.when(self.goes_up(s))
        def _():
            self.up(s).start()

        @pl.when(self.goes_down(s))
        def _():
            self.down(s).start()

        self.right(s).start()
        self.left(s).start()

    def take_x(self, s):
        ref = self.block(s, self.p.bm)
        remote(ref, ref, self.send.at[2, s], self.recv.at[1, s], self.p.xm).wait_recv()
        self.half_right(s).start()
        ref = self.block(s, self.p.bp)
        remote(ref, ref, self.send.at[3, s], self.recv.at[2, s], self.p.xp).wait_recv()
        self.half_left(s).start()

    def take_halves(self, s):
        ref = self.half(s, self.p.bo, 0)
        remote(ref, ref, self.send.at[4, s], self.recv.at[3, s], self.p.xm).wait_recv()
        ref = self.half(s, self.p.bo, 1)
        remote(ref, ref, self.send.at[5, s], self.recv.at[4, s], self.p.xp).wait_recv()

    def drain(self):
        def each(s, _):
            @pl.when(self.goes_up(s))
            def _():
                self.up(s).wait_send()

            @pl.when(self.goes_down(s))
            def _():
                self.down(s).wait_send()

            self.right(s).wait_send()
            self.left(s).wait_send()
            self.half_right(s).wait_send()
            self.half_left(s).wait_send()
            return 0

        lax.fori_loop(0, ZL, each, 0)


class RingGather:
    def __init__(self, place, buf, rows, send, recv):
        self.p, self.buf, self.n, self.send, self.recv = place, buf, rows, send, recv

    def ref(self, z, hop, upward):
        z = (z + 2 * ZR) % ZR
        if hop < 4:
            return rows_of(self.buf, z * self.n, self.n, self.n)
        n = self.n // 2
        return rows_of(self.buf, z * self.n + (0 if upward else n), n, n)

    def copies(self, hop):
        up = self.ref(self.p.z - hop + 1, hop, True)
        down = self.ref(self.p.z + hop - 1, hop, False)
        return (
            remote(up, up, self.send.at[0, hop - 1], self.recv.at[0, hop - 1], self.p.zp),
            remote(down, down, self.send.at[1, hop - 1], self.recv.at[1, hop - 1], self.p.zm),
        )

    def start(self, hop):
        for copy in self.copies(hop):
            copy.start()

    def take(self, hop):
        up = self.ref(self.p.z - hop, hop, True)
        down = self.ref(self.p.z + hop, hop, False)
        remote(up, up, self.send.at[0, hop - 1], self.recv.at[0, hop - 1], self.p.zm).wait_recv()
        remote(down, down, self.send.at[1, hop - 1], self.recv.at[1, hop - 1], self.p.zp).wait_recv()

    def drain(self):
        for hop in range(1, 5):
            for copy in self.copies(hop):
                copy.wait_send()


class RingSum:
    def __init__(self, place, buf, land, rows, send, recv):
        self.p, self.buf, self.land = place, buf, land
        self.n, self.send, self.recv = rows, send, recv

    def part(self, z, half):
        z = (z + 2 * ZR) % ZR
        if half is None:
            return rows_of(self.buf, z * self.n, self.n, self.n)
        n = self.n // 2
        return rows_of(self.buf, z * self.n + half * n, n, n)

    def slot(self, way, hop):
        if hop == 1:
            return self.land.at[way, 0, pl.ds(0, self.n // 2), :]
        return self.land.at[way, hop - 1]

    def copies(self, hop):
        half = (0, 1) if hop == 1 else (None, None)
        up = self.part(self.p.z + 5 - hop, half[0])
        down = self.part(self.p.z - 5 + hop, half[1])
        return (
            remote(up, self.slot(0, hop), self.send.at[0, hop - 1], self.recv.at[0, hop - 1], self.p.zp),
            remote(down, self.slot(1, hop), self.send.at[1, hop - 1], self.recv.at[1, hop - 1], self.p.zm),
        )

    def start(self, hop):
        for copy in self.copies(hop):
            copy.start()

    def take(self, hop):
        for copy in self.copies(hop):
            copy.wait_recv()

    def add(self, hop):
        half = (0, 1) if hop == 1 else (None, None)
        for way, z in ((0, self.p.z + 4 - hop), (1, self.p.z - 4 + hop)):
            ref = self.part(z, half[way])
            ref[...] = (ref[...].astype(F32) + self.slot(way, hop)[...].astype(F32)).astype(BF16)

    def drain(self):
        for hop in range(1, 5):
            for copy in self.copies(hop):
                copy.wait_send()


def gain_row(ref):
    return ref[...].astype(F32).reshape(1, -1)


def normed_rows(act, gain):
    values = act.astype(F32)
    return (values * rms_scale(values) * gain).astype(BF16)


def gated(gate_val, up_val):
    return (jax.nn.silu(gate_val) * up_val).astype(BF16)


def at_step(i, step):
    return pl.when(i == step)


def split_rows(row):
    high = row.astype(BF16).astype(F32)
    rest = row - high
    mid = rest.astype(BF16).astype(F32)
    low = rest - mid
    index = lax.broadcasted_iota(jnp.int32, (8, row.shape[1]), 0)
    out = jnp.where(index == 0, high, jnp.where(index == 1, mid, jnp.where(index == 2, low, 0.0)))
    return out.astype(BF16)


def unit_scale(vec):
    return lax.rsqrt(jnp.sum(vec * vec, axis=-1, keepdims=True) + EPS)


def unit_back(vec, scales, upstream):
    inner = jnp.sum(vec * upstream, axis=-1, keepdims=True)
    return scales * upstream - vec * (scales * scales * scales) * inner


def contrast(query_hat, item_hat, ranks, positive):
    logits = dot(query_hat, item_hat, ((1,), (1,)), HIGH) / TAU
    shifted = logits - 1.0 / TAU
    log_student = shifted - jnp.log(jnp.sum(jnp.exp(shifted), axis=1, keepdims=True))
    teach = -ranks.astype(F32) / TEACH
    log_teacher = teach - jnp.log(jnp.sum(jnp.exp(teach), axis=1, keepdims=True))
    teacher = jnp.exp(log_teacher)
    columns = lax.broadcasted_iota(jnp.int32, logits.shape, 1)
    onehot = (columns == positive).astype(F32)
    per_row = jnp.sum(
        teacher * (log_teacher - log_student) - onehot * log_student, axis=1, keepdims=True
    )
    slopes = 2.0 * jnp.exp(log_student) - onehot - teacher
    return (per_row, slopes)


def grad_rows(resid, scales, gain, upstream):
    along = gain * upstream
    inner = jnp.mean(along * resid, axis=-1, keepdims=True)
    return (scales * along - resid * (scales * scales * scales) * inner).astype(BF16)


def by_tower(values, parts, tower):
    wide = values.shape[1] // parts
    blocks = [values[:, d * wide : (d + 1) * wide] for d in range(tower, parts, 2)]
    return jnp.concatenate(blocks, axis=1)


def kernel(
    qa, qg, gate_hbm, up_hbm, down_hbm, ia, ig, ig_w, iu_w, id_w, qf, if_, proj_hbm, ranks, positive,
    loss, q_out, i_out,
    w, proj, nq, part, gate_val, h2, pm, r1, r2, zs, zin, ni, wi, ip, land, hq, hi,
    sums, hats, scal, yq, grad, yi, gq, gi, qc1, qb1, qb2, qc, ic1, ib1, ib2, ic,
    loads, gs, gr, ss, sr, ws, wr, vs, vr, hs, hr, ias, iar, irs, irr,
    s1, r1s, s2, r2s, s3, r3s, ys, yr, iys, iyr, qs, qv, bs, bv,
):
    p = Place()
    n, dq = qa.shape
    m, di = ia.shape
    f, k = down_hbm.shape[0], id_w.shape[0]
    group = X * n
    h = n // 2
    parts = X * ZL
    count = hats.shape[0]
    block_wide = dq // count
    piece = w.shape[2] // 4
    wide, thin = dq // 2, dq // 4
    dp = lax.axis_index("dp")
    own = dp * 2 + p.w
    y, c = dp // 2, dp % 2
    yp, ym, y2 = (y + 1) % 4, (y + 3) % 4, (y + 2) % 4
    line_y = (y2, yp, ym, y)
    to_yp, to_ym, to_core = {"dp": yp * 2 + c}, {"dp": ym * 2 + c}, {"dp": y * 2 + 1 - c}
    to_y = (to_yp, to_ym)
    to_tower = {"tower": 1 - p.w}
    a2 = (p.a + 2) % ZL
    mate = p.a + 1 - 2 * (p.a % 2)
    to_a2, to_mate = p.column(a2), p.column(mate)

    def member(step):
        return {"tensor": (p.t + step) % parts}

    def replica(step):
        other = (own + step) % count
        return {"dp": other // 2, "tower": other % 2}

    own_weights = [
        pltpu.make_async_copy(ref, w.at[0, index, pl.ds(0, f), :], loads.at[index])
        for index, ref in enumerate((gate_hbm, up_hbm, down_hbm))
    ]
    proj_copy = pltpu.make_async_copy(proj_hbm, proj, loads.at[3])
    for copy in own_weights:
        copy.start()
    proj_copy.start()
    barrier = pltpu.get_barrier_semaphore()

    def greet(step, _):
        pl.semaphore_signal(barrier, inc=1, device_id=member(step), device_id_type=MESH)
        pl.semaphore_signal(barrier, inc=1, device_id=replica(step), device_id_type=MESH)
        return 0

    lax.fori_loop(1, parts, greet, 0)
    for where in (p.zp, p.zm):
        pl.semaphore_signal(barrier, inc=1, device_id=where, device_id_type=MESH)
    for index in range(3):
        w[0, index, f:, :] = jnp.zeros((w.shape[2] - f, dq), BF16)
    nq[pl.ds(pl.multiple_of(p.b * n, n), n), :] = normed_rows(qa[...], gain_row(qg))
    ni[pl.ds(pl.multiple_of(p.z * m, m), m), :] = normed_rows(ia[...], gain_row(ig))
    for index, ref in enumerate((ig_w, iu_w, id_w)):
        wi[index, pl.ds(pl.multiple_of(p.b * k, k), k), :] = ref[...]
    pl.semaphore_wait(barrier, 2 * (parts - 1) + 2)

    rows = RowGather(p, nq, n, gs, gr)
    items = RingGather(p, ni, m, ias, iar)
    isum = RingSum(p, ip, land, m, irs, irr)

    def across():
        return remote(rows.block(0, p.b), rows.block(1, p.b), gs.at[0, 0], gr.at[0, 0], to_a2)

    def wpiece(which, index, line, core):
        first = pl.multiple_of(line * piece, piece)
        return w.at[which, index, pl.ds(first, piece), pl.ds(pl.multiple_of(core * wide, wide), wide)]

    def whalf(index, line, part_of):
        first = pl.multiple_of(line * piece, piece)
        column = pl.multiple_of(c * wide + part_of * thin, thin)
        return w.at[1, index, pl.ds(first, piece), pl.ds(column, thin)]

    def w_send(index, kind):
        here = wpiece(1, index, y, c)
        low, high = wpiece(1, index, ym, c), wpiece(1, index, yp, c)
        src, dst, where = (
            (wpiece(0, index, y, c), here, to_mate),
            (here, here, to_yp),
            (here, here, to_ym),
            (whalf(index, ym, 0), whalf(index, ym, 0), to_yp),
            (whalf(index, yp, 1), whalf(index, yp, 1), to_ym),
            (here, here, to_core),
            (low, low, to_core),
            (high, high, to_core),
            (wpiece(1, index, y2, c), wpiece(1, index, y2, c), to_core),
        )[kind]
        return remote(src, dst, ws.at[kind, index], wr.at[kind, index], where)

    def w_got(index, kind):
        dst = (
            wpiece(1, index, y, c),
            wpiece(1, index, ym, c),
            wpiece(1, index, yp, c),
            whalf(index, y2, 0),
            whalf(index, y2, 1),
            wpiece(1, index, y, 1 - c),
            wpiece(1, index, ym, 1 - c),
            wpiece(1, index, yp, 1 - c),
            wpiece(1, index, y2, 1 - c),
        )[kind]
        remote(dst, dst, ws.at[kind, index], wr.at[kind, index], to_core).wait_recv()

    def w_near(index):
        w_got(index, 0)
        for kind in (1, 2, 5):
            w_send(index, kind).start()

    def w_ring(index):
        w_got(index, 1)
        w_send(index, 3).start()
        w_send(index, 6).start()
        w_got(index, 2)
        w_send(index, 4).start()
        w_send(index, 7).start()

    def w_far(index):
        w_got(index, 3)
        w_got(index, 4)
        w_send(index, 8).start()

    def w_done(index):
        for kind in (5, 6, 7, 8):
            w_got(index, kind)

    def vpiece(b, core):
        column = pl.multiple_of(core * (di // 2), di // 2)
        return wi.at[:, pl.ds(pl.multiple_of(b * k, k), k), pl.ds(column, di // 2)]

    def vhalf(b, part_of):
        first = pl.multiple_of(b * k + part_of * (k // 2), k // 2)
        column = pl.multiple_of(c * (di // 2), di // 2)
        return wi.at[:, pl.ds(first, k // 2), pl.ds(column, di // 2)]

    def v_send(kind):
        ref, where = (
            (vpiece(p.b, c), p.xp),
            (vpiece(p.b, c), p.xm),
            (vhalf(p.bm, 0), p.xp),
            (vhalf(p.bp, 1), p.xm),
            (vpiece(p.bm, c), to_core),
            (vpiece(p.bp, c), to_core),
            (vpiece(p.bo, c), to_core),
        )[kind]
        return remote(ref, ref, vs.at[kind], vr.at[kind], where)

    def v_got(kind):
        ref = (
            vpiece(p.bm, c),
            vpiece(p.bp, c),
            vhalf(p.bo, 0),
            vhalf(p.bo, 1),
            vpiece(p.bm, 1 - c),
            vpiece(p.bp, 1 - c),
            vpiece(p.bo, 1 - c),
        )[kind]
        remote(ref, ref, vs.at[kind], vr.at[kind], to_core).wait_recv()

    def block(j, q, b):
        return rows_of(pm.at[q], (j * X + b) * n, n, n)

    def half(j, q, b, part_of):
        return rows_of(pm.at[q], (j * X + b) * n + part_of * h, h, h)

    def first(j, q, way):
        src = half(j, q, p.bo, way)
        where = (p.xp, p.xm)[way]
        return remote(src, r1.at[way, j, q], ss.at[way, j, q], sr.at[way, j, q], where)

    def second(j, q, way):
        src = block(j, q, (p.bp, p.bm)[way])
        where = (p.xp, p.xm)[way]
        return remote(src, r2.at[way, j, q], ss.at[2 + way, j, q], sr.at[2 + way, j, q], where)

    def to_owner(q):
        return remote(zs.at[q], zin.at[q], ss.at[4, 0, q], sr.at[4, 0, q], to_a2)

    def back(j):
        s = (p.a, a2)[j]
        dst = hq.at[pl.ds(pl.multiple_of(s * group, group), group), :]
        return remote(h2.at[j], dst, hs.at[j], hr.at[j], to_mate)

    def back_got(j):
        other = (mate, (mate + 2) % ZL)[j]
        dst = hq.at[pl.ds(pl.multiple_of(other * group, group), group), :]
        remote(h2.at[j], dst, hs.at[j], hr.at[j], to_mate).wait_recv()

    def rows_in(j):
        return nq[j * group : (j + 1) * group, :]

    def own_units(j):
        left = rows_in(j)
        value = gated(
            dot(left, w[0, 0, :f, :], ((1,), (1,))), dot(left, w[0, 1, :f, :], ((1,), (1,)))
        )
        hq[pl.ds(pl.multiple_of((p.a, a2)[j] * group, group), group), :] = value
        part[j] = dot(value, w[0, 2, :f, :])

    def mate_gate(j):
        gate_val[j] = dot(rows_in(j), w[1, 0, :f, :], ((1,), (1,)))

    def mate_up(j):
        h2[j] = gated(gate_val[j], dot(rows_in(j), w[1, 1, :f, :], ((1,), (1,))))
        back(j).start()

    def mate_down(j, q):
        columns = slice(q * wide, (q + 1) * wide)
        total = part[j, :, columns] + dot(h2[j], w[1, 2, :f, columns])
        pm[q, j * group : (j + 1) * group, :] = total.astype(BF16)
        first(j, q, 0).start()
        first(j, q, 1).start()

    def combine(j, q):
        for way in range(2):
            first(j, q, way).wait_recv()
            ref = half(j, q, (p.bp, p.bm)[way], way)
            ref[...] = (ref[...].astype(F32) + r1[way, j, q].astype(F32)).astype(BF16)
            second(j, q, way).start()

    def summed(j, q):
        second(j, q, 0).wait_recv()
        second(j, q, 1).wait_recv()
        total = block(j, q, p.b)[...].astype(F32)
        return total + r2[0, j, q].astype(F32) + r2[1, j, q].astype(F32)

    def send_sum(q):
        zs[q] = summed(1, q).astype(BF16)
        to_owner(q).start()

    def item_hop(hop):
        items.take(hop)
        if hop < 4:
            items.start(hop + 1)

    def isum_hop(hop):
        isum.take(hop)
        isum.add(hop)
        isum.start(hop + 1)

    def item_product():
        left = ni[...]
        partial = 0.0
        for b in range(X):
            here = slice(b * k, (b + 1) * k)
            value = gated(
                dot(left, wi[0, here, :], ((1,), (1,))), dot(left, wi[1, here, :], ((1,), (1,)))
            )
            hi[b] = value
            partial = partial + dot(value, wi[2, here, :])
        ip[...] = partial.astype(BF16)
        isum.start(1)

    rows.right(0).start()
    rows.left(0).start()
    items.start(1)
    own_weights[0].wait()
    w_send(0, 0).start()
    across().start()
    v_send(0).start()
    v_send(1).start()
    own_weights[1].wait()
    own_weights[2].wait()
    rows.take_x(0)
    item_hop(1)
    w_near(0)
    w_send(1, 0).start()
    rows.take_halves(0)
    own_units(0)
    remote(rows.block(0, p.b), rows.block(1, p.b), gs.at[0, 0], gr.at[0, 0], to_a2).wait_recv()
    rows.right(1).start()
    rows.left(1).start()
    item_hop(2)
    w_ring(0)
    w_near(1)
    w_send(2, 0).start()
    for kind in range(2):
        v_got(kind)
        v_send(2 + kind).start()
        v_send(4 + kind).start()
    item_hop(3)
    w_far(0)
    rows.take_x(1)
    v_got(2)
    v_got(3)
    v_send(6).start()
    w_ring(1)
    item_hop(4)
    for kind in (4, 5, 6):
        v_got(kind)
    w_near(2)
    item_product()
    w_far(1)
    w_done(0)
    mate_gate(0)
    rows.take_halves(1)
    mate_gate(1)
    isum_hop(1)
    w_ring(2)
    own_units(1)
    w_done(1)
    mate_up(1)
    isum_hop(2)
    w_far(2)
    mate_up(0)
    w_done(2)
    mate_down(1, 0)
    mate_down(1, 1)
    combine(1, 0)
    mate_down(0, 0)
    combine(1, 1)
    mate_down(0, 1)
    isum_hop(3)
    send_sum(0)
    combine(0, 0)
    send_sum(1)
    combine(0, 1)
    isum.take(4)
    own_item = ip[pl.ds(pl.multiple_of(p.z * m, m), m), :].astype(F32)
    i_resid = ia[...].astype(F32) + (own_item + land[0, 3].astype(F32) + land[1, 3].astype(F32))
    mlp = []
    for q in range(2):
        total = summed(0, q)
        to_owner(q).wait_recv()
        mlp.append(total + zin[q].astype(F32))
    q_resid = qa[...].astype(F32) + jnp.concatenate(mlp, axis=1)

    q_gain, i_gain = gain_row(qf), gain_row(if_)
    q_scale, i_scale = rms_scale(q_resid), rms_scale(i_resid)
    sums[p.t, :, :dq] = jnp.sum(q_resid * q_scale * q_gain, axis=0, keepdims=True)
    sums[p.t, :, dq:] = jnp.sum(i_resid * i_scale * i_gain, axis=0, keepdims=True)

    def spread_members(buf, send, recv):
        def each(step, _):
            remote(buf.at[p.t], buf.at[p.t], send.at[step], recv.at[p.t], member(step)).start()
            return 0

        lax.fori_loop(1, parts, each, 0)

    def await_members(buf, send, recv):
        def each(step, _):
            other = (p.t + step) % parts
            remote(buf.at[p.t], buf.at[other], send.at[step], recv.at[other], member(step)).wait()
            return 0

        lax.fori_loop(1, parts, each, 0)

    def spread_hats(step, _):
        remote(hats.at[own], hats.at[own], s2.at[step], r2s.at[own], replica(step)).start()
        return 0

    def gathered_hats(step, _):
        other = (own + step) % count
        remote(hats.at[own], hats.at[other], s2.at[step], r2s.at[other], replica(step)).wait()
        return 0

    def q_rows(tower, line_of, core):
        return rows_of(gq.at[tower], (line_of * 2 + core) * block_wide, block_wide, block_wide)

    def q_half(tower, line_of, way):
        first = (line_of * 2 + c) * block_wide + way * (block_wide // 2)
        return rows_of(gq.at[tower], first, block_wide // 2, block_wide // 2)

    def q_core(tower, j):
        src = q_rows(tower, line_y[j], 1 - c)
        return remote(src, qc1.at[tower, j], qs.at[tower, j], qv.at[tower, j], to_core)

    def q_first(tower, way):
        src, dst = q_half(tower, y2, way), qb1.at[tower, way]
        return remote(src, dst, qs.at[tower, 4 + way], qv.at[tower, 4 + way], to_y[way])

    def q_second(tower, way):
        src, dst = q_rows(tower, (yp, ym)[way], c), qb2.at[tower, way]
        return remote(src, dst, qs.at[tower, 6 + way], qv.at[tower, 6 + way], to_y[way])

    def q_tower(tower):
        return remote(q_rows(tower, y, c), qc, qs.at[tower, 8], qv.at[tower, 8], to_tower)

    def q_start(tower):
        for j in range(4):
            q_core(tower, j).start()

    def q_far(tower):
        q_core(tower, 0).wait_recv()
        ref = q_rows(tower, y2, c)
        ref[...] += qc1[tower, 0]
        for way in range(2):
            q_first(tower, way).start()

    def q_near(tower):
        for way in range(2):
            q_core(tower, 1 + way).wait_recv()
            ref = q_rows(tower, (yp, ym)[way], c)
            ref[...] += qc1[tower, 1 + way]
            q_first(tower, way).wait_recv()
            ref = q_half(tower, (yp, ym)[way], way)
            ref[...] += qb1[tower, way]
            q_second(tower, way).start()

    def q_own(tower):
        q_core(tower, 3).wait_recv()
        for way in range(2):
            q_second(tower, way).wait_recv()
        ref = q_rows(tower, y, c)
        ref[...] = ref[...] + qc1[tower, 3] + qb2[tower, 0] + qb2[tower, 1]

        @pl.when(p.w != tower)
        def _():
            q_tower(tower).start()

    def q_finish(tower):
        @pl.when(p.w == tower)
        def _():
            q_tower(tower).wait_recv()
            q_out[...] = q_rows(tower, y, c)[...] + qc[...]

    def i_rows(line_of, core):
        first = pl.multiple_of((line_of * 2 + core) * block_wide, block_wide)
        return gi.at[:, pl.ds(first, block_wide), :]

    def i_half(line_of, way):
        first = pl.multiple_of((line_of * 2 + c) * block_wide, block_wide)
        return gi.at[pl.ds(way * 2, 2), pl.ds(first, block_wide), :]

    def i_slab(b):
        return gi.at[b, pl.ds(pl.multiple_of((y * 2 + c) * block_wide, block_wide), block_wide), :]

    def i_core(j):
        return remote(i_rows(line_y[j], 1 - c), ic1.at[j], bs.at[j], bv.at[j], to_core)

    def i_first(way):
        return remote(i_half(y2, way), ib1.at[way], bs.at[4 + way], bv.at[4 + way], to_y[way])

    def i_second(way):
        src = i_rows((yp, ym)[way], c)
        return remote(src, ib2.at[way], bs.at[6 + way], bv.at[6 + way], to_y[way])

    def i_x(hop):
        other = (p.b + hop) % X
        where = {"tensor": p.a * X + other}
        return remote(i_slab(other), ic.at[p.b], bs.at[8 + hop], bv.at[8 + p.b], where)

    def i_product():
        for b in range(X):
            gi[b] = dot(yi[...], hi[b], ((0,), (0,)))
        for j in range(4):
            i_core(j).start()

    def i_far():
        for j in range(4):
            i_core(j).wait_recv()
            ref = i_rows(line_y[j], c)
            ref[...] += ic1[j]
        for way in range(2):
            i_first(way).start()

    def i_near():
        for way in range(2):
            i_first(way).wait_recv()
            ref = i_half((yp, ym)[way], way)
            ref[...] += ib1[way]
            i_second(way).start()

    def i_own():
        for way in range(2):
            i_second(way).wait_recv()
        ref = i_rows(y, c)
        ref[...] = ref[...] + ib2[0] + ib2[1]
        for hop in range(1, X):
            i_x(hop).start()

    def i_finish():
        total = i_slab(p.b)[...]
        for hop in range(1, X):
            other = (p.b + hop) % X
            remote(i_slab(other), ic.at[other], bs.at[8 + hop], bv.at[8 + other], p.xp).wait_recv()
            total = total + ic[other]
        i_out[...] = total

    gather = [RowGather(p, yq.at[tower], n, ys.at[tower], yr.at[tower]) for tower in range(2)]
    igather = RingGather(p, yi, m, iys, iyr)

    def take_z(g):
        gather[g // ZL].take_z(p.order(g % ZL))

    def take_x(g):
        gather[g // ZL].take_x(p.order(g % ZL))

    def item_grad_hop(hop):
        igather.take(hop)
        if hop < 4:
            igather.start(hop + 1)

    def product(g):
        tower = g // ZL
        s = p.order(g % ZL)
        gather[tower].take_halves(s)
        for b in range(X):
            tile = scal[s * X + b]
            columns = jnp.concatenate([tile] * 16, axis=0).T[:n]
            first_row = pl.multiple_of((s * X + b) * n, n)
            resid = yq[tower, pl.ds(first_row, n), :].astype(F32)
            value = columns[:, 0:1] * along_of[tower] - resid * columns[:, 1:2]
            grad[b * n : (b + 1) * n, :] = value.astype(BF16)
        here = pl.ds(pl.multiple_of(s * group, group), group)
        value = dot(grad[...], hq[here, :], ((0,), (0,)))
        gq[tower] = value if g % ZL == 0 else gq[tower] + value

    spread_members(sums, s1, r1s)
    for tower in range(2):
        here = pl.ds(pl.multiple_of(p.t * n, n), n)
        yq[tower, here, :] = by_tower(q_resid, count, tower).astype(BF16)
    take_z(0)
    proj_copy.wait()
    await_members(sums, s1, r1s)
    total = sums[0]
    for slot in range(1, parts):
        total = total + sums[slot]
    q_pooled = total[:, :dq] / QLEN
    i_pooled = total[:, dq:] / ILEN
    q_e = jnp.sum(dot(split_rows(q_pooled), proj[...]), axis=0, keepdims=True)
    q_norm, i_norm = unit_scale(q_e), unit_scale(i_pooled)
    hats[own, :, :di] = q_e * q_norm
    hats[own, :, di:] = i_pooled * i_norm
    lax.fori_loop(1, count, spread_hats, 0)
    take_z(1)
    take_z(4)
    take_x(0)
    lax.fori_loop(1, count, gathered_hats, 0)
    index = lax.broadcasted_iota(jnp.int32, (count, 2 * di), 0)
    every = jnp.zeros((count, 2 * di), F32)
    for slot in range(count):
        every = jnp.where(index == slot, hats[slot], every)
    every_query, every_items = every[:, :di], every[:, di:]
    line = lax.broadcasted_iota(jnp.int32, (count, count), 0)
    target = jnp.zeros((count, count), jnp.int32)
    for slot in range(count):
        target = jnp.where(line == slot, positive[slot], target)
    per_row, slopes = contrast(every_query, every_items, ranks[...], target)
    loss[...] = jnp.sum(per_row, axis=0, keepdims=True) / count
    weights = slopes * (LOSS_SCALE / (TAU * count))
    take_z(2)
    take_x(1)
    mine = lax.broadcasted_iota(jnp.int32, (count, di), 0) == own
    q_back = jnp.sum(
        jnp.where(mine, dot(weights, every_items, precision=HIGH), 0.0), axis=0, keepdims=True
    )
    column = lax.broadcasted_iota(jnp.int32, (count, count), 1) == own
    i_back = jnp.sum(
        jnp.sum(jnp.where(column, weights, 0.0), axis=1, keepdims=True) * every_query,
        axis=0,
        keepdims=True,
    )
    q_grad_e = unit_back(q_e, q_norm, q_back)
    q_up = jnp.sum(dot(split_rows(q_grad_e), proj[...], ((1,), (1,))), axis=0, keepdims=True) / QLEN
    i_up = unit_back(i_pooled, i_norm, i_back) / ILEN
    along = q_gain * q_up
    along_of = [by_tower(along, count, tower) for tower in range(2)]
    inner = jnp.mean(along * q_resid, axis=-1, keepdims=True)
    slope = (q_scale * q_scale * q_scale) * inner
    lane = lax.broadcasted_iota(jnp.int32, (n, 128), 1)
    columns = jnp.where(lane == 0, q_scale, jnp.where(lane == 1, slope, 0.0))
    columns = jnp.concatenate([columns, jnp.zeros((128 - n, 128), F32)], axis=0)
    scal[p.t] = columns.T[:8]
    spread_members(scal, s3, r3s)
    yi[pl.ds(pl.multiple_of(p.z * m, m), m), :] = grad_rows(i_resid, i_scale, i_gain, i_up)
    igather.start(1)
    take_z(3)
    take_x(4)
    item_grad_hop(1)
    await_members(scal, s3, r3s)
    back_got(0)
    back_got(1)
    product(0)
    take_z(5)
    take_x(2)
    product(1)
    item_grad_hop(2)
    take_z(6)
    take_x(3)
    product(2)
    take_z(7)
    item_grad_hop(3)
    product(3)
    q_start(0)
    take_x(5)
    q_far(0)
    product(4)
    item_grad_hop(4)
    take_x(6)
    q_near(0)
    i_product()
    product(5)
    take_x(7)
    i_far()
    product(6)
    q_own(0)
    i_near()
    product(7)
    q_start(1)
    q_far(1)
    i_own()
    q_near(1)
    i_finish()
    q_finish(0)
    q_own(1)
    q_finish(1)

    for j in range(2):
        back(j).wait_send()
        for copy in (rows.right(j), rows.left(j), rows.half_right(j), rows.half_left(j)):
            copy.wait_send()
        for q in range(2):
            for way in range(2):
                first(j, q, way).wait_send()
                second(j, q, way).wait_send()
    for q in range(2):
        to_owner(q).wait_send()
    across().wait_send()
    items.drain()
    isum.drain()
    for index in range(3):
        for kind in range(9):
            w_send(index, kind).wait_send()
    for kind in range(7):
        v_send(kind).wait_send()
    for tower in range(2):
        gather[tower].drain()
        for j in range(4):
            q_core(tower, j).wait_send()
        for way in range(2):
            q_first(tower, way).wait_send()
            q_second(tower, way).wait_send()

        @pl.when(p.w != tower)
        def _():
            q_tower(tower).wait_send()

    igather.drain()
    for j in range(4):
        i_core(j).wait_send()
    for way in range(2):
        i_first(way).wait_send()
        i_second(way).wait_send()
    for hop in range(1, X):
        i_x(hop).wait_send()


def step(qa, qg, gate, up, down, ia, ig, ig_w, iu_w, id_w, qf, if_, proj, ranks, positive):
    n, dq = qa.shape
    m, di = ia.shape
    f, k = down.shape[0], id_w.shape[0]
    padded = 64 * ((f + 63) // 64)
    vmem, hbm = pl.BlockSpec(memory_space=pltpu.VMEM), pl.BlockSpec(memory_space=pl.ANY)
    smem = pl.BlockSpec(memory_space=pltpu.SMEM)
    all_i = ZR * m
    group = X * n
    parts = X * ZL
    count = ranks.shape[0]
    wide = dq // count
    dma = pltpu.SemaphoreType.DMA
    return pl.pallas_call(
        kernel,
        out_shape=(
            jax.ShapeDtypeStruct((1, 1), F32),
            jax.ShapeDtypeStruct((wide, f), F32),
            jax.ShapeDtypeStruct((wide, k), F32),
        ),
        in_specs=[vmem, vmem, hbm, hbm, hbm] + [vmem] * 7 + [hbm, vmem, smem],
        out_specs=[vmem] * 3,
        scratch_shapes=[
            pltpu.VMEM((2, 3, padded, dq), BF16),
            pltpu.VMEM(proj.shape, BF16),
            pltpu.VMEM((2 * group, dq), BF16),
            pltpu.VMEM((2, group, dq), F32),
            pltpu.VMEM((2, group, f), F32),
            pltpu.VMEM((2, group, f), BF16),
            pltpu.VMEM((2, 2 * group, dq // 2), BF16),
            pltpu.VMEM((2, 2, 2, n // 2, dq // 2), BF16),
            pltpu.VMEM((2, 2, 2, n, dq // 2), BF16),
            pltpu.VMEM((2, n, dq // 2), BF16),
            pltpu.VMEM((2, n, dq // 2), BF16),
            pltpu.VMEM((all_i, di), BF16),
            pltpu.VMEM((3, X * k, di), BF16),
            pltpu.VMEM((all_i, di), BF16),
            pltpu.VMEM((2, 4, m, di), BF16),
            pltpu.VMEM((ZL * group, f), BF16),
            pltpu.VMEM((X, all_i, k), BF16),
            pltpu.VMEM((parts, 1, dq + di), F32),
            pltpu.VMEM((count, 1, 2 * di), F32),
            pltpu.VMEM((parts, 8, 128), F32),
            pltpu.VMEM((2, parts * n, dq // 2), BF16),
            pltpu.VMEM((group, dq // 2), BF16),
            pltpu.VMEM((all_i, di), BF16),
            pltpu.VMEM((2, dq // 2, f), F32),
            pltpu.VMEM((X, di, k), F32),
            pltpu.VMEM((2, 4, wide, f), F32),
            pltpu.VMEM((2, 2, wide // 2, f), F32),
            pltpu.VMEM((2, 2, wide, f), F32),
            pltpu.VMEM((wide, f), F32),
            pltpu.VMEM((4, X, wide, k), F32),
            pltpu.VMEM((2, 2, wide, k), F32),
            pltpu.VMEM((2, X, wide, k), F32),
            pltpu.VMEM((X, wide, k), F32),
            dma((4,)),
            dma((6, 2)),
            dma((5, 2)),
            dma((5, 2, 2)),
            dma((5, 2, 2)),
            dma((9, 3)),
            dma((9, 3)),
            dma((7,)),
            dma((7,)),
            dma((2,)),
            dma((2,)),
            dma((2, 4)),
            dma((2, 4)),
            dma((2, 4)),
            dma((2, 4)),
            dma((parts,)),
            dma((parts,)),
            dma((count,)),
            dma((count,)),
            dma((parts,)),
            dma((parts,)),
            dma((2, 6, ZL)),
            dma((2, 5, ZL)),
            dma((2, 4)),
            dma((2, 4)),
            dma((2, 9)),
            dma((2, 9)),
            dma((12,)),
            dma((12,)),
        ],
        compiler_params=pltpu.CompilerParams(
            collective_id=0, has_side_effects=True, vmem_limit_bytes=VMEM_LIMIT
        ),
        name="towers_step",
    )(qa, qg, gate, up, down, ia, ig, ig_w, iu_w, id_w, qf, if_, proj, ranks, positive)


def body(
    q_act,
    q_norm_gain,
    q_gate,
    q_up,
    q_down,
    q_final_gain,
    projection,
    i_act,
    i_norm_gain,
    i_gate,
    i_up,
    i_down,
    i_final_gain,
    ranks,
    positive,
):
    loss, q_grad, i_grad = step(
        q_act,
        q_norm_gain,
        q_gate.T,
        q_up.T,
        q_down,
        i_act,
        i_norm_gain,
        i_gate.T,
        i_up.T,
        i_down,
        q_final_gain,
        i_final_gain,
        projection,
        ranks,
        positive,
    )
    return (loss.reshape(()), q_grad.T, i_grad.T)


def solution(mesh):
    in_specs = (
        P(("dp", "tower", "tensor"), None),
        P(),
        P(None, "tensor"),
        P(None, "tensor"),
        P("tensor", None),
        P(),
        P(),
        P(("dp", "tower", "tensor"), None),
        P(),
        P(None, ("tower", "tensor")),
        P(None, ("tower", "tensor")),
        P(("tower", "tensor"), None),
        P(),
        P(),
        P(),
    )
    out_specs = (P(), P("tensor", ("dp", "tower")), P(("tower", "tensor"), "dp"))
    return jax.shard_map(body, mesh=mesh, in_specs=in_specs, out_specs=out_specs, check_vma=False)
```

```python
import functools

import jax
import jax.numpy as jnp
from jax import lax
from jax.experimental import pallas as pl
from jax.experimental.pallas import tpu as pltpu
from jax.sharding import PartitionSpec as P

QLEN = 1536
ILEN = 512
EPS = 1e-06
TAU = 0.05
TEACH = 2.0
LOSS_SCALE = 64.0
HIGH = lax.Precision.HIGHEST
MESH = pl.DeviceIdType.MESH
F32 = jnp.float32
BF16 = jnp.bfloat16

X = 4
ZL = 4
ZR = 8
VMEM_LIMIT = 60 * 1024 * 1024


def rms_scale(values):
    return lax.rsqrt(jnp.mean(values * values, axis=-1, keepdims=True) + EPS)


def dot(left, right, dims=((1,), (0,)), precision=None):
    return lax.dot_general(
        left, right, (dims, ((), ())), preferred_element_type=F32, precision=precision
    )


def remote(src, dst, send, recv, where):
    return pltpu.make_async_remote_copy(
        src_ref=src, dst_ref=dst, send_sem=send, recv_sem=recv, device_id=where, device_id_type=MESH
    )


class Place:
    def __init__(self):
        self.t = lax.axis_index("tensor")
        self.w = lax.axis_index("tower")
        self.a = self.t // X
        self.b = self.t % X
        self.z = self.w * ZL + self.a
        self.bp = (self.b + 1) % X
        self.bm = (self.b + X - 1) % X
        self.bo = (self.b + 2) % X
        self.xp = {"tensor": self.a * X + self.bp}
        self.xm = {"tensor": self.a * X + self.bm}
        self.zp = self.ring(1)
        self.zm = self.ring(ZR - 1)

    def ring(self, step):
        z = (self.z + step) % ZR
        return {"tower": z // ZL, "tensor": (z % ZL) * X + self.b}

    def column(self, row):
        return {"tensor": row * X + self.b}

    def order(self, j):
        near = jnp.minimum(self.a, ZL - 1 - self.a)
        swapped = jnp.where(j == 0, 1, jnp.where(j == 1, 0, j))
        row = jnp.where(near == 1, swapped, j)
        return jnp.where(self.a >= 2, ZL - 1 - row, row)


def rows_of(ref, first, count, unit):
    return ref.at[pl.ds(pl.multiple_of(first, unit), count), :]


class RowGather:
    def __init__(self, place, buf, rows, send, recv):
        self.p, self.buf, self.n, self.send, self.recv = place, buf, rows, send, recv

    def block(self, s, b):
        return rows_of(self.buf, (s * X + b) * self.n, self.n, self.n)

    def half(self, s, b, h):
        n = self.n // 2
        return rows_of(self.buf, (s * X + b) * self.n + h * n, n, n)

    def along_z(self, hop):
        ref = self.block(self.p.a, self.p.b)
        where = self.p.column((self.p.a + hop) % ZL)
        return remote(ref, ref, self.send.at[0, hop], self.recv.at[0, self.p.a], where)

    def right(self, s):
        ref = self.block(s, self.p.b)
        return remote(ref, ref, self.send.at[1, s], self.recv.at[1, s], self.p.xp)

    def left(self, s):
        ref = self.block(s, self.p.b)
        return remote(ref, ref, self.send.at[2, s], self.recv.at[2, s], self.p.xm)

    def half_right(self, s):
        ref = self.half(s, self.p.bm, 0)
        return remote(ref, ref, self.send.at[3, s], self.recv.at[3, s], self.p.xp)

    def half_left(self, s):
        ref = self.half(s, self.p.bp, 1)
        return remote(ref, ref, self.send.at[4, s], self.recv.at[4, s], self.p.xm)

    def take_z(self, s):
        @pl.when(s != self.p.a)
        def _():
            ref = self.block(s, self.p.b)
            where = self.p.column(s)
            remote(ref, ref, self.send.at[0, 0], self.recv.at[0, s], where).wait_recv()

        self.right(s).start()
        self.left(s).start()

    def take_x(self, s):
        ref = self.block(s, self.p.bm)
        remote(ref, ref, self.send.at[1, s], self.recv.at[1, s], self.p.xm).wait_recv()
        self.half_right(s).start()
        ref = self.block(s, self.p.bp)
        remote(ref, ref, self.send.at[2, s], self.recv.at[2, s], self.p.xp).wait_recv()
        self.half_left(s).start()

    def take_halves(self, s):
        ref = self.half(s, self.p.bo, 0)
        remote(ref, ref, self.send.at[3, s], self.recv.at[3, s], self.p.xm).wait_recv()
        ref = self.half(s, self.p.bo, 1)
        remote(ref, ref, self.send.at[4, s], self.recv.at[4, s], self.p.xp).wait_recv()

    def drain(self):
        for hop in range(1, ZL):
            self.along_z(hop).wait_send()

        def each(s, _):
            self.right(s).wait_send()
            self.left(s).wait_send()
            self.half_right(s).wait_send()
            self.half_left(s).wait_send()
            return 0

        lax.fori_loop(0, ZL, each, 0)


class RingGather:
    def __init__(self, place, buf, rows, send, recv):
        self.p, self.buf, self.n, self.send, self.recv = place, buf, rows, send, recv

    def ref(self, z, hop, upward):
        z = (z + 2 * ZR) % ZR
        if hop < 4:
            return rows_of(self.buf, z * self.n, self.n, self.n)
        n = self.n // 2
        return rows_of(self.buf, z * self.n + (0 if upward else n), n, n)

    def copies(self, hop):
        up = self.ref(self.p.z - hop + 1, hop, True)
        down = self.ref(self.p.z + hop - 1, hop, False)
        return (
            remote(up, up, self.send.at[0, hop - 1], self.recv.at[0, hop - 1], self.p.zp),
            remote(down, down, self.send.at[1, hop - 1], self.recv.at[1, hop - 1], self.p.zm),
        )

    def start(self, hop):
        for copy in self.copies(hop):
            copy.start()

    def take(self, hop):
        up = self.ref(self.p.z - hop, hop, True)
        down = self.ref(self.p.z + hop, hop, False)
        remote(up, up, self.send.at[0, hop - 1], self.recv.at[0, hop - 1], self.p.zm).wait_recv()
        remote(down, down, self.send.at[1, hop - 1], self.recv.at[1, hop - 1], self.p.zp).wait_recv()

    def drain(self):
        for hop in range(1, 5):
            for copy in self.copies(hop):
                copy.wait_send()


class RingSum:
    def __init__(self, place, buf, land, rows, send, recv):
        self.p, self.buf, self.land = place, buf, land
        self.n, self.send, self.recv = rows, send, recv

    def part(self, z, half):
        z = (z + 2 * ZR) % ZR
        if half is None:
            return rows_of(self.buf, z * self.n, self.n, self.n)
        n = self.n // 2
        return rows_of(self.buf, z * self.n + half * n, n, n)

    def slot(self, way, hop):
        if hop == 1:
            return self.land.at[way, 0, pl.ds(0, self.n // 2), :]
        return self.land.at[way, hop - 1]

    def copies(self, hop):
        half = (0, 1) if hop == 1 else (None, None)
        up = self.part(self.p.z + 5 - hop, half[0])
        down = self.part(self.p.z - 5 + hop, half[1])
        return (
            remote(up, self.slot(0, hop), self.send.at[0, hop - 1], self.recv.at[0, hop - 1], self.p.zp),
            remote(down, self.slot(1, hop), self.send.at[1, hop - 1], self.recv.at[1, hop - 1], self.p.zm),
        )

    def start(self, hop):
        for copy in self.copies(hop):
            copy.start()

    def take(self, hop):
        for copy in self.copies(hop):
            copy.wait_recv()

    def add(self, hop):
        half = (0, 1) if hop == 1 else (None, None)
        for way, z in ((0, self.p.z + 4 - hop), (1, self.p.z - 4 + hop)):
            ref = self.part(z, half[way])
            ref[...] = (ref[...].astype(F32) + self.slot(way, hop)[...].astype(F32)).astype(BF16)

    def drain(self):
        for hop in range(1, 5):
            for copy in self.copies(hop):
                copy.wait_send()


def gain_row(ref):
    return ref[...].astype(F32).reshape(1, -1)


def normed_rows(act, gain):
    values = act.astype(F32)
    return (values * rms_scale(values) * gain).astype(BF16)


def gated(gate_val, up_val):
    return (jax.nn.silu(gate_val) * up_val).astype(BF16)


def at_step(i, step):
    return pl.when(i == step)


def split_rows(row):
    high = row.astype(BF16).astype(F32)
    rest = row - high
    mid = rest.astype(BF16).astype(F32)
    low = rest - mid
    index = lax.broadcasted_iota(jnp.int32, (8, row.shape[1]), 0)
    out = jnp.where(index == 0, high, jnp.where(index == 1, mid, jnp.where(index == 2, low, 0.0)))
    return out.astype(BF16)


def unit_scale(vec):
    return lax.rsqrt(jnp.sum(vec * vec, axis=-1, keepdims=True) + EPS)


def unit_back(vec, scales, upstream):
    inner = jnp.sum(vec * upstream, axis=-1, keepdims=True)
    return scales * upstream - vec * (scales * scales * scales) * inner


def contrast(query_hat, item_hat, ranks, positive):
    logits = dot(query_hat, item_hat, ((1,), (1,)), HIGH) / TAU
    shifted = logits - 1.0 / TAU
    log_student = shifted - jnp.log(jnp.sum(jnp.exp(shifted), axis=1, keepdims=True))
    teach = -ranks.astype(F32) / TEACH
    log_teacher = teach - jnp.log(jnp.sum(jnp.exp(teach), axis=1, keepdims=True))
    teacher = jnp.exp(log_teacher)
    columns = lax.broadcasted_iota(jnp.int32, logits.shape, 1)
    onehot = (columns == positive).astype(F32)
    per_row = jnp.sum(
        teacher * (log_teacher - log_student) - onehot * log_student, axis=1, keepdims=True
    )
    slopes = 2.0 * jnp.exp(log_student) - onehot - teacher
    return (per_row, slopes)


def grad_rows(resid, scales, gain, upstream):
    along = gain * upstream
    inner = jnp.mean(along * resid, axis=-1, keepdims=True)
    return (scales * along - resid * (scales * scales * scales) * inner).astype(BF16)


def by_chunk(values, parts, q):
    wide = values.shape[1] // parts
    part = wide // 2
    firsts = [d * wide + (q // 2) * part for d in range(q % 2, parts, 2)]
    return jnp.concatenate([values[:, first : first + part] for first in firsts], axis=1)


def kernel(
    qa, qg, gate_hbm, up_hbm, down_hbm, ia, ig, ig_w, iu_w, id_w, qf, if_, proj_hbm, ranks, positive,
    loss, q_out, i_out,
    w, proj, nq, part, gate_val, h2, pm, r1, r2, zs, zin, ni, wi, ip, land, hq, hi,
    sums, hats, scal, yq, hs_w, yi, gq, gi, qc1, qb1, qb2, qc, ic1, ib1, ib2, ic,
    loads, gs, gr, ss, sr, ws, wr, vs, vr, hs, hr, ias, iar, irs, irr,
    s1, r1s, s2, r2s, s3, r3s, ys, yr, iys, iyr, qs, qv, bs, bv,
):
    p = Place()
    n, dq = qa.shape
    m, di = ia.shape
    f, k = down_hbm.shape[0], id_w.shape[0]
    group = X * n
    h = n // 2
    parts = X * ZL
    count = hats.shape[0]
    block_wide = dq // count
    piece = w.shape[2] // 4
    wide, thin = dq // 2, dq // 4
    dp = lax.axis_index("dp")
    own = dp * 2 + p.w
    y, c = dp // 2, dp % 2
    yp, ym, y2 = (y + 1) % 4, (y + 3) % 4, (y + 2) % 4
    line_y = (y2, yp, ym, y)
    to_yp, to_ym, to_core = {"dp": yp * 2 + c}, {"dp": ym * 2 + c}, {"dp": y * 2 + 1 - c}
    to_y = (to_yp, to_ym)
    to_tower = {"tower": 1 - p.w}
    a2 = (p.a + 2) % ZL
    mate = p.a + 1 - 2 * (p.a % 2)
    to_a2, to_mate = p.column(a2), p.column(mate)

    def member(step):
        return {"tensor": (p.t + step) % parts}

    def replica(step):
        other = (own + step) % count
        return {"dp": other // 2, "tower": other % 2}

    own_weights = [
        pltpu.make_async_copy(ref, w.at[0, index, pl.ds(0, f), :], loads.at[index])
        for index, ref in enumerate((gate_hbm, up_hbm, down_hbm))
    ]
    proj_copy = pltpu.make_async_copy(proj_hbm, proj, loads.at[3])
    for copy in own_weights:
        copy.start()
    proj_copy.start()
    barrier = pltpu.get_barrier_semaphore()

    def greet(step, _):
        pl.semaphore_signal(barrier, inc=1, device_id=member(step), device_id_type=MESH)
        pl.semaphore_signal(barrier, inc=1, device_id=replica(step), device_id_type=MESH)
        return 0

    lax.fori_loop(1, parts, greet, 0)
    for where in (p.zp, p.zm):
        pl.semaphore_signal(barrier, inc=1, device_id=where, device_id_type=MESH)
    for index in range(3):
        w[0, index, f:, :] = jnp.zeros((w.shape[2] - f, dq), BF16)
    nq[pl.ds(pl.multiple_of(p.b * n, n), n), :] = normed_rows(qa[...], gain_row(qg))
    ni[pl.ds(pl.multiple_of(p.z * m, m), m), :] = normed_rows(ia[...], gain_row(ig))
    for index, ref in enumerate((ig_w, iu_w, id_w)):
        wi[index, pl.ds(pl.multiple_of(p.b * k, k), k), :] = ref[...]
    pl.semaphore_wait(barrier, 2 * (parts - 1) + 2)

    rows = RowGather(p, nq, n, gs, gr)
    items = RingGather(p, ni, m, ias, iar)
    isum = RingSum(p, ip, land, m, irs, irr)

    def across():
        return remote(rows.block(0, p.b), rows.block(1, p.b), gs.at[0, 0], gr.at[0, 0], to_a2)

    def wpiece(which, index, line, core):
        first = pl.multiple_of(line * piece, piece)
        return w.at[which, index, pl.ds(first, piece), pl.ds(pl.multiple_of(core * wide, wide), wide)]

    def whalf(index, line, part_of):
        first = pl.multiple_of(line * piece, piece)
        column = pl.multiple_of(c * wide + part_of * thin, thin)
        return w.at[1, index, pl.ds(first, piece), pl.ds(column, thin)]

    def w_send(index, kind):
        here = wpiece(1, index, y, c)
        low, high = wpiece(1, index, ym, c), wpiece(1, index, yp, c)
        src, dst, where = (
            (wpiece(0, index, y, c), here, to_mate),
            (here, here, to_yp),
            (here, here, to_ym),
            (whalf(index, ym, 0), whalf(index, ym, 0), to_yp),
            (whalf(index, yp, 1), whalf(index, yp, 1), to_ym),
            (here, here, to_core),
            (low, low, to_core),
            (high, high, to_core),
            (wpiece(1, index, y2, c), wpiece(1, index, y2, c), to_core),
        )[kind]
        return remote(src, dst, ws.at[kind, index], wr.at[kind, index], where)

    def w_got(index, kind):
        dst = (
            wpiece(1, index, y, c),
            wpiece(1, index, ym, c),
            wpiece(1, index, yp, c),
            whalf(index, y2, 0),
            whalf(index, y2, 1),
            wpiece(1, index, y, 1 - c),
            wpiece(1, index, ym, 1 - c),
            wpiece(1, index, yp, 1 - c),
            wpiece(1, index, y2, 1 - c),
        )[kind]
        remote(dst, dst, ws.at[kind, index], wr.at[kind, index], to_core).wait_recv()

    def w_near(index):
        w_got(index, 0)
        for kind in (1, 2, 5):
            w_send(index, kind).start()

    def w_ring(index):
        w_got(index, 1)
        w_send(index, 3).start()
        w_send(index, 6).start()
        w_got(index, 2)
        w_send(index, 4).start()
        w_send(index, 7).start()

    def w_far(index):
        w_got(index, 3)
        w_got(index, 4)
        w_send(index, 8).start()

    def w_done(index):
        for kind in (5, 6, 7, 8):
            w_got(index, kind)

    def vpiece(b, core):
        column = pl.multiple_of(core * (di // 2), di // 2)
        return wi.at[:, pl.ds(pl.multiple_of(b * k, k), k), pl.ds(column, di // 2)]

    def vhalf(b, part_of):
        first = pl.multiple_of(b * k + part_of * (k // 2), k // 2)
        column = pl.multiple_of(c * (di // 2), di // 2)
        return wi.at[:, pl.ds(first, k // 2), pl.ds(column, di // 2)]

    def v_send(kind):
        ref, where = (
            (vpiece(p.b, c), p.xp),
            (vpiece(p.b, c), p.xm),
            (vhalf(p.bm, 0), p.xp),
            (vhalf(p.bp, 1), p.xm),
            (vpiece(p.bm, c), to_core),
            (vpiece(p.bp, c), to_core),
            (vpiece(p.bo, c), to_core),
        )[kind]
        return remote(ref, ref, vs.at[kind], vr.at[kind], where)

    def v_got(kind):
        ref = (
            vpiece(p.bm, c),
            vpiece(p.bp, c),
            vhalf(p.bo, 0),
            vhalf(p.bo, 1),
            vpiece(p.bm, 1 - c),
            vpiece(p.bp, 1 - c),
            vpiece(p.bo, 1 - c),
        )[kind]
        remote(ref, ref, vs.at[kind], vr.at[kind], to_core).wait_recv()

    def block(j, q, b):
        return rows_of(pm.at[q], (j * X + b) * n, n, n)

    def half(j, q, b, part_of):
        return rows_of(pm.at[q], (j * X + b) * n + part_of * h, h, h)

    def first(j, q, way):
        src = half(j, q, p.bo, way)
        where = (p.xp, p.xm)[way]
        return remote(src, r1.at[way, j, q], ss.at[way, j, q], sr.at[way, j, q], where)

    def second(j, q, way):
        src = block(j, q, (p.bp, p.bm)[way])
        where = (p.xp, p.xm)[way]
        return remote(src, r2.at[way, j, q], ss.at[2 + way, j, q], sr.at[2 + way, j, q], where)

    def to_owner(q):
        return remote(zs.at[q], zin.at[q], ss.at[4, 0, q], sr.at[4, 0, q], to_a2)

    def back(j):
        s = (p.a, a2)[j]
        dst = hq.at[pl.ds(pl.multiple_of(s * group, group), group), :]
        return remote(h2.at[j], dst, hs.at[j], hr.at[j], to_mate)

    def back_got(j):
        other = (mate, (mate + 2) % ZL)[j]
        dst = hq.at[pl.ds(pl.multiple_of(other * group, group), group), :]
        remote(h2.at[j], dst, hs.at[j], hr.at[j], to_mate).wait_recv()

    def rows_in(j):
        return nq[j * group : (j + 1) * group, :]

    def own_units(j):
        left = rows_in(j)
        value = gated(
            dot(left, w[0, 0, :f, :], ((1,), (1,))), dot(left, w[0, 1, :f, :], ((1,), (1,)))
        )
        hq[pl.ds(pl.multiple_of((p.a, a2)[j] * group, group), group), :] = value
        part[j] = dot(value, w[0, 2, :f, :])

    def mate_gate(j):
        gate_val[j] = dot(rows_in(j), w[1, 0, :f, :], ((1,), (1,)))

    def mate_up(j):
        h2[j] = gated(gate_val[j], dot(rows_in(j), w[1, 1, :f, :], ((1,), (1,))))

    def mate_down(j, q):
        columns = slice(q * wide, (q + 1) * wide)
        total = part[j, :, columns] + dot(h2[j], w[1, 2, :f, columns])
        pm[q, j * group : (j + 1) * group, :] = total.astype(BF16)
        first(j, q, 0).start()
        first(j, q, 1).start()

    def combine(j, q):
        for way in range(2):
            first(j, q, way).wait_recv()
            ref = half(j, q, (p.bp, p.bm)[way], way)
            ref[...] = (ref[...].astype(F32) + r1[way, j, q].astype(F32)).astype(BF16)
            second(j, q, way).start()

    def summed(j, q):
        second(j, q, 0).wait_recv()
        second(j, q, 1).wait_recv()
        total = block(j, q, p.b)[...].astype(F32)
        return total + r2[0, j, q].astype(F32) + r2[1, j, q].astype(F32)

    def send_sum(q):
        zs[q] = summed(1, q).astype(BF16)
        to_owner(q).start()

    def item_hop(hop):
        items.take(hop)
        if hop < 4:
            items.start(hop + 1)

    def isum_hop(hop):
        isum.take(hop)
        isum.add(hop)
        isum.start(hop + 1)

    def item_product():
        left = ni[...]
        partial = 0.0
        for b in range(X):
            here = slice(b * k, (b + 1) * k)
            value = gated(
                dot(left, wi[0, here, :], ((1,), (1,))), dot(left, wi[1, here, :], ((1,), (1,)))
            )
            hi[b] = value
            partial = partial + dot(value, wi[2, here, :])
        ip[...] = partial.astype(BF16)
        isum.start(1)

    rows.right(0).start()
    rows.left(0).start()
    items.start(1)
    own_weights[0].wait()
    w_send(0, 0).start()
    across().start()
    own_weights[1].wait()
    own_weights[2].wait()
    w_near(0)
    w_send(1, 0).start()
    rows.take_x(0)
    item_hop(1)
    v_send(0).start()
    v_send(1).start()
    rows.take_halves(0)
    own_units(0)
    item_hop(2)
    w_ring(0)
    w_near(1)
    w_send(2, 0).start()
    remote(rows.block(0, p.b), rows.block(1, p.b), gs.at[0, 0], gr.at[0, 0], to_a2).wait_recv()
    rows.right(1).start()
    rows.left(1).start()
    item_hop(3)
    w_far(0)
    for kind in range(2):
        v_got(kind)
        v_send(2 + kind).start()
        v_send(4 + kind).start()
    item_hop(4)
    w_ring(1)
    w_near(2)
    w_done(0)
    mate_gate(0)
    v_got(2)
    v_got(3)
    v_send(6).start()
    w_far(1)
    for kind in (4, 5, 6):
        v_got(kind)
    item_product()
    rows.take_x(1)
    w_done(1)
    mate_up(0)
    w_ring(2)
    isum_hop(1)
    rows.take_halves(1)
    own_units(1)
    isum_hop(2)
    w_far(2)
    mate_gate(1)
    mate_up(1)
    isum_hop(3)
    w_done(2)
    mate_down(0, 0)
    mate_down(0, 1)
    mate_down(1, 0)
    mate_down(1, 1)
    back(0).start()
    combine(1, 0)
    combine(1, 1)
    combine(0, 0)
    send_sum(0)
    combine(0, 1)
    send_sum(1)
    isum.take(4)
    own_item = ip[pl.ds(pl.multiple_of(p.z * m, m), m), :].astype(F32)
    i_resid = ia[...].astype(F32) + (own_item + land[0, 3].astype(F32) + land[1, 3].astype(F32))
    mlp = []
    for q in range(2):
        total = summed(0, q)
        to_owner(q).wait_recv()
        mlp.append(total + zin[q].astype(F32))
    q_resid = qa[...].astype(F32) + jnp.concatenate(mlp, axis=1)

    q_gain, i_gain = gain_row(qf), gain_row(if_)
    q_scale, i_scale = rms_scale(q_resid), rms_scale(i_resid)
    sums[p.t, :, :dq] = jnp.sum(q_resid * q_scale * q_gain, axis=0, keepdims=True)
    sums[p.t, :, dq:] = jnp.sum(i_resid * i_scale * i_gain, axis=0, keepdims=True)

    def spread_members(buf, send, recv):
        def each(step, _):
            remote(buf.at[p.t], buf.at[p.t], send.at[step], recv.at[p.t], member(step)).start()
            return 0

        lax.fori_loop(1, parts, each, 0)

    def await_members(buf, send, recv):
        def each(step, _):
            other = (p.t + step) % parts
            remote(buf.at[p.t], buf.at[other], send.at[step], recv.at[other], member(step)).wait()
            return 0

        lax.fori_loop(1, parts, each, 0)

    def spread_hats(step, _):
        remote(hats.at[own], hats.at[own], s2.at[step], r2s.at[own], replica(step)).start()
        return 0

    def gathered_hats(step, _):
        other = (own + step) % count
        remote(hats.at[own], hats.at[other], s2.at[step], r2s.at[other], replica(step)).wait()
        return 0

    strip = block_wide // 2

    def q_rows(q, line_of, core):
        return rows_of(gq.at[q], (line_of * 2 + core) * strip, strip, strip)

    def q_half(q, line_of, way):
        first_row = (line_of * 2 + c) * strip + way * (strip // 2)
        return rows_of(gq.at[q], first_row, strip // 2, strip // 2)

    def q_core(q, j):
        src = q_rows(q, line_y[j], 1 - c)
        return remote(src, qc1.at[q, j], qs.at[q, j], qv.at[q, j], to_core)

    def q_first(q, way):
        src, dst = q_half(q, y2, way), qb1.at[q, way]
        return remote(src, dst, qs.at[q, 4 + way], qv.at[q, 4 + way], to_y[way])

    def q_second(q, way):
        src, dst = q_rows(q, (yp, ym)[way], c), qb2.at[q, way]
        return remote(src, dst, qs.at[q, 6 + way], qv.at[q, 6 + way], to_y[way])

    def q_tower(q):
        return remote(q_rows(q, y, c), qc.at[q // 2], qs.at[q, 8], qv.at[q, 8], to_tower)

    def q_start(q):
        for j in range(4):
            q_core(q, j).start()

    def q_far(q):
        q_core(q, 0).wait_recv()
        ref = q_rows(q, y2, c)
        ref[...] += qc1[q, 0]
        for way in range(2):
            q_first(q, way).start()

    def q_near(q):
        for way in range(2):
            q_core(q, 1 + way).wait_recv()
            ref = q_rows(q, (yp, ym)[way], c)
            ref[...] += qc1[q, 1 + way]
            q_first(q, way).wait_recv()
            ref = q_half(q, (yp, ym)[way], way)
            ref[...] += qb1[q, way]
            q_second(q, way).start()

    def q_own(q):
        q_core(q, 3).wait_recv()
        for way in range(2):
            q_second(q, way).wait_recv()
        ref = q_rows(q, y, c)
        ref[...] = ref[...] + qc1[q, 3] + qb2[q, 0] + qb2[q, 1]

        @pl.when(p.w != q % 2)
        def _():
            q_tower(q).start()

    def q_finish(q):
        @pl.when(p.w == q % 2)
        def _():
            q_tower(q).wait_recv()
            here = slice((q // 2) * strip, (q // 2 + 1) * strip)
            q_out[here, :] = q_rows(q, y, c)[...] + qc[q // 2]

    def i_rows(line_of, core):
        first = pl.multiple_of((line_of * 2 + core) * block_wide, block_wide)
        return gi.at[:, pl.ds(first, block_wide), :]

    def i_half(line_of, way):
        first = pl.multiple_of((line_of * 2 + c) * block_wide, block_wide)
        return gi.at[pl.ds(way * 2, 2), pl.ds(first, block_wide), :]

    def i_slab(b):
        return gi.at[b, pl.ds(pl.multiple_of((y * 2 + c) * block_wide, block_wide), block_wide), :]

    def i_core(j):
        return remote(i_rows(line_y[j], 1 - c), ic1.at[j], bs.at[j], bv.at[j], to_core)

    def i_first(way):
        return remote(i_half(y2, way), ib1.at[way], bs.at[4 + way], bv.at[4 + way], to_y[way])

    def i_second(way):
        src = i_rows((yp, ym)[way], c)
        return remote(src, ib2.at[way], bs.at[6 + way], bv.at[6 + way], to_y[way])

    def i_x(hop):
        other = (p.b + hop) % X
        where = {"tensor": p.a * X + other}
        return remote(i_slab(other), ic.at[p.b], bs.at[8 + hop], bv.at[8 + p.b], where)

    def i_product():
        for b in range(X):
            gi[b] = dot(yi[...], hi[b], ((0,), (0,)))
        for j in range(4):
            i_core(j).start()

    def i_far():
        for j in range(4):
            i_core(j).wait_recv()
            ref = i_rows(line_y[j], c)
            ref[...] += ic1[j]
        for way in range(2):
            i_first(way).start()

    def i_near():
        for way in range(2):
            i_first(way).wait_recv()
            ref = i_half((yp, ym)[way], way)
            ref[...] += ib1[way]
            i_second(way).start()

    def i_own():
        for way in range(2):
            i_second(way).wait_recv()
        ref = i_rows(y, c)
        ref[...] = ref[...] + ib2[0] + ib2[1]
        for hop in range(1, X):
            i_x(hop).start()

    def i_finish():
        total = i_slab(p.b)[...]
        for hop in range(1, X):
            other = (p.b + hop) % X
            remote(i_slab(other), ic.at[other], bs.at[8 + hop], bv.at[8 + other], p.xp).wait_recv()
            total = total + ic[other]
        i_out[...] = total

    chunks = 4
    gather = [RowGather(p, yq.at[q], n, ys.at[q], yr.at[q]) for q in range(chunks)]
    igather = RingGather(p, yi, m, iys, iyr)
    steps = (0, 1, 4, 2, 3, 8, 5, 12, 6, 7, 9, 10, 11, 13, 14, 15)

    def along_z(q):
        for hop in range(1, ZL):
            gather[q].along_z(hop).start()

    def advance(index):
        if index < len(steps):
            gather[steps[index] // ZL].take_z(p.order(steps[index] % ZL))
        if 0 <= index - 2 < len(steps):
            gather[steps[index - 2] // ZL].take_x(p.order(steps[index - 2] % ZL))

    def item_grad_hop(hop):
        igather.take(hop)
        if hop < 4:
            igather.start(hop + 1)

    def scaled(j):
        s = p.order(j)
        columns = []
        for b in range(X):
            tile = scal[s * X + b]
            columns.append(jnp.concatenate([tile] * 16, axis=0).T[:n])
        columns = jnp.concatenate(columns, axis=0)
        here = pl.ds(pl.multiple_of(s * group, group), group)
        value = hq[here, :].astype(F32)
        hs_w[here, :] = (value * columns[:, 1:2]).astype(BF16)
        return jnp.sum(value * columns[:, 0:1], axis=0, keepdims=True)

    def product(q):
        for s in range(ZL):
            gather[q].take_halves(s)
        column = jnp.broadcast_to(along_of[q], (128, along_of[q].shape[1])).T[:, 0:1]
        gq[q] = column * summed_hidden - dot(yq[q], hs_w[...], ((0,), (0,)))
        q_start(q)

    spread_members(sums, s1, r1s)
    here = pl.ds(pl.multiple_of(p.t * n, n), n)
    for q in range(chunks):
        yq[q, here, :] = by_chunk(q_resid, count, q).astype(BF16)
    advance(0)
    along_z(0)
    along_z(1)
    back(1).start()
    proj_copy.wait()
    await_members(sums, s1, r1s)
    total = sums[0]
    for slot in range(1, parts):
        total = total + sums[slot]
    q_pooled = total[:, :dq] / QLEN
    i_pooled = total[:, dq:] / ILEN
    advance(1)
    q_e = jnp.sum(dot(split_rows(q_pooled), proj[...]), axis=0, keepdims=True)
    q_norm, i_norm = unit_scale(q_e), unit_scale(i_pooled)
    hats[own, :, :di] = q_e * q_norm
    hats[own, :, di:] = i_pooled * i_norm
    lax.fori_loop(1, count, spread_hats, 0)
    advance(2)
    advance(3)
    lax.fori_loop(1, count, gathered_hats, 0)
    index = lax.broadcasted_iota(jnp.int32, (count, 2 * di), 0)
    every = jnp.zeros((count, 2 * di), F32)
    for slot in range(count):
        every = jnp.where(index == slot, hats[slot], every)
    every_query, every_items = every[:, :di], every[:, di:]
    line = lax.broadcasted_iota(jnp.int32, (count, count), 0)
    target = jnp.zeros((count, count), jnp.int32)
    for slot in range(count):
        target = jnp.where(line == slot, positive[slot], target)
    per_row, slopes = contrast(every_query, every_items, ranks[...], target)
    advance(5)
    loss[...] = jnp.sum(per_row, axis=0, keepdims=True) / count
    weights = slopes * (LOSS_SCALE / (TAU * count))
    advance(4)
    mine = lax.broadcasted_iota(jnp.int32, (count, di), 0) == own
    q_back = jnp.sum(
        jnp.where(mine, dot(weights, every_items, precision=HIGH), 0.0), axis=0, keepdims=True
    )
    column = lax.broadcasted_iota(jnp.int32, (count, count), 1) == own
    i_back = jnp.sum(
        jnp.sum(jnp.where(column, weights, 0.0), axis=1, keepdims=True) * every_query,
        axis=0,
        keepdims=True,
    )
    advance(6)
    along_z(2)
    q_grad_e = unit_back(q_e, q_norm, q_back)
    q_up = jnp.sum(dot(split_rows(q_grad_e), proj[...], ((1,), (1,))), axis=0, keepdims=True) / QLEN
    i_up = unit_back(i_pooled, i_norm, i_back) / ILEN
    advance(7)
    along = q_gain * q_up
    along_of = [by_chunk(along, count, q) for q in range(chunks)]
    inner = jnp.mean(along * q_resid, axis=-1, keepdims=True)
    slope = (q_scale * q_scale * q_scale) * inner
    lane = lax.broadcasted_iota(jnp.int32, (n, 128), 1)
    columns = jnp.where(lane == 0, q_scale, jnp.where(lane == 1, slope, 0.0))
    columns = jnp.concatenate([columns, jnp.zeros((128 - n, 128), F32)], axis=0)
    scal[p.t] = columns.T[:8]
    spread_members(scal, s3, r3s)
    yi[pl.ds(pl.multiple_of(p.z * m, m), m), :] = grad_rows(i_resid, i_scale, i_gain, i_up)
    igather.start(1)
    advance(8)
    along_z(3)
    await_members(scal, s3, r3s)
    back_got(0)
    back_got(1)
    summed_hidden = scaled(0) + scaled(1) + scaled(2) + scaled(3)
    product(0)
    advance(9)
    item_grad_hop(1)
    q_far(0)
    advance(10)
    advance(11)
    item_grad_hop(2)
    q_near(0)
    product(1)
    advance(12)
    q_far(1)
    item_grad_hop(3)
    advance(13)
    q_own(0)
    q_near(1)
    advance(14)
    product(2)
    item_grad_hop(4)
    i_product()
    q_far(2)
    advance(15)
    q_own(1)
    i_far()
    advance(16)
    q_near(2)
    q_finish(0)
    advance(17)
    i_near()
    product(3)
    q_far(3)
    q_own(2)
    q_near(3)
    i_own()
    q_finish(1)
    q_finish(2)
    i_finish()
    q_own(3)
    q_finish(3)

    for j in range(2):
        back(j).wait_send()
        for copy in (rows.right(j), rows.left(j), rows.half_right(j), rows.half_left(j)):
            copy.wait_send()
        for q in range(2):
            for way in range(2):
                first(j, q, way).wait_send()
                second(j, q, way).wait_send()
    for q in range(2):
        to_owner(q).wait_send()
    across().wait_send()
    items.drain()
    isum.drain()
    for index in range(3):
        for kind in range(9):
            w_send(index, kind).wait_send()
    for kind in range(7):
        v_send(kind).wait_send()
    for q in range(chunks):
        gather[q].drain()
        for j in range(4):
            q_core(q, j).wait_send()
        for way in range(2):
            q_first(q, way).wait_send()
            q_second(q, way).wait_send()

        @pl.when(p.w != q % 2)
        def _():
            q_tower(q).wait_send()

    igather.drain()
    for j in range(4):
        i_core(j).wait_send()
    for way in range(2):
        i_first(way).wait_send()
        i_second(way).wait_send()
    for hop in range(1, X):
        i_x(hop).wait_send()


def step(qa, qg, gate, up, down, ia, ig, ig_w, iu_w, id_w, qf, if_, proj, ranks, positive):
    n, dq = qa.shape
    m, di = ia.shape
    f, k = down.shape[0], id_w.shape[0]
    padded = 64 * ((f + 63) // 64)
    vmem, hbm = pl.BlockSpec(memory_space=pltpu.VMEM), pl.BlockSpec(memory_space=pl.ANY)
    smem = pl.BlockSpec(memory_space=pltpu.SMEM)
    all_i = ZR * m
    group = X * n
    parts = X * ZL
    count = ranks.shape[0]
    wide = dq // count
    dma = pltpu.SemaphoreType.DMA
    return pl.pallas_call(
        kernel,
        out_shape=(
            jax.ShapeDtypeStruct((1, 1), F32),
            jax.ShapeDtypeStruct((wide, f), F32),
            jax.ShapeDtypeStruct((wide, k), F32),
        ),
        in_specs=[vmem, vmem, hbm, hbm, hbm] + [vmem] * 7 + [hbm, vmem, smem],
        out_specs=[vmem] * 3,
        scratch_shapes=[
            pltpu.VMEM((2, 3, padded, dq), BF16),
            pltpu.VMEM(proj.shape, BF16),
            pltpu.VMEM((2 * group, dq), BF16),
            pltpu.VMEM((2, group, dq), F32),
            pltpu.VMEM((2, group, f), F32),
            pltpu.VMEM((2, group, f), BF16),
            pltpu.VMEM((2, 2 * group, dq // 2), BF16),
            pltpu.VMEM((2, 2, 2, n // 2, dq // 2), BF16),
            pltpu.VMEM((2, 2, 2, n, dq // 2), BF16),
            pltpu.VMEM((2, n, dq // 2), BF16),
            pltpu.VMEM((2, n, dq // 2), BF16),
            pltpu.VMEM((all_i, di), BF16),
            pltpu.VMEM((3, X * k, di), BF16),
            pltpu.VMEM((all_i, di), BF16),
            pltpu.VMEM((2, 4, m, di), BF16),
            pltpu.VMEM((ZL * group, f), BF16),
            pltpu.VMEM((X, all_i, k), BF16),
            pltpu.VMEM((parts, 1, dq + di), F32),
            pltpu.VMEM((count, 1, 2 * di), F32),
            pltpu.VMEM((parts, 8, 128), F32),
            pltpu.VMEM((4, parts * n, dq // 4), BF16),
            pltpu.VMEM((ZL * group, f), BF16),
            pltpu.VMEM((all_i, di), BF16),
            pltpu.VMEM((4, dq // 4, f), F32),
            pltpu.VMEM((X, di, k), F32),
            pltpu.VMEM((4, 4, wide // 2, f), F32),
            pltpu.VMEM((4, 2, wide // 4, f), F32),
            pltpu.VMEM((4, 2, wide // 2, f), F32),
            pltpu.VMEM((2, wide // 2, f), F32),
            pltpu.VMEM((4, X, wide, k), F32),
            pltpu.VMEM((2, 2, wide, k), F32),
            pltpu.VMEM((2, X, wide, k), F32),
            pltpu.VMEM((X, wide, k), F32),
            dma((4,)),
            dma((5, 2)),
            dma((5, 2)),
            dma((5, 2, 2)),
            dma((5, 2, 2)),
            dma((9, 3)),
            dma((9, 3)),
            dma((7,)),
            dma((7,)),
            dma((2,)),
            dma((2,)),
            dma((2, 4)),
            dma((2, 4)),
            dma((2, 4)),
            dma((2, 4)),
            dma((parts,)),
            dma((parts,)),
            dma((count,)),
            dma((count,)),
            dma((parts,)),
            dma((parts,)),
            dma((4, 5, ZL)),
            dma((4, 5, ZL)),
            dma((2, 4)),
            dma((2, 4)),
            dma((4, 9)),
            dma((4, 9)),
            dma((12,)),
            dma((12,)),
        ],
        compiler_params=pltpu.CompilerParams(
            collective_id=0, has_side_effects=True, vmem_limit_bytes=VMEM_LIMIT
        ),
        name="towers_step",
    )(qa, qg, gate, up, down, ia, ig, ig_w, iu_w, id_w, qf, if_, proj, ranks, positive)


def body(
    q_act,
    q_norm_gain,
    q_gate,
    q_up,
    q_down,
    q_final_gain,
    projection,
    i_act,
    i_norm_gain,
    i_gate,
    i_up,
    i_down,
    i_final_gain,
    ranks,
    positive,
):
    loss, q_grad, i_grad = step(
        q_act,
        q_norm_gain,
        q_gate.T,
        q_up.T,
        q_down,
        i_act,
        i_norm_gain,
        i_gate.T,
        i_up.T,
        i_down,
        q_final_gain,
        i_final_gain,
        projection,
        ranks,
        positive,
    )
    return (loss.reshape(()), q_grad.T, i_grad.T)


def solution(mesh):
    in_specs = (
        P(("dp", "tower", "tensor"), None),
        P(),
        P(None, "tensor"),
        P(None, "tensor"),
        P("tensor", None),
        P(),
        P(),
        P(("dp", "tower", "tensor"), None),
        P(),
        P(None, ("tower", "tensor")),
        P(None, ("tower", "tensor")),
        P(("tower", "tensor"), None),
        P(),
        P(),
        P(),
    )
    out_specs = (P(), P("tensor", ("dp", "tower")), P(("tower", "tensor"), "dp"))
    return jax.shard_map(body, mesh=mesh, in_specs=in_specs, out_specs=out_specs, check_vma=False)
```

```python
import functools

import jax
import jax.numpy as jnp
from jax import lax
from jax.experimental import pallas as pl
from jax.experimental.pallas import tpu as pltpu
from jax.sharding import PartitionSpec as P

QLEN = 1536
ILEN = 512
EPS = 1e-06
TAU = 0.05
TEACH = 2.0
LOSS_SCALE = 64.0
HIGH = lax.Precision.HIGHEST
MESH = pl.DeviceIdType.MESH
F32 = jnp.float32
BF16 = jnp.bfloat16

X = 4
ZL = 4
ZR = 8
VMEM_LIMIT = 60 * 1024 * 1024


def rms_scale(values):
    return lax.rsqrt(jnp.mean(values * values, axis=-1, keepdims=True) + EPS)


def dot(left, right, dims=((1,), (0,)), precision=None):
    return lax.dot_general(
        left, right, (dims, ((), ())), preferred_element_type=F32, precision=precision
    )


def remote(src, dst, send, recv, where):
    return pltpu.make_async_remote_copy(
        src_ref=src, dst_ref=dst, send_sem=send, recv_sem=recv, device_id=where, device_id_type=MESH
    )


class Place:
    def __init__(self):
        self.t = lax.axis_index("tensor")
        self.w = lax.axis_index("tower")
        self.a = self.t // X
        self.b = self.t % X
        self.z = self.w * ZL + self.a
        self.bp = (self.b + 1) % X
        self.bm = (self.b + X - 1) % X
        self.bo = (self.b + 2) % X
        self.xp = {"tensor": self.a * X + self.bp}
        self.xm = {"tensor": self.a * X + self.bm}
        self.zp = self.ring(1)
        self.zm = self.ring(ZR - 1)

    def ring(self, step):
        z = (self.z + step) % ZR
        return {"tower": z // ZL, "tensor": (z % ZL) * X + self.b}

    def column(self, row):
        return {"tensor": row * X + self.b}

    def order(self, j):
        near = jnp.minimum(self.a, ZL - 1 - self.a)
        swapped = jnp.where(j == 0, 1, jnp.where(j == 1, 0, j))
        row = jnp.where(near == 1, swapped, j)
        return jnp.where(self.a >= 2, ZL - 1 - row, row)


def rows_of(ref, first, count, unit):
    return ref.at[pl.ds(pl.multiple_of(first, unit), count), :]


class RowGather:
    def __init__(self, place, buf, rows, send, recv):
        self.p, self.buf, self.n, self.send, self.recv = place, buf, rows, send, recv

    def block(self, s, b):
        return rows_of(self.buf, (s * X + b) * self.n, self.n, self.n)

    def half(self, s, b, h):
        n = self.n // 2
        return rows_of(self.buf, (s * X + b) * self.n + h * n, n, n)

    def up(self, s):
        ref = self.block(s, self.p.b)
        where = self.p.column(jnp.minimum(self.p.a + 1, ZL - 1))
        return remote(ref, ref, self.send.at[0, s], self.recv.at[0, s], where)

    def down(self, s):
        ref = self.block(s, self.p.b)
        where = self.p.column(jnp.maximum(self.p.a - 1, 0))
        return remote(ref, ref, self.send.at[5, s], self.recv.at[0, s], where)

    def goes_up(self, s):
        return (s <= self.p.a) & (self.p.a < ZL - 1)

    def goes_down(self, s):
        return (s >= self.p.a) & (self.p.a > 0)

    def right(self, s):
        ref = self.block(s, self.p.b)
        return remote(ref, ref, self.send.at[1, s], self.recv.at[1, s], self.p.xp)

    def left(self, s):
        ref = self.block(s, self.p.b)
        return remote(ref, ref, self.send.at[2, s], self.recv.at[2, s], self.p.xm)

    def half_right(self, s):
        ref = self.half(s, self.p.bm, 0)
        return remote(ref, ref, self.send.at[3, s], self.recv.at[3, s], self.p.xp)

    def half_left(self, s):
        ref = self.half(s, self.p.bp, 1)
        return remote(ref, ref, self.send.at[4, s], self.recv.at[4, s], self.p.xm)

    def take_z(self, s):
        @pl.when(s != self.p.a)
        def _():
            self.up(s).wait_recv()

        @pl.when(self.goes_up(s))
        def _():
            self.up(s).start()

        @pl.when(self.goes_down(s))
        def _():
            self.down(s).start()

        self.right(s).start()
        self.left(s).start()

    def take_x(self, s):
        ref = self.block(s, self.p.bm)
        remote(ref, ref, self.send.at[1, s], self.recv.at[1, s], self.p.xm).wait_recv()
        self.half_right(s).start()
        ref = self.block(s, self.p.bp)
        remote(ref, ref, self.send.at[2, s], self.recv.at[2, s], self.p.xp).wait_recv()
        self.half_left(s).start()

    def take_halves(self, s):
        ref = self.half(s, self.p.bo, 0)
        remote(ref, ref, self.send.at[3, s], self.recv.at[3, s], self.p.xm).wait_recv()
        ref = self.half(s, self.p.bo, 1)
        remote(ref, ref, self.send.at[4, s], self.recv.at[4, s], self.p.xp).wait_recv()

    def drain(self):
        def each(s, _):
            @pl.when(self.goes_up(s))
            def _():
                self.up(s).wait_send()

            @pl.when(self.goes_down(s))
            def _():
                self.down(s).wait_send()

            self.right(s).wait_send()
            self.left(s).wait_send()
            self.half_right(s).wait_send()
            self.half_left(s).wait_send()
            return 0

        lax.fori_loop(0, ZL, each, 0)


class RingGather:
    def __init__(self, place, buf, rows, send, recv):
        self.p, self.buf, self.n, self.send, self.recv = place, buf, rows, send, recv

    def ref(self, z, hop, upward):
        z = (z + 2 * ZR) % ZR
        if hop < 4:
            return rows_of(self.buf, z * self.n, self.n, self.n)
        n = self.n // 2
        return rows_of(self.buf, z * self.n + (0 if upward else n), n, n)

    def copies(self, hop):
        up = self.ref(self.p.z - hop + 1, hop, True)
        down = self.ref(self.p.z + hop - 1, hop, False)
        return (
            remote(up, up, self.send.at[0, hop - 1], self.recv.at[0, hop - 1], self.p.zp),
            remote(down, down, self.send.at[1, hop - 1], self.recv.at[1, hop - 1], self.p.zm),
        )

    def start(self, hop):
        for copy in self.copies(hop):
            copy.start()

    def take(self, hop):
        up = self.ref(self.p.z - hop, hop, True)
        down = self.ref(self.p.z + hop, hop, False)
        remote(up, up, self.send.at[0, hop - 1], self.recv.at[0, hop - 1], self.p.zm).wait_recv()
        remote(down, down, self.send.at[1, hop - 1], self.recv.at[1, hop - 1], self.p.zp).wait_recv()

    def drain(self):
        for hop in range(1, 5):
            for copy in self.copies(hop):
                copy.wait_send()


class RingSum:
    def __init__(self, place, buf, land, rows, send, recv):
        self.p, self.buf, self.land = place, buf, land
        self.n, self.send, self.recv = rows, send, recv

    def part(self, z, half):
        z = (z + 2 * ZR) % ZR
        if half is None:
            return rows_of(self.buf, z * self.n, self.n, self.n)
        n = self.n // 2
        return rows_of(self.buf, z * self.n + half * n, n, n)

    def slot(self, way, hop):
        if hop == 1:
            return self.land.at[way, 0, pl.ds(0, self.n // 2), :]
        return self.land.at[way, hop - 1]

    def copies(self, hop):
        half = (0, 1) if hop == 1 else (None, None)
        up = self.part(self.p.z + 5 - hop, half[0])
        down = self.part(self.p.z - 5 + hop, half[1])
        return (
            remote(up, self.slot(0, hop), self.send.at[0, hop - 1], self.recv.at[0, hop - 1], self.p.zp),
            remote(down, self.slot(1, hop), self.send.at[1, hop - 1], self.recv.at[1, hop - 1], self.p.zm),
        )

    def start(self, hop):
        for copy in self.copies(hop):
            copy.start()

    def take(self, hop):
        for copy in self.copies(hop):
            copy.wait_recv()

    def add(self, hop):
        half = (0, 1) if hop == 1 else (None, None)
        for way, z in ((0, self.p.z + 4 - hop), (1, self.p.z - 4 + hop)):
            ref = self.part(z, half[way])
            ref[...] = (ref[...].astype(F32) + self.slot(way, hop)[...].astype(F32)).astype(BF16)

    def drain(self):
        for hop in range(1, 5):
            for copy in self.copies(hop):
                copy.wait_send()


def gain_row(ref):
    return ref[...].astype(F32).reshape(1, -1)


def normed_rows(act, gain):
    values = act.astype(F32)
    return (values * rms_scale(values) * gain).astype(BF16)


def gated(gate_val, up_val):
    return (jax.nn.silu(gate_val) * up_val).astype(BF16)


def at_step(i, step):
    return pl.when(i == step)


def split_rows(row):
    high = row.astype(BF16).astype(F32)
    rest = row - high
    mid = rest.astype(BF16).astype(F32)
    low = rest - mid
    index = lax.broadcasted_iota(jnp.int32, (8, row.shape[1]), 0)
    out = jnp.where(index == 0, high, jnp.where(index == 1, mid, jnp.where(index == 2, low, 0.0)))
    return out.astype(BF16)


def unit_scale(vec):
    return lax.rsqrt(jnp.sum(vec * vec, axis=-1, keepdims=True) + EPS)


def unit_back(vec, scales, upstream):
    inner = jnp.sum(vec * upstream, axis=-1, keepdims=True)
    return scales * upstream - vec * (scales * scales * scales) * inner


def contrast(query_hat, item_hat, ranks, positive):
    logits = dot(query_hat, item_hat, ((1,), (1,)), HIGH) / TAU
    shifted = logits - 1.0 / TAU
    log_student = shifted - jnp.log(jnp.sum(jnp.exp(shifted), axis=1, keepdims=True))
    teach = -ranks.astype(F32) / TEACH
    log_teacher = teach - jnp.log(jnp.sum(jnp.exp(teach), axis=1, keepdims=True))
    teacher = jnp.exp(log_teacher)
    columns = lax.broadcasted_iota(jnp.int32, logits.shape, 1)
    onehot = (columns == positive).astype(F32)
    per_row = jnp.sum(
        teacher * (log_teacher - log_student) - onehot * log_student, axis=1, keepdims=True
    )
    slopes = 2.0 * jnp.exp(log_student) - onehot - teacher
    return (per_row, slopes)


def grad_rows(resid, scales, gain, upstream):
    along = gain * upstream
    inner = jnp.mean(along * resid, axis=-1, keepdims=True)
    return (scales * along - resid * (scales * scales * scales) * inner).astype(BF16)


def by_chunk(values, parts, q):
    wide = values.shape[1] // parts
    part = wide // 2
    firsts = [d * wide + (q // 2) * part for d in range(q % 2, parts, 2)]
    return jnp.concatenate([values[:, first : first + part] for first in firsts], axis=1)


def kernel(
    qa, qg, gate_hbm, up_hbm, down_hbm, ia, ig, ig_w, iu_w, id_w, qf, if_, proj_hbm, ranks, positive,
    loss, q_out, i_out,
    w, proj, nq, part, gate_val, h2, pm, r1, r2, zs, zin, ni, wi, ip, land, hq, hi,
    sums, hats, scal, yq, hs_w, yi, gq, gi, qc1, qb1, qb2, qc, ic1, ib1, ib2, ic,
    loads, gs, gr, ss, sr, ws, wr, vs, vr, hs, hr, ias, iar, irs, irr,
    s1, r1s, s2, r2s, s3, r3s, ys, yr, iys, iyr, qs, qv, bs, bv,
):
    p = Place()
    n, dq = qa.shape
    m, di = ia.shape
    f, k = down_hbm.shape[0], id_w.shape[0]
    group = X * n
    h = n // 2
    parts = X * ZL
    count = hats.shape[0]
    block_wide = dq // count
    piece = w.shape[2] // 4
    wide, thin = dq // 2, dq // 4
    dp = lax.axis_index("dp")
    own = dp * 2 + p.w
    y, c = dp // 2, dp % 2
    yp, ym, y2 = (y + 1) % 4, (y + 3) % 4, (y + 2) % 4
    line_y = (y2, yp, ym, y)
    to_yp, to_ym, to_core = {"dp": yp * 2 + c}, {"dp": ym * 2 + c}, {"dp": y * 2 + 1 - c}
    to_y = (to_yp, to_ym)
    to_tower = {"tower": 1 - p.w}
    a2 = (p.a + 2) % ZL
    mate = p.a + 1 - 2 * (p.a % 2)
    to_a2, to_mate = p.column(a2), p.column(mate)

    def member(step):
        return {"tensor": (p.t + step) % parts}

    def replica(step):
        other = (own + step) % count
        return {"dp": other // 2, "tower": other % 2}

    own_weights = [
        pltpu.make_async_copy(ref, w.at[0, index, pl.ds(0, f), :], loads.at[index])
        for index, ref in enumerate((gate_hbm, up_hbm, down_hbm))
    ]
    proj_copy = pltpu.make_async_copy(proj_hbm, proj, loads.at[3])
    for copy in own_weights:
        copy.start()
    proj_copy.start()
    barrier = pltpu.get_barrier_semaphore()

    def greet(step, _):
        pl.semaphore_signal(barrier, inc=1, device_id=member(step), device_id_type=MESH)
        pl.semaphore_signal(barrier, inc=1, device_id=replica(step), device_id_type=MESH)
        return 0

    lax.fori_loop(1, parts, greet, 0)
    for where in (p.zp, p.zm):
        pl.semaphore_signal(barrier, inc=1, device_id=where, device_id_type=MESH)
    for index in range(3):
        w[0, index, f:, :] = jnp.zeros((w.shape[2] - f, dq), BF16)
    nq[pl.ds(pl.multiple_of(p.b * n, n), n), :] = normed_rows(qa[...], gain_row(qg))
    ni[pl.ds(pl.multiple_of(p.z * m, m), m), :] = normed_rows(ia[...], gain_row(ig))
    for index, ref in enumerate((ig_w, iu_w, id_w)):
        wi[index, pl.ds(pl.multiple_of(p.b * k, k), k), :] = ref[...]
    pl.semaphore_wait(barrier, 2 * (parts - 1) + 2)

    rows = RowGather(p, nq, n, gs, gr)
    items = RingGather(p, ni, m, ias, iar)
    isum = RingSum(p, ip, land, m, irs, irr)

    def across():
        return remote(rows.block(0, p.b), rows.block(1, p.b), gs.at[0, 0], gr.at[0, 0], to_a2)

    def wpiece(which, index, line, core):
        first = pl.multiple_of(line * piece, piece)
        return w.at[which, index, pl.ds(first, piece), pl.ds(pl.multiple_of(core * wide, wide), wide)]

    def whalf(index, line, part_of):
        first = pl.multiple_of(line * piece, piece)
        column = pl.multiple_of(c * wide + part_of * thin, thin)
        return w.at[1, index, pl.ds(first, piece), pl.ds(column, thin)]

    def w_send(index, kind):
        here = wpiece(1, index, y, c)
        low, high = wpiece(1, index, ym, c), wpiece(1, index, yp, c)
        src, dst, where = (
            (wpiece(0, index, y, c), here, to_mate),
            (here, here, to_yp),
            (here, here, to_ym),
            (whalf(index, ym, 0), whalf(index, ym, 0), to_yp),
            (whalf(index, yp, 1), whalf(index, yp, 1), to_ym),
            (here, here, to_core),
            (low, low, to_core),
            (high, high, to_core),
            (wpiece(1, index, y2, c), wpiece(1, index, y2, c), to_core),
        )[kind]
        return remote(src, dst, ws.at[kind, index], wr.at[kind, index], where)

    def w_got(index, kind):
        dst = (
            wpiece(1, index, y, c),
            wpiece(1, index, ym, c),
            wpiece(1, index, yp, c),
            whalf(index, y2, 0),
            whalf(index, y2, 1),
            wpiece(1, index, y, 1 - c),
            wpiece(1, index, ym, 1 - c),
            wpiece(1, index, yp, 1 - c),
            wpiece(1, index, y2, 1 - c),
        )[kind]
        remote(dst, dst, ws.at[kind, index], wr.at[kind, index], to_core).wait_recv()

    def w_near(index):
        w_got(index, 0)
        for kind in (1, 2, 5):
            w_send(index, kind).start()

    def w_ring(index):
        w_got(index, 1)
        w_send(index, 3).start()
        w_send(index, 6).start()
        w_got(index, 2)
        w_send(index, 4).start()
        w_send(index, 7).start()

    def w_far(index):
        w_got(index, 3)
        w_got(index, 4)
        w_send(index, 8).start()

    def w_done(index):
        for kind in (5, 6, 7, 8):
            w_got(index, kind)

    def vpiece(b, core):
        column = pl.multiple_of(core * (di // 2), di // 2)
        return wi.at[:, pl.ds(pl.multiple_of(b * k, k), k), pl.ds(column, di // 2)]

    def vhalf(b, part_of):
        first = pl.multiple_of(b * k + part_of * (k // 2), k // 2)
        column = pl.multiple_of(c * (di // 2), di // 2)
        return wi.at[:, pl.ds(first, k // 2), pl.ds(column, di // 2)]

    def v_send(kind):
        ref, where = (
            (vpiece(p.b, c), p.xp),
            (vpiece(p.b, c), p.xm),
            (vhalf(p.bm, 0), p.xp),
            (vhalf(p.bp, 1), p.xm),
            (vpiece(p.bm, c), to_core),
            (vpiece(p.bp, c), to_core),
            (vpiece(p.bo, c), to_core),
        )[kind]
        return remote(ref, ref, vs.at[kind], vr.at[kind], where)

    def v_got(kind):
        ref = (
            vpiece(p.bm, c),
            vpiece(p.bp, c),
            vhalf(p.bo, 0),
            vhalf(p.bo, 1),
            vpiece(p.bm, 1 - c),
            vpiece(p.bp, 1 - c),
            vpiece(p.bo, 1 - c),
        )[kind]
        remote(ref, ref, vs.at[kind], vr.at[kind], to_core).wait_recv()

    def block(j, q, b):
        return rows_of(pm.at[q], (j * X + b) * n, n, n)

    def half(j, q, b, part_of):
        return rows_of(pm.at[q], (j * X + b) * n + part_of * h, h, h)

    def first(j, q, way):
        src = half(j, q, p.bo, way)
        where = (p.xp, p.xm)[way]
        return remote(src, r1.at[way, j, q], ss.at[way, j, q], sr.at[way, j, q], where)

    def second(j, q, way):
        src = block(j, q, (p.bp, p.bm)[way])
        where = (p.xp, p.xm)[way]
        return remote(src, r2.at[way, j, q], ss.at[2 + way, j, q], sr.at[2 + way, j, q], where)

    def to_owner(q):
        return remote(zs.at[q], zin.at[q], ss.at[4, 0, q], sr.at[4, 0, q], to_a2)

    def back(j):
        s = (p.a, a2)[j]
        dst = hq.at[pl.ds(pl.multiple_of(s * group, group), group), :]
        return remote(h2.at[j], dst, hs.at[j], hr.at[j], to_mate)

    def back_got(j):
        other = (mate, (mate + 2) % ZL)[j]
        dst = hq.at[pl.ds(pl.multiple_of(other * group, group), group), :]
        remote(h2.at[j], dst, hs.at[j], hr.at[j], to_mate).wait_recv()

    def rows_in(j):
        return nq[j * group : (j + 1) * group, :]

    def own_units(j):
        left = rows_in(j)
        value = gated(
            dot(left, w[0, 0, :f, :], ((1,), (1,))), dot(left, w[0, 1, :f, :], ((1,), (1,)))
        )
        hq[pl.ds(pl.multiple_of((p.a, a2)[j] * group, group), group), :] = value
        part[j] = dot(value, w[0, 2, :f, :])

    def mate_gate(j):
        gate_val[j] = dot(rows_in(j), w[1, 0, :f, :], ((1,), (1,)))

    def mate_up(j):
        h2[j] = gated(gate_val[j], dot(rows_in(j), w[1, 1, :f, :], ((1,), (1,))))

    def mate_down(j, q):
        columns = slice(q * wide, (q + 1) * wide)
        total = part[j, :, columns] + dot(h2[j], w[1, 2, :f, columns])
        pm[q, j * group : (j + 1) * group, :] = total.astype(BF16)
        first(j, q, 0).start()
        first(j, q, 1).start()

    def combine(j, q):
        for way in range(2):
            first(j, q, way).wait_recv()
            ref = half(j, q, (p.bp, p.bm)[way], way)
            ref[...] = (ref[...].astype(F32) + r1[way, j, q].astype(F32)).astype(BF16)
            second(j, q, way).start()

    def summed(j, q):
        second(j, q, 0).wait_recv()
        second(j, q, 1).wait_recv()
        total = block(j, q, p.b)[...].astype(F32)
        return total + r2[0, j, q].astype(F32) + r2[1, j, q].astype(F32)

    def send_sum(q):
        zs[q] = summed(1, q).astype(BF16)
        to_owner(q).start()

    def item_hop(hop):
        items.take(hop)
        if hop < 4:
            items.start(hop + 1)

    def isum_hop(hop):
        isum.take(hop)
        isum.add(hop)
        isum.start(hop + 1)

    def item_product():
        left = ni[...]
        partial = 0.0
        for b in range(X):
            here = slice(b * k, (b + 1) * k)
            value = gated(
                dot(left, wi[0, here, :], ((1,), (1,))), dot(left, wi[1, here, :], ((1,), (1,)))
            )
            hi[b] = value
            partial = partial + dot(value, wi[2, here, :])
        ip[...] = partial.astype(BF16)
        isum.start(1)

    rows.right(0).start()
    rows.left(0).start()
    items.start(1)
    own_weights[0].wait()
    w_send(0, 0).start()
    across().start()
    own_weights[1].wait()
    own_weights[2].wait()
    w_near(0)
    w_send(1, 0).start()
    rows.take_x(0)
    item_hop(1)
    v_send(0).start()
    v_send(1).start()
    rows.take_halves(0)
    own_units(0)
    item_hop(2)
    w_ring(0)
    w_near(1)
    w_send(2, 0).start()
    remote(rows.block(0, p.b), rows.block(1, p.b), gs.at[0, 0], gr.at[0, 0], to_a2).wait_recv()
    rows.right(1).start()
    rows.left(1).start()
    item_hop(3)
    w_far(0)
    for kind in range(2):
        v_got(kind)
        v_send(2 + kind).start()
        v_send(4 + kind).start()
    item_hop(4)
    w_ring(1)
    w_near(2)
    w_done(0)
    mate_gate(0)
    v_got(2)
    v_got(3)
    v_send(6).start()
    w_far(1)
    for kind in (4, 5, 6):
        v_got(kind)
    item_product()
    rows.take_x(1)
    w_done(1)
    mate_up(0)
    w_ring(2)
    isum_hop(1)
    rows.take_halves(1)
    own_units(1)
    isum_hop(2)
    w_far(2)
    mate_gate(1)
    mate_up(1)
    isum_hop(3)
    w_done(2)
    mate_down(0, 0)
    mate_down(0, 1)
    mate_down(1, 0)
    mate_down(1, 1)
    back(0).start()
    combine(1, 0)
    combine(1, 1)
    combine(0, 0)
    send_sum(0)
    combine(0, 1)
    send_sum(1)
    back(1).start()
    isum.take(4)
    own_item = ip[pl.ds(pl.multiple_of(p.z * m, m), m), :].astype(F32)
    i_resid = ia[...].astype(F32) + (own_item + land[0, 3].astype(F32) + land[1, 3].astype(F32))
    mlp = []
    for q in range(2):
        total = summed(0, q)
        to_owner(q).wait_recv()
        mlp.append(total + zin[q].astype(F32))
    q_resid = qa[...].astype(F32) + jnp.concatenate(mlp, axis=1)

    q_gain, i_gain = gain_row(qf), gain_row(if_)
    q_scale, i_scale = rms_scale(q_resid), rms_scale(i_resid)
    sums[p.t, :, :dq] = jnp.sum(q_resid * q_scale * q_gain, axis=0, keepdims=True)
    sums[p.t, :, dq:] = jnp.sum(i_resid * i_scale * i_gain, axis=0, keepdims=True)

    def spread_members(buf, send, recv):
        def each(step, _):
            remote(buf.at[p.t], buf.at[p.t], send.at[step], recv.at[p.t], member(step)).start()
            return 0

        lax.fori_loop(1, parts, each, 0)

    def await_members(buf, send, recv):
        def each(step, _):
            other = (p.t + step) % parts
            remote(buf.at[p.t], buf.at[other], send.at[step], recv.at[other], member(step)).wait()
            return 0

        lax.fori_loop(1, parts, each, 0)

    def spread_hats(step, _):
        remote(hats.at[own], hats.at[own], s2.at[step], r2s.at[own], replica(step)).start()
        return 0

    def gathered_hats(step, _):
        other = (own + step) % count
        remote(hats.at[own], hats.at[other], s2.at[step], r2s.at[other], replica(step)).wait()
        return 0

    strip = block_wide // 2

    def q_rows(q, line_of, core):
        return rows_of(gq.at[q], (line_of * 2 + core) * strip, strip, strip)

    def q_half(q, line_of, way):
        first_row = (line_of * 2 + c) * strip + way * (strip // 2)
        return rows_of(gq.at[q], first_row, strip // 2, strip // 2)

    def q_core(q, j):
        src = q_rows(q, line_y[j], 1 - c)
        return remote(src, qc1.at[q, j], qs.at[q, j], qv.at[q, j], to_core)

    def q_first(q, way):
        src, dst = q_half(q, y2, way), qb1.at[q, way]
        return remote(src, dst, qs.at[q, 4 + way], qv.at[q, 4 + way], to_y[way])

    def q_second(q, way):
        src, dst = q_rows(q, (yp, ym)[way], c), qb2.at[q, way]
        return remote(src, dst, qs.at[q, 6 + way], qv.at[q, 6 + way], to_y[way])

    def q_tower(q):
        return remote(q_rows(q, y, c), qc.at[q // 2], qs.at[q, 8], qv.at[q, 8], to_tower)

    def q_start(q):
        for j in range(4):
            q_core(q, j).start()

    def q_far(q):
        q_core(q, 0).wait_recv()
        ref = q_rows(q, y2, c)
        ref[...] += qc1[q, 0]
        for way in range(2):
            q_first(q, way).start()

    def q_near(q):
        for way in range(2):
            q_core(q, 1 + way).wait_recv()
            ref = q_rows(q, (yp, ym)[way], c)
            ref[...] += qc1[q, 1 + way]
            q_first(q, way).wait_recv()
            ref = q_half(q, (yp, ym)[way], way)
            ref[...] += qb1[q, way]
            q_second(q, way).start()

    def q_own(q):
        q_core(q, 3).wait_recv()
        for way in range(2):
            q_second(q, way).wait_recv()
        ref = q_rows(q, y, c)
        ref[...] = ref[...] + qc1[q, 3] + qb2[q, 0] + qb2[q, 1]

        @pl.when(p.w != q % 2)
        def _():
            q_tower(q).start()

    def q_finish(q):
        @pl.when(p.w == q % 2)
        def _():
            q_tower(q).wait_recv()
            here = slice((q // 2) * strip, (q // 2 + 1) * strip)
            q_out[here, :] = q_rows(q, y, c)[...] + qc[q // 2]

    def i_rows(line_of, core):
        first = pl.multiple_of((line_of * 2 + core) * block_wide, block_wide)
        return gi.at[:, pl.ds(first, block_wide), :]

    def i_half(line_of, way):
        first = pl.multiple_of((line_of * 2 + c) * block_wide, block_wide)
        return gi.at[pl.ds(way * 2, 2), pl.ds(first, block_wide), :]

    def i_slab(b):
        return gi.at[b, pl.ds(pl.multiple_of((y * 2 + c) * block_wide, block_wide), block_wide), :]

    def i_core(j):
        return remote(i_rows(line_y[j], 1 - c), ic1.at[j], bs.at[j], bv.at[j], to_core)

    def i_first(way):
        return remote(i_half(y2, way), ib1.at[way], bs.at[4 + way], bv.at[4 + way], to_y[way])

    def i_second(way):
        src = i_rows((yp, ym)[way], c)
        return remote(src, ib2.at[way], bs.at[6 + way], bv.at[6 + way], to_y[way])

    def i_x(hop):
        other = (p.b + hop) % X
        where = {"tensor": p.a * X + other}
        return remote(i_slab(other), ic.at[p.b], bs.at[8 + hop], bv.at[8 + p.b], where)

    def i_product():
        for b in range(X):
            gi[b] = dot(yi[...], hi[b], ((0,), (0,)))
        for j in range(4):
            i_core(j).start()

    def i_far():
        for j in range(4):
            i_core(j).wait_recv()
            ref = i_rows(line_y[j], c)
            ref[...] += ic1[j]
        for way in range(2):
            i_first(way).start()

    def i_near():
        for way in range(2):
            i_first(way).wait_recv()
            ref = i_half((yp, ym)[way], way)
            ref[...] += ib1[way]
            i_second(way).start()

    def i_own():
        for way in range(2):
            i_second(way).wait_recv()
        ref = i_rows(y, c)
        ref[...] = ref[...] + ib2[0] + ib2[1]
        for hop in range(1, X):
            i_x(hop).start()

    def i_finish():
        total = i_slab(p.b)[...]
        for hop in range(1, X):
            other = (p.b + hop) % X
            remote(i_slab(other), ic.at[other], bs.at[8 + hop], bv.at[8 + other], p.xp).wait_recv()
            total = total + ic[other]
        i_out[...] = total

    chunks = 4
    gather = [RowGather(p, yq.at[q], n, ys.at[q], yr.at[q]) for q in range(chunks)]
    igather = RingGather(p, yi, m, iys, iyr)
    steps = (0, 4, 1, 8, 2, 12, 3, 5, 6, 7, 9, 10, 11, 13, 14, 15)

    def advance(index):
        if index < len(steps):
            gather[steps[index] // ZL].take_z(p.order(steps[index] % ZL))
        if 0 <= index - 2 < len(steps):
            gather[steps[index - 2] // ZL].take_x(p.order(steps[index - 2] % ZL))

    def item_grad_hop(hop):
        igather.take(hop)
        if hop < 4:
            igather.start(hop + 1)

    def scaled(j):
        s = p.order(j)
        columns = []
        for b in range(X):
            tile = scal[s * X + b]
            columns.append(jnp.concatenate([tile] * 16, axis=0).T[:n])
        columns = jnp.concatenate(columns, axis=0)
        here = pl.ds(pl.multiple_of(s * group, group), group)
        value = hq[here, :].astype(F32)
        hs_w[here, :] = (value * columns[:, 1:2]).astype(BF16)
        return jnp.sum(value * columns[:, 0:1], axis=0, keepdims=True)

    def product(q, part_of):
        first_group = 2 * part_of
        total = 0.0
        for j in (first_group, first_group + 1):
            s = p.order(j)
            gather[q].take_halves(s)
            here = pl.ds(pl.multiple_of(s * group, group), group)
            total = total + dot(yq[q, here, :], hs_w[here, :], ((0,), (0,)))
        if part_of == 0:
            column = jnp.broadcast_to(along_of[q], (128, along_of[q].shape[1])).T[:, 0:1]
            gq[q] = column * summed_hidden - total
        else:
            gq[q] -= total
            q_start(q)

    spread_members(sums, s1, r1s)
    here = pl.ds(pl.multiple_of(p.t * n, n), n)
    for q in range(chunks):
        yq[q, here, :] = by_chunk(q_resid, count, q).astype(BF16)
    advance(0)
    proj_copy.wait()
    await_members(sums, s1, r1s)
    total = sums[0]
    for slot in range(1, parts):
        total = total + sums[slot]
    q_pooled = total[:, :dq] / QLEN
    i_pooled = total[:, dq:] / ILEN
    advance(1)
    q_e = jnp.sum(dot(split_rows(q_pooled), proj[...]), axis=0, keepdims=True)
    q_norm, i_norm = unit_scale(q_e), unit_scale(i_pooled)
    hats[own, :, :di] = q_e * q_norm
    hats[own, :, di:] = i_pooled * i_norm
    lax.fori_loop(1, count, spread_hats, 0)
    advance(2)
    advance(3)
    lax.fori_loop(1, count, gathered_hats, 0)
    index = lax.broadcasted_iota(jnp.int32, (count, 2 * di), 0)
    every = jnp.zeros((count, 2 * di), F32)
    for slot in range(count):
        every = jnp.where(index == slot, hats[slot], every)
    every_query, every_items = every[:, :di], every[:, di:]
    line = lax.broadcasted_iota(jnp.int32, (count, count), 0)
    target = jnp.zeros((count, count), jnp.int32)
    for slot in range(count):
        target = jnp.where(line == slot, positive[slot], target)
    per_row, slopes = contrast(every_query, every_items, ranks[...], target)
    advance(4)
    loss[...] = jnp.sum(per_row, axis=0, keepdims=True) / count
    weights = slopes * (LOSS_SCALE / (TAU * count))
    advance(5)
    mine = lax.broadcasted_iota(jnp.int32, (count, di), 0) == own
    q_back = jnp.sum(
        jnp.where(mine, dot(weights, every_items, precision=HIGH), 0.0), axis=0, keepdims=True
    )
    column = lax.broadcasted_iota(jnp.int32, (count, count), 1) == own
    i_back = jnp.sum(
        jnp.sum(jnp.where(column, weights, 0.0), axis=1, keepdims=True) * every_query,
        axis=0,
        keepdims=True,
    )
    advance(6)
    q_grad_e = unit_back(q_e, q_norm, q_back)
    q_up = jnp.sum(dot(split_rows(q_grad_e), proj[...], ((1,), (1,))), axis=0, keepdims=True) / QLEN
    i_up = unit_back(i_pooled, i_norm, i_back) / ILEN
    advance(7)
    along = q_gain * q_up
    along_of = [by_chunk(along, count, q) for q in range(chunks)]
    inner = jnp.mean(along * q_resid, axis=-1, keepdims=True)
    slope = (q_scale * q_scale * q_scale) * inner
    lane = lax.broadcasted_iota(jnp.int32, (n, 128), 1)
    columns = jnp.where(lane == 0, q_scale, jnp.where(lane == 1, slope, 0.0))
    columns = jnp.concatenate([columns, jnp.zeros((128 - n, 128), F32)], axis=0)
    scal[p.t] = columns.T[:8]
    spread_members(scal, s3, r3s)
    yi[pl.ds(pl.multiple_of(p.z * m, m), m), :] = grad_rows(i_resid, i_scale, i_gain, i_up)
    igather.start(1)
    advance(8)
    await_members(scal, s3, r3s)
    summed_hidden = scaled(0)
    advance(9)
    back_got(0)
    back_got(1)
    for j in range(1, ZL):
        summed_hidden = summed_hidden + scaled(j)
    item_grad_hop(1)
    product(0, 0)
    advance(10)
    product(0, 1)
    item_grad_hop(2)
    advance(11)
    q_far(0)
    product(1, 0)
    advance(12)
    item_grad_hop(3)
    q_near(0)
    product(1, 1)
    advance(13)
    q_far(1)
    product(2, 0)
    item_grad_hop(4)
    advance(14)
    q_own(0)
    q_near(1)
    i_product()
    advance(15)
    product(2, 1)
    q_far(2)
    advance(16)
    q_own(1)
    i_far()
    product(3, 0)
    advance(17)
    q_near(2)
    q_finish(0)
    product(3, 1)
    q_far(3)
    i_near()
    q_own(2)
    q_near(3)
    i_own()
    q_finish(1)
    q_finish(2)
    i_finish()
    q_own(3)
    q_finish(3)

    for j in range(2):
        back(j).wait_send()
        for copy in (rows.right(j), rows.left(j), rows.half_right(j), rows.half_left(j)):
            copy.wait_send()
        for q in range(2):
            for way in range(2):
                first(j, q, way).wait_send()
                second(j, q, way).wait_send()
    for q in range(2):
        to_owner(q).wait_send()
    across().wait_send()
    items.drain()
    isum.drain()
    for index in range(3):
        for kind in range(9):
            w_send(index, kind).wait_send()
    for kind in range(7):
        v_send(kind).wait_send()
    for q in range(chunks):
        gather[q].drain()
        for j in range(4):
            q_core(q, j).wait_send()
        for way in range(2):
            q_first(q, way).wait_send()
            q_second(q, way).wait_send()

        @pl.when(p.w != q % 2)
        def _():
            q_tower(q).wait_send()

    igather.drain()
    for j in range(4):
        i_core(j).wait_send()
    for way in range(2):
        i_first(way).wait_send()
        i_second(way).wait_send()
    for hop in range(1, X):
        i_x(hop).wait_send()


def step(qa, qg, gate, up, down, ia, ig, ig_w, iu_w, id_w, qf, if_, proj, ranks, positive):
    n, dq = qa.shape
    m, di = ia.shape
    f, k = down.shape[0], id_w.shape[0]
    padded = 64 * ((f + 63) // 64)
    vmem, hbm = pl.BlockSpec(memory_space=pltpu.VMEM), pl.BlockSpec(memory_space=pl.ANY)
    smem = pl.BlockSpec(memory_space=pltpu.SMEM)
    all_i = ZR * m
    group = X * n
    parts = X * ZL
    count = ranks.shape[0]
    wide = dq // count
    dma = pltpu.SemaphoreType.DMA
    return pl.pallas_call(
        kernel,
        out_shape=(
            jax.ShapeDtypeStruct((1, 1), F32),
            jax.ShapeDtypeStruct((wide, f), F32),
            jax.ShapeDtypeStruct((wide, k), F32),
        ),
        in_specs=[vmem, vmem, hbm, hbm, hbm] + [vmem] * 7 + [hbm, vmem, smem],
        out_specs=[vmem] * 3,
        scratch_shapes=[
            pltpu.VMEM((2, 3, padded, dq), BF16),
            pltpu.VMEM(proj.shape, BF16),
            pltpu.VMEM((2 * group, dq), BF16),
            pltpu.VMEM((2, group, dq), F32),
            pltpu.VMEM((2, group, f), F32),
            pltpu.VMEM((2, group, f), BF16),
            pltpu.VMEM((2, 2 * group, dq // 2), BF16),
            pltpu.VMEM((2, 2, 2, n // 2, dq // 2), BF16),
            pltpu.VMEM((2, 2, 2, n, dq // 2), BF16),
            pltpu.VMEM((2, n, dq // 2), BF16),
            pltpu.VMEM((2, n, dq // 2), BF16),
            pltpu.VMEM((all_i, di), BF16),
            pltpu.VMEM((3, X * k, di), BF16),
            pltpu.VMEM((all_i, di), BF16),
            pltpu.VMEM((2, 4, m, di), BF16),
            pltpu.VMEM((ZL * group, f), BF16),
            pltpu.VMEM((X, all_i, k), BF16),
            pltpu.VMEM((parts, 1, dq + di), F32),
            pltpu.VMEM((count, 1, 2 * di), F32),
            pltpu.VMEM((parts, 8, 128), F32),
            pltpu.VMEM((4, parts * n, dq // 4), BF16),
            pltpu.VMEM((ZL * group, f), BF16),
            pltpu.VMEM((all_i, di), BF16),
            pltpu.VMEM((4, dq // 4, f), F32),
            pltpu.VMEM((X, di, k), F32),
            pltpu.VMEM((4, 4, wide // 2, f), F32),
            pltpu.VMEM((4, 2, wide // 4, f), F32),
            pltpu.VMEM((4, 2, wide // 2, f), F32),
            pltpu.VMEM((2, wide // 2, f), F32),
            pltpu.VMEM((4, X, wide, k), F32),
            pltpu.VMEM((2, 2, wide, k), F32),
            pltpu.VMEM((2, X, wide, k), F32),
            pltpu.VMEM((X, wide, k), F32),
            dma((4,)),
            dma((5, 2)),
            dma((5, 2)),
            dma((5, 2, 2)),
            dma((5, 2, 2)),
            dma((9, 3)),
            dma((9, 3)),
            dma((7,)),
            dma((7,)),
            dma((2,)),
            dma((2,)),
            dma((2, 4)),
            dma((2, 4)),
            dma((2, 4)),
            dma((2, 4)),
            dma((parts,)),
            dma((parts,)),
            dma((count,)),
            dma((count,)),
            dma((parts,)),
            dma((parts,)),
            dma((4, 6, ZL)),
            dma((4, 5, ZL)),
            dma((2, 4)),
            dma((2, 4)),
            dma((4, 9)),
            dma((4, 9)),
            dma((12,)),
            dma((12,)),
        ],
        compiler_params=pltpu.CompilerParams(
            collective_id=0, has_side_effects=True, vmem_limit_bytes=VMEM_LIMIT
        ),
        name="towers_step",
    )(qa, qg, gate, up, down, ia, ig, ig_w, iu_w, id_w, qf, if_, proj, ranks, positive)


def body(
    q_act,
    q_norm_gain,
    q_gate,
    q_up,
    q_down,
    q_final_gain,
    projection,
    i_act,
    i_norm_gain,
    i_gate,
    i_up,
    i_down,
    i_final_gain,
    ranks,
    positive,
):
    loss, q_grad, i_grad = step(
        q_act,
        q_norm_gain,
        q_gate.T,
        q_up.T,
        q_down,
        i_act,
        i_norm_gain,
        i_gate.T,
        i_up.T,
        i_down,
        q_final_gain,
        i_final_gain,
        projection,
        ranks,
        positive,
    )
    return (loss.reshape(()), q_grad.T, i_grad.T)


def solution(mesh):
    in_specs = (
        P(("dp", "tower", "tensor"), None),
        P(),
        P(None, "tensor"),
        P(None, "tensor"),
        P("tensor", None),
        P(),
        P(),
        P(("dp", "tower", "tensor"), None),
        P(),
        P(None, ("tower", "tensor")),
        P(None, ("tower", "tensor")),
        P(("tower", "tensor"), None),
        P(),
        P(),
        P(),
    )
    out_specs = (P(), P("tensor", ("dp", "tower")), P(("tower", "tensor"), "dp"))
    return jax.shard_map(body, mesh=mesh, in_specs=in_specs, out_specs=out_specs, check_vma=False)
```

```python
import functools

import jax
import jax.numpy as jnp
from jax import lax
from jax.experimental import pallas as pl
from jax.experimental.pallas import tpu as pltpu
from jax.sharding import PartitionSpec as P

QLEN = 1536
ILEN = 512
EPS = 1e-06
TAU = 0.05
TEACH = 2.0
LOSS_SCALE = 64.0
HIGH = lax.Precision.HIGHEST
MESH = pl.DeviceIdType.MESH
F32 = jnp.float32
BF16 = jnp.bfloat16

X = 4
ZL = 4
ZR = 8
VMEM_LIMIT = 60 * 1024 * 1024


def rms_scale(values):
    return lax.rsqrt(jnp.mean(values * values, axis=-1, keepdims=True) + EPS)


def dot(left, right, dims=((1,), (0,)), precision=None):
    return lax.dot_general(
        left, right, (dims, ((), ())), preferred_element_type=F32, precision=precision
    )


def remote(src, dst, send, recv, where):
    return pltpu.make_async_remote_copy(
        src_ref=src, dst_ref=dst, send_sem=send, recv_sem=recv, device_id=where, device_id_type=MESH
    )


class Place:
    def __init__(self):
        self.t = lax.axis_index("tensor")
        self.w = lax.axis_index("tower")
        self.a = self.t // X
        self.b = self.t % X
        self.z = self.w * ZL + self.a
        self.bp = (self.b + 1) % X
        self.bm = (self.b + X - 1) % X
        self.bo = (self.b + 2) % X
        self.xp = {"tensor": self.a * X + self.bp}
        self.xm = {"tensor": self.a * X + self.bm}
        self.zp = self.ring(1)
        self.zm = self.ring(ZR - 1)

    def ring(self, step):
        z = (self.z + step) % ZR
        return {"tower": z // ZL, "tensor": (z % ZL) * X + self.b}

    def column(self, row):
        return {"tensor": row * X + self.b}

    def order(self, j):
        near = jnp.minimum(self.a, ZL - 1 - self.a)
        swapped = jnp.where(j == 0, 1, jnp.where(j == 1, 0, j))
        row = jnp.where(near == 1, swapped, j)
        return jnp.where(self.a >= 2, ZL - 1 - row, row)


def rows_of(ref, first, count, unit):
    return ref.at[pl.ds(pl.multiple_of(first, unit), count), :]


class RowGather:
    def __init__(self, place, buf, rows, send, recv):
        self.p, self.buf, self.n, self.send, self.recv = place, buf, rows, send, recv

    def block(self, s, b):
        return rows_of(self.buf, (s * X + b) * self.n, self.n, self.n)

    def half(self, s, b, h):
        n = self.n // 2
        return rows_of(self.buf, (s * X + b) * self.n + h * n, n, n)

    def up(self, s):
        ref = self.block(s, self.p.b)
        where = self.p.column(jnp.minimum(self.p.a + 1, ZL - 1))
        return remote(ref, ref, self.send.at[0, s], self.recv.at[0, s], where)

    def down(self, s):
        ref = self.block(s, self.p.b)
        where = self.p.column(jnp.maximum(self.p.a - 1, 0))
        return remote(ref, ref, self.send.at[1, s], self.recv.at[0, s], where)

    def right(self, s):
        ref = self.block(s, self.p.b)
        return remote(ref, ref, self.send.at[2, s], self.recv.at[1, s], self.p.xp)

    def left(self, s):
        ref = self.block(s, self.p.b)
        return remote(ref, ref, self.send.at[3, s], self.recv.at[2, s], self.p.xm)

    def half_right(self, s):
        ref = self.half(s, self.p.bm, 0)
        return remote(ref, ref, self.send.at[4, s], self.recv.at[3, s], self.p.xp)

    def half_left(self, s):
        ref = self.half(s, self.p.bp, 1)
        return remote(ref, ref, self.send.at[5, s], self.recv.at[4, s], self.p.xm)

    def goes_up(self, s):
        return (s <= self.p.a) & (self.p.a < ZL - 1)

    def goes_down(self, s):
        return (s >= self.p.a) & (self.p.a > 0)

    def take_z(self, s):
        @pl.when(s != self.p.a)
        def _():
            self.up(s).wait_recv()

        @pl.when(self.goes_up(s))
        def _():
            self.up(s).start()

        @pl.when(self.goes_down(s))
        def _():
            self.down(s).start()

        self.right(s).start()
        self.left(s).start()

    def take_x(self, s):
        ref = self.block(s, self.p.bm)
        remote(ref, ref, self.send.at[2, s], self.recv.at[1, s], self.p.xm).wait_recv()
        self.half_right(s).start()
        ref = self.block(s, self.p.bp)
        remote(ref, ref, self.send.at[3, s], self.recv.at[2, s], self.p.xp).wait_recv()
        self.half_left(s).start()

    def take_halves(self, s):
        ref = self.half(s, self.p.bo, 0)
        remote(ref, ref, self.send.at[4, s], self.recv.at[3, s], self.p.xm).wait_recv()
        ref = self.half(s, self.p.bo, 1)
        remote(ref, ref, self.send.at[5, s], self.recv.at[4, s], self.p.xp).wait_recv()

    def drain(self):
        def each(s, _):
            @pl.when(self.goes_up(s))
            def _():
                self.up(s).wait_send()

            @pl.when(self.goes_down(s))
            def _():
                self.down(s).wait_send()

            self.right(s).wait_send()
            self.left(s).wait_send()
            self.half_right(s).wait_send()
            self.half_left(s).wait_send()
            return 0

        lax.fori_loop(0, ZL, each, 0)


class RingGather:
    def __init__(self, place, buf, rows, send, recv):
        self.p, self.buf, self.n, self.send, self.recv = place, buf, rows, send, recv

    def ref(self, z, hop, upward):
        z = (z + 2 * ZR) % ZR
        if hop < 4:
            return rows_of(self.buf, z * self.n, self.n, self.n)
        n = self.n // 2
        return rows_of(self.buf, z * self.n + (0 if upward else n), n, n)

    def copies(self, hop):
        up = self.ref(self.p.z - hop + 1, hop, True)
        down = self.ref(self.p.z + hop - 1, hop, False)
        return (
            remote(up, up, self.send.at[0, hop - 1], self.recv.at[0, hop - 1], self.p.zp),
            remote(down, down, self.send.at[1, hop - 1], self.recv.at[1, hop - 1], self.p.zm),
        )

    def start(self, hop):
        for copy in self.copies(hop):
            copy.start()

    def take(self, hop):
        up = self.ref(self.p.z - hop, hop, True)
        down = self.ref(self.p.z + hop, hop, False)
        remote(up, up, self.send.at[0, hop - 1], self.recv.at[0, hop - 1], self.p.zm).wait_recv()
        remote(down, down, self.send.at[1, hop - 1], self.recv.at[1, hop - 1], self.p.zp).wait_recv()

    def drain(self):
        for hop in range(1, 5):
            for copy in self.copies(hop):
                copy.wait_send()


class RingSum:
    def __init__(self, place, buf, land, rows, send, recv):
        self.p, self.buf, self.land = place, buf, land
        self.n, self.send, self.recv = rows, send, recv

    def part(self, z, half):
        z = (z + 2 * ZR) % ZR
        if half is None:
            return rows_of(self.buf, z * self.n, self.n, self.n)
        n = self.n // 2
        return rows_of(self.buf, z * self.n + half * n, n, n)

    def slot(self, way, hop):
        if hop == 1:
            return self.land.at[way, 0, pl.ds(0, self.n // 2), :]
        return self.land.at[way, hop - 1]

    def copies(self, hop):
        half = (0, 1) if hop == 1 else (None, None)
        up = self.part(self.p.z + 5 - hop, half[0])
        down = self.part(self.p.z - 5 + hop, half[1])
        return (
            remote(up, self.slot(0, hop), self.send.at[0, hop - 1], self.recv.at[0, hop - 1], self.p.zp),
            remote(down, self.slot(1, hop), self.send.at[1, hop - 1], self.recv.at[1, hop - 1], self.p.zm),
        )

    def start(self, hop):
        for copy in self.copies(hop):
            copy.start()

    def take(self, hop):
        for copy in self.copies(hop):
            copy.wait_recv()

    def add(self, hop):
        half = (0, 1) if hop == 1 else (None, None)
        for way, z in ((0, self.p.z + 4 - hop), (1, self.p.z - 4 + hop)):
            ref = self.part(z, half[way])
            ref[...] = (ref[...].astype(F32) + self.slot(way, hop)[...].astype(F32)).astype(BF16)

    def drain(self):
        for hop in range(1, 5):
            for copy in self.copies(hop):
                copy.wait_send()


def gain_row(ref):
    return ref[...].astype(F32).reshape(1, -1)


def normed_rows(act, gain):
    values = act.astype(F32)
    return (values * rms_scale(values) * gain).astype(BF16)


def gated(gate_val, up_val):
    return (jax.nn.silu(gate_val) * up_val).astype(BF16)


def at_step(i, step):
    return pl.when(i == step)


def split_rows(row):
    high = row.astype(BF16).astype(F32)
    rest = row - high
    mid = rest.astype(BF16).astype(F32)
    low = rest - mid
    index = lax.broadcasted_iota(jnp.int32, (8, row.shape[1]), 0)
    out = jnp.where(index == 0, high, jnp.where(index == 1, mid, jnp.where(index == 2, low, 0.0)))
    return out.astype(BF16)


def unit_scale(vec):
    return lax.rsqrt(jnp.sum(vec * vec, axis=-1, keepdims=True) + EPS)


def unit_back(vec, scales, upstream):
    inner = jnp.sum(vec * upstream, axis=-1, keepdims=True)
    return scales * upstream - vec * (scales * scales * scales) * inner


def contrast(query_hat, item_hat, ranks, positive):
    logits = dot(query_hat, item_hat, ((1,), (1,)), HIGH) / TAU
    shifted = logits - 1.0 / TAU
    log_student = shifted - jnp.log(jnp.sum(jnp.exp(shifted), axis=1, keepdims=True))
    teach = -ranks.astype(F32) / TEACH
    log_teacher = teach - jnp.log(jnp.sum(jnp.exp(teach), axis=1, keepdims=True))
    teacher = jnp.exp(log_teacher)
    columns = lax.broadcasted_iota(jnp.int32, logits.shape, 1)
    onehot = (columns == positive).astype(F32)
    per_row = jnp.sum(
        teacher * (log_teacher - log_student) - onehot * log_student, axis=1, keepdims=True
    )
    slopes = 2.0 * jnp.exp(log_student) - onehot - teacher
    return (per_row, slopes)


def grad_rows(resid, scales, gain, upstream):
    along = gain * upstream
    inner = jnp.mean(along * resid, axis=-1, keepdims=True)
    return (scales * along - resid * (scales * scales * scales) * inner).astype(BF16)


def by_tower(values, parts, tower):
    wide = values.shape[1] // parts
    blocks = [values[:, d * wide : (d + 1) * wide] for d in range(tower, parts, 2)]
    return jnp.concatenate(blocks, axis=1)


def kernel(
    qa, qg, gate_hbm, up_hbm, down_hbm, ia, ig, ig_w, iu_w, id_w, qf, if_, proj_hbm, ranks, positive,
    loss, q_out, i_out,
    w, proj, nq, part, gate_val, h2, pm, r1, r2, zs, zin, ni, wi, ip, land, hq, hi,
    sums, hats, scal, yq, grad, yi, gq, gi, qc1, qb1, qb2, qc, ic1, ib1, ib2, ic,
    loads, gs, gr, ss, sr, ws, wr, vs, vr, hs, hr, ias, iar, irs, irr,
    s1, r1s, s2, r2s, s3, r3s, ys, yr, iys, iyr, qs, qv, bs, bv,
):
    p = Place()
    n, dq = qa.shape
    m, di = ia.shape
    f, k = down_hbm.shape[0], id_w.shape[0]
    group = X * n
    h = n // 2
    parts = X * ZL
    count = hats.shape[0]
    block_wide = dq // count
    piece = w.shape[2] // 4
    wide, thin = dq // 2, dq // 4
    dp = lax.axis_index("dp")
    own = dp * 2 + p.w
    y, c = dp // 2, dp % 2
    yp, ym, y2 = (y + 1) % 4, (y + 3) % 4, (y + 2) % 4
    line_y = (y2, yp, ym, y)
    to_yp, to_ym, to_core = {"dp": yp * 2 + c}, {"dp": ym * 2 + c}, {"dp": y * 2 + 1 - c}
    to_y = (to_yp, to_ym)
    to_tower = {"tower": 1 - p.w}
    a2 = (p.a + 2) % ZL
    mate = p.a + 1 - 2 * (p.a % 2)
    to_a2, to_mate = p.column(a2), p.column(mate)

    def member(step):
        return {"tensor": (p.t + step) % parts}

    def replica(step):
        other = (own + step) % count
        return {"dp": other // 2, "tower": other % 2}

    own_weights = [
        pltpu.make_async_copy(ref, w.at[0, index, pl.ds(0, f), :], loads.at[index])
        for index, ref in enumerate((gate_hbm, up_hbm, down_hbm))
    ]
    proj_copy = pltpu.make_async_copy(proj_hbm, proj, loads.at[3])
    for copy in own_weights:
        copy.start()
    proj_copy.start()
    barrier = pltpu.get_barrier_semaphore()

    def greet(step, _):
        pl.semaphore_signal(barrier, inc=1, device_id=member(step), device_id_type=MESH)
        pl.semaphore_signal(barrier, inc=1, device_id=replica(step), device_id_type=MESH)
        return 0

    lax.fori_loop(1, parts, greet, 0)
    for where in (p.zp, p.zm):
        pl.semaphore_signal(barrier, inc=1, device_id=where, device_id_type=MESH)
    for index in range(3):
        w[0, index, f:, :] = jnp.zeros((w.shape[2] - f, dq), BF16)
    nq[pl.ds(pl.multiple_of(p.b * n, n), n), :] = normed_rows(qa[...], gain_row(qg))
    ni[pl.ds(pl.multiple_of(p.z * m, m), m), :] = normed_rows(ia[...], gain_row(ig))
    for index, ref in enumerate((ig_w, iu_w, id_w)):
        wi[index, pl.ds(pl.multiple_of(p.b * k, k), k), :] = ref[...]
    pl.semaphore_wait(barrier, 2 * (parts - 1) + 2)

    rows = RowGather(p, nq, n, gs, gr)
    items = RingGather(p, ni, m, ias, iar)
    isum = RingSum(p, ip, land, m, irs, irr)

    def across():
        return remote(rows.block(0, p.b), rows.block(1, p.b), gs.at[0, 0], gr.at[0, 0], to_a2)

    def wpiece(which, index, line, core):
        first = pl.multiple_of(line * piece, piece)
        return w.at[which, index, pl.ds(first, piece), pl.ds(pl.multiple_of(core * wide, wide), wide)]

    def whalf(index, line, part_of):
        first = pl.multiple_of(line * piece, piece)
        column = pl.multiple_of(c * wide + part_of * thin, thin)
        return w.at[1, index, pl.ds(first, piece), pl.ds(column, thin)]

    def w_send(index, kind):
        here = wpiece(1, index, y, c)
        low, high = wpiece(1, index, ym, c), wpiece(1, index, yp, c)
        src, dst, where = (
            (wpiece(0, index, y, c), here, to_mate),
            (here, here, to_yp),
            (here, here, to_ym),
            (whalf(index, ym, 0), whalf(index, ym, 0), to_yp),
            (whalf(index, yp, 1), whalf(index, yp, 1), to_ym),
            (here, here, to_core),
            (low, low, to_core),
            (high, high, to_core),
            (wpiece(1, index, y2, c), wpiece(1, index, y2, c), to_core),
        )[kind]
        return remote(src, dst, ws.at[kind, index], wr.at[kind, index], where)

    def w_got(index, kind):
        dst = (
            wpiece(1, index, y, c),
            wpiece(1, index, ym, c),
            wpiece(1, index, yp, c),
            whalf(index, y2, 0),
            whalf(index, y2, 1),
            wpiece(1, index, y, 1 - c),
            wpiece(1, index, ym, 1 - c),
            wpiece(1, index, yp, 1 - c),
            wpiece(1, index, y2, 1 - c),
        )[kind]
        remote(dst, dst, ws.at[kind, index], wr.at[kind, index], to_core).wait_recv()

    def w_near(index):
        w_got(index, 0)
        for kind in (1, 2, 5):
            w_send(index, kind).start()

    def w_ring(index):
        w_got(index, 1)
        w_send(index, 3).start()
        w_send(index, 6).start()
        w_got(index, 2)
        w_send(index, 4).start()
        w_send(index, 7).start()

    def w_far(index):
        w_got(index, 3)
        w_got(index, 4)
        w_send(index, 8).start()

    def w_done(index):
        for kind in (5, 6, 7, 8):
            w_got(index, kind)

    def vpiece(b, core):
        column = pl.multiple_of(core * (di // 2), di // 2)
        return wi.at[:, pl.ds(pl.multiple_of(b * k, k), k), pl.ds(column, di // 2)]

    def vhalf(b, part_of):
        first = pl.multiple_of(b * k + part_of * (k // 2), k // 2)
        column = pl.multiple_of(c * (di // 2), di // 2)
        return wi.at[:, pl.ds(first, k // 2), pl.ds(column, di // 2)]

    def v_send(kind):
        ref, where = (
            (vpiece(p.b, c), p.xp),
            (vpiece(p.b, c), p.xm),
            (vhalf(p.bm, 0), p.xp),
            (vhalf(p.bp, 1), p.xm),
            (vpiece(p.bm, c), to_core),
            (vpiece(p.bp, c), to_core),
            (vpiece(p.bo, c), to_core),
        )[kind]
        return remote(ref, ref, vs.at[kind], vr.at[kind], where)

    def v_got(kind):
        ref = (
            vpiece(p.bm, c),
            vpiece(p.bp, c),
            vhalf(p.bo, 0),
            vhalf(p.bo, 1),
            vpiece(p.bm, 1 - c),
            vpiece(p.bp, 1 - c),
            vpiece(p.bo, 1 - c),
        )[kind]
        remote(ref, ref, vs.at[kind], vr.at[kind], to_core).wait_recv()

    def block(j, q, b):
        return rows_of(pm.at[q], (j * X + b) * n, n, n)

    def half(j, q, b, part_of):
        return rows_of(pm.at[q], (j * X + b) * n + part_of * h, h, h)

    def first(j, q, way):
        src = half(j, q, p.bo, way)
        where = (p.xp, p.xm)[way]
        return remote(src, r1.at[way, j, q], ss.at[way, j, q], sr.at[way, j, q], where)

    def second(j, q, way):
        src = block(j, q, (p.bp, p.bm)[way])
        where = (p.xp, p.xm)[way]
        return remote(src, r2.at[way, j, q], ss.at[2 + way, j, q], sr.at[2 + way, j, q], where)

    def to_owner(q):
        return remote(zs.at[q], zin.at[q], ss.at[4, 0, q], sr.at[4, 0, q], to_a2)

    def back(j):
        s = (p.a, a2)[j]
        dst = hq.at[pl.ds(pl.multiple_of(s * group, group), group), :]
        return remote(h2.at[j], dst, hs.at[j], hr.at[j], to_mate)

    def back_got(j):
        other = (mate, (mate + 2) % ZL)[j]
        dst = hq.at[pl.ds(pl.multiple_of(other * group, group), group), :]
        remote(h2.at[j], dst, hs.at[j], hr.at[j], to_mate).wait_recv()

    def rows_in(j):
        return nq[j * group : (j + 1) * group, :]

    def own_units(j):
        left = rows_in(j)
        value = gated(
            dot(left, w[0, 0, :f, :], ((1,), (1,))), dot(left, w[0, 1, :f, :], ((1,), (1,)))
        )
        hq[pl.ds(pl.multiple_of((p.a, a2)[j] * group, group), group), :] = value
        part[j] = dot(value, w[0, 2, :f, :])

    def mate_gate(j):
        gate_val[j] = dot(rows_in(j), w[1, 0, :f, :], ((1,), (1,)))

    def mate_up(j):
        h2[j] = gated(gate_val[j], dot(rows_in(j), w[1, 1, :f, :], ((1,), (1,))))

    def mate_down(j, q):
        columns = slice(q * wide, (q + 1) * wide)
        total = part[j, :, columns] + dot(h2[j], w[1, 2, :f, columns])
        pm[q, j * group : (j + 1) * group, :] = total.astype(BF16)
        first(j, q, 0).start()
        first(j, q, 1).start()

    def combine(j, q):
        for way in range(2):
            first(j, q, way).wait_recv()
            ref = half(j, q, (p.bp, p.bm)[way], way)
            ref[...] = (ref[...].astype(F32) + r1[way, j, q].astype(F32)).astype(BF16)
            second(j, q, way).start()

    def summed(j, q):
        second(j, q, 0).wait_recv()
        second(j, q, 1).wait_recv()
        total = block(j, q, p.b)[...].astype(F32)
        return total + r2[0, j, q].astype(F32) + r2[1, j, q].astype(F32)

    def send_sum(q):
        zs[q] = summed(1, q).astype(BF16)
        to_owner(q).start()

    def item_hop(hop):
        items.take(hop)
        if hop < 4:
            items.start(hop + 1)

    def isum_hop(hop):
        isum.take(hop)
        isum.add(hop)
        isum.start(hop + 1)

    def item_product():
        left = ni[...]
        partial = 0.0
        for b in range(X):
            here = slice(b * k, (b + 1) * k)
            value = gated(
                dot(left, wi[0, here, :], ((1,), (1,))), dot(left, wi[1, here, :], ((1,), (1,)))
            )
            hi[b] = value
            partial = partial + dot(value, wi[2, here, :])
        ip[...] = partial.astype(BF16)
        isum.start(1)

    rows.right(0).start()
    rows.left(0).start()
    items.start(1)
    own_weights[0].wait()
    w_send(0, 0).start()
    across().start()
    own_weights[1].wait()
    own_weights[2].wait()
    w_near(0)
    w_send(1, 0).start()
    rows.take_x(0)
    item_hop(1)
    v_send(0).start()
    v_send(1).start()
    rows.take_halves(0)
    own_units(0)
    item_hop(2)
    w_ring(0)
    w_near(1)
    w_send(2, 0).start()
    remote(rows.block(0, p.b), rows.block(1, p.b), gs.at[0, 0], gr.at[0, 0], to_a2).wait_recv()
    rows.right(1).start()
    rows.left(1).start()
    item_hop(3)
    w_far(0)
    for kind in range(2):
        v_got(kind)
        v_send(2 + kind).start()
        v_send(4 + kind).start()
    item_hop(4)
    w_ring(1)
    w_near(2)
    w_done(0)
    mate_gate(0)
    v_got(2)
    v_got(3)
    v_send(6).start()
    w_far(1)
    for kind in (4, 5, 6):
        v_got(kind)
    item_product()
    rows.take_x(1)
    w_done(1)
    mate_up(0)
    w_ring(2)
    isum_hop(1)
    rows.take_halves(1)
    own_units(1)
    isum_hop(2)
    w_far(2)
    mate_gate(1)
    mate_up(1)
    isum_hop(3)
    w_done(2)
    mate_down(0, 0)
    mate_down(0, 1)
    mate_down(1, 0)
    mate_down(1, 1)
    back(0).start()
    combine(1, 0)
    combine(1, 1)
    combine(0, 0)
    send_sum(0)
    combine(0, 1)
    send_sum(1)
    back(1).start()
    isum.take(4)
    own_item = ip[pl.ds(pl.multiple_of(p.z * m, m), m), :].astype(F32)
    i_resid = ia[...].astype(F32) + (own_item + land[0, 3].astype(F32) + land[1, 3].astype(F32))
    mlp = []
    for q in range(2):
        total = summed(0, q)
        to_owner(q).wait_recv()
        mlp.append(total + zin[q].astype(F32))
    q_resid = qa[...].astype(F32) + jnp.concatenate(mlp, axis=1)

    q_gain, i_gain = gain_row(qf), gain_row(if_)
    q_scale, i_scale = rms_scale(q_resid), rms_scale(i_resid)
    sums[p.t, :, :dq] = jnp.sum(q_resid * q_scale * q_gain, axis=0, keepdims=True)
    sums[p.t, :, dq:] = jnp.sum(i_resid * i_scale * i_gain, axis=0, keepdims=True)

    def spread_members(buf, send, recv):
        def each(step, _):
            remote(buf.at[p.t], buf.at[p.t], send.at[step], recv.at[p.t], member(step)).start()
            return 0

        lax.fori_loop(1, parts, each, 0)

    def await_members(buf, send, recv):
        def each(step, _):
            other = (p.t + step) % parts
            remote(buf.at[p.t], buf.at[other], send.at[step], recv.at[other], member(step)).wait()
            return 0

        lax.fori_loop(1, parts, each, 0)

    def spread_hats(step, _):
        remote(hats.at[own], hats.at[own], s2.at[step], r2s.at[own], replica(step)).start()
        return 0

    def gathered_hats(step, _):
        other = (own + step) % count
        remote(hats.at[own], hats.at[other], s2.at[step], r2s.at[other], replica(step)).wait()
        return 0

    def q_rows(tower, line_of, core):
        return rows_of(gq.at[tower], (line_of * 2 + core) * block_wide, block_wide, block_wide)

    def q_half(tower, line_of, way):
        first = (line_of * 2 + c) * block_wide + way * (block_wide // 2)
        return rows_of(gq.at[tower], first, block_wide // 2, block_wide // 2)

    def q_core(tower, j):
        src = q_rows(tower, line_y[j], 1 - c)
        return remote(src, qc1.at[tower, j], qs.at[tower, j], qv.at[tower, j], to_core)

    def q_first(tower, way):
        src, dst = q_half(tower, y2, way), qb1.at[tower, way]
        return remote(src, dst, qs.at[tower, 4 + way], qv.at[tower, 4 + way], to_y[way])

    def q_second(tower, way):
        src, dst = q_rows(tower, (yp, ym)[way], c), qb2.at[tower, way]
        return remote(src, dst, qs.at[tower, 6 + way], qv.at[tower, 6 + way], to_y[way])

    def q_tower(tower):
        return remote(q_rows(tower, y, c), qc, qs.at[tower, 8], qv.at[tower, 8], to_tower)

    def q_start(tower):
        for j in range(4):
            q_core(tower, j).start()

    def q_far(tower):
        q_core(tower, 0).wait_recv()
        ref = q_rows(tower, y2, c)
        ref[...] += qc1[tower, 0]
        for way in range(2):
            q_first(tower, way).start()

    def q_near(tower):
        for way in range(2):
            q_core(tower, 1 + way).wait_recv()
            ref = q_rows(tower, (yp, ym)[way], c)
            ref[...] += qc1[tower, 1 + way]
            q_first(tower, way).wait_recv()
            ref = q_half(tower, (yp, ym)[way], way)
            ref[...] += qb1[tower, way]
            q_second(tower, way).start()

    def q_own(tower):
        q_core(tower, 3).wait_recv()
        for way in range(2):
            q_second(tower, way).wait_recv()
        ref = q_rows(tower, y, c)
        ref[...] = ref[...] + qc1[tower, 3] + qb2[tower, 0] + qb2[tower, 1]

        @pl.when(p.w != tower)
        def _():
            q_tower(tower).start()

    def q_finish(tower):
        @pl.when(p.w == tower)
        def _():
            q_tower(tower).wait_recv()
            q_out[...] = q_rows(tower, y, c)[...] + qc[...]

    def i_rows(line_of, core):
        first = pl.multiple_of((line_of * 2 + core) * block_wide, block_wide)
        return gi.at[:, pl.ds(first, block_wide), :]

    def i_half(line_of, way):
        first = pl.multiple_of((line_of * 2 + c) * block_wide, block_wide)
        return gi.at[pl.ds(way * 2, 2), pl.ds(first, block_wide), :]

    def i_slab(b):
        return gi.at[b, pl.ds(pl.multiple_of((y * 2 + c) * block_wide, block_wide), block_wide), :]

    def i_core(j):
        return remote(i_rows(line_y[j], 1 - c), ic1.at[j], bs.at[j], bv.at[j], to_core)

    def i_first(way):
        return remote(i_half(y2, way), ib1.at[way], bs.at[4 + way], bv.at[4 + way], to_y[way])

    def i_second(way):
        src = i_rows((yp, ym)[way], c)
        return remote(src, ib2.at[way], bs.at[6 + way], bv.at[6 + way], to_y[way])

    def i_x(hop):
        other = (p.b + hop) % X
        where = {"tensor": p.a * X + other}
        return remote(i_slab(other), ic.at[p.b], bs.at[8 + hop], bv.at[8 + p.b], where)

    def i_product():
        for b in range(X):
            gi[b] = dot(yi[...], hi[b], ((0,), (0,)))
        for j in range(4):
            i_core(j).start()

    def i_far():
        for j in range(4):
            i_core(j).wait_recv()
            ref = i_rows(line_y[j], c)
            ref[...] += ic1[j]
        for way in range(2):
            i_first(way).start()

    def i_near():
        for way in range(2):
            i_first(way).wait_recv()
            ref = i_half((yp, ym)[way], way)
            ref[...] += ib1[way]
            i_second(way).start()

    def i_own():
        for way in range(2):
            i_second(way).wait_recv()
        ref = i_rows(y, c)
        ref[...] = ref[...] + ib2[0] + ib2[1]
        for hop in range(1, X):
            i_x(hop).start()

    def i_finish():
        total = i_slab(p.b)[...]
        for hop in range(1, X):
            other = (p.b + hop) % X
            remote(i_slab(other), ic.at[other], bs.at[8 + hop], bv.at[8 + other], p.xp).wait_recv()
            total = total + ic[other]
        i_out[...] = total

    gather = [RowGather(p, yq.at[tower], n, ys.at[tower], yr.at[tower]) for tower in range(2)]
    igather = RingGather(p, yi, m, iys, iyr)

    def take_z(g):
        gather[g // ZL].take_z(p.order(g % ZL))

    def take_x(g):
        gather[g // ZL].take_x(p.order(g % ZL))

    def item_grad_hop(hop):
        igather.take(hop)
        if hop < 4:
            igather.start(hop + 1)

    def product(g):
        tower = g // ZL
        s = p.order(g % ZL)
        gather[tower].take_halves(s)
        for b in range(X):
            tile = scal[s * X + b]
            columns = jnp.concatenate([tile] * 16, axis=0).T[:n]
            first_row = pl.multiple_of((s * X + b) * n, n)
            resid = yq[tower, pl.ds(first_row, n), :].astype(F32)
            value = columns[:, 0:1] * along_of[tower] - resid * columns[:, 1:2]
            grad[b * n : (b + 1) * n, :] = value.astype(BF16)
        here = pl.ds(pl.multiple_of(s * group, group), group)
        value = dot(grad[...], hq[here, :], ((0,), (0,)))
        gq[tower] = value if g % ZL == 0 else gq[tower] + value

    spread_members(sums, s1, r1s)
    for tower in range(2):
        here = pl.ds(pl.multiple_of(p.t * n, n), n)
        yq[tower, here, :] = by_tower(q_resid, count, tower).astype(BF16)
    take_z(0)
    proj_copy.wait()
    await_members(sums, s1, r1s)
    total = sums[0]
    for slot in range(1, parts):
        total = total + sums[slot]
    q_pooled = total[:, :dq] / QLEN
    i_pooled = total[:, dq:] / ILEN
    q_e = jnp.sum(dot(split_rows(q_pooled), proj[...]), axis=0, keepdims=True)
    q_norm, i_norm = unit_scale(q_e), unit_scale(i_pooled)
    hats[own, :, :di] = q_e * q_norm
    hats[own, :, di:] = i_pooled * i_norm
    lax.fori_loop(1, count, spread_hats, 0)
    take_z(1)
    take_z(4)
    take_x(0)
    lax.fori_loop(1, count, gathered_hats, 0)
    index = lax.broadcasted_iota(jnp.int32, (count, 2 * di), 0)
    every = jnp.zeros((count, 2 * di), F32)
    for slot in range(count):
        every = jnp.where(index == slot, hats[slot], every)
    every_query, every_items = every[:, :di], every[:, di:]
    line = lax.broadcasted_iota(jnp.int32, (count, count), 0)
    target = jnp.zeros((count, count), jnp.int32)
    for slot in range(count):
        target = jnp.where(line == slot, positive[slot], target)
    per_row, slopes = contrast(every_query, every_items, ranks[...], target)
    loss[...] = jnp.sum(per_row, axis=0, keepdims=True) / count
    weights = slopes * (LOSS_SCALE / (TAU * count))
    take_z(2)
    take_x(1)
    mine = lax.broadcasted_iota(jnp.int32, (count, di), 0) == own
    q_back = jnp.sum(
        jnp.where(mine, dot(weights, every_items, precision=HIGH), 0.0), axis=0, keepdims=True
    )
    column = lax.broadcasted_iota(jnp.int32, (count, count), 1) == own
    i_back = jnp.sum(
        jnp.sum(jnp.where(column, weights, 0.0), axis=1, keepdims=True) * every_query,
        axis=0,
        keepdims=True,
    )
    q_grad_e = unit_back(q_e, q_norm, q_back)
    q_up = jnp.sum(dot(split_rows(q_grad_e), proj[...], ((1,), (1,))), axis=0, keepdims=True) / QLEN
    i_up = unit_back(i_pooled, i_norm, i_back) / ILEN
    along = q_gain * q_up
    along_of = [by_tower(along, count, tower) for tower in range(2)]
    inner = jnp.mean(along * q_resid, axis=-1, keepdims=True)
    slope = (q_scale * q_scale * q_scale) * inner
    lane = lax.broadcasted_iota(jnp.int32, (n, 128), 1)
    columns = jnp.where(lane == 0, q_scale, jnp.where(lane == 1, slope, 0.0))
    columns = jnp.concatenate([columns, jnp.zeros((128 - n, 128), F32)], axis=0)
    scal[p.t] = columns.T[:8]
    spread_members(scal, s3, r3s)
    yi[pl.ds(pl.multiple_of(p.z * m, m), m), :] = grad_rows(i_resid, i_scale, i_gain, i_up)
    igather.start(1)
    take_z(3)
    take_x(4)
    item_grad_hop(1)
    await_members(scal, s3, r3s)
    back_got(0)
    back_got(1)
    product(0)
    take_z(5)
    take_x(2)
    product(1)
    item_grad_hop(2)
    take_z(6)
    take_x(3)
    product(2)
    take_z(7)
    item_grad_hop(3)
    product(3)
    q_start(0)
    take_x(5)
    q_far(0)
    product(4)
    item_grad_hop(4)
    take_x(6)
    q_near(0)
    i_product()
    product(5)
    take_x(7)
    i_far()
    product(6)
    q_own(0)
    i_near()
    product(7)
    q_start(1)
    q_far(1)
    i_own()
    q_near(1)
    i_finish()
    q_finish(0)
    q_own(1)
    q_finish(1)

    for j in range(2):
        back(j).wait_send()
        for copy in (rows.right(j), rows.left(j), rows.half_right(j), rows.half_left(j)):
            copy.wait_send()
        for q in range(2):
            for way in range(2):
                first(j, q, way).wait_send()
                second(j, q, way).wait_send()
    for q in range(2):
        to_owner(q).wait_send()
    across().wait_send()
    items.drain()
    isum.drain()
    for index in range(3):
        for kind in range(9):
            w_send(index, kind).wait_send()
    for kind in range(7):
        v_send(kind).wait_send()
    for tower in range(2):
        gather[tower].drain()
        for j in range(4):
            q_core(tower, j).wait_send()
        for way in range(2):
            q_first(tower, way).wait_send()
            q_second(tower, way).wait_send()

        @pl.when(p.w != tower)
        def _():
            q_tower(tower).wait_send()

    igather.drain()
    for j in range(4):
        i_core(j).wait_send()
    for way in range(2):
        i_first(way).wait_send()
        i_second(way).wait_send()
    for hop in range(1, X):
        i_x(hop).wait_send()


def step(qa, qg, gate, up, down, ia, ig, ig_w, iu_w, id_w, qf, if_, proj, ranks, positive):
    n, dq = qa.shape
    m, di = ia.shape
    f, k = down.shape[0], id_w.shape[0]
    padded = 64 * ((f + 63) // 64)
    vmem, hbm = pl.BlockSpec(memory_space=pltpu.VMEM), pl.BlockSpec(memory_space=pl.ANY)
    smem = pl.BlockSpec(memory_space=pltpu.SMEM)
    all_i = ZR * m
    group = X * n
    parts = X * ZL
    count = ranks.shape[0]
    wide = dq // count
    dma = pltpu.SemaphoreType.DMA
    return pl.pallas_call(
        kernel,
        out_shape=(
            jax.ShapeDtypeStruct((1, 1), F32),
            jax.ShapeDtypeStruct((wide, f), F32),
            jax.ShapeDtypeStruct((wide, k), F32),
        ),
        in_specs=[vmem, vmem, hbm, hbm, hbm] + [vmem] * 7 + [hbm, vmem, smem],
        out_specs=[vmem] * 3,
        scratch_shapes=[
            pltpu.VMEM((2, 3, padded, dq), BF16),
            pltpu.VMEM(proj.shape, BF16),
            pltpu.VMEM((2 * group, dq), BF16),
            pltpu.VMEM((2, group, dq), F32),
            pltpu.VMEM((2, group, f), F32),
            pltpu.VMEM((2, group, f), BF16),
            pltpu.VMEM((2, 2 * group, dq // 2), BF16),
            pltpu.VMEM((2, 2, 2, n // 2, dq // 2), BF16),
            pltpu.VMEM((2, 2, 2, n, dq // 2), BF16),
            pltpu.VMEM((2, n, dq // 2), BF16),
            pltpu.VMEM((2, n, dq // 2), BF16),
            pltpu.VMEM((all_i, di), BF16),
            pltpu.VMEM((3, X * k, di), BF16),
            pltpu.VMEM((all_i, di), BF16),
            pltpu.VMEM((2, 4, m, di), BF16),
            pltpu.VMEM((ZL * group, f), BF16),
            pltpu.VMEM((X, all_i, k), BF16),
            pltpu.VMEM((parts, 1, dq + di), F32),
            pltpu.VMEM((count, 1, 2 * di), F32),
            pltpu.VMEM((parts, 8, 128), F32),
            pltpu.VMEM((2, parts * n, dq // 2), BF16),
            pltpu.VMEM((group, dq // 2), BF16),
            pltpu.VMEM((all_i, di), BF16),
            pltpu.VMEM((2, dq // 2, f), F32),
            pltpu.VMEM((X, di, k), F32),
            pltpu.VMEM((2, 4, wide, f), F32),
            pltpu.VMEM((2, 2, wide // 2, f), F32),
            pltpu.VMEM((2, 2, wide, f), F32),
            pltpu.VMEM((wide, f), F32),
            pltpu.VMEM((4, X, wide, k), F32),
            pltpu.VMEM((2, 2, wide, k), F32),
            pltpu.VMEM((2, X, wide, k), F32),
            pltpu.VMEM((X, wide, k), F32),
            dma((4,)),
            dma((6, 2)),
            dma((5, 2)),
            dma((5, 2, 2)),
            dma((5, 2, 2)),
            dma((9, 3)),
            dma((9, 3)),
            dma((7,)),
            dma((7,)),
            dma((2,)),
            dma((2,)),
            dma((2, 4)),
            dma((2, 4)),
            dma((2, 4)),
            dma((2, 4)),
            dma((parts,)),
            dma((parts,)),
            dma((count,)),
            dma((count,)),
            dma((parts,)),
            dma((parts,)),
            dma((2, 6, ZL)),
            dma((2, 5, ZL)),
            dma((2, 4)),
            dma((2, 4)),
            dma((2, 9)),
            dma((2, 9)),
            dma((12,)),
            dma((12,)),
        ],
        compiler_params=pltpu.CompilerParams(
            collective_id=0, has_side_effects=True, vmem_limit_bytes=VMEM_LIMIT
        ),
        name="towers_step",
    )(qa, qg, gate, up, down, ia, ig, ig_w, iu_w, id_w, qf, if_, proj, ranks, positive)


def body(
    q_act,
    q_norm_gain,
    q_gate,
    q_up,
    q_down,
    q_final_gain,
    projection,
    i_act,
    i_norm_gain,
    i_gate,
    i_up,
    i_down,
    i_final_gain,
    ranks,
    positive,
):
    loss, q_grad, i_grad = step(
        q_act,
        q_norm_gain,
        q_gate.T,
        q_up.T,
        q_down,
        i_act,
        i_norm_gain,
        i_gate.T,
        i_up.T,
        i_down,
        q_final_gain,
        i_final_gain,
        projection,
        ranks,
        positive,
    )
    return (loss.reshape(()), q_grad.T, i_grad.T)


def solution(mesh):
    in_specs = (
        P(("dp", "tower", "tensor"), None),
        P(),
        P(None, "tensor"),
        P(None, "tensor"),
        P("tensor", None),
        P(),
        P(),
        P(("dp", "tower", "tensor"), None),
        P(),
        P(None, ("tower", "tensor")),
        P(None, ("tower", "tensor")),
        P(("tower", "tensor"), None),
        P(),
        P(),
        P(),
    )
    out_specs = (P(), P("tensor", ("dp", "tower")), P(("tower", "tensor"), "dp"))
    return jax.shard_map(body, mesh=mesh, in_specs=in_specs, out_specs=out_specs, check_vma=False)
```

```python
import functools

import jax
import jax.numpy as jnp
from jax import lax
from jax.experimental import pallas as pl
from jax.experimental.pallas import tpu as pltpu
from jax.sharding import PartitionSpec as P

QLEN = 1536
ILEN = 512
EPS = 1e-06
TAU = 0.05
TEACH = 2.0
LOSS_SCALE = 64.0
HIGH = lax.Precision.HIGHEST
MESH = pl.DeviceIdType.MESH
F32 = jnp.float32
BF16 = jnp.bfloat16

X = 4
ZL = 4
ZR = 8
VMEM_LIMIT = 60 * 1024 * 1024


def rms_scale(values):
    return lax.rsqrt(jnp.mean(values * values, axis=-1, keepdims=True) + EPS)


def dot(left, right, dims=((1,), (0,)), precision=None):
    return lax.dot_general(
        left, right, (dims, ((), ())), preferred_element_type=F32, precision=precision
    )


def remote(src, dst, send, recv, where):
    return pltpu.make_async_remote_copy(
        src_ref=src, dst_ref=dst, send_sem=send, recv_sem=recv, device_id=where, device_id_type=MESH
    )


class Place:
    def __init__(self):
        self.t = lax.axis_index("tensor")
        self.w = lax.axis_index("tower")
        self.a = self.t // X
        self.b = self.t % X
        self.z = self.w * ZL + self.a
        self.bp = (self.b + 1) % X
        self.bm = (self.b + X - 1) % X
        self.bo = (self.b + 2) % X
        self.xp = {"tensor": self.a * X + self.bp}
        self.xm = {"tensor": self.a * X + self.bm}
        self.zp = self.ring(1)
        self.zm = self.ring(ZR - 1)

    def ring(self, step):
        z = (self.z + step) % ZR
        return {"tower": z // ZL, "tensor": (z % ZL) * X + self.b}

    def column(self, row):
        return {"tensor": row * X + self.b}

    def order(self, j):
        near = jnp.minimum(self.a, ZL - 1 - self.a)
        swapped = jnp.where(j == 0, 1, jnp.where(j == 1, 0, j))
        row = jnp.where(near == 1, swapped, j)
        return jnp.where(self.a >= 2, ZL - 1 - row, row)


def rows_of(ref, first, count, unit):
    return ref.at[pl.ds(pl.multiple_of(first, unit), count), :]


class RowGather:
    def __init__(self, place, buf, rows, send, recv):
        self.p, self.buf, self.n, self.send, self.recv = place, buf, rows, send, recv

    def block(self, s, b):
        return rows_of(self.buf, (s * X + b) * self.n, self.n, self.n)

    def up(self, s):
        ref = self.block(s, self.p.b)
        where = self.p.column(jnp.minimum(self.p.a + 1, ZL - 1))
        return remote(ref, ref, self.send.at[0], self.recv.at[0, s], where)

    def down(self, s):
        ref = self.block(s, self.p.b)
        where = self.p.column(jnp.maximum(self.p.a - 1, 0))
        return remote(ref, ref, self.send.at[1], self.recv.at[0, s], where)

    def right(self, s):
        ref = self.block(s, self.p.b)
        return remote(ref, ref, self.send.at[2], self.recv.at[1, s], self.p.xp)

    def left(self, s):
        ref = self.block(s, self.p.b)
        return remote(ref, ref, self.send.at[3], self.recv.at[2, s], self.p.xm)

    def onward(self, s, way):
        ref = self.block(s, (self.p.bm, self.p.bp)[way])
        where = (self.p.xp, self.p.xm)[way]
        return remote(ref, ref, self.send.at[2 + way], self.recv.at[3, s], where)

    def goes_up(self, s):
        return (s <= self.p.a) & (self.p.a < ZL - 1)

    def goes_down(self, s):
        return (s >= self.p.a) & (self.p.a > 0)

    def take_z(self, s):
        @pl.when(s != self.p.a)
        def _():
            self.up(s).wait_recv()

        @pl.when(self.goes_up(s))
        def _():
            self.up(s).start()

        @pl.when(self.goes_down(s))
        def _():
            self.down(s).start()

        self.right(s).start()
        self.left(s).start()

    def take_x(self, s, way):
        for side in (way, 1 - way):
            ref = self.block(s, (self.p.bm, self.p.bp)[side])
            remote(ref, ref, self.send.at[2], self.recv.at[1 + side, s], self.p.xp).wait_recv()
            if side == way:
                self.onward(s, way).start()

    def take_far(self, s):
        ref = self.block(s, self.p.bo)
        remote(ref, ref, self.send.at[2], self.recv.at[3, s], self.p.xp).wait_recv()

    def drain_z(self):
        for count in range(1, ZL):
            ref = rows_of(self.buf, 0, count * self.n, self.n)

            @pl.when(self.p.a == count - 1)
            def _():
                remote(ref, ref, self.send.at[0], self.recv.at[0, 0], self.p.xp).wait_send()

            @pl.when(self.p.a == ZL - count)
            def _():
                remote(ref, ref, self.send.at[1], self.recv.at[0, 0], self.p.xp).wait_send()

    def drain_x(self, right, left):
        for index, count in ((2, right), (3, left)):
            ref = rows_of(self.buf, 0, count * self.n, self.n)
            remote(ref, ref, self.send.at[index], self.recv.at[0, 0], self.p.xp).wait_send()


class RingGather:
    def __init__(self, place, buf, rows, send, recv):
        self.p, self.buf, self.n, self.send, self.recv = place, buf, rows, send, recv

    def ref(self, z, hop, upward):
        z = (z + 2 * ZR) % ZR
        if hop < 4:
            return rows_of(self.buf, z * self.n, self.n, self.n)
        n = self.n // 2
        return rows_of(self.buf, z * self.n + (0 if upward else n), n, n)

    def copies(self, hop):
        up = self.ref(self.p.z - hop + 1, hop, True)
        down = self.ref(self.p.z + hop - 1, hop, False)
        return (
            remote(up, up, self.send.at[0, hop - 1], self.recv.at[0, hop - 1], self.p.zp),
            remote(down, down, self.send.at[1, hop - 1], self.recv.at[1, hop - 1], self.p.zm),
        )

    def start(self, hop):
        for copy in self.copies(hop):
            copy.start()

    def take(self, hop):
        up = self.ref(self.p.z - hop, hop, True)
        down = self.ref(self.p.z + hop, hop, False)
        remote(up, up, self.send.at[0, hop - 1], self.recv.at[0, hop - 1], self.p.zm).wait_recv()
        remote(down, down, self.send.at[1, hop - 1], self.recv.at[1, hop - 1], self.p.zp).wait_recv()

    def drain(self):
        for hop in range(1, 5):
            for copy in self.copies(hop):
                copy.wait_send()


class RingSum:
    def __init__(self, place, buf, land, rows, send, recv):
        self.p, self.buf, self.land = place, buf, land
        self.n, self.send, self.recv = rows, send, recv

    def part(self, z, half):
        z = (z + 2 * ZR) % ZR
        if half is None:
            return rows_of(self.buf, z * self.n, self.n, self.n)
        n = self.n // 2
        return rows_of(self.buf, z * self.n + half * n, n, n)

    def slot(self, way, hop):
        if hop == 1:
            return self.land.at[way, 0, pl.ds(0, self.n // 2), :]
        return self.land.at[way, hop - 1]

    def copies(self, hop):
        half = (0, 1) if hop == 1 else (None, None)
        up = self.part(self.p.z + 5 - hop, half[0])
        down = self.part(self.p.z - 5 + hop, half[1])
        return (
            remote(up, self.slot(0, hop), self.send.at[0, hop - 1], self.recv.at[0, hop - 1], self.p.zp),
            remote(down, self.slot(1, hop), self.send.at[1, hop - 1], self.recv.at[1, hop - 1], self.p.zm),
        )

    def start(self, hop):
        for copy in self.copies(hop):
            copy.start()

    def take(self, hop):
        for copy in self.copies(hop):
            copy.wait_recv()

    def add(self, hop):
        half = (0, 1) if hop == 1 else (None, None)
        for way, z in ((0, self.p.z + 4 - hop), (1, self.p.z - 4 + hop)):
            ref = self.part(z, half[way])
            ref[...] = (ref[...].astype(F32) + self.slot(way, hop)[...].astype(F32)).astype(BF16)

    def drain(self):
        for hop in range(1, 5):
            for copy in self.copies(hop):
                copy.wait_send()


def gain_row(ref):
    return ref[...].astype(F32).reshape(1, -1)


def normed_rows(act, gain):
    values = act.astype(F32)
    return (values * rms_scale(values) * gain).astype(BF16)


def gated(gate_val, up_val):
    return (jax.nn.silu(gate_val) * up_val).astype(BF16)


def at_step(i, step):
    return pl.when(i == step)


def split_rows(row):
    high = row.astype(BF16).astype(F32)
    rest = row - high
    mid = rest.astype(BF16).astype(F32)
    low = rest - mid
    index = lax.broadcasted_iota(jnp.int32, (8, row.shape[1]), 0)
    out = jnp.where(index == 0, high, jnp.where(index == 1, mid, jnp.where(index == 2, low, 0.0)))
    return out.astype(BF16)


def unit_scale(vec):
    return lax.rsqrt(jnp.sum(vec * vec, axis=-1, keepdims=True) + EPS)


def unit_back(vec, scales, upstream):
    inner = jnp.sum(vec * upstream, axis=-1, keepdims=True)
    return scales * upstream - vec * (scales * scales * scales) * inner


def contrast(query_hat, item_hat, ranks, positive):
    logits = dot(query_hat, item_hat, ((1,), (1,)), HIGH) / TAU
    shifted = logits - 1.0 / TAU
    log_student = shifted - jnp.log(jnp.sum(jnp.exp(shifted), axis=1, keepdims=True))
    teach = -ranks.astype(F32) / TEACH
    log_teacher = teach - jnp.log(jnp.sum(jnp.exp(teach), axis=1, keepdims=True))
    teacher = jnp.exp(log_teacher)
    columns = lax.broadcasted_iota(jnp.int32, logits.shape, 1)
    onehot = (columns == positive).astype(F32)
    per_row = jnp.sum(
        teacher * (log_teacher - log_student) - onehot * log_student, axis=1, keepdims=True
    )
    slopes = 2.0 * jnp.exp(log_student) - onehot - teacher
    return (per_row, slopes)


def grad_rows(resid, scales, gain, upstream):
    along = gain * upstream
    inner = jnp.mean(along * resid, axis=-1, keepdims=True)
    return (scales * along - resid * (scales * scales * scales) * inner).astype(BF16)


def by_tower(values, parts, tower):
    wide = values.shape[1] // parts
    blocks = [values[:, d * wide : (d + 1) * wide] for d in range(tower, parts, 2)]
    return jnp.concatenate(blocks, axis=1)


def kernel(
    qa, qg, gate_hbm, up_hbm, down_hbm, ia, ig, ig_w, iu_w, id_w, qf, if_, proj_hbm, ranks, positive,
    loss, q_out, i_out,
    w, proj, nq, part, gate_val, h2, pm, r1, r2, zs, zin, ni, wi, ip, land, hq, hi,
    sums, hats, scal, yq, hw, yi, gq, gi, qc1, qb1, qb2, qc, ic1, ib1, ib2, ic,
    loads, gs, gr, ss, sr, ws, wr, vs, vr, hs, hr, ias, iar, irs, irr,
    s1, s2, s3, ys, yr, iys, iyr, qs, qv, bs, bv,
):
    p = Place()
    n, dq = qa.shape
    m, di = ia.shape
    f, k = down_hbm.shape[0], id_w.shape[0]
    group = X * n
    parts = X * ZL
    count = hats.shape[0]
    block_wide = dq // count
    piece = w.shape[2] // 4
    wide, thin = dq // 2, dq // 4
    dp = lax.axis_index("dp")
    own = dp * 2 + p.w
    y, c = dp // 2, dp % 2
    yp, ym, y2 = (y + 1) % 4, (y + 3) % 4, (y + 2) % 4
    line_y = (y2, yp, ym, y)
    to_yp, to_ym, to_core = {"dp": yp * 2 + c}, {"dp": ym * 2 + c}, {"dp": y * 2 + 1 - c}
    to_y = (to_yp, to_ym)
    to_tower = {"tower": 1 - p.w}
    a2 = (p.a + 2) % ZL
    mate = p.a + 1 - 2 * (p.a % 2)
    to_a2, to_mate = p.column(a2), p.column(mate)

    def member(step):
        return {"tensor": (p.t + step) % parts}

    def replica(step):
        other = (own + step) % count
        return {"dp": other // 2, "tower": other % 2}

    own_weights = [
        pltpu.make_async_copy(ref, w.at[0, index, pl.ds(0, f), :], loads.at[index])
        for index, ref in enumerate((gate_hbm, up_hbm, down_hbm))
    ]
    proj_copy = pltpu.make_async_copy(proj_hbm, proj, loads.at[3])
    for copy in own_weights:
        copy.start()
    proj_copy.start()
    barrier = pltpu.get_barrier_semaphore()

    def greet(step, _):
        pl.semaphore_signal(barrier, inc=1, device_id=member(step), device_id_type=MESH)
        pl.semaphore_signal(barrier, inc=1, device_id=replica(step), device_id_type=MESH)
        return 0

    lax.fori_loop(1, parts, greet, 0)
    for where in (p.zp, p.zm):
        pl.semaphore_signal(barrier, inc=1, device_id=where, device_id_type=MESH)
    for index in range(3):
        w[0, index, f:, :] = jnp.zeros((w.shape[2] - f, dq), BF16)
    nq[pl.ds(pl.multiple_of(p.b * n, n), n), :] = normed_rows(qa[...], gain_row(qg))
    ni[pl.ds(pl.multiple_of(p.z * m, m), m), :] = normed_rows(ia[...], gain_row(ig))
    for index, ref in enumerate((ig_w, iu_w, id_w)):
        wi[index, pl.ds(pl.multiple_of(p.b * k, k), k), :] = ref[...]
    pl.semaphore_wait(barrier, 2 * (parts - 1) + 2)

    rows = RowGather(p, nq, n, gs, gr)
    items = RingGather(p, ni, m, ias, iar)
    isum = RingSum(p, ip, land, m, irs, irr)

    def across():
        return remote(rows.block(0, p.b), rows.block(1, p.b), gs.at[0], gr.at[0, 0], to_a2)

    def wpiece(which, index, line, core):
        first = pl.multiple_of(line * piece, piece)
        return w.at[which, index, pl.ds(first, piece), pl.ds(pl.multiple_of(core * wide, wide), wide)]

    def whalf(index, line, part_of):
        first = pl.multiple_of(line * piece, piece)
        column = pl.multiple_of(c * wide + part_of * thin, thin)
        return w.at[1, index, pl.ds(first, piece), pl.ds(column, thin)]

    def w_send(index, kind):
        here = wpiece(1, index, y, c)
        low, high = wpiece(1, index, ym, c), wpiece(1, index, yp, c)
        src, dst, where = (
            (wpiece(0, index, y, c), here, to_mate),
            (here, here, to_yp),
            (here, here, to_ym),
            (whalf(index, ym, 0), whalf(index, ym, 0), to_yp),
            (whalf(index, yp, 1), whalf(index, yp, 1), to_ym),
            (here, here, to_core),
            (low, low, to_core),
            (high, high, to_core),
            (wpiece(1, index, y2, c), wpiece(1, index, y2, c), to_core),
        )[kind]
        return remote(src, dst, ws.at[kind, index], wr.at[kind, index], where)

    def w_got(index, kind):
        dst = (
            wpiece(1, index, y, c),
            wpiece(1, index, ym, c),
            wpiece(1, index, yp, c),
            whalf(index, y2, 0),
            whalf(index, y2, 1),
            wpiece(1, index, y, 1 - c),
            wpiece(1, index, ym, 1 - c),
            wpiece(1, index, yp, 1 - c),
            wpiece(1, index, y2, 1 - c),
        )[kind]
        remote(dst, dst, ws.at[kind, index], wr.at[kind, index], to_core).wait_recv()

    def w_near(index):
        w_got(index, 0)
        for kind in (1, 2, 5) if index == 2 else (1, 2):
            w_send(index, kind).start()

    def w_onward(index):
        src, where = ((wpiece(1, index, ym, c), to_yp), (wpiece(1, index, yp, c), to_ym))[index]
        return remote(src, src, ws.at[3, index], wr.at[3, index], where)

    def w_column(index, core):
        ref = w.at[1, index, :, pl.ds(pl.multiple_of(core * wide, wide), wide)]
        return remote(ref, ref, ws.at[8, index], wr.at[8, index], to_core)

    def w_ring(index):
        if index < 2:
            w_got(index, 1 + index)
            w_onward(index).start()
            w_got(index, 2 - index)
        else:
            w_got(index, 1)
            w_send(index, 3).start()
            w_send(index, 6).start()
            w_got(index, 2)
            w_send(index, 4).start()
            w_send(index, 7).start()

    def w_far(index):
        if index < 2:
            ref = wpiece(1, index, y2, c)
            remote(ref, ref, ws.at[3, index], wr.at[3, index], to_core).wait_recv()
            w_column(index, c).start()
        else:
            w_got(index, 3)
            w_got(index, 4)
            w_send(index, 8).start()

    def w_done(index):
        if index < 2:
            w_column(index, 1 - c).wait_recv()
        else:
            for kind in (5, 6, 7, 8):
                w_got(index, kind)

    def w_drain():
        for index in range(2):
            for kind in (0, 1, 2):
                w_send(index, kind).wait_send()
            w_onward(index).wait_send()
            w_column(index, c).wait_send()
        for kind in range(9):
            w_send(2, kind).wait_send()

    def vpiece(b, core):
        column = pl.multiple_of(core * (di // 2), di // 2)
        return wi.at[:, pl.ds(pl.multiple_of(b * k, k), k), pl.ds(column, di // 2)]

    def vhalf(b, part_of):
        first = pl.multiple_of(b * k + part_of * (k // 2), k // 2)
        column = pl.multiple_of(c * (di // 2), di // 2)
        return wi.at[:, pl.ds(first, k // 2), pl.ds(column, di // 2)]

    def v_send(kind):
        ref, where = (
            (vpiece(p.b, c), p.xp),
            (vpiece(p.b, c), p.xm),
            (vhalf(p.bm, 0), p.xp),
            (vhalf(p.bp, 1), p.xm),
            (vpiece(p.bm, c), to_core),
            (vpiece(p.bp, c), to_core),
            (vpiece(p.bo, c), to_core),
        )[kind]
        return remote(ref, ref, vs.at[kind], vr.at[kind], where)

    def v_got(kind):
        ref = (
            vpiece(p.bm, c),
            vpiece(p.bp, c),
            vhalf(p.bo, 0),
            vhalf(p.bo, 1),
            vpiece(p.bm, 1 - c),
            vpiece(p.bp, 1 - c),
            vpiece(p.bo, 1 - c),
        )[kind]
        remote(ref, ref, vs.at[kind], vr.at[kind], to_core).wait_recv()

    def block(j, q, b):
        return rows_of(pm.at[q], (j * X + b) * n, n, n)

    def first(j, q):
        where = (p.xp, p.xm)[(j + q) % 2]
        return remote(block(j, q, p.bo), r1.at[j, q], ss.at[0, j, q], sr.at[0, j, q], where)

    def second(j, q, way):
        src = block(j, q, (p.bp, p.bm)[way])
        where = (p.xp, p.xm)[way]
        return remote(src, r2.at[way, j, q], ss.at[2 + way, j, q], sr.at[2 + way, j, q], where)

    def to_owner(q):
        return remote(zs.at[q], zin.at[q], ss.at[4, 0, q], sr.at[4, 0, q], to_a2)

    def back(j):
        s = (p.a, a2)[j]
        dst = hq.at[pl.ds(pl.multiple_of(s * group, group), group), :]
        return remote(h2.at[j], dst, hs.at[j], hr.at[j], to_mate)

    def back_got(j):
        other = (mate, (mate + 2) % ZL)[j]
        dst = hq.at[pl.ds(pl.multiple_of(other * group, group), group), :]
        remote(h2.at[j], dst, hs.at[j], hr.at[j], to_mate).wait_recv()

    def rows_in(j):
        return nq[j * group : (j + 1) * group, :]

    def own_units(j):
        left = rows_in(j)
        value = gated(
            dot(left, w[0, 0, :f, :], ((1,), (1,))), dot(left, w[0, 1, :f, :], ((1,), (1,)))
        )
        hq[pl.ds(pl.multiple_of((p.a, a2)[j] * group, group), group), :] = value
        part[j] = dot(value, w[0, 2, :f, :])

    def mate_gate(j):
        gate_val[j] = dot(rows_in(j), w[1, 0, :f, :], ((1,), (1,)))

    def mate_up(j):
        h2[j] = gated(gate_val[j], dot(rows_in(j), w[1, 1, :f, :], ((1,), (1,))))
        back(j).start()

    def mate_down(j, q):
        columns = slice(q * wide, (q + 1) * wide)
        total = part[j, :, columns] + dot(h2[j], w[1, 2, :f, columns])
        pm[q, j * group : (j + 1) * group, :] = total.astype(BF16)
        first(j, q).start()
        second(j, q, 1 - (j + q) % 2).start()

    def combine(j, q):
        way = (j + q) % 2
        first(j, q).wait_recv()
        ref = block(j, q, (p.bp, p.bm)[way])
        ref[...] = (ref[...].astype(F32) + r1[j, q].astype(F32)).astype(BF16)
        second(j, q, way).start()

    def summed(j, q):
        second(j, q, 0).wait_recv()
        second(j, q, 1).wait_recv()
        total = block(j, q, p.b)[...].astype(F32)
        return total + r2[0, j, q].astype(F32) + r2[1, j, q].astype(F32)

    def send_sum(q):
        zs[q] = summed(1, q).astype(BF16)
        to_owner(q).start()

    def item_hop(hop):
        items.take(hop)
        if hop < 4:
            items.start(hop + 1)

    def isum_hop(hop):
        isum.take(hop)
        isum.add(hop)
        isum.start(hop + 1)

    def item_product():
        left = ni[...]
        partial = 0.0
        for b in range(X):
            here = slice(b * k, (b + 1) * k)
            value = gated(
                dot(left, wi[0, here, :], ((1,), (1,))), dot(left, wi[1, here, :], ((1,), (1,)))
            )
            hi[b] = value
            partial = partial + dot(value, wi[2, here, :])
        ip[...] = partial.astype(BF16)
        isum.start(1)

    rows.right(0).start()
    rows.left(0).start()
    items.start(1)
    own_weights[0].wait()
    w_send(0, 0).start()
    across().start()
    v_send(0).start()
    v_send(1).start()
    own_weights[1].wait()
    own_weights[2].wait()
    rows.take_x(0, 0)
    item_hop(1)
    w_near(0)
    w_send(1, 0).start()
    rows.take_far(0)
    own_units(0)
    remote(rows.block(0, p.b), rows.block(1, p.b), gs.at[0], gr.at[0, 0], to_a2).wait_recv()
    rows.right(1).start()
    rows.left(1).start()
    item_hop(2)
    w_ring(0)
    w_near(1)
    w_send(2, 0).start()
    for kind in range(2):
        v_got(kind)
        v_send(2 + kind).start()
        v_send(4 + kind).start()
    item_hop(3)
    w_far(0)
    rows.take_x(1, 1)
    v_got(2)
    v_got(3)
    v_send(6).start()
    w_ring(1)
    item_hop(4)
    for kind in (4, 5, 6):
        v_got(kind)
    w_near(2)
    item_product()
    w_far(1)
    w_done(0)
    mate_gate(0)
    rows.take_far(1)
    mate_gate(1)
    isum_hop(1)
    w_ring(2)
    own_units(1)
    w_done(1)
    mate_up(1)
    isum_hop(2)
    w_far(2)
    mate_up(0)
    w_done(2)
    mate_down(1, 0)
    mate_down(1, 1)
    combine(1, 0)
    mate_down(0, 0)
    combine(1, 1)
    mate_down(0, 1)
    isum_hop(3)
    send_sum(0)
    combine(0, 0)
    send_sum(1)
    combine(0, 1)
    isum.take(4)
    own_item = ip[pl.ds(pl.multiple_of(p.z * m, m), m), :].astype(F32)
    i_resid = ia[...].astype(F32) + (own_item + land[0, 3].astype(F32) + land[1, 3].astype(F32))
    mlp = []
    for q in range(2):
        total = summed(0, q)
        to_owner(q).wait_recv()
        mlp.append(total + zin[q].astype(F32))
    q_resid = qa[...].astype(F32) + jnp.concatenate(mlp, axis=1)

    q_gain, i_gain = gain_row(qf), gain_row(if_)
    q_scale, i_scale = rms_scale(q_resid), rms_scale(i_resid)
    sums[p.t, :, :dq] = jnp.sum(q_resid * q_scale * q_gain, axis=0, keepdims=True)
    sums[p.t, :, dq:] = jnp.sum(i_resid * i_scale * i_gain, axis=0, keepdims=True)

    def spread(buf, mine, sems, partner):
        def each(hop, _):
            remote(buf.at[mine], buf.at[mine], sems.at[0], sems.at[1], partner(hop)).start()
            return 0

        lax.fori_loop(1, buf.shape[0], each, 0)

    def gathered(buf, sems):
        ref = buf.at[pl.ds(0, buf.shape[0] - 1)]
        remote(ref, ref, sems.at[0], sems.at[1], member(1)).wait()

    def q_rows(tower, line_of, core):
        return rows_of(gq.at[tower], (line_of * 2 + core) * block_wide, block_wide, block_wide)

    def q_half(tower, line_of, way):
        first = (line_of * 2 + c) * block_wide + way * (block_wide // 2)
        return rows_of(gq.at[tower], first, block_wide // 2, block_wide // 2)

    def q_core(tower, j):
        src = q_rows(tower, line_y[j], 1 - c)
        return remote(src, qc1.at[tower, j], qs.at[tower, j], qv.at[tower, j], to_core)

    def q_first(tower, way):
        src, dst = q_half(tower, y2, way), qb1.at[tower, way]
        return remote(src, dst, qs.at[tower, 4 + way], qv.at[tower, 4 + way], to_y[way])

    def q_second(tower, way):
        src, dst = q_rows(tower, (yp, ym)[way], c), qb2.at[tower, way]
        return remote(src, dst, qs.at[tower, 6 + way], qv.at[tower, 6 + way], to_y[way])

    def q_tower(tower):
        return remote(q_rows(tower, y, c), qc, qs.at[tower, 8], qv.at[tower, 8], to_tower)

    def q_start(tower):
        for j in range(4):
            q_core(tower, j).start()

    def q_far(tower):
        q_core(tower, 0).wait_recv()
        ref = q_rows(tower, y2, c)
        ref[...] += qc1[tower, 0]
        for way in range(2):
            q_first(tower, way).start()

    def q_near(tower):
        for way in range(2):
            q_core(tower, 1 + way).wait_recv()
            ref = q_rows(tower, (yp, ym)[way], c)
            ref[...] += qc1[tower, 1 + way]
            q_first(tower, way).wait_recv()
            ref = q_half(tower, (yp, ym)[way], way)
            ref[...] += qb1[tower, way]
            q_second(tower, way).start()

    def q_own(tower):
        q_core(tower, 3).wait_recv()
        for way in range(2):
            q_second(tower, way).wait_recv()
        ref = q_rows(tower, y, c)
        ref[...] = ref[...] + qc1[tower, 3] + qb2[tower, 0] + qb2[tower, 1]

        @pl.when(p.w != tower)
        def _():
            q_tower(tower).start()

    def q_finish(tower):
        @pl.when(p.w == tower)
        def _():
            q_tower(tower).wait_recv()
            q_out[...] = q_rows(tower, y, c)[...] + qc[...]

    def i_rows(line_of, core):
        first = pl.multiple_of((line_of * 2 + core) * block_wide, block_wide)
        return gi.at[:, pl.ds(first, block_wide), :]

    def i_half(line_of, way):
        first = pl.multiple_of((line_of * 2 + c) * block_wide, block_wide)
        return gi.at[pl.ds(way * 2, 2), pl.ds(first, block_wide), :]

    def i_slab(b):
        return gi.at[b, pl.ds(pl.multiple_of((y * 2 + c) * block_wide, block_wide), block_wide), :]

    def i_core(j):
        return remote(i_rows(line_y[j], 1 - c), ic1.at[j], bs.at[j], bv.at[j], to_core)

    def i_first(way):
        return remote(i_half(y2, way), ib1.at[way], bs.at[4 + way], bv.at[4 + way], to_y[way])

    def i_second(way):
        src = i_rows((yp, ym)[way], c)
        return remote(src, ib2.at[way], bs.at[6 + way], bv.at[6 + way], to_y[way])

    def i_x(hop):
        other = (p.b + hop) % X
        where = {"tensor": p.a * X + other}
        return remote(i_slab(other), ic.at[p.b], bs.at[8 + hop], bv.at[8 + p.b], where)

    def i_product():
        for b in range(X):
            gi[b] = dot(yi[...], hi[b], ((0,), (0,)))
        for j in range(4):
            i_core(j).start()

    def i_far():
        for j in range(4):
            i_core(j).wait_recv()
            ref = i_rows(line_y[j], c)
            ref[...] += ic1[j]
        for way in range(2):
            i_first(way).start()

    def i_near():
        for way in range(2):
            i_first(way).wait_recv()
            ref = i_half((yp, ym)[way], way)
            ref[...] += ib1[way]
            i_second(way).start()

    def i_own():
        for way in range(2):
            i_second(way).wait_recv()
        ref = i_rows(y, c)
        ref[...] = ref[...] + ib2[0] + ib2[1]
        for hop in range(1, X):
            i_x(hop).start()

    def i_finish():
        total = i_slab(p.b)[...]
        for hop in range(1, X):
            other = (p.b + hop) % X
            remote(i_slab(other), ic.at[other], bs.at[8 + hop], bv.at[8 + other], p.xp).wait_recv()
            total = total + ic[other]
        i_out[...] = total

    gather = [RowGather(p, yq.at[tower], n, ys.at[tower], yr.at[tower]) for tower in range(2)]
    igather = RingGather(p, yi, m, iys, iyr)

    steps = (0, 4, 1, 2, 3, 5, 6, 7)

    def advance(index):
        if index < len(steps):
            g = steps[index]
            gather[g // ZL].take_z(p.order(g % ZL))
        if 0 <= index - 2 < len(steps):
            g = steps[index - 2]
            gather[g // ZL].take_x(p.order(g % ZL), g % 2)

    def item_grad_hop(hop):
        igather.take(hop)
        if hop < 4:
            igather.start(hop + 1)

    def scale_hidden():
        line = lax.broadcasted_iota(jnp.int32, (128, 128), 0)
        tiles = [jnp.zeros((128, 128), F32)] * 2
        for t in range(parts):
            for kind in range(2):
                tiles[kind] = jnp.where(line == t, scal[t, kind : kind + 1, :], tiles[kind])
        scale_of, slope_of = tiles[0].T[:n], tiles[1].T[:n]
        total = jnp.zeros((1, f), F32)
        for t in range(parts):
            here = slice(t * n, (t + 1) * n)
            value = hq[here, :].astype(F32)
            hw[here, :] = (value * slope_of[:, t : t + 1]).astype(BF16)
            total = total + jnp.sum(value * scale_of[:, t : t + 1], axis=0, keepdims=True)
        return total

    def product(tower, part_of):
        total = 0.0
        for j in (2 * part_of, 2 * part_of + 1):
            s = p.order(j)
            gather[tower].take_far(s)
            here = pl.ds(pl.multiple_of(s * group, group), group)
            total = total + dot(yq[tower, here, :], hw[here, :], ((0,), (0,)))
        if part_of == 0:
            column = jnp.broadcast_to(along_of[tower], (128, wide)).T[:, 0:1]
            gq[tower] = column * summed_hidden - total
        else:
            gq[tower] -= total

    spread(sums, p.t, s1, member)
    for tower in range(2):
        here = pl.ds(pl.multiple_of(p.t * n, n), n)
        yq[tower, here, :] = by_tower(q_resid, count, tower).astype(BF16)
    advance(0)
    proj_copy.wait()
    gathered(sums, s1)
    total = sums[0]
    for slot in range(1, parts):
        total = total + sums[slot]
    q_pooled = total[:, :dq] / QLEN
    i_pooled = total[:, dq:] / ILEN
    advance(1)
    q_e = jnp.sum(dot(split_rows(q_pooled), proj[...]), axis=0, keepdims=True)
    q_norm, i_norm = unit_scale(q_e), unit_scale(i_pooled)
    hats[own, :, :di] = q_e * q_norm
    hats[own, :, di:] = i_pooled * i_norm
    spread(hats, own, s2, replica)
    advance(2)
    gathered(hats, s2)
    index = lax.broadcasted_iota(jnp.int32, (count, 2 * di), 0)
    every = jnp.zeros((count, 2 * di), F32)
    for slot in range(count):
        every = jnp.where(index == slot, hats[slot], every)
    every_query, every_items = every[:, :di], every[:, di:]
    line = lax.broadcasted_iota(jnp.int32, (count, count), 0)
    target = jnp.zeros((count, count), jnp.int32)
    for slot in range(count):
        target = jnp.where(line == slot, positive[slot], target)
    per_row, slopes = contrast(every_query, every_items, ranks[...], target)
    loss[...] = jnp.sum(per_row, axis=0, keepdims=True) / count
    weights = slopes * (LOSS_SCALE / (TAU * count))
    advance(3)
    mine = lax.broadcasted_iota(jnp.int32, (count, di), 0) == own
    q_back = jnp.sum(
        jnp.where(mine, dot(weights, every_items, precision=HIGH), 0.0), axis=0, keepdims=True
    )
    column = lax.broadcasted_iota(jnp.int32, (count, count), 1) == own
    i_back = jnp.sum(
        jnp.sum(jnp.where(column, weights, 0.0), axis=1, keepdims=True) * every_query,
        axis=0,
        keepdims=True,
    )
    advance(4)
    q_grad_e = unit_back(q_e, q_norm, q_back)
    q_up = jnp.sum(dot(split_rows(q_grad_e), proj[...], ((1,), (1,))), axis=0, keepdims=True) / QLEN
    i_up = unit_back(i_pooled, i_norm, i_back) / ILEN
    advance(5)
    along = q_gain * q_up
    along_of = [by_tower(along, count, tower) for tower in range(2)]
    inner = jnp.mean(along * q_resid, axis=-1, keepdims=True)
    slope = (q_scale * q_scale * q_scale) * inner
    lane = lax.broadcasted_iota(jnp.int32, (n, 128), 1)
    columns = jnp.where(lane == 0, q_scale, jnp.where(lane == 1, slope, 0.0))
    columns = jnp.concatenate([columns, jnp.zeros((128 - n, 128), F32)], axis=0)
    scal[p.t] = columns.T[:8]
    spread(scal, p.t, s3, member)
    yi[pl.ds(pl.multiple_of(p.z * m, m), m), :] = grad_rows(i_resid, i_scale, i_gain, i_up)
    igather.start(1)
    advance(6)
    gathered(scal, s3)
    back_got(0)
    back_got(1)
    summed_hidden = scale_hidden()
    advance(7)
    item_grad_hop(1)
    product(0, 0)
    advance(8)
    item_grad_hop(2)
    product(0, 1)
    q_start(0)
    advance(9)
    item_grad_hop(3)
    q_far(0)
    product(1, 0)
    item_grad_hop(4)
    q_near(0)
    i_product()
    product(1, 1)
    q_start(1)
    i_far()
    q_far(1)
    q_own(0)
    i_near()
    q_near(1)
    q_finish(0)
    i_own()
    q_own(1)
    i_finish()
    q_finish(1)

    for j in range(2):
        back(j).wait_send()
        for q in range(2):
            first(j, q).wait_send()
            for way in range(2):
                second(j, q, way).wait_send()
    for q in range(2):
        to_owner(q).wait_send()
    across().wait_send()
    rows.drain_x(3, 3)
    items.drain()
    isum.drain()
    w_drain()
    for kind in range(7):
        v_send(kind).wait_send()
    for tower in range(2):
        gather[tower].drain_z()
        gather[tower].drain_x(6, 6)
        for j in range(4):
            q_core(tower, j).wait_send()
        for way in range(2):
            q_first(tower, way).wait_send()
            q_second(tower, way).wait_send()

        @pl.when(p.w != tower)
        def _():
            q_tower(tower).wait_send()

    igather.drain()
    for j in range(4):
        i_core(j).wait_send()
    for way in range(2):
        i_first(way).wait_send()
        i_second(way).wait_send()
    for hop in range(1, X):
        i_x(hop).wait_send()


def step(qa, qg, gate, up, down, ia, ig, ig_w, iu_w, id_w, qf, if_, proj, ranks, positive):
    n, dq = qa.shape
    m, di = ia.shape
    f, k = down.shape[0], id_w.shape[0]
    padded = 64 * ((f + 63) // 64)
    vmem, hbm = pl.BlockSpec(memory_space=pltpu.VMEM), pl.BlockSpec(memory_space=pl.ANY)
    smem = pl.BlockSpec(memory_space=pltpu.SMEM)
    all_i = ZR * m
    group = X * n
    parts = X * ZL
    count = ranks.shape[0]
    wide = dq // count
    dma = pltpu.SemaphoreType.DMA
    return pl.pallas_call(
        kernel,
        out_shape=(
            jax.ShapeDtypeStruct((1, 1), F32),
            jax.ShapeDtypeStruct((wide, f), F32),
            jax.ShapeDtypeStruct((wide, k), F32),
        ),
        in_specs=[vmem, vmem, hbm, hbm, hbm] + [vmem] * 7 + [hbm, vmem, smem],
        out_specs=[vmem] * 3,
        scratch_shapes=[
            pltpu.VMEM((2, 3, padded, dq), BF16),
            pltpu.VMEM(proj.shape, BF16),
            pltpu.VMEM((2 * group, dq), BF16),
            pltpu.VMEM((2, group, dq), F32),
            pltpu.VMEM((2, group, f), F32),
            pltpu.VMEM((2, group, f), BF16),
            pltpu.VMEM((2, 2 * group, dq // 2), BF16),
            pltpu.VMEM((2, 2, n, dq // 2), BF16),
            pltpu.VMEM((2, 2, 2, n, dq // 2), BF16),
            pltpu.VMEM((2, n, dq // 2), BF16),
            pltpu.VMEM((2, n, dq // 2), BF16),
            pltpu.VMEM((all_i, di), BF16),
            pltpu.VMEM((3, X * k, di), BF16),
            pltpu.VMEM((all_i, di), BF16),
            pltpu.VMEM((2, 4, m, di), BF16),
            pltpu.VMEM((ZL * group, f), BF16),
            pltpu.VMEM((X, all_i, k), BF16),
            pltpu.VMEM((parts, 1, dq + di), F32),
            pltpu.VMEM((count, 1, 2 * di), F32),
            pltpu.VMEM((parts, 8, 128), F32),
            pltpu.VMEM((2, parts * n, dq // 2), BF16),
            pltpu.VMEM((ZL * group, f), BF16),
            pltpu.VMEM((all_i, di), BF16),
            pltpu.VMEM((2, dq // 2, f), F32),
            pltpu.VMEM((X, di, k), F32),
            pltpu.VMEM((2, 4, wide, f), F32),
            pltpu.VMEM((2, 2, wide // 2, f), F32),
            pltpu.VMEM((2, 2, wide, f), F32),
            pltpu.VMEM((wide, f), F32),
            pltpu.VMEM((4, X, wide, k), F32),
            pltpu.VMEM((2, 2, wide, k), F32),
            pltpu.VMEM((2, X, wide, k), F32),
            pltpu.VMEM((X, wide, k), F32),
            dma((4,)),
            dma((4,)),
            dma((4, 2)),
            dma((5, 2, 2)),
            dma((5, 2, 2)),
            dma((9, 3)),
            dma((9, 3)),
            dma((7,)),
            dma((7,)),
            dma((2,)),
            dma((2,)),
            dma((2, 4)),
            dma((2, 4)),
            dma((2, 4)),
            dma((2, 4)),
            dma((2,)),
            dma((2,)),
            dma((2,)),
            dma((2, 4)),
            dma((2, 4, ZL)),
            dma((2, 4)),
            dma((2, 4)),
            dma((2, 9)),
            dma((2, 9)),
            dma((12,)),
            dma((12,)),
        ],
        compiler_params=pltpu.CompilerParams(
            collective_id=0, has_side_effects=True, vmem_limit_bytes=VMEM_LIMIT
        ),
        name="towers_step",
    )(qa, qg, gate, up, down, ia, ig, ig_w, iu_w, id_w, qf, if_, proj, ranks, positive)


def body(
    q_act,
    q_norm_gain,
    q_gate,
    q_up,
    q_down,
    q_final_gain,
    projection,
    i_act,
    i_norm_gain,
    i_gate,
    i_up,
    i_down,
    i_final_gain,
    ranks,
    positive,
):
    loss, q_grad, i_grad = step(
        q_act,
        q_norm_gain,
        q_gate.T,
        q_up.T,
        q_down,
        i_act,
        i_norm_gain,
        i_gate.T,
        i_up.T,
        i_down,
        q_final_gain,
        i_final_gain,
        projection,
        ranks,
        positive,
    )
    return (loss.reshape(()), q_grad.T, i_grad.T)


def solution(mesh):
    in_specs = (
        P(("dp", "tower", "tensor"), None),
        P(),
        P(None, "tensor"),
        P(None, "tensor"),
        P("tensor", None),
        P(),
        P(),
        P(("dp", "tower", "tensor"), None),
        P(),
        P(None, ("tower", "tensor")),
        P(None, ("tower", "tensor")),
        P(("tower", "tensor"), None),
        P(),
        P(),
        P(),
    )
    out_specs = (P(), P("tensor", ("dp", "tower")), P(("tower", "tensor"), "dp"))
    return jax.shard_map(body, mesh=mesh, in_specs=in_specs, out_specs=out_specs, check_vma=False)
```

```python
import functools

import jax
import jax.numpy as jnp
from jax import lax
from jax.experimental import pallas as pl
from jax.experimental.pallas import tpu as pltpu
from jax.sharding import PartitionSpec as P

QLEN = 1536
ILEN = 512
EPS = 1e-06
TAU = 0.05
TEACH = 2.0
LOSS_SCALE = 64.0
HIGH = lax.Precision.HIGHEST
MESH = pl.DeviceIdType.MESH
F32 = jnp.float32
BF16 = jnp.bfloat16

X = 4
ZL = 4
ZR = 8
VMEM_LIMIT = 60 * 1024 * 1024


def rms_scale(values):
    return lax.rsqrt(jnp.mean(values * values, axis=-1, keepdims=True) + EPS)


def dot(left, right, dims=((1,), (0,)), precision=None):
    return lax.dot_general(
        left, right, (dims, ((), ())), preferred_element_type=F32, precision=precision
    )


def remote(src, dst, send, recv, where):
    return pltpu.make_async_remote_copy(
        src_ref=src, dst_ref=dst, send_sem=send, recv_sem=recv, device_id=where, device_id_type=MESH
    )


class Place:
    def __init__(self):
        self.t = lax.axis_index("tensor")
        self.w = lax.axis_index("tower")
        self.a = self.t // X
        self.b = self.t % X
        self.z = self.w * ZL + self.a
        self.bp = (self.b + 1) % X
        self.bm = (self.b + X - 1) % X
        self.bo = (self.b + 2) % X
        self.xp = {"tensor": self.a * X + self.bp}
        self.xm = {"tensor": self.a * X + self.bm}
        self.zp = self.ring(1)
        self.zm = self.ring(ZR - 1)

    def ring(self, step):
        z = (self.z + step) % ZR
        return {"tower": z // ZL, "tensor": (z % ZL) * X + self.b}

    def column(self, row):
        return {"tensor": row * X + self.b}

    def order(self, j):
        near = jnp.minimum(self.a, ZL - 1 - self.a)
        swapped = jnp.where(j == 0, 1, jnp.where(j == 1, 0, j))
        row = jnp.where(near == 1, swapped, j)
        return jnp.where(self.a >= 2, ZL - 1 - row, row)


def rows_of(ref, first, count, unit):
    return ref.at[pl.ds(pl.multiple_of(first, unit), count), :]


class RowGather:
    def __init__(self, place, buf, rows, send, recv):
        self.p, self.buf, self.n, self.send, self.recv = place, buf, rows, send, recv

    def block(self, s, b):
        return rows_of(self.buf, (s * X + b) * self.n, self.n, self.n)

    def half(self, s, b, h):
        n = self.n // 2
        return rows_of(self.buf, (s * X + b) * self.n + h * n, n, n)

    def up(self, s):
        ref = self.block(s, self.p.b)
        where = self.p.column(jnp.minimum(self.p.a + 1, ZL - 1))
        return remote(ref, ref, self.send.at[0, s], self.recv.at[0, s], where)

    def down(self, s):
        ref = self.block(s, self.p.b)
        where = self.p.column(jnp.maximum(self.p.a - 1, 0))
        return remote(ref, ref, self.send.at[1, s], self.recv.at[0, s], where)

    def right(self, s):
        ref = self.block(s, self.p.b)
        return remote(ref, ref, self.send.at[2, s], self.recv.at[1, s], self.p.xp)

    def left(self, s):
        ref = self.block(s, self.p.b)
        return remote(ref, ref, self.send.at[3, s], self.recv.at[2, s], self.p.xm)

    def half_right(self, s):
        ref = self.half(s, self.p.bm, 0)
        return remote(ref, ref, self.send.at[4, s], self.recv.at[3, s], self.p.xp)

    def half_left(self, s):
        ref = self.half(s, self.p.bp, 1)
        return remote(ref, ref, self.send.at[5, s], self.recv.at[4, s], self.p.xm)

    def goes_up(self, s):
        return (s <= self.p.a) & (self.p.a < ZL - 1)

    def goes_down(self, s):
        return (s >= self.p.a) & (self.p.a > 0)

    def take_z(self, s):
        @pl.when(s != self.p.a)
        def _():
            self.up(s).wait_recv()

        @pl.when(self.goes_up(s))
        def _():
            self.up(s).start()

        @pl.when(self.goes_down(s))
        def _():
            self.down(s).start()

        self.right(s).start()
        self.left(s).start()

    def take_x(self, s):
        ref = self.block(s, self.p.bm)
        remote(ref, ref, self.send.at[2, s], self.recv.at[1, s], self.p.xm).wait_recv()
        self.half_right(s).start()
        ref = self.block(s, self.p.bp)
        remote(ref, ref, self.send.at[3, s], self.recv.at[2, s], self.p.xp).wait_recv()
        self.half_left(s).start()

    def take_halves(self, s):
        ref = self.half(s, self.p.bo, 0)
        remote(ref, ref, self.send.at[4, s], self.recv.at[3, s], self.p.xm).wait_recv()
        ref = self.half(s, self.p.bo, 1)
        remote(ref, ref, self.send.at[5, s], self.recv.at[4, s], self.p.xp).wait_recv()

    def drain(self):
        def each(s, _):
            @pl.when(self.goes_up(s))
            def _():
                self.up(s).wait_send()

            @pl.when(self.goes_down(s))
            def _():
                self.down(s).wait_send()

            self.right(s).wait_send()
            self.left(s).wait_send()
            self.half_right(s).wait_send()
            self.half_left(s).wait_send()
            return 0

        lax.fori_loop(0, ZL, each, 0)


class RingGather:
    def __init__(self, place, buf, rows, send, recv):
        self.p, self.buf, self.n, self.send, self.recv = place, buf, rows, send, recv

    def ref(self, z, hop, upward):
        z = (z + 2 * ZR) % ZR
        if hop < 4:
            return rows_of(self.buf, z * self.n, self.n, self.n)
        n = self.n // 2
        return rows_of(self.buf, z * self.n + (0 if upward else n), n, n)

    def copies(self, hop):
        up = self.ref(self.p.z - hop + 1, hop, True)
        down = self.ref(self.p.z + hop - 1, hop, False)
        return (
            remote(up, up, self.send.at[0, hop - 1], self.recv.at[0, hop - 1], self.p.zp),
            remote(down, down, self.send.at[1, hop - 1], self.recv.at[1, hop - 1], self.p.zm),
        )

    def start(self, hop):
        for copy in self.copies(hop):
            copy.start()

    def take(self, hop):
        up = self.ref(self.p.z - hop, hop, True)
        down = self.ref(self.p.z + hop, hop, False)
        remote(up, up, self.send.at[0, hop - 1], self.recv.at[0, hop - 1], self.p.zm).wait_recv()
        remote(down, down, self.send.at[1, hop - 1], self.recv.at[1, hop - 1], self.p.zp).wait_recv()

    def drain(self):
        for hop in range(1, 5):
            for copy in self.copies(hop):
                copy.wait_send()


class RingSum:
    def __init__(self, place, buf, land, rows, send, recv):
        self.p, self.buf, self.land = place, buf, land
        self.n, self.send, self.recv = rows, send, recv

    def part(self, z, half):
        z = (z + 2 * ZR) % ZR
        if half is None:
            return rows_of(self.buf, z * self.n, self.n, self.n)
        n = self.n // 2
        return rows_of(self.buf, z * self.n + half * n, n, n)

    def slot(self, way, hop):
        if hop == 1:
            return self.land.at[way, 0, pl.ds(0, self.n // 2), :]
        return self.land.at[way, hop - 1]

    def copies(self, hop):
        half = (0, 1) if hop == 1 else (None, None)
        up = self.part(self.p.z + 5 - hop, half[0])
        down = self.part(self.p.z - 5 + hop, half[1])
        return (
            remote(up, self.slot(0, hop), self.send.at[0, hop - 1], self.recv.at[0, hop - 1], self.p.zp),
            remote(down, self.slot(1, hop), self.send.at[1, hop - 1], self.recv.at[1, hop - 1], self.p.zm),
        )

    def start(self, hop):
        for copy in self.copies(hop):
            copy.start()

    def take(self, hop):
        for copy in self.copies(hop):
            copy.wait_recv()

    def add(self, hop):
        half = (0, 1) if hop == 1 else (None, None)
        for way, z in ((0, self.p.z + 4 - hop), (1, self.p.z - 4 + hop)):
            ref = self.part(z, half[way])
            ref[...] = (ref[...].astype(F32) + self.slot(way, hop)[...].astype(F32)).astype(BF16)

    def drain(self):
        for hop in range(1, 5):
            for copy in self.copies(hop):
                copy.wait_send()


def gain_row(ref):
    return ref[...].astype(F32).reshape(1, -1)


def normed_rows(act, gain):
    values = act.astype(F32)
    return (values * rms_scale(values) * gain).astype(BF16)


def gated(gate_val, up_val):
    return (jax.nn.silu(gate_val) * up_val).astype(BF16)


def at_step(i, step):
    return pl.when(i == step)


def split_rows(row):
    high = row.astype(BF16).astype(F32)
    rest = row - high
    mid = rest.astype(BF16).astype(F32)
    low = rest - mid
    index = lax.broadcasted_iota(jnp.int32, (8, row.shape[1]), 0)
    out = jnp.where(index == 0, high, jnp.where(index == 1, mid, jnp.where(index == 2, low, 0.0)))
    return out.astype(BF16)


def unit_scale(vec):
    return lax.rsqrt(jnp.sum(vec * vec, axis=-1, keepdims=True) + EPS)


def unit_back(vec, scales, upstream):
    inner = jnp.sum(vec * upstream, axis=-1, keepdims=True)
    return scales * upstream - vec * (scales * scales * scales) * inner


def contrast(query_hat, item_hat, ranks, positive):
    logits = dot(query_hat, item_hat, ((1,), (1,)), HIGH) / TAU
    shifted = logits - 1.0 / TAU
    log_student = shifted - jnp.log(jnp.sum(jnp.exp(shifted), axis=1, keepdims=True))
    teach = -ranks.astype(F32) / TEACH
    log_teacher = teach - jnp.log(jnp.sum(jnp.exp(teach), axis=1, keepdims=True))
    teacher = jnp.exp(log_teacher)
    columns = lax.broadcasted_iota(jnp.int32, logits.shape, 1)
    onehot = (columns == positive).astype(F32)
    per_row = jnp.sum(
        teacher * (log_teacher - log_student) - onehot * log_student, axis=1, keepdims=True
    )
    slopes = 2.0 * jnp.exp(log_student) - onehot - teacher
    return (per_row, slopes)


def grad_rows(resid, scales, gain, upstream):
    along = gain * upstream
    inner = jnp.mean(along * resid, axis=-1, keepdims=True)
    return (scales * along - resid * (scales * scales * scales) * inner).astype(BF16)


def by_tower(values, parts, tower):
    wide = values.shape[1] // parts
    blocks = [values[:, d * wide : (d + 1) * wide] for d in range(tower, parts, 2)]
    return jnp.concatenate(blocks, axis=1)


def kernel(
    qa, qg, gate_hbm, up_hbm, down_hbm, ia, ig, ig_w, iu_w, id_w, qf, if_, proj_hbm, ranks, positive,
    loss, q_out, i_out,
    w, stage, proj, nq, part, gate_val, h2, pm, r1, r2, zs, zin, ni, wi, ip, land, hq, hi,
    sums, hats, scal, yq, hw, yi, gq, gi, qc1, qb1, qb2, qc, ic1, ib1, ib2, ic,
    loads, gs, gr, ss, sr, ws, wr, vs, vr, hs, hr, ias, iar, irs, irr,
    s1, s2, s3, ys, yr, iys, iyr, qs, qv, bs, bv,
):
    p = Place()
    n, dq = qa.shape
    m, di = ia.shape
    f, k = down_hbm.shape[0], id_w.shape[0]
    group = X * n
    h = n // 2
    parts = X * ZL
    count = hats.shape[0]
    block_wide = dq // count
    piece = w.shape[2] // 4
    wide, thin = dq // 2, dq // 4
    dp = lax.axis_index("dp")
    own = dp * 2 + p.w
    y, c = dp // 2, dp % 2
    yp, ym, y2 = (y + 1) % 4, (y + 3) % 4, (y + 2) % 4
    line_y = (y2, yp, ym, y)
    to_yp, to_ym, to_core = {"dp": yp * 2 + c}, {"dp": ym * 2 + c}, {"dp": y * 2 + 1 - c}
    to_y = (to_yp, to_ym)
    to_tower = {"tower": 1 - p.w}
    a2 = (p.a + 2) % ZL
    mate = p.a + 1 - 2 * (p.a % 2)
    to_a2, to_mate = p.column(a2), p.column(mate)

    def member(step):
        return {"tensor": (p.t + step) % parts}

    def replica(step):
        other = (own + step) % count
        return {"dp": other // 2, "tower": other % 2}

    own_weights = [
        pltpu.make_async_copy(ref, dst, loads.at[index])
        for index, (ref, dst) in enumerate(
            (
                (gate_hbm, w.at[0, 0, pl.ds(0, f), :]),
                (up_hbm, w.at[0, 1, pl.ds(0, f), :]),
                (down_hbm, stage),
            )
        )
    ]
    proj_copy = pltpu.make_async_copy(proj_hbm, proj, loads.at[3])
    for copy in own_weights:
        copy.start()
    proj_copy.start()
    barrier = pltpu.get_barrier_semaphore()

    def greet(step, _):
        pl.semaphore_signal(barrier, inc=1, device_id=member(step), device_id_type=MESH)
        pl.semaphore_signal(barrier, inc=1, device_id=replica(step), device_id_type=MESH)
        return 0

    lax.fori_loop(1, parts, greet, 0)
    for where in (p.zp, p.zm):
        pl.semaphore_signal(barrier, inc=1, device_id=where, device_id_type=MESH)
    for index in range(3):
        w[0, index, f:, :] = jnp.zeros((w.shape[2] - f, dq), BF16)
    nq[pl.ds(pl.multiple_of(p.b * n, n), n), :] = normed_rows(qa[...], gain_row(qg))
    ni[pl.ds(pl.multiple_of(p.z * m, m), m), :] = normed_rows(ia[...], gain_row(ig))
    for index, ref in enumerate((ig_w, iu_w, id_w)):
        wi[index, pl.ds(pl.multiple_of(p.b * k, k), k), :] = ref[...]
    pl.semaphore_wait(barrier, 2 * (parts - 1) + 2)

    rows = RowGather(p, nq, n, gs, gr)
    items = RingGather(p, ni, m, ias, iar)
    isum = RingSum(p, ip, land, m, irs, irr)

    def across():
        return remote(rows.block(0, p.b), rows.block(1, p.b), gs.at[0, 0], gr.at[0, 0], to_a2)

    def wpiece(which, index, line, core):
        first = pl.multiple_of(line * piece, piece)
        return w.at[which, index, pl.ds(first, piece), pl.ds(pl.multiple_of(core * wide, wide), wide)]

    def whalf(index, line, part_of):
        first = pl.multiple_of(line * piece, piece)
        column = pl.multiple_of(c * wide + part_of * thin, thin)
        return w.at[1, index, pl.ds(first, piece), pl.ds(column, thin)]

    def w_send(index, kind):
        here = wpiece(1, index, y, c)
        low, high = wpiece(1, index, ym, c), wpiece(1, index, yp, c)
        src, dst, where = (
            (wpiece(0, index, y, c), here, to_mate),
            (here, here, to_yp),
            (here, here, to_ym),
            (whalf(index, ym, 0), whalf(index, ym, 0), to_yp),
            (whalf(index, yp, 1), whalf(index, yp, 1), to_ym),
            (here, here, to_core),
            (low, low, to_core),
            (high, high, to_core),
            (wpiece(1, index, y2, c), wpiece(1, index, y2, c), to_core),
        )[kind]
        return remote(src, dst, ws.at[kind, index], wr.at[kind, index], where)

    def w_got(index, kind):
        dst = (
            wpiece(1, index, y, c),
            wpiece(1, index, ym, c),
            wpiece(1, index, yp, c),
            whalf(index, y2, 0),
            whalf(index, y2, 1),
            wpiece(1, index, y, 1 - c),
            wpiece(1, index, ym, 1 - c),
            wpiece(1, index, yp, 1 - c),
            wpiece(1, index, y2, 1 - c),
        )[kind]
        remote(dst, dst, ws.at[kind, index], wr.at[kind, index], to_core).wait_recv()

    def w_near(index):
        w_got(index, 0)
        for kind in (1, 2, 5) if index == 2 else (1, 2):
            w_send(index, kind).start()

    def w_ring(index):
        w_got(index, 1)
        w_send(index, 3).start()
        w_got(index, 2)
        w_send(index, 4).start()
        if index == 2:
            w_send(index, 6).start()
            w_send(index, 7).start()

    def w_far(index):
        w_got(index, 3)
        w_got(index, 4)
        if index == 2:
            w_send(index, 8).start()
        else:
            w_column(index, c).start()

    def w_column(index, core):
        ref = w.at[1, index, :, pl.ds(pl.multiple_of(core * wide, wide), wide)]
        return remote(ref, ref, ws.at[8, index], wr.at[8, index], to_core)

    def w_done(index):
        if index < 2:
            w_column(index, 1 - c).wait_recv()
        else:
            for kind in (5, 6, 7, 8):
                w_got(index, kind)

    def vpiece(b, core):
        column = pl.multiple_of(core * (di // 2), di // 2)
        return wi.at[:, pl.ds(pl.multiple_of(b * k, k), k), pl.ds(column, di // 2)]

    def vhalf(b, part_of):
        first = pl.multiple_of(b * k + part_of * (k // 2), k // 2)
        column = pl.multiple_of(c * (di // 2), di // 2)
        return wi.at[:, pl.ds(first, k // 2), pl.ds(column, di // 2)]

    def v_send(kind):
        ref, where = (
            (vpiece(p.b, c), p.xp),
            (vpiece(p.b, c), p.xm),
            (vhalf(p.bm, 0), p.xp),
            (vhalf(p.bp, 1), p.xm),
            (vpiece(p.bm, c), to_core),
            (vpiece(p.bp, c), to_core),
            (vpiece(p.bo, c), to_core),
        )[kind]
        return remote(ref, ref, vs.at[kind], vr.at[kind], where)

    def v_got(kind):
        ref = (
            vpiece(p.bm, c),
            vpiece(p.bp, c),
            vhalf(p.bo, 0),
            vhalf(p.bo, 1),
            vpiece(p.bm, 1 - c),
            vpiece(p.bp, 1 - c),
            vpiece(p.bo, 1 - c),
        )[kind]
        remote(ref, ref, vs.at[kind], vr.at[kind], to_core).wait_recv()

    def block(j, q, b):
        return rows_of(pm.at[q], (j * X + b) * n, n, n)

    def half(j, q, b, part_of):
        return rows_of(pm.at[q], (j * X + b) * n + part_of * h, h, h)

    def first(j, q, way):
        src = half(j, q, p.bo, way)
        where = (p.xp, p.xm)[way]
        return remote(src, r1.at[way, j, q], ss.at[way, j, q], sr.at[way, j, q], where)

    def second(j, q, way):
        src = block(j, q, (p.bp, p.bm)[way])
        where = (p.xp, p.xm)[way]
        return remote(src, r2.at[way, j, q], ss.at[2 + way, j, q], sr.at[2 + way, j, q], where)

    def to_owner(q):
        return remote(zs.at[q], zin.at[q], ss.at[4, 0, q], sr.at[4, 0, q], to_a2)

    def back(j):
        s = (p.a, a2)[j]
        dst = hq.at[pl.ds(pl.multiple_of(s * group, group), group), :]
        return remote(h2.at[j], dst, hs.at[j], hr.at[j], to_mate)

    def back_got(j):
        other = (mate, (mate + 2) % ZL)[j]
        dst = hq.at[pl.ds(pl.multiple_of(other * group, group), group), :]
        remote(h2.at[j], dst, hs.at[j], hr.at[j], to_mate).wait_recv()

    def rows_in(j):
        return nq[j * group : (j + 1) * group, :]

    def own_units(j):
        left = rows_in(j)
        value = gated(
            dot(left, w[0, 0, :f, :], ((1,), (1,))), dot(left, w[0, 1, :f, :], ((1,), (1,)))
        )
        hq[pl.ds(pl.multiple_of((p.a, a2)[j] * group, group), group), :] = value
        part[j] = dot(value, w[0, 2, :f, :])

    def mate_gate(j):
        gate_val[j] = dot(rows_in(j), w[1, 0, :f, :], ((1,), (1,)))

    def mate_up(j):
        h2[j] = gated(gate_val[j], dot(rows_in(j), w[1, 1, :f, :], ((1,), (1,))))
        back(j).start()

    def mate_down(j, q):
        columns = slice(q * wide, (q + 1) * wide)
        total = part[j, :, columns] + dot(h2[j], w[1, 2, :f, columns])
        pm[q, j * group : (j + 1) * group, :] = total.astype(BF16)
        first(j, q, 0).start()
        first(j, q, 1).start()

    def combine(j, q):
        for way in range(2):
            first(j, q, way).wait_recv()
            ref = half(j, q, (p.bp, p.bm)[way], way)
            ref[...] = (ref[...].astype(F32) + r1[way, j, q].astype(F32)).astype(BF16)
            second(j, q, way).start()

    def summed(j, q):
        second(j, q, 0).wait_recv()
        second(j, q, 1).wait_recv()
        total = block(j, q, p.b)[...].astype(F32)
        return total + r2[0, j, q].astype(F32) + r2[1, j, q].astype(F32)

    def send_sum(q):
        zs[q] = summed(1, q).astype(BF16)
        to_owner(q).start()

    def item_hop(hop):
        items.take(hop)
        if hop < 4:
            items.start(hop + 1)

    def isum_hop(hop):
        isum.take(hop)
        isum.add(hop)
        isum.start(hop + 1)

    def item_product():
        left = ni[...]
        partial = 0.0
        for b in range(X):
            here = slice(b * k, (b + 1) * k)
            value = gated(
                dot(left, wi[0, here, :], ((1,), (1,))), dot(left, wi[1, here, :], ((1,), (1,)))
            )
            hi[b] = value
            partial = partial + dot(value, wi[2, here, :])
        ip[...] = partial.astype(BF16)
        isum.start(1)

    rows.right(0).start()
    rows.left(0).start()
    items.start(1)
    own_weights[0].wait()
    w_send(0, 0).start()
    across().start()
    v_send(0).start()
    v_send(1).start()
    own_weights[1].wait()
    own_weights[2].wait()
    for first_row in range(0, f, 112):
        chunk = stage[first_row : first_row + 112, :]
        for tower in range(2):
            columns = slice(tower * wide, (tower + 1) * wide)
            w[0, 2, first_row : first_row + 112, columns] = by_tower(chunk, count, tower)
    rows.take_x(0)
    item_hop(1)
    w_near(0)
    w_send(1, 0).start()
    rows.take_halves(0)
    own_units(0)
    remote(rows.block(0, p.b), rows.block(1, p.b), gs.at[0, 0], gr.at[0, 0], to_a2).wait_recv()
    rows.right(1).start()
    rows.left(1).start()
    item_hop(2)
    w_ring(0)
    w_near(1)
    w_send(2, 0).start()
    for kind in range(2):
        v_got(kind)
        v_send(2 + kind).start()
        v_send(4 + kind).start()
    item_hop(3)
    w_far(0)
    rows.take_x(1)
    v_got(2)
    v_got(3)
    v_send(6).start()
    w_ring(1)
    item_hop(4)
    for kind in (4, 5, 6):
        v_got(kind)
    w_near(2)
    item_product()
    w_far(1)
    w_done(0)
    mate_gate(0)
    rows.take_halves(1)
    mate_gate(1)
    isum_hop(1)
    w_ring(2)
    own_units(1)
    w_done(1)
    mate_up(1)
    isum_hop(2)
    w_far(2)
    mate_up(0)
    w_done(2)
    def spread(buf, mine, sems, partner):
        def each(hop, _):
            remote(buf.at[mine], buf.at[mine], sems.at[0], sems.at[1], partner(hop)).start()
            return 0

        lax.fori_loop(1, buf.shape[0], each, 0)

    def gathered(buf, sems):
        ref = buf.at[pl.ds(0, buf.shape[0] - 1)]
        remote(ref, ref, sems.at[0], sems.at[1], member(1)).wait()

    def q_rows(tower, line_of, core):
        return rows_of(gq.at[tower], (line_of * 2 + core) * block_wide, block_wide, block_wide)

    def q_half(tower, line_of, way):
        first = (line_of * 2 + c) * block_wide + way * (block_wide // 2)
        return rows_of(gq.at[tower], first, block_wide // 2, block_wide // 2)

    def q_core(tower, j):
        src = q_rows(tower, line_y[j], 1 - c)
        return remote(src, qc1.at[tower, j], qs.at[tower, j], qv.at[tower, j], to_core)

    def q_first(tower, way):
        src, dst = q_half(tower, y2, way), qb1.at[tower, way]
        return remote(src, dst, qs.at[tower, 4 + way], qv.at[tower, 4 + way], to_y[way])

    def q_second(tower, way):
        src, dst = q_rows(tower, (yp, ym)[way], c), qb2.at[tower, way]
        return remote(src, dst, qs.at[tower, 6 + way], qv.at[tower, 6 + way], to_y[way])

    def q_tower(tower):
        return remote(q_rows(tower, y, c), qc, qs.at[tower, 8], qv.at[tower, 8], to_tower)

    def q_start(tower):
        for j in range(4):
            q_core(tower, j).start()

    def q_far(tower):
        q_core(tower, 0).wait_recv()
        ref = q_rows(tower, y2, c)
        ref[...] += qc1[tower, 0]
        for way in range(2):
            q_first(tower, way).start()

    def q_near(tower):
        for way in range(2):
            q_core(tower, 1 + way).wait_recv()
            ref = q_rows(tower, (yp, ym)[way], c)
            ref[...] += qc1[tower, 1 + way]
            q_first(tower, way).wait_recv()
            ref = q_half(tower, (yp, ym)[way], way)
            ref[...] += qb1[tower, way]
            q_second(tower, way).start()

    def q_own(tower):
        q_core(tower, 3).wait_recv()
        for way in range(2):
            q_second(tower, way).wait_recv()
        ref = q_rows(tower, y, c)
        ref[...] = ref[...] + qc1[tower, 3] + qb2[tower, 0] + qb2[tower, 1]

        @pl.when(p.w != tower)
        def _():
            q_tower(tower).start()

    def q_finish(tower):
        @pl.when(p.w == tower)
        def _():
            q_tower(tower).wait_recv()
            q_out[...] = q_rows(tower, y, c)[...] + qc[...]

    def i_rows(line_of, core):
        first = pl.multiple_of((line_of * 2 + core) * block_wide, block_wide)
        return gi.at[:, pl.ds(first, block_wide), :]

    def i_half(line_of, way):
        first = pl.multiple_of((line_of * 2 + c) * block_wide, block_wide)
        return gi.at[pl.ds(way * 2, 2), pl.ds(first, block_wide), :]

    def i_slab(b):
        return gi.at[b, pl.ds(pl.multiple_of((y * 2 + c) * block_wide, block_wide), block_wide), :]

    def i_core(j):
        return remote(i_rows(line_y[j], 1 - c), ic1.at[j], bs.at[j], bv.at[j], to_core)

    def i_first(way):
        return remote(i_half(y2, way), ib1.at[way], bs.at[4 + way], bv.at[4 + way], to_y[way])

    def i_second(way):
        src = i_rows((yp, ym)[way], c)
        return remote(src, ib2.at[way], bs.at[6 + way], bv.at[6 + way], to_y[way])

    def i_x(hop):
        other = (p.b + hop) % X
        where = {"tensor": p.a * X + other}
        return remote(i_slab(other), ic.at[p.b], bs.at[8 + hop], bv.at[8 + p.b], where)

    def i_product():
        for b in range(X):
            gi[b] = dot(yi[...], hi[b], ((0,), (0,)))
        for j in range(4):
            i_core(j).start()

    def i_far():
        for j in range(4):
            i_core(j).wait_recv()
            ref = i_rows(line_y[j], c)
            ref[...] += ic1[j]
        for way in range(2):
            i_first(way).start()

    def i_near():
        for way in range(2):
            i_first(way).wait_recv()
            ref = i_half((yp, ym)[way], way)
            ref[...] += ib1[way]
            i_second(way).start()

    def i_own():
        for way in range(2):
            i_second(way).wait_recv()
        ref = i_rows(y, c)
        ref[...] = ref[...] + ib2[0] + ib2[1]
        for hop in range(1, X):
            i_x(hop).start()

    def i_finish():
        total = i_slab(p.b)[...]
        for hop in range(1, X):
            other = (p.b + hop) % X
            remote(i_slab(other), ic.at[other], bs.at[8 + hop], bv.at[8 + other], p.xp).wait_recv()
            total = total + ic[other]
        i_out[...] = total

    gather = [RowGather(p, yq.at[tower], n, ys.at[tower], yr.at[tower]) for tower in range(2)]
    igather = RingGather(p, yi, m, iys, iyr)

    steps = (0, 1, 4, 2, 3, 5, 6, 7)

    def advance(index):
        if index < len(steps):
            g = steps[index]
            gather[g // ZL].take_z(p.order(g % ZL))
        if 0 <= index - 2 < len(steps):
            g = steps[index - 2]
            gather[g // ZL].take_x(p.order(g % ZL))

    def item_grad_hop(hop):
        igather.take(hop)
        if hop < 4:
            igather.start(hop + 1)

    def scale_hidden():
        line = lax.broadcasted_iota(jnp.int32, (128, 128), 0)
        tiles = [jnp.zeros((128, 128), F32)] * 2
        for t in range(parts):
            for kind in range(2):
                tiles[kind] = jnp.where(line == t, scal[t, kind : kind + 1, :], tiles[kind])
        scale_of, slope_of = tiles[0].T[:n], tiles[1].T[:n]
        total = jnp.zeros((1, f), F32)
        for t in range(parts):
            here = slice(t * n, (t + 1) * n)
            value = hq[here, :].astype(F32)
            hw[here, :] = (value * slope_of[:, t : t + 1]).astype(BF16)
            total = total + jnp.sum(value * scale_of[:, t : t + 1], axis=0, keepdims=True)
        return total

    def product(tower, part_of):
        total = 0.0
        for j in (2 * part_of, 2 * part_of + 1):
            s = p.order(j)
            gather[tower].take_halves(s)
            here = pl.ds(pl.multiple_of(s * group, group), group)
            total = total + dot(yq[tower, here, :], hw[here, :], ((0,), (0,)))
        if part_of == 0:
            column = jnp.broadcast_to(along_of[tower], (128, wide)).T[:, 0:1]
            gq[tower] = column * summed_hidden - total
        else:
            gq[tower] -= total

    def resid_half(tower):
        total = summed(0, tower)
        to_owner(tower).wait_recv()
        total = total + zin[tower].astype(F32)
        value = by_tower(qa[...], count, tower).astype(F32) + total
        yq[tower, pl.ds(pl.multiple_of(p.t * n, n), n), :] = value.astype(BF16)
        return value

    mate_down(1, 0)
    mate_down(0, 0)
    combine(1, 0)
    mate_down(1, 1)
    combine(0, 0)
    mate_down(0, 1)
    send_sum(0)
    combine(1, 1)
    combine(0, 1)
    isum_hop(3)
    send_sum(1)
    q_resid = [resid_half(0)]
    advance(0)
    isum.take(4)
    own_item = ip[pl.ds(pl.multiple_of(p.z * m, m), m), :].astype(F32)
    i_resid = ia[...].astype(F32) + (own_item + land[0, 3].astype(F32) + land[1, 3].astype(F32))
    i_gain = gain_row(if_)
    i_scale = rms_scale(i_resid)
    sums[p.t, :, dq:] = jnp.sum(i_resid * i_scale * i_gain, axis=0, keepdims=True)
    q_gain = gain_row(qf)
    gain_of = [by_tower(q_gain, count, tower) for tower in range(2)]
    advance(1)
    q_resid.append(resid_half(1))
    square = sum(jnp.sum(value * value, axis=-1, keepdims=True) for value in q_resid)
    q_scale = lax.rsqrt(square / dq + EPS)
    for tower in range(2):
        part_sum = jnp.sum(q_resid[tower] * q_scale * gain_of[tower], axis=0, keepdims=True)
        sums[p.t, :, tower * wide : (tower + 1) * wide] = part_sum
    spread(sums, p.t, s1, member)
    advance(2)
    proj_copy.wait()
    gathered(sums, s1)
    total = sums[0]
    for slot in range(1, parts):
        total = total + sums[slot]
    firsts = [(d % 2) * wide + (d // 2) * block_wide for d in range(count)]
    q_pooled = jnp.concatenate([total[:, at : at + block_wide] for at in firsts], axis=1) / QLEN
    i_pooled = total[:, dq:] / ILEN
    q_e = jnp.sum(dot(split_rows(q_pooled), proj[...]), axis=0, keepdims=True)
    q_norm, i_norm = unit_scale(q_e), unit_scale(i_pooled)
    hats[own, :, :di] = q_e * q_norm
    hats[own, :, di:] = i_pooled * i_norm
    spread(hats, own, s2, replica)
    advance(3)
    gathered(hats, s2)
    index = lax.broadcasted_iota(jnp.int32, (count, 2 * di), 0)
    every = jnp.zeros((count, 2 * di), F32)
    for slot in range(count):
        every = jnp.where(index == slot, hats[slot], every)
    every_query, every_items = every[:, :di], every[:, di:]
    line = lax.broadcasted_iota(jnp.int32, (count, count), 0)
    target = jnp.zeros((count, count), jnp.int32)
    for slot in range(count):
        target = jnp.where(line == slot, positive[slot], target)
    per_row, slopes = contrast(every_query, every_items, ranks[...], target)
    loss[...] = jnp.sum(per_row, axis=0, keepdims=True) / count
    weights = slopes * (LOSS_SCALE / (TAU * count))
    advance(4)
    mine = lax.broadcasted_iota(jnp.int32, (count, di), 0) == own
    q_back = jnp.sum(
        jnp.where(mine, dot(weights, every_items, precision=HIGH), 0.0), axis=0, keepdims=True
    )
    column = lax.broadcasted_iota(jnp.int32, (count, count), 1) == own
    i_back = jnp.sum(
        jnp.sum(jnp.where(column, weights, 0.0), axis=1, keepdims=True) * every_query,
        axis=0,
        keepdims=True,
    )
    advance(5)
    q_grad_e = unit_back(q_e, q_norm, q_back)
    q_up = jnp.sum(dot(split_rows(q_grad_e), proj[...], ((1,), (1,))), axis=0, keepdims=True) / QLEN
    i_up = unit_back(i_pooled, i_norm, i_back) / ILEN
    along = q_gain * q_up
    along_of = [by_tower(along, count, tower) for tower in range(2)]
    inner = sum(
        jnp.sum(along_of[tower] * q_resid[tower], axis=-1, keepdims=True) for tower in range(2)
    )
    inner = inner / dq
    slope = (q_scale * q_scale * q_scale) * inner
    lane = lax.broadcasted_iota(jnp.int32, (n, 128), 1)
    columns = jnp.where(lane == 0, q_scale, jnp.where(lane == 1, slope, 0.0))
    columns = jnp.concatenate([columns, jnp.zeros((128 - n, 128), F32)], axis=0)
    scal[p.t] = columns.T[:8]
    spread(scal, p.t, s3, member)
    yi[pl.ds(pl.multiple_of(p.z * m, m), m), :] = grad_rows(i_resid, i_scale, i_gain, i_up)
    igather.start(1)
    advance(6)
    gathered(scal, s3)
    back_got(0)
    back_got(1)
    summed_hidden = scale_hidden()
    advance(7)
    item_grad_hop(1)
    product(0, 0)
    advance(8)
    item_grad_hop(2)
    product(0, 1)
    q_start(0)
    advance(9)
    item_grad_hop(3)
    q_far(0)
    product(1, 0)
    item_grad_hop(4)
    q_near(0)
    product(1, 1)
    q_start(1)
    i_product()
    q_far(1)
    q_own(0)
    i_far()
    q_near(1)
    i_near()
    q_own(1)
    i_own()
    q_finish(0)
    i_finish()
    q_finish(1)

    for j in range(2):
        back(j).wait_send()
        for copy in (rows.right(j), rows.left(j), rows.half_right(j), rows.half_left(j)):
            copy.wait_send()
        for q in range(2):
            for way in range(2):
                first(j, q, way).wait_send()
                second(j, q, way).wait_send()
    for q in range(2):
        to_owner(q).wait_send()
    across().wait_send()
    items.drain()
    isum.drain()
    for index in range(3):
        for kind in range(9) if index == 2 else range(5):
            w_send(index, kind).wait_send()
    for index in range(2):
        w_column(index, c).wait_send()
    for kind in range(7):
        v_send(kind).wait_send()
    for tower in range(2):
        gather[tower].drain()
        for j in range(4):
            q_core(tower, j).wait_send()
        for way in range(2):
            q_first(tower, way).wait_send()
            q_second(tower, way).wait_send()

        @pl.when(p.w != tower)
        def _():
            q_tower(tower).wait_send()

    igather.drain()
    for j in range(4):
        i_core(j).wait_send()
    for way in range(2):
        i_first(way).wait_send()
        i_second(way).wait_send()
    for hop in range(1, X):
        i_x(hop).wait_send()


def step(qa, qg, gate, up, down, ia, ig, ig_w, iu_w, id_w, qf, if_, proj, ranks, positive):
    n, dq = qa.shape
    m, di = ia.shape
    f, k = down.shape[0], id_w.shape[0]
    padded = 64 * ((f + 63) // 64)
    vmem, hbm = pl.BlockSpec(memory_space=pltpu.VMEM), pl.BlockSpec(memory_space=pl.ANY)
    smem = pl.BlockSpec(memory_space=pltpu.SMEM)
    all_i = ZR * m
    group = X * n
    parts = X * ZL
    count = ranks.shape[0]
    wide = dq // count
    dma = pltpu.SemaphoreType.DMA
    return pl.pallas_call(
        kernel,
        out_shape=(
            jax.ShapeDtypeStruct((1, 1), F32),
            jax.ShapeDtypeStruct((wide, f), F32),
            jax.ShapeDtypeStruct((wide, k), F32),
        ),
        in_specs=[vmem, vmem, hbm, hbm, hbm] + [vmem] * 7 + [hbm, vmem, smem],
        out_specs=[vmem] * 3,
        scratch_shapes=[
            pltpu.VMEM((2, 3, padded, dq), BF16),
            pltpu.VMEM(down.shape, BF16),
            pltpu.VMEM(proj.shape, BF16),
            pltpu.VMEM((2 * group, dq), BF16),
            pltpu.VMEM((2, group, dq), F32),
            pltpu.VMEM((2, group, f), F32),
            pltpu.VMEM((2, group, f), BF16),
            pltpu.VMEM((2, 2 * group, dq // 2), BF16),
            pltpu.VMEM((2, 2, 2, n // 2, dq // 2), BF16),
            pltpu.VMEM((2, 2, 2, n, dq // 2), BF16),
            pltpu.VMEM((2, n, dq // 2), BF16),
            pltpu.VMEM((2, n, dq // 2), BF16),
            pltpu.VMEM((all_i, di), BF16),
            pltpu.VMEM((3, X * k, di), BF16),
            pltpu.VMEM((all_i, di), BF16),
            pltpu.VMEM((2, 4, m, di), BF16),
            pltpu.VMEM((ZL * group, f), BF16),
            pltpu.VMEM((X, all_i, k), BF16),
            pltpu.VMEM((parts, 1, dq + di), F32),
            pltpu.VMEM((count, 1, 2 * di), F32),
            pltpu.VMEM((parts, 8, 128), F32),
            pltpu.VMEM((2, parts * n, dq // 2), BF16),
            pltpu.VMEM((ZL * group, f), BF16),
            pltpu.VMEM((all_i, di), BF16),
            pltpu.VMEM((2, dq // 2, f), F32),
            pltpu.VMEM((X, di, k), F32),
            pltpu.VMEM((2, 4, wide, f), F32),
            pltpu.VMEM((2, 2, wide // 2, f), F32),
            pltpu.VMEM((2, 2, wide, f), F32),
            pltpu.VMEM((wide, f), F32),
            pltpu.VMEM((4, X, wide, k), F32),
            pltpu.VMEM((2, 2, wide, k), F32),
            pltpu.VMEM((2, X, wide, k), F32),
            pltpu.VMEM((X, wide, k), F32),
            dma((4,)),
            dma((6, 2)),
            dma((5, 2)),
            dma((5, 2, 2)),
            dma((5, 2, 2)),
            dma((9, 3)),
            dma((9, 3)),
            dma((7,)),
            dma((7,)),
            dma((2,)),
            dma((2,)),
            dma((2, 4)),
            dma((2, 4)),
            dma((2, 4)),
            dma((2, 4)),
            dma((2,)),
            dma((2,)),
            dma((2,)),
            dma((2, 6, ZL)),
            dma((2, 5, ZL)),
            dma((2, 4)),
            dma((2, 4)),
            dma((2, 9)),
            dma((2, 9)),
            dma((12,)),
            dma((12,)),
        ],
        compiler_params=pltpu.CompilerParams(
            collective_id=0, has_side_effects=True, vmem_limit_bytes=VMEM_LIMIT
        ),
        name="towers_step",
    )(qa, qg, gate, up, down, ia, ig, ig_w, iu_w, id_w, qf, if_, proj, ranks, positive)


def body(
    q_act,
    q_norm_gain,
    q_gate,
    q_up,
    q_down,
    q_final_gain,
    projection,
    i_act,
    i_norm_gain,
    i_gate,
    i_up,
    i_down,
    i_final_gain,
    ranks,
    positive,
):
    loss, q_grad, i_grad = step(
        q_act,
        q_norm_gain,
        q_gate.T,
        q_up.T,
        q_down,
        i_act,
        i_norm_gain,
        i_gate.T,
        i_up.T,
        i_down,
        q_final_gain,
        i_final_gain,
        projection,
        ranks,
        positive,
    )
    return (loss.reshape(()), q_grad.T, i_grad.T)


def solution(mesh):
    in_specs = (
        P(("dp", "tower", "tensor"), None),
        P(),
        P(None, "tensor"),
        P(None, "tensor"),
        P("tensor", None),
        P(),
        P(),
        P(("dp", "tower", "tensor"), None),
        P(),
        P(None, ("tower", "tensor")),
        P(None, ("tower", "tensor")),
        P(("tower", "tensor"), None),
        P(),
        P(),
        P(),
    )
    out_specs = (P(), P("tensor", ("dp", "tower")), P(("tower", "tensor"), "dp"))
    return jax.shard_map(body, mesh=mesh, in_specs=in_specs, out_specs=out_specs, check_vma=False)
```

```python
import functools

import jax
import jax.numpy as jnp
from jax import lax
from jax.experimental import pallas as pl
from jax.experimental.pallas import tpu as pltpu
from jax.sharding import PartitionSpec as P

QLEN = 1536
ILEN = 512
EPS = 1e-06
TAU = 0.05
TEACH = 2.0
LOSS_SCALE = 64.0
HIGH = lax.Precision.HIGHEST
MESH = pl.DeviceIdType.MESH
F32 = jnp.float32
BF16 = jnp.bfloat16

X = 4
ZL = 4
ZR = 8
VMEM_LIMIT = 60 * 1024 * 1024


def rms_scale(values):
    return lax.rsqrt(jnp.mean(values * values, axis=-1, keepdims=True) + EPS)


def dot(left, right, dims=((1,), (0,)), precision=None):
    return lax.dot_general(
        left, right, (dims, ((), ())), preferred_element_type=F32, precision=precision
    )


def remote(src, dst, send, recv, where):
    return pltpu.make_async_remote_copy(
        src_ref=src, dst_ref=dst, send_sem=send, recv_sem=recv, device_id=where, device_id_type=MESH
    )


class Place:
    def __init__(self):
        self.t = lax.axis_index("tensor")
        self.w = lax.axis_index("tower")
        self.a = self.t // X
        self.b = self.t % X
        self.z = self.w * ZL + self.a
        self.bp = (self.b + 1) % X
        self.bm = (self.b + X - 1) % X
        self.bo = (self.b + 2) % X
        self.xp = {"tensor": self.a * X + self.bp}
        self.xm = {"tensor": self.a * X + self.bm}
        self.zp = self.ring(1)
        self.zm = self.ring(ZR - 1)

    def ring(self, step):
        z = (self.z + step) % ZR
        return {"tower": z // ZL, "tensor": (z % ZL) * X + self.b}

    def column(self, row):
        return {"tensor": row * X + self.b}

    def order(self, j):
        near = jnp.minimum(self.a, ZL - 1 - self.a)
        swapped = jnp.where(j == 0, 1, jnp.where(j == 1, 0, j))
        row = jnp.where(near == 1, swapped, j)
        return jnp.where(self.a >= 2, ZL - 1 - row, row)


def rows_of(ref, first, count, unit):
    return ref.at[pl.ds(pl.multiple_of(first, unit), count), :]


class RowGather:
    def __init__(self, place, buf, rows, send, recv):
        self.p, self.buf, self.n, self.send, self.recv = place, buf, rows, send, recv

    def block(self, s, b):
        return rows_of(self.buf, (s * X + b) * self.n, self.n, self.n)

    def half(self, s, b, h):
        n = self.n // 2
        return rows_of(self.buf, (s * X + b) * self.n + h * n, n, n)

    def up(self, s):
        ref = self.block(s, self.p.b)
        where = self.p.column(jnp.minimum(self.p.a + 1, ZL - 1))
        return remote(ref, ref, self.send.at[0, s], self.recv.at[0, s], where)

    def down(self, s):
        ref = self.block(s, self.p.b)
        where = self.p.column(jnp.maximum(self.p.a - 1, 0))
        return remote(ref, ref, self.send.at[1, s], self.recv.at[0, s], where)

    def right(self, s):
        ref = self.block(s, self.p.b)
        return remote(ref, ref, self.send.at[2, s], self.recv.at[1, s], self.p.xp)

    def left(self, s):
        ref = self.block(s, self.p.b)
        return remote(ref, ref, self.send.at[3, s], self.recv.at[2, s], self.p.xm)

    def half_right(self, s):
        ref = self.half(s, self.p.bm, 0)
        return remote(ref, ref, self.send.at[4, s], self.recv.at[3, s], self.p.xp)

    def half_left(self, s):
        ref = self.half(s, self.p.bp, 1)
        return remote(ref, ref, self.send.at[5, s], self.recv.at[4, s], self.p.xm)

    def goes_up(self, s):
        return (s <= self.p.a) & (self.p.a < ZL - 1)

    def goes_down(self, s):
        return (s >= self.p.a) & (self.p.a > 0)

    def take_z(self, s):
        @pl.when(s != self.p.a)
        def _():
            self.up(s).wait_recv()

        @pl.when(self.goes_up(s))
        def _():
            self.up(s).start()

        @pl.when(self.goes_down(s))
        def _():
            self.down(s).start()

        self.right(s).start()
        self.left(s).start()

    def take_x(self, s):
        ref = self.block(s, self.p.bm)
        remote(ref, ref, self.send.at[2, s], self.recv.at[1, s], self.p.xm).wait_recv()
        self.half_right(s).start()
        ref = self.block(s, self.p.bp)
        remote(ref, ref, self.send.at[3, s], self.recv.at[2, s], self.p.xp).wait_recv()
        self.half_left(s).start()

    def take_halves(self, s):
        ref = self.half(s, self.p.bo, 0)
        remote(ref, ref, self.send.at[4, s], self.recv.at[3, s], self.p.xm).wait_recv()
        ref = self.half(s, self.p.bo, 1)
        remote(ref, ref, self.send.at[5, s], self.recv.at[4, s], self.p.xp).wait_recv()

    def drain(self):
        def each(s, _):
            @pl.when(self.goes_up(s))
            def _():
                self.up(s).wait_send()

            @pl.when(self.goes_down(s))
            def _():
                self.down(s).wait_send()

            self.right(s).wait_send()
            self.left(s).wait_send()
            self.half_right(s).wait_send()
            self.half_left(s).wait_send()
            return 0

        lax.fori_loop(0, ZL, each, 0)


class RingGather:
    def __init__(self, place, buf, rows, send, recv):
        self.p, self.buf, self.n, self.send, self.recv = place, buf, rows, send, recv

    def ref(self, z, hop, upward):
        z = (z + 2 * ZR) % ZR
        if hop < 4:
            return rows_of(self.buf, z * self.n, self.n, self.n)
        n = self.n // 2
        return rows_of(self.buf, z * self.n + (0 if upward else n), n, n)

    def copies(self, hop):
        up = self.ref(self.p.z - hop + 1, hop, True)
        down = self.ref(self.p.z + hop - 1, hop, False)
        return (
            remote(up, up, self.send.at[0, hop - 1], self.recv.at[0, hop - 1], self.p.zp),
            remote(down, down, self.send.at[1, hop - 1], self.recv.at[1, hop - 1], self.p.zm),
        )

    def start(self, hop):
        for copy in self.copies(hop):
            copy.start()

    def take(self, hop):
        up = self.ref(self.p.z - hop, hop, True)
        down = self.ref(self.p.z + hop, hop, False)
        remote(up, up, self.send.at[0, hop - 1], self.recv.at[0, hop - 1], self.p.zm).wait_recv()
        remote(down, down, self.send.at[1, hop - 1], self.recv.at[1, hop - 1], self.p.zp).wait_recv()

    def drain(self):
        for hop in range(1, 5):
            for copy in self.copies(hop):
                copy.wait_send()


class RingSum:
    def __init__(self, place, buf, land, rows, send, recv):
        self.p, self.buf, self.land = place, buf, land
        self.n, self.send, self.recv = rows, send, recv

    def part(self, z, half):
        z = (z + 2 * ZR) % ZR
        if half is None:
            return rows_of(self.buf, z * self.n, self.n, self.n)
        n = self.n // 2
        return rows_of(self.buf, z * self.n + half * n, n, n)

    def slot(self, way, hop):
        if hop == 1:
            return self.land.at[way, 0, pl.ds(0, self.n // 2), :]
        return self.land.at[way, hop - 1]

    def copies(self, hop):
        half = (0, 1) if hop == 1 else (None, None)
        up = self.part(self.p.z + 5 - hop, half[0])
        down = self.part(self.p.z - 5 + hop, half[1])
        return (
            remote(up, self.slot(0, hop), self.send.at[0, hop - 1], self.recv.at[0, hop - 1], self.p.zp),
            remote(down, self.slot(1, hop), self.send.at[1, hop - 1], self.recv.at[1, hop - 1], self.p.zm),
        )

    def start(self, hop):
        for copy in self.copies(hop):
            copy.start()

    def take(self, hop):
        for copy in self.copies(hop):
            copy.wait_recv()

    def add(self, hop):
        half = (0, 1) if hop == 1 else (None, None)
        for way, z in ((0, self.p.z + 4 - hop), (1, self.p.z - 4 + hop)):
            ref = self.part(z, half[way])
            ref[...] = (ref[...].astype(F32) + self.slot(way, hop)[...].astype(F32)).astype(BF16)

    def drain(self):
        for hop in range(1, 5):
            for copy in self.copies(hop):
                copy.wait_send()


def gain_row(ref):
    return ref[...].astype(F32).reshape(1, -1)


def normed_rows(act, gain):
    values = act.astype(F32)
    return (values * rms_scale(values) * gain).astype(BF16)


def gated(gate_val, up_val):
    return (jax.nn.silu(gate_val) * up_val).astype(BF16)


def at_step(i, step):
    return pl.when(i == step)


def split_rows(row):
    high = row.astype(BF16).astype(F32)
    rest = row - high
    mid = rest.astype(BF16).astype(F32)
    low = rest - mid
    index = lax.broadcasted_iota(jnp.int32, (8, row.shape[1]), 0)
    out = jnp.where(index == 0, high, jnp.where(index == 1, mid, jnp.where(index == 2, low, 0.0)))
    return out.astype(BF16)


def unit_scale(vec):
    return lax.rsqrt(jnp.sum(vec * vec, axis=-1, keepdims=True) + EPS)


def unit_back(vec, scales, upstream):
    inner = jnp.sum(vec * upstream, axis=-1, keepdims=True)
    return scales * upstream - vec * (scales * scales * scales) * inner


def contrast(query_hat, item_hat, ranks, positive):
    logits = dot(query_hat, item_hat, ((1,), (1,)), HIGH) / TAU
    shifted = logits - 1.0 / TAU
    log_student = shifted - jnp.log(jnp.sum(jnp.exp(shifted), axis=1, keepdims=True))
    teach = -ranks.astype(F32) / TEACH
    log_teacher = teach - jnp.log(jnp.sum(jnp.exp(teach), axis=1, keepdims=True))
    teacher = jnp.exp(log_teacher)
    columns = lax.broadcasted_iota(jnp.int32, logits.shape, 1)
    onehot = (columns == positive).astype(F32)
    per_row = jnp.sum(
        teacher * (log_teacher - log_student) - onehot * log_student, axis=1, keepdims=True
    )
    slopes = 2.0 * jnp.exp(log_student) - onehot - teacher
    return (per_row, slopes)


def grad_rows(resid, scales, gain, upstream):
    along = gain * upstream
    inner = jnp.mean(along * resid, axis=-1, keepdims=True)
    return (scales * along - resid * (scales * scales * scales) * inner).astype(BF16)


def by_tower(values, parts, tower):
    wide = values.shape[1] // parts
    blocks = [values[:, d * wide : (d + 1) * wide] for d in range(tower, parts, 2)]
    return jnp.concatenate(blocks, axis=1)


def kernel(
    qa, qg, gate_hbm, up_hbm, down_hbm, ia, ig, ig_w, iu_w, id_w, qf, if_, proj_hbm, ranks, positive,
    loss, q_out, i_out,
    w, stage, proj, nq, part, gate_val, h2, pm, r1, r2, zs, zin, ni, wi, ip, land, hq, hi,
    sums, hats, scal, yq, hw, yi, gq, gi, qc1, qb1, qb2, qc, ic1, ib1, ib2, ic,
    loads, gs, gr, ss, sr, ws, wr, vs, vr, hs, hr, ias, iar, irs, irr,
    s1, s2, s3, ys, yr, iys, iyr, qs, qv, bs, bv,
):
    p = Place()
    n, dq = qa.shape
    m, di = ia.shape
    f, k = down_hbm.shape[0], id_w.shape[0]
    group = X * n
    h = n // 2
    parts = X * ZL
    count = hats.shape[0]
    block_wide = dq // count
    piece = w.shape[2] // 4
    wide, thin = dq // 2, dq // 4
    dp = lax.axis_index("dp")
    own = dp * 2 + p.w
    y, c = dp // 2, dp % 2
    yp, ym, y2 = (y + 1) % 4, (y + 3) % 4, (y + 2) % 4
    line_y = (y2, yp, ym, y)
    to_yp, to_ym, to_core = {"dp": yp * 2 + c}, {"dp": ym * 2 + c}, {"dp": y * 2 + 1 - c}
    to_y = (to_yp, to_ym)
    to_tower = {"tower": 1 - p.w}
    a2 = (p.a + 2) % ZL
    mate = p.a + 1 - 2 * (p.a % 2)
    to_a2, to_mate = p.column(a2), p.column(mate)

    def member(step):
        return {"tensor": (p.t + step) % parts}

    def replica(step):
        other = (own + step) % count
        return {"dp": other // 2, "tower": other % 2}

    own_weights = [
        pltpu.make_async_copy(ref, dst, loads.at[index])
        for index, (ref, dst) in enumerate(
            (
                (gate_hbm, w.at[0, 0, pl.ds(0, f), :]),
                (up_hbm, w.at[0, 1, pl.ds(0, f), :]),
                (down_hbm, stage),
            )
        )
    ]
    proj_copy = pltpu.make_async_copy(proj_hbm, proj, loads.at[3])
    for copy in own_weights:
        copy.start()
    proj_copy.start()
    barrier = pltpu.get_barrier_semaphore()

    def greet(step, _):
        pl.semaphore_signal(barrier, inc=1, device_id=member(step), device_id_type=MESH)
        pl.semaphore_signal(barrier, inc=1, device_id=replica(step), device_id_type=MESH)
        return 0

    lax.fori_loop(1, parts, greet, 0)
    for where in (p.zp, p.zm):
        pl.semaphore_signal(barrier, inc=1, device_id=where, device_id_type=MESH)
    for index in range(3):
        w[0, index, f:, :] = jnp.zeros((w.shape[2] - f, dq), BF16)
    nq[pl.ds(pl.multiple_of(p.b * n, n), n), :] = normed_rows(qa[...], gain_row(qg))
    ni[pl.ds(pl.multiple_of(p.z * m, m), m), :] = normed_rows(ia[...], gain_row(ig))
    for index, ref in enumerate((ig_w, iu_w, id_w)):
        wi[index, pl.ds(pl.multiple_of(p.b * k, k), k), :] = ref[...]
    pl.semaphore_wait(barrier, 2 * (parts - 1) + 2)

    rows = RowGather(p, nq, n, gs, gr)
    items = RingGather(p, ni, m, ias, iar)
    isum = RingSum(p, ip, land, m, irs, irr)

    def across():
        return remote(rows.block(0, p.b), rows.block(1, p.b), gs.at[0, 0], gr.at[0, 0], to_a2)

    def wpiece(which, index, line, core):
        first = pl.multiple_of(line * piece, piece)
        return w.at[which, index, pl.ds(first, piece), pl.ds(pl.multiple_of(core * wide, wide), wide)]

    def whalf(index, line, part_of):
        first = pl.multiple_of(line * piece, piece)
        column = pl.multiple_of(c * wide + part_of * thin, thin)
        return w.at[1, index, pl.ds(first, piece), pl.ds(column, thin)]

    def w_send(index, kind):
        here = wpiece(1, index, y, c)
        low, high = wpiece(1, index, ym, c), wpiece(1, index, yp, c)
        src, dst, where = (
            (wpiece(0, index, y, c), here, to_mate),
            (here, here, to_yp),
            (here, here, to_ym),
            (whalf(index, ym, 0), whalf(index, ym, 0), to_yp),
            (whalf(index, yp, 1), whalf(index, yp, 1), to_ym),
            (here, here, to_core),
            (low, low, to_core),
            (high, high, to_core),
            (wpiece(1, index, y2, c), wpiece(1, index, y2, c), to_core),
        )[kind]
        return remote(src, dst, ws.at[kind, index], wr.at[kind, index], where)

    def w_got(index, kind):
        dst = (
            wpiece(1, index, y, c),
            wpiece(1, index, ym, c),
            wpiece(1, index, yp, c),
            whalf(index, y2, 0),
            whalf(index, y2, 1),
            wpiece(1, index, y, 1 - c),
            wpiece(1, index, ym, 1 - c),
            wpiece(1, index, yp, 1 - c),
            wpiece(1, index, y2, 1 - c),
        )[kind]
        remote(dst, dst, ws.at[kind, index], wr.at[kind, index], to_core).wait_recv()

    def w_near(index):
        w_got(index, 0)
        for kind in (1, 2, 5) if index == 2 else (1, 2):
            w_send(index, kind).start()

    def w_ring(index):
        w_got(index, 1)
        w_send(index, 3).start()
        w_got(index, 2)
        w_send(index, 4).start()
        if index == 2:
            w_send(index, 6).start()
            w_send(index, 7).start()

    def w_far(index):
        w_got(index, 3)
        w_got(index, 4)
        if index == 2:
            w_send(index, 8).start()
        else:
            w_column(index, c).start()

    def w_column(index, core):
        ref = w.at[1, index, :, pl.ds(pl.multiple_of(core * wide, wide), wide)]
        return remote(ref, ref, ws.at[8, index], wr.at[8, index], to_core)

    def w_done(index):
        if index < 2:
            w_column(index, 1 - c).wait_recv()
        else:
            for kind in (5, 6, 7, 8):
                w_got(index, kind)

    def vpiece(b, core):
        column = pl.multiple_of(core * (di // 2), di // 2)
        return wi.at[:, pl.ds(pl.multiple_of(b * k, k), k), pl.ds(column, di // 2)]

    def vhalf(b, part_of):
        first = pl.multiple_of(b * k + part_of * (k // 2), k // 2)
        column = pl.multiple_of(c * (di // 2), di // 2)
        return wi.at[:, pl.ds(first, k // 2), pl.ds(column, di // 2)]

    def v_send(kind):
        ref, where = (
            (vpiece(p.b, c), p.xp),
            (vpiece(p.b, c), p.xm),
            (vhalf(p.bm, 0), p.xp),
            (vhalf(p.bp, 1), p.xm),
            (vpiece(p.bm, c), to_core),
            (vpiece(p.bp, c), to_core),
            (vpiece(p.bo, c), to_core),
        )[kind]
        return remote(ref, ref, vs.at[kind], vr.at[kind], where)

    def v_got(kind):
        ref = (
            vpiece(p.bm, c),
            vpiece(p.bp, c),
            vhalf(p.bo, 0),
            vhalf(p.bo, 1),
            vpiece(p.bm, 1 - c),
            vpiece(p.bp, 1 - c),
            vpiece(p.bo, 1 - c),
        )[kind]
        remote(ref, ref, vs.at[kind], vr.at[kind], to_core).wait_recv()

    def block(j, q, b):
        return rows_of(pm.at[q], (j * X + b) * n, n, n)

    def half(j, q, b, part_of):
        return rows_of(pm.at[q], (j * X + b) * n + part_of * h, h, h)

    def first(j, q, way):
        src = half(j, q, p.bo, way)
        where = (p.xp, p.xm)[way]
        return remote(src, r1.at[way, j, q], ss.at[way, j, q], sr.at[way, j, q], where)

    def second(j, q, way):
        src = block(j, q, (p.bp, p.bm)[way])
        where = (p.xp, p.xm)[way]
        return remote(src, r2.at[way, j, q], ss.at[2 + way, j, q], sr.at[2 + way, j, q], where)

    def to_owner(q):
        return remote(zs.at[q], zin.at[q], ss.at[4, 0, q], sr.at[4, 0, q], to_a2)

    def back(j, b):
        dst = rows_of(hq, ((p.a, a2)[j] * X + b) * n, n, n)
        src = h2.at[j, pl.ds(b * n, n), :]
        return remote(src, dst, hs.at[j, b], hr.at[j, b], to_mate)

    def back_got(j):
        other = (mate, (mate + 2) % ZL)[j]
        for b in range(X):
            dst = rows_of(hq, (other * X + b) * n, n, n)
            remote(dst, dst, hs.at[j, b], hr.at[j, b], to_mate).wait_recv()

    def rows_in(j):
        return nq[j * group : (j + 1) * group, :]

    def own_units(j):
        left = rows_in(j)
        value = gated(
            dot(left, w[0, 0, :f, :], ((1,), (1,))), dot(left, w[0, 1, :f, :], ((1,), (1,)))
        )
        hq[pl.ds(pl.multiple_of((p.a, a2)[j] * group, group), group), :] = value
        part[j] = dot(value, w[0, 2, :f, :])

    def mate_gate(j):
        gate_val[j] = dot(rows_in(j), w[1, 0, :f, :], ((1,), (1,)))

    def mate_up(j):
        h2[j] = gated(gate_val[j], dot(rows_in(j), w[1, 1, :f, :], ((1,), (1,))))

    def mate_down(j, q):
        columns = slice(q * wide, (q + 1) * wide)
        total = part[j, :, columns] + dot(h2[j], w[1, 2, :f, columns])
        pm[q, j * group : (j + 1) * group, :] = total.astype(BF16)
        first(j, q, 0).start()
        first(j, q, 1).start()

    def combine(j, q):
        for way in range(2):
            first(j, q, way).wait_recv()
            ref = half(j, q, (p.bp, p.bm)[way], way)
            ref[...] = (ref[...].astype(F32) + r1[way, j, q].astype(F32)).astype(BF16)
            second(j, q, way).start()

    def summed(j, q):
        second(j, q, 0).wait_recv()
        second(j, q, 1).wait_recv()
        total = block(j, q, p.b)[...].astype(F32)
        return total + r2[0, j, q].astype(F32) + r2[1, j, q].astype(F32)

    def send_sum(q):
        zs[q] = summed(1, q).astype(BF16)
        to_owner(q).start()

    def item_hop(hop):
        items.take(hop)
        if hop < 4:
            items.start(hop + 1)

    def isum_hop(hop):
        isum.take(hop)
        isum.add(hop)
        isum.start(hop + 1)

    def item_product():
        left = ni[...]
        partial = 0.0
        for b in range(X):
            here = slice(b * k, (b + 1) * k)
            value = gated(
                dot(left, wi[0, here, :], ((1,), (1,))), dot(left, wi[1, here, :], ((1,), (1,)))
            )
            hi[b] = value
            partial = partial + dot(value, wi[2, here, :])
        ip[...] = partial.astype(BF16)
        isum.start(1)

    rows.right(0).start()
    rows.left(0).start()
    items.start(1)
    own_weights[0].wait()
    w_send(0, 0).start()
    across().start()
    v_send(0).start()
    v_send(1).start()
    own_weights[1].wait()
    own_weights[2].wait()
    for first_row in range(0, f, 112):
        chunk = stage[first_row : first_row + 112, :]
        for tower in range(2):
            columns = slice(tower * wide, (tower + 1) * wide)
            w[0, 2, first_row : first_row + 112, columns] = by_tower(chunk, count, tower)
    rows.take_x(0)
    item_hop(1)
    w_near(0)
    w_send(1, 0).start()
    rows.take_halves(0)
    own_units(0)
    remote(rows.block(0, p.b), rows.block(1, p.b), gs.at[0, 0], gr.at[0, 0], to_a2).wait_recv()
    rows.right(1).start()
    rows.left(1).start()
    item_hop(2)
    w_ring(0)
    w_near(1)
    w_send(2, 0).start()
    for kind in range(2):
        v_got(kind)
        v_send(2 + kind).start()
        v_send(4 + kind).start()
    item_hop(3)
    w_far(0)
    rows.take_x(1)
    v_got(2)
    v_got(3)
    v_send(6).start()
    w_ring(1)
    item_hop(4)
    for kind in (4, 5, 6):
        v_got(kind)
    w_near(2)
    item_product()
    w_far(1)
    w_done(0)
    mate_gate(0)
    rows.take_halves(1)
    mate_gate(1)
    isum_hop(1)
    w_ring(2)
    own_units(1)
    w_done(1)
    mate_up(1)
    isum_hop(2)
    w_far(2)
    back(1, 0).start()
    back(1, 1).start()
    mate_up(0)
    w_done(2)
    back(1, 2).start()
    def spread(buf, mine, sems, partner):
        def each(hop, _):
            remote(buf.at[mine], buf.at[mine], sems.at[0], sems.at[1], partner(hop)).start()
            return 0

        lax.fori_loop(1, buf.shape[0], each, 0)

    def gathered(buf, sems):
        ref = buf.at[pl.ds(0, buf.shape[0] - 1)]
        remote(ref, ref, sems.at[0], sems.at[1], member(1)).wait()

    def q_rows(tower, line_of, core):
        return rows_of(gq.at[tower], (line_of * 2 + core) * block_wide, block_wide, block_wide)

    def q_half(tower, line_of, way):
        first = (line_of * 2 + c) * block_wide + way * (block_wide // 2)
        return rows_of(gq.at[tower], first, block_wide // 2, block_wide // 2)

    def q_core(tower, j):
        src = q_rows(tower, line_y[j], 1 - c)
        return remote(src, qc1.at[tower, j], qs.at[tower, j], qv.at[tower, j], to_core)

    def q_first(tower, way):
        src, dst = q_half(tower, y2, way), qb1.at[tower, way]
        return remote(src, dst, qs.at[tower, 4 + way], qv.at[tower, 4 + way], to_y[way])

    def q_second(tower, way):
        src, dst = q_rows(tower, (yp, ym)[way], c), qb2.at[tower, way]
        return remote(src, dst, qs.at[tower, 6 + way], qv.at[tower, 6 + way], to_y[way])

    def q_tower(tower):
        return remote(q_rows(tower, y, c), qc, qs.at[tower, 8], qv.at[tower, 8], to_tower)

    def q_start(tower):
        for j in range(4):
            q_core(tower, j).start()

    def q_far(tower):
        q_core(tower, 0).wait_recv()
        ref = q_rows(tower, y2, c)
        ref[...] += qc1[tower, 0]
        for way in range(2):
            q_first(tower, way).start()

    def q_near(tower):
        for way in range(2):
            q_core(tower, 1 + way).wait_recv()
            ref = q_rows(tower, (yp, ym)[way], c)
            ref[...] += qc1[tower, 1 + way]
            q_first(tower, way).wait_recv()
            ref = q_half(tower, (yp, ym)[way], way)
            ref[...] += qb1[tower, way]
            q_second(tower, way).start()

    def q_own(tower):
        q_core(tower, 3).wait_recv()
        for way in range(2):
            q_second(tower, way).wait_recv()
        ref = q_rows(tower, y, c)
        ref[...] = ref[...] + qc1[tower, 3] + qb2[tower, 0] + qb2[tower, 1]

        @pl.when(p.w != tower)
        def _():
            q_tower(tower).start()

    def q_finish(tower):
        @pl.when(p.w == tower)
        def _():
            q_tower(tower).wait_recv()
            q_out[...] = q_rows(tower, y, c)[...] + qc[...]

    def i_rows(line_of, core):
        first = pl.multiple_of((line_of * 2 + core) * block_wide, block_wide)
        return gi.at[:, pl.ds(first, block_wide), :]

    def i_half(line_of, way):
        first = pl.multiple_of((line_of * 2 + c) * block_wide, block_wide)
        return gi.at[pl.ds(way * 2, 2), pl.ds(first, block_wide), :]

    def i_slab(b):
        return gi.at[b, pl.ds(pl.multiple_of((y * 2 + c) * block_wide, block_wide), block_wide), :]

    def i_core(j):
        return remote(i_rows(line_y[j], 1 - c), ic1.at[j], bs.at[j], bv.at[j], to_core)

    def i_first(way):
        return remote(i_half(y2, way), ib1.at[way], bs.at[4 + way], bv.at[4 + way], to_y[way])

    def i_second(way):
        src = i_rows((yp, ym)[way], c)
        return remote(src, ib2.at[way], bs.at[6 + way], bv.at[6 + way], to_y[way])

    def i_x(hop):
        other = (p.b + hop) % X
        where = {"tensor": p.a * X + other}
        return remote(i_slab(other), ic.at[p.b], bs.at[8 + hop], bv.at[8 + p.b], where)

    def i_product():
        for b in range(X):
            gi[b] = dot(yi[...], hi[b], ((0,), (0,)))
        for j in range(4):
            i_core(j).start()

    def i_far():
        for j in range(4):
            i_core(j).wait_recv()
            ref = i_rows(line_y[j], c)
            ref[...] += ic1[j]
        for way in range(2):
            i_first(way).start()

    def i_near():
        for way in range(2):
            i_first(way).wait_recv()
            ref = i_half((yp, ym)[way], way)
            ref[...] += ib1[way]
            i_second(way).start()

    def i_own():
        for way in range(2):
            i_second(way).wait_recv()
        ref = i_rows(y, c)
        ref[...] = ref[...] + ib2[0] + ib2[1]
        for hop in range(1, X):
            i_x(hop).start()

    def i_finish():
        total = i_slab(p.b)[...]
        for hop in range(1, X):
            other = (p.b + hop) % X
            remote(i_slab(other), ic.at[other], bs.at[8 + hop], bv.at[8 + other], p.xp).wait_recv()
            total = total + ic[other]
        i_out[...] = total

    gather = [RowGather(p, yq.at[tower], n, ys.at[tower], yr.at[tower]) for tower in range(2)]
    igather = RingGather(p, yi, m, iys, iyr)

    steps = (0, 1, 4, 2, 3, 5, 6, 7)

    def advance(index):
        if index < len(steps):
            g = steps[index]
            gather[g // ZL].take_z(p.order(g % ZL))
        if 0 <= index - 2 < len(steps):
            g = steps[index - 2]
            gather[g // ZL].take_x(p.order(g % ZL))

    def item_grad_hop(hop):
        igather.take(hop)
        if hop < 4:
            igather.start(hop + 1)

    def scale_hidden():
        line = lax.broadcasted_iota(jnp.int32, (128, 128), 0)
        tiles = [jnp.zeros((128, 128), F32)] * 2
        for t in range(parts):
            for kind in range(2):
                tiles[kind] = jnp.where(line == t, scal[t, kind : kind + 1, :], tiles[kind])
        scale_of, slope_of = tiles[0].T[:n], tiles[1].T[:n]
        total = jnp.zeros((1, f), F32)
        for t in range(parts):
            here = slice(t * n, (t + 1) * n)
            value = hq[here, :].astype(F32)
            hw[here, :] = (value * slope_of[:, t : t + 1]).astype(BF16)
            total = total + jnp.sum(value * scale_of[:, t : t + 1], axis=0, keepdims=True)
        return total

    def product(tower, part_of):
        total = 0.0
        for j in (2 * part_of, 2 * part_of + 1):
            s = p.order(j)
            gather[tower].take_halves(s)
            here = pl.ds(pl.multiple_of(s * group, group), group)
            total = total + dot(yq[tower, here, :], hw[here, :], ((0,), (0,)))
        if part_of == 0:
            column = jnp.broadcast_to(along_of[tower], (128, wide)).T[:, 0:1]
            gq[tower] = column * summed_hidden - total
        else:
            gq[tower] -= total

    def resid_half(tower):
        total = summed(0, tower)
        to_owner(tower).wait_recv()
        total = total + zin[tower].astype(F32)
        value = by_tower(qa[...], count, tower).astype(F32) + total
        yq[tower, pl.ds(pl.multiple_of(p.t * n, n), n), :] = value.astype(BF16)
        return value

    mate_down(1, 0)
    mate_down(0, 0)
    back(1, 3).start()
    combine(1, 0)
    mate_down(1, 1)
    combine(0, 0)
    mate_down(0, 1)
    send_sum(0)
    combine(1, 1)
    combine(0, 1)
    isum_hop(3)
    send_sum(1)
    q_resid = [resid_half(0)]
    advance(0)
    isum.take(4)
    own_item = ip[pl.ds(pl.multiple_of(p.z * m, m), m), :].astype(F32)
    i_resid = ia[...].astype(F32) + (own_item + land[0, 3].astype(F32) + land[1, 3].astype(F32))
    i_gain = gain_row(if_)
    i_scale = rms_scale(i_resid)
    sums[p.t, :, dq:] = jnp.sum(i_resid * i_scale * i_gain, axis=0, keepdims=True)
    q_gain = gain_row(qf)
    gain_of = [by_tower(q_gain, count, tower) for tower in range(2)]
    q_resid.append(resid_half(1))
    square = sum(jnp.sum(value * value, axis=-1, keepdims=True) for value in q_resid)
    q_scale = lax.rsqrt(square / dq + EPS)
    for tower in range(2):
        part_sum = jnp.sum(q_resid[tower] * q_scale * gain_of[tower], axis=0, keepdims=True)
        sums[p.t, :, tower * wide : (tower + 1) * wide] = part_sum
    spread(sums, p.t, s1, member)
    proj_copy.wait()
    gathered(sums, s1)
    back(0, 0).start()
    back(0, 1).start()
    advance(1)
    total = sums[0]
    for slot in range(1, parts):
        total = total + sums[slot]
    firsts = [(d % 2) * wide + (d // 2) * block_wide for d in range(count)]
    q_pooled = jnp.concatenate([total[:, at : at + block_wide] for at in firsts], axis=1) / QLEN
    i_pooled = total[:, dq:] / ILEN
    q_e = jnp.sum(dot(split_rows(q_pooled), proj[...]), axis=0, keepdims=True)
    q_norm, i_norm = unit_scale(q_e), unit_scale(i_pooled)
    hats[own, :, :di] = q_e * q_norm
    hats[own, :, di:] = i_pooled * i_norm
    spread(hats, own, s2, replica)
    advance(2)
    gathered(hats, s2)
    back(0, 2).start()
    back(0, 3).start()
    advance(3)
    advance(4)
    index = lax.broadcasted_iota(jnp.int32, (count, 2 * di), 0)
    every = jnp.zeros((count, 2 * di), F32)
    for slot in range(count):
        every = jnp.where(index == slot, hats[slot], every)
    every_query, every_items = every[:, :di], every[:, di:]
    line = lax.broadcasted_iota(jnp.int32, (count, count), 0)
    target = jnp.zeros((count, count), jnp.int32)
    for slot in range(count):
        target = jnp.where(line == slot, positive[slot], target)
    per_row, slopes = contrast(every_query, every_items, ranks[...], target)
    loss[...] = jnp.sum(per_row, axis=0, keepdims=True) / count
    weights = slopes * (LOSS_SCALE / (TAU * count))
    mine = lax.broadcasted_iota(jnp.int32, (count, di), 0) == own
    q_back = jnp.sum(
        jnp.where(mine, dot(weights, every_items, precision=HIGH), 0.0), axis=0, keepdims=True
    )
    column = lax.broadcasted_iota(jnp.int32, (count, count), 1) == own
    i_back = jnp.sum(
        jnp.sum(jnp.where(column, weights, 0.0), axis=1, keepdims=True) * every_query,
        axis=0,
        keepdims=True,
    )
    q_grad_e = unit_back(q_e, q_norm, q_back)
    q_up = jnp.sum(dot(split_rows(q_grad_e), proj[...], ((1,), (1,))), axis=0, keepdims=True) / QLEN
    i_up = unit_back(i_pooled, i_norm, i_back) / ILEN
    along = q_gain * q_up
    along_of = [by_tower(along, count, tower) for tower in range(2)]
    inner = sum(
        jnp.sum(along_of[tower] * q_resid[tower], axis=-1, keepdims=True) for tower in range(2)
    )
    inner = inner / dq
    slope = (q_scale * q_scale * q_scale) * inner
    lane = lax.broadcasted_iota(jnp.int32, (n, 128), 1)
    columns = jnp.where(lane == 0, q_scale, jnp.where(lane == 1, slope, 0.0))
    columns = jnp.concatenate([columns, jnp.zeros((128 - n, 128), F32)], axis=0)
    scal[p.t] = columns.T[:8]
    spread(scal, p.t, s3, member)
    yi[pl.ds(pl.multiple_of(p.z * m, m), m), :] = grad_rows(i_resid, i_scale, i_gain, i_up)
    igather.start(1)
    gathered(scal, s3)
    advance(5)
    advance(6)
    back_got(0)
    back_got(1)
    summed_hidden = scale_hidden()
    advance(7)
    item_grad_hop(1)
    product(0, 0)
    advance(8)
    item_grad_hop(2)
    product(0, 1)
    q_start(0)
    advance(9)
    item_grad_hop(3)
    q_far(0)
    product(1, 0)
    item_grad_hop(4)
    q_near(0)
    product(1, 1)
    q_start(1)
    i_product()
    q_far(1)
    q_own(0)
    i_far()
    q_near(1)
    i_near()
    q_own(1)
    i_own()
    q_finish(0)
    i_finish()
    q_finish(1)

    for j in range(2):
        for b in range(X):
            back(j, b).wait_send()
        for copy in (rows.right(j), rows.left(j), rows.half_right(j), rows.half_left(j)):
            copy.wait_send()
        for q in range(2):
            for way in range(2):
                first(j, q, way).wait_send()
                second(j, q, way).wait_send()
    for q in range(2):
        to_owner(q).wait_send()
    across().wait_send()
    items.drain()
    isum.drain()
    for index in range(3):
        for kind in range(9) if index == 2 else range(5):
            w_send(index, kind).wait_send()
    for index in range(2):
        w_column(index, c).wait_send()
    for kind in range(7):
        v_send(kind).wait_send()
    for tower in range(2):
        gather[tower].drain()
        for j in range(4):
            q_core(tower, j).wait_send()
        for way in range(2):
            q_first(tower, way).wait_send()
            q_second(tower, way).wait_send()

        @pl.when(p.w != tower)
        def _():
            q_tower(tower).wait_send()

    igather.drain()
    for j in range(4):
        i_core(j).wait_send()
    for way in range(2):
        i_first(way).wait_send()
        i_second(way).wait_send()
    for hop in range(1, X):
        i_x(hop).wait_send()


def step(qa, qg, gate, up, down, ia, ig, ig_w, iu_w, id_w, qf, if_, proj, ranks, positive):
    n, dq = qa.shape
    m, di = ia.shape
    f, k = down.shape[0], id_w.shape[0]
    padded = 64 * ((f + 63) // 64)
    vmem, hbm = pl.BlockSpec(memory_space=pltpu.VMEM), pl.BlockSpec(memory_space=pl.ANY)
    smem = pl.BlockSpec(memory_space=pltpu.SMEM)
    all_i = ZR * m
    group = X * n
    parts = X * ZL
    count = ranks.shape[0]
    wide = dq // count
    dma = pltpu.SemaphoreType.DMA
    return pl.pallas_call(
        kernel,
        out_shape=(
            jax.ShapeDtypeStruct((1, 1), F32),
            jax.ShapeDtypeStruct((wide, f), F32),
            jax.ShapeDtypeStruct((wide, k), F32),
        ),
        in_specs=[vmem, vmem, hbm, hbm, hbm] + [vmem] * 7 + [hbm, vmem, smem],
        out_specs=[vmem] * 3,
        scratch_shapes=[
            pltpu.VMEM((2, 3, padded, dq), BF16),
            pltpu.VMEM(down.shape, BF16),
            pltpu.VMEM(proj.shape, BF16),
            pltpu.VMEM((2 * group, dq), BF16),
            pltpu.VMEM((2, group, dq), F32),
            pltpu.VMEM((2, group, f), F32),
            pltpu.VMEM((2, group, f), BF16),
            pltpu.VMEM((2, 2 * group, dq // 2), BF16),
            pltpu.VMEM((2, 2, 2, n // 2, dq // 2), BF16),
            pltpu.VMEM((2, 2, 2, n, dq // 2), BF16),
            pltpu.VMEM((2, n, dq // 2), BF16),
            pltpu.VMEM((2, n, dq // 2), BF16),
            pltpu.VMEM((all_i, di), BF16),
            pltpu.VMEM((3, X * k, di), BF16),
            pltpu.VMEM((all_i, di), BF16),
            pltpu.VMEM((2, 4, m, di), BF16),
            pltpu.VMEM((ZL * group, f), BF16),
            pltpu.VMEM((X, all_i, k), BF16),
            pltpu.VMEM((parts, 1, dq + di), F32),
            pltpu.VMEM((count, 1, 2 * di), F32),
            pltpu.VMEM((parts, 8, 128), F32),
            pltpu.VMEM((2, parts * n, dq // 2), BF16),
            pltpu.VMEM((ZL * group, f), BF16),
            pltpu.VMEM((all_i, di), BF16),
            pltpu.VMEM((2, dq // 2, f), F32),
            pltpu.VMEM((X, di, k), F32),
            pltpu.VMEM((2, 4, wide, f), F32),
            pltpu.VMEM((2, 2, wide // 2, f), F32),
            pltpu.VMEM((2, 2, wide, f), F32),
            pltpu.VMEM((wide, f), F32),
            pltpu.VMEM((4, X, wide, k), F32),
            pltpu.VMEM((2, 2, wide, k), F32),
            pltpu.VMEM((2, X, wide, k), F32),
            pltpu.VMEM((X, wide, k), F32),
            dma((4,)),
            dma((6, 2)),
            dma((5, 2)),
            dma((5, 2, 2)),
            dma((5, 2, 2)),
            dma((9, 3)),
            dma((9, 3)),
            dma((7,)),
            dma((7,)),
            dma((2, X)),
            dma((2, X)),
            dma((2, 4)),
            dma((2, 4)),
            dma((2, 4)),
            dma((2, 4)),
            dma((2,)),
            dma((2,)),
            dma((2,)),
            dma((2, 6, ZL)),
            dma((2, 5, ZL)),
            dma((2, 4)),
            dma((2, 4)),
            dma((2, 9)),
            dma((2, 9)),
            dma((12,)),
            dma((12,)),
        ],
        compiler_params=pltpu.CompilerParams(
            collective_id=0, has_side_effects=True, vmem_limit_bytes=VMEM_LIMIT
        ),
        name="towers_step",
    )(qa, qg, gate, up, down, ia, ig, ig_w, iu_w, id_w, qf, if_, proj, ranks, positive)


def body(
    q_act,
    q_norm_gain,
    q_gate,
    q_up,
    q_down,
    q_final_gain,
    projection,
    i_act,
    i_norm_gain,
    i_gate,
    i_up,
    i_down,
    i_final_gain,
    ranks,
    positive,
):
    loss, q_grad, i_grad = step(
        q_act,
        q_norm_gain,
        q_gate.T,
        q_up.T,
        q_down,
        i_act,
        i_norm_gain,
        i_gate.T,
        i_up.T,
        i_down,
        q_final_gain,
        i_final_gain,
        projection,
        ranks,
        positive,
    )
    return (loss.reshape(()), q_grad.T, i_grad.T)


def solution(mesh):
    in_specs = (
        P(("dp", "tower", "tensor"), None),
        P(),
        P(None, "tensor"),
        P(None, "tensor"),
        P("tensor", None),
        P(),
        P(),
        P(("dp", "tower", "tensor"), None),
        P(),
        P(None, ("tower", "tensor")),
        P(None, ("tower", "tensor")),
        P(("tower", "tensor"), None),
        P(),
        P(),
        P(),
    )
    out_specs = (P(), P("tensor", ("dp", "tower")), P(("tower", "tensor"), "dp"))
    return jax.shard_map(body, mesh=mesh, in_specs=in_specs, out_specs=out_specs, check_vma=False)
```

```python
import functools

import jax
import jax.numpy as jnp
from jax import lax
from jax.experimental import pallas as pl
from jax.experimental.pallas import tpu as pltpu
from jax.sharding import PartitionSpec as P

QLEN = 1536
ILEN = 512
EPS = 1e-06
TAU = 0.05
TEACH = 2.0
LOSS_SCALE = 64.0
HIGH = lax.Precision.HIGHEST
MESH = pl.DeviceIdType.MESH
F32 = jnp.float32
BF16 = jnp.bfloat16

X = 4
ZL = 4
ZR = 8
VMEM_LIMIT = 60 * 1024 * 1024


def rms_scale(values):
    return lax.rsqrt(jnp.mean(values * values, axis=-1, keepdims=True) + EPS)


def dot(left, right, dims=((1,), (0,)), precision=None):
    return lax.dot_general(
        left, right, (dims, ((), ())), preferred_element_type=F32, precision=precision
    )


def remote(src, dst, send, recv, where):
    return pltpu.make_async_remote_copy(
        src_ref=src, dst_ref=dst, send_sem=send, recv_sem=recv, device_id=where, device_id_type=MESH
    )


class Place:
    def __init__(self):
        self.t = lax.axis_index("tensor")
        self.w = lax.axis_index("tower")
        self.a = self.t // X
        self.b = self.t % X
        self.z = self.w * ZL + self.a
        self.bp = (self.b + 1) % X
        self.bm = (self.b + X - 1) % X
        self.bo = (self.b + 2) % X
        self.xp = {"tensor": self.a * X + self.bp}
        self.xm = {"tensor": self.a * X + self.bm}
        self.zp = self.ring(1)
        self.zm = self.ring(ZR - 1)

    def ring(self, step):
        z = (self.z + step) % ZR
        return {"tower": z // ZL, "tensor": (z % ZL) * X + self.b}

    def column(self, row):
        return {"tensor": row * X + self.b}

    def order(self, j):
        near = jnp.minimum(self.a, ZL - 1 - self.a)
        swapped = jnp.where(j == 0, 1, jnp.where(j == 1, 0, j))
        row = jnp.where(near == 1, swapped, j)
        return jnp.where(self.a >= 2, ZL - 1 - row, row)


def rows_of(ref, first, count, unit):
    return ref.at[pl.ds(pl.multiple_of(first, unit), count), :]


class RowGather:
    def __init__(self, place, buf, rows, send, recv):
        self.p, self.buf, self.n, self.send, self.recv = place, buf, rows, send, recv

    def block(self, s, b):
        return rows_of(self.buf, (s * X + b) * self.n, self.n, self.n)

    def half(self, s, b, h):
        n = self.n // 2
        return rows_of(self.buf, (s * X + b) * self.n + h * n, n, n)

    def up(self, s):
        ref = self.block(s, self.p.b)
        where = self.p.column(jnp.minimum(self.p.a + 1, ZL - 1))
        return remote(ref, ref, self.send.at[0, s], self.recv.at[0, s], where)

    def down(self, s):
        ref = self.block(s, self.p.b)
        where = self.p.column(jnp.maximum(self.p.a - 1, 0))
        return remote(ref, ref, self.send.at[1, s], self.recv.at[0, s], where)

    def right(self, s):
        ref = self.block(s, self.p.b)
        return remote(ref, ref, self.send.at[2, s], self.recv.at[1, s], self.p.xp)

    def left(self, s):
        ref = self.block(s, self.p.b)
        return remote(ref, ref, self.send.at[3, s], self.recv.at[2, s], self.p.xm)

    def half_right(self, s):
        ref = self.half(s, self.p.bm, 0)
        return remote(ref, ref, self.send.at[4, s], self.recv.at[3, s], self.p.xp)

    def half_left(self, s):
        ref = self.half(s, self.p.bp, 1)
        return remote(ref, ref, self.send.at[5, s], self.recv.at[4, s], self.p.xm)

    def goes_up(self, s):
        return (s <= self.p.a) & (self.p.a < ZL - 1)

    def goes_down(self, s):
        return (s >= self.p.a) & (self.p.a > 0)

    def take_z(self, s):
        @pl.when(s != self.p.a)
        def _():
            self.up(s).wait_recv()

        @pl.when(self.goes_up(s))
        def _():
            self.up(s).start()

        @pl.when(self.goes_down(s))
        def _():
            self.down(s).start()

        self.right(s).start()
        self.left(s).start()

    def take_x(self, s):
        ref = self.block(s, self.p.bm)
        remote(ref, ref, self.send.at[2, s], self.recv.at[1, s], self.p.xm).wait_recv()
        self.half_right(s).start()
        ref = self.block(s, self.p.bp)
        remote(ref, ref, self.send.at[3, s], self.recv.at[2, s], self.p.xp).wait_recv()
        self.half_left(s).start()

    def take_halves(self, s):
        ref = self.half(s, self.p.bo, 0)
        remote(ref, ref, self.send.at[4, s], self.recv.at[3, s], self.p.xm).wait_recv()
        ref = self.half(s, self.p.bo, 1)
        remote(ref, ref, self.send.at[5, s], self.recv.at[4, s], self.p.xp).wait_recv()

    def drain(self):
        def each(s, _):
            @pl.when(self.goes_up(s))
            def _():
                self.up(s).wait_send()

            @pl.when(self.goes_down(s))
            def _():
                self.down(s).wait_send()

            self.right(s).wait_send()
            self.left(s).wait_send()
            self.half_right(s).wait_send()
            self.half_left(s).wait_send()
            return 0

        lax.fori_loop(0, ZL, each, 0)


class RingGather:
    def __init__(self, place, buf, rows, send, recv):
        self.p, self.buf, self.n, self.send, self.recv = place, buf, rows, send, recv

    def ref(self, z, hop, upward):
        z = (z + 2 * ZR) % ZR
        if hop < 4:
            return rows_of(self.buf, z * self.n, self.n, self.n)
        n = self.n // 2
        return rows_of(self.buf, z * self.n + (0 if upward else n), n, n)

    def copies(self, hop):
        up = self.ref(self.p.z - hop + 1, hop, True)
        down = self.ref(self.p.z + hop - 1, hop, False)
        return (
            remote(up, up, self.send.at[0, hop - 1], self.recv.at[0, hop - 1], self.p.zp),
            remote(down, down, self.send.at[1, hop - 1], self.recv.at[1, hop - 1], self.p.zm),
        )

    def start(self, hop):
        for copy in self.copies(hop):
            copy.start()

    def take(self, hop):
        up = self.ref(self.p.z - hop, hop, True)
        down = self.ref(self.p.z + hop, hop, False)
        remote(up, up, self.send.at[0, hop - 1], self.recv.at[0, hop - 1], self.p.zm).wait_recv()
        remote(down, down, self.send.at[1, hop - 1], self.recv.at[1, hop - 1], self.p.zp).wait_recv()

    def drain(self):
        for hop in range(1, 5):
            for copy in self.copies(hop):
                copy.wait_send()


class RingSum:
    def __init__(self, place, buf, land, rows, send, recv):
        self.p, self.buf, self.land = place, buf, land
        self.n, self.send, self.recv = rows, send, recv

    def part(self, z, half):
        z = (z + 2 * ZR) % ZR
        if half is None:
            return rows_of(self.buf, z * self.n, self.n, self.n)
        n = self.n // 2
        return rows_of(self.buf, z * self.n + half * n, n, n)

    def slot(self, way, hop):
        if hop == 1:
            return self.land.at[way, 0, pl.ds(0, self.n // 2), :]
        return self.land.at[way, hop - 1]

    def copies(self, hop):
        half = (0, 1) if hop == 1 else (None, None)
        up = self.part(self.p.z + 5 - hop, half[0])
        down = self.part(self.p.z - 5 + hop, half[1])
        return (
            remote(up, self.slot(0, hop), self.send.at[0, hop - 1], self.recv.at[0, hop - 1], self.p.zp),
            remote(down, self.slot(1, hop), self.send.at[1, hop - 1], self.recv.at[1, hop - 1], self.p.zm),
        )

    def start(self, hop):
        for copy in self.copies(hop):
            copy.start()

    def take(self, hop):
        for copy in self.copies(hop):
            copy.wait_recv()

    def add(self, hop):
        half = (0, 1) if hop == 1 else (None, None)
        for way, z in ((0, self.p.z + 4 - hop), (1, self.p.z - 4 + hop)):
            ref = self.part(z, half[way])
            ref[...] = (ref[...].astype(F32) + self.slot(way, hop)[...].astype(F32)).astype(BF16)

    def drain(self):
        for hop in range(1, 5):
            for copy in self.copies(hop):
                copy.wait_send()


def gain_row(ref):
    return ref[...].astype(F32).reshape(1, -1)


def normed_rows(act, gain):
    values = act.astype(F32)
    return (values * rms_scale(values) * gain).astype(BF16)


def gated(gate_val, up_val):
    return (jax.nn.silu(gate_val) * up_val).astype(BF16)


def at_step(i, step):
    return pl.when(i == step)


def split_rows(row):
    high = row.astype(BF16).astype(F32)
    rest = row - high
    mid = rest.astype(BF16).astype(F32)
    low = rest - mid
    index = lax.broadcasted_iota(jnp.int32, (8, row.shape[1]), 0)
    out = jnp.where(index == 0, high, jnp.where(index == 1, mid, jnp.where(index == 2, low, 0.0)))
    return out.astype(BF16)


def unit_scale(vec):
    return lax.rsqrt(jnp.sum(vec * vec, axis=-1, keepdims=True) + EPS)


def unit_back(vec, scales, upstream):
    inner = jnp.sum(vec * upstream, axis=-1, keepdims=True)
    return scales * upstream - vec * (scales * scales * scales) * inner


def contrast(query_hat, item_hat, ranks, positive):
    logits = dot(query_hat, item_hat, ((1,), (1,)), HIGH) / TAU
    shifted = logits - 1.0 / TAU
    log_student = shifted - jnp.log(jnp.sum(jnp.exp(shifted), axis=1, keepdims=True))
    teach = -ranks.astype(F32) / TEACH
    log_teacher = teach - jnp.log(jnp.sum(jnp.exp(teach), axis=1, keepdims=True))
    teacher = jnp.exp(log_teacher)
    columns = lax.broadcasted_iota(jnp.int32, logits.shape, 1)
    onehot = (columns == positive).astype(F32)
    per_row = jnp.sum(
        teacher * (log_teacher - log_student) - onehot * log_student, axis=1, keepdims=True
    )
    slopes = 2.0 * jnp.exp(log_student) - onehot - teacher
    return (per_row, slopes)


def grad_rows(resid, scales, gain, upstream):
    along = gain * upstream
    inner = jnp.mean(along * resid, axis=-1, keepdims=True)
    return (scales * along - resid * (scales * scales * scales) * inner).astype(BF16)


def by_tower(values, parts, tower):
    wide = values.shape[1] // parts
    blocks = [values[:, d * wide : (d + 1) * wide] for d in range(tower, parts, 2)]
    return jnp.concatenate(blocks, axis=1)


def kernel(
    qa, qg, gate_hbm, up_hbm, down_hbm, ia, ig, ig_w, iu_w, id_w, qf, if_, proj_hbm, ranks, positive,
    loss, q_out, i_out,
    w, stage, proj, nq, part, gate_val, h2, pm, r1, r2, zs, zin, ni, wi, ip, land, hq, hi,
    sums, hats, scal, yq, hw, yi, gq, gi, qc1, qb1, qb2, qc, ic1, ib1, ib2, ic,
    loads, gs, gr, ss, sr, ws, wr, vs, vr, hs, hr, ias, iar, irs, irr,
    s1, s2, s3, ys, yr, iys, iyr, qs, qv, bs, bv,
):
    p = Place()
    n, dq = qa.shape
    m, di = ia.shape
    f, k = down_hbm.shape[0], id_w.shape[0]
    group = X * n
    h = n // 2
    parts = X * ZL
    count = hats.shape[0]
    block_wide = dq // count
    piece = w.shape[2] // 4
    wide, thin = dq // 2, dq // 4
    dp = lax.axis_index("dp")
    own = dp * 2 + p.w
    y, c = dp // 2, dp % 2
    yp, ym, y2 = (y + 1) % 4, (y + 3) % 4, (y + 2) % 4
    line_y = (y2, yp, ym, y)
    to_yp, to_ym, to_core = {"dp": yp * 2 + c}, {"dp": ym * 2 + c}, {"dp": y * 2 + 1 - c}
    to_y = (to_yp, to_ym)
    to_tower = {"tower": 1 - p.w}
    a2 = (p.a + 2) % ZL
    mate = p.a + 1 - 2 * (p.a % 2)
    to_a2, to_mate = p.column(a2), p.column(mate)

    def member(step):
        return {"tensor": (p.t + step) % parts}

    def replica(step):
        other = (own + step) % count
        return {"dp": other // 2, "tower": other % 2}

    own_weights = [
        pltpu.make_async_copy(ref, dst, loads.at[index])
        for index, (ref, dst) in enumerate(
            (
                (gate_hbm, w.at[0, 0, pl.ds(0, f), :]),
                (up_hbm, w.at[0, 1, pl.ds(0, f), :]),
                (down_hbm, stage),
            )
        )
    ]
    proj_copy = pltpu.make_async_copy(proj_hbm, proj, loads.at[3])
    for copy in own_weights:
        copy.start()
    proj_copy.start()
    barrier = pltpu.get_barrier_semaphore()

    def greet(step, _):
        pl.semaphore_signal(barrier, inc=1, device_id=member(step), device_id_type=MESH)
        pl.semaphore_signal(barrier, inc=1, device_id=replica(step), device_id_type=MESH)
        return 0

    lax.fori_loop(1, parts, greet, 0)
    for where in (p.zp, p.zm):
        pl.semaphore_signal(barrier, inc=1, device_id=where, device_id_type=MESH)
    for index in range(3):
        w[0, index, f:, :] = jnp.zeros((w.shape[2] - f, dq), BF16)
    nq[pl.ds(pl.multiple_of(p.b * n, n), n), :] = normed_rows(qa[...], gain_row(qg))
    ni[pl.ds(pl.multiple_of(p.z * m, m), m), :] = normed_rows(ia[...], gain_row(ig))
    for index, ref in enumerate((ig_w, iu_w, id_w)):
        wi[index, pl.ds(pl.multiple_of(p.b * k, k), k), :] = ref[...]
    pl.semaphore_wait(barrier, 2 * (parts - 1) + 2)

    rows = RowGather(p, nq, n, gs, gr)
    items = RingGather(p, ni, m, ias, iar)
    isum = RingSum(p, ip, land, m, irs, irr)

    def across():
        return remote(rows.block(0, p.b), rows.block(1, p.b), gs.at[0, 0], gr.at[0, 0], to_a2)

    def wpiece(which, index, line, core):
        first = pl.multiple_of(line * piece, piece)
        return w.at[which, index, pl.ds(first, piece), pl.ds(pl.multiple_of(core * wide, wide), wide)]

    def whalf(index, line, part_of):
        first = pl.multiple_of(line * piece, piece)
        column = pl.multiple_of(c * wide + part_of * thin, thin)
        return w.at[1, index, pl.ds(first, piece), pl.ds(column, thin)]

    def w_send(index, kind):
        here = wpiece(1, index, y, c)
        low, high = wpiece(1, index, ym, c), wpiece(1, index, yp, c)
        src, dst, where = (
            (wpiece(0, index, y, c), here, to_mate),
            (here, here, to_yp),
            (here, here, to_ym),
            (whalf(index, ym, 0), whalf(index, ym, 0), to_yp),
            (whalf(index, yp, 1), whalf(index, yp, 1), to_ym),
            (here, here, to_core),
            (low, low, to_core),
            (high, high, to_core),
            (wpiece(1, index, y2, c), wpiece(1, index, y2, c), to_core),
        )[kind]
        return remote(src, dst, ws.at[kind, index], wr.at[kind, index], where)

    def w_got(index, kind):
        dst = (
            wpiece(1, index, y, c),
            wpiece(1, index, ym, c),
            wpiece(1, index, yp, c),
            whalf(index, y2, 0),
            whalf(index, y2, 1),
            wpiece(1, index, y, 1 - c),
            wpiece(1, index, ym, 1 - c),
            wpiece(1, index, yp, 1 - c),
            wpiece(1, index, y2, 1 - c),
        )[kind]
        remote(dst, dst, ws.at[kind, index], wr.at[kind, index], to_core).wait_recv()

    def w_near(index):
        w_got(index, 0)
        for kind in (1, 2, 5) if index == 2 else (1, 2):
            w_send(index, kind).start()

    def w_ring(index):
        w_got(index, 1)
        w_send(index, 3).start()
        w_got(index, 2)
        w_send(index, 4).start()
        if index == 2:
            w_send(index, 6).start()
            w_send(index, 7).start()

    def w_far(index):
        w_got(index, 3)
        w_got(index, 4)
        if index == 2:
            w_send(index, 8).start()
        else:
            w_column(index, c).start()

    def w_column(index, core):
        ref = w.at[1, index, :, pl.ds(pl.multiple_of(core * wide, wide), wide)]
        return remote(ref, ref, ws.at[8, index], wr.at[8, index], to_core)

    def w_done(index):
        if index < 2:
            w_column(index, 1 - c).wait_recv()
        else:
            for kind in (5, 6, 7, 8):
                w_got(index, kind)

    def vpiece(b, core):
        column = pl.multiple_of(core * (di // 2), di // 2)
        return wi.at[:, pl.ds(pl.multiple_of(b * k, k), k), pl.ds(column, di // 2)]

    def vhalf(b, part_of):
        first = pl.multiple_of(b * k + part_of * (k // 2), k // 2)
        column = pl.multiple_of(c * (di // 2), di // 2)
        return wi.at[:, pl.ds(first, k // 2), pl.ds(column, di // 2)]

    def v_send(kind):
        ref, where = (
            (vpiece(p.b, c), p.xp),
            (vpiece(p.b, c), p.xm),
            (vhalf(p.bm, 0), p.xp),
            (vhalf(p.bp, 1), p.xm),
            (vpiece(p.bm, c), to_core),
            (vpiece(p.bp, c), to_core),
            (vpiece(p.bo, c), to_core),
        )[kind]
        return remote(ref, ref, vs.at[kind], vr.at[kind], where)

    def v_got(kind):
        ref = (
            vpiece(p.bm, c),
            vpiece(p.bp, c),
            vhalf(p.bo, 0),
            vhalf(p.bo, 1),
            vpiece(p.bm, 1 - c),
            vpiece(p.bp, 1 - c),
            vpiece(p.bo, 1 - c),
        )[kind]
        remote(ref, ref, vs.at[kind], vr.at[kind], to_core).wait_recv()

    def block(j, q, b):
        return rows_of(pm.at[q], (j * X + b) * n, n, n)

    def half(j, q, b, part_of):
        return rows_of(pm.at[q], (j * X + b) * n + part_of * h, h, h)

    def first(j, q, way):
        src = half(j, q, p.bo, way)
        where = (p.xp, p.xm)[way]
        return remote(src, r1.at[way, j, q], ss.at[way, j, q], sr.at[way, j, q], where)

    def second(j, q, way):
        src = block(j, q, (p.bp, p.bm)[way])
        where = (p.xp, p.xm)[way]
        return remote(src, r2.at[way, j, q], ss.at[2 + way, j, q], sr.at[2 + way, j, q], where)

    def to_owner(q):
        return remote(zs.at[q], zin.at[q], ss.at[4, 0, q], sr.at[4, 0, q], to_a2)

    def back(j):
        s = (p.a, a2)[j]
        dst = hq.at[pl.ds(pl.multiple_of(s * group, group), group), :]
        return remote(h2.at[j], dst, hs.at[j], hr.at[j], to_mate)

    def back_got(j):
        other = (mate, (mate + 2) % ZL)[j]
        dst = hq.at[pl.ds(pl.multiple_of(other * group, group), group), :]
        remote(h2.at[j], dst, hs.at[j], hr.at[j], to_mate).wait_recv()

    def rows_in(j):
        return nq[j * group : (j + 1) * group, :]

    def own_units(j):
        left = rows_in(j)
        value = gated(
            dot(left, w[0, 0, :f, :], ((1,), (1,))), dot(left, w[0, 1, :f, :], ((1,), (1,)))
        )
        hq[pl.ds(pl.multiple_of((p.a, a2)[j] * group, group), group), :] = value
        part[j] = dot(value, w[0, 2, :f, :])

    def mate_gate(j):
        gate_val[j] = dot(rows_in(j), w[1, 0, :f, :], ((1,), (1,)))

    def mate_up(j):
        h2[j] = gated(gate_val[j], dot(rows_in(j), w[1, 1, :f, :], ((1,), (1,))))
        back(j).start()

    def mate_down(j, q):
        columns = slice(q * wide, (q + 1) * wide)
        total = part[j, :, columns] + dot(h2[j], w[1, 2, :f, columns])
        pm[q, j * group : (j + 1) * group, :] = total.astype(BF16)
        first(j, q, 0).start()
        first(j, q, 1).start()

    def combine(j, q):
        for way in range(2):
            first(j, q, way).wait_recv()
            ref = half(j, q, (p.bp, p.bm)[way], way)
            ref[...] = (ref[...].astype(F32) + r1[way, j, q].astype(F32)).astype(BF16)
            second(j, q, way).start()

    def summed(j, q):
        second(j, q, 0).wait_recv()
        second(j, q, 1).wait_recv()
        total = block(j, q, p.b)[...].astype(F32)
        return total + r2[0, j, q].astype(F32) + r2[1, j, q].astype(F32)

    def send_sum(q):
        zs[q] = summed(1, q).astype(BF16)
        to_owner(q).start()

    def item_hop(hop):
        items.take(hop)
        if hop < 4:
            items.start(hop + 1)

    def isum_hop(hop):
        isum.take(hop)
        isum.add(hop)
        isum.start(hop + 1)

    def item_product():
        left = ni[...]
        partial = 0.0
        for b in range(X):
            here = slice(b * k, (b + 1) * k)
            value = gated(
                dot(left, wi[0, here, :], ((1,), (1,))), dot(left, wi[1, here, :], ((1,), (1,)))
            )
            hi[b] = value
            partial = partial + dot(value, wi[2, here, :])
        ip[...] = partial.astype(BF16)
        isum.start(1)

    rows.right(0).start()
    rows.left(0).start()
    items.start(1)
    own_weights[0].wait()
    w_send(0, 0).start()
    across().start()
    v_send(0).start()
    v_send(1).start()
    own_weights[1].wait()
    own_weights[2].wait()
    for first_row in range(0, f, 112):
        chunk = stage[first_row : first_row + 112, :]
        for tower in range(2):
            columns = slice(tower * wide, (tower + 1) * wide)
            w[0, 2, first_row : first_row + 112, columns] = by_tower(chunk, count, tower)
    rows.take_x(0)
    item_hop(1)
    w_near(0)
    w_send(1, 0).start()
    rows.take_halves(0)
    own_units(0)
    remote(rows.block(0, p.b), rows.block(1, p.b), gs.at[0, 0], gr.at[0, 0], to_a2).wait_recv()
    rows.right(1).start()
    rows.left(1).start()
    item_hop(2)
    w_ring(0)
    w_near(1)
    w_send(2, 0).start()
    for kind in range(2):
        v_got(kind)
        v_send(2 + kind).start()
        v_send(4 + kind).start()
    item_hop(3)
    w_far(0)
    rows.take_x(1)
    v_got(2)
    v_got(3)
    v_send(6).start()
    w_ring(1)
    item_hop(4)
    for kind in (4, 5, 6):
        v_got(kind)
    w_near(2)
    item_product()
    w_far(1)
    w_done(0)
    mate_gate(0)
    rows.take_halves(1)
    mate_gate(1)
    isum_hop(1)
    w_ring(2)
    own_units(1)
    w_done(1)
    mate_up(1)
    isum_hop(2)
    w_far(2)
    mate_up(0)
    w_done(2)
    def spread(buf, mine, sems, partner):
        def each(hop, _):
            remote(buf.at[mine], buf.at[mine], sems.at[0], sems.at[1], partner(hop)).start()
            return 0

        lax.fori_loop(1, buf.shape[0], each, 0)

    def gathered(buf, sems):
        ref = buf.at[pl.ds(0, buf.shape[0] - 1)]
        remote(ref, ref, sems.at[0], sems.at[1], member(1)).wait()

    def q_rows(tower, line_of, core):
        return rows_of(gq.at[tower], (line_of * 2 + core) * block_wide, block_wide, block_wide)

    def q_half(tower, line_of, way):
        first = (line_of * 2 + c) * block_wide + way * (block_wide // 2)
        return rows_of(gq.at[tower], first, block_wide // 2, block_wide // 2)

    def q_core(tower, j):
        src = q_rows(tower, line_y[j], 1 - c)
        return remote(src, qc1.at[tower, j], qs.at[tower, j], qv.at[tower, j], to_core)

    def q_first(tower, way):
        src, dst = q_half(tower, y2, way), qb1.at[tower, way]
        return remote(src, dst, qs.at[tower, 4 + way], qv.at[tower, 4 + way], to_y[way])

    def q_second(tower, way):
        src, dst = q_rows(tower, (yp, ym)[way], c), qb2.at[tower, way]
        return remote(src, dst, qs.at[tower, 6 + way], qv.at[tower, 6 + way], to_y[way])

    def q_tower(tower):
        return remote(q_rows(tower, y, c), qc, qs.at[tower, 8], qv.at[tower, 8], to_tower)

    def q_start(tower):
        for j in range(4):
            q_core(tower, j).start()

    def q_far(tower):
        q_core(tower, 0).wait_recv()
        ref = q_rows(tower, y2, c)
        ref[...] += qc1[tower, 0]
        for way in range(2):
            q_first(tower, way).start()

    def q_near(tower):
        for way in range(2):
            q_core(tower, 1 + way).wait_recv()
            ref = q_rows(tower, (yp, ym)[way], c)
            ref[...] += qc1[tower, 1 + way]
            q_first(tower, way).wait_recv()
            ref = q_half(tower, (yp, ym)[way], way)
            ref[...] += qb1[tower, way]
            q_second(tower, way).start()

    def q_own(tower):
        q_core(tower, 3).wait_recv()
        for way in range(2):
            q_second(tower, way).wait_recv()
        ref = q_rows(tower, y, c)
        ref[...] = ref[...] + qc1[tower, 3] + qb2[tower, 0] + qb2[tower, 1]

        @pl.when(p.w != tower)
        def _():
            q_tower(tower).start()

    def q_finish(tower):
        @pl.when(p.w == tower)
        def _():
            q_tower(tower).wait_recv()
            q_out[...] = q_rows(tower, y, c)[...] + qc[...]

    def i_rows(line_of, core):
        first = pl.multiple_of((line_of * 2 + core) * block_wide, block_wide)
        return gi.at[:, pl.ds(first, block_wide), :]

    def i_half(line_of, way):
        first = pl.multiple_of((line_of * 2 + c) * block_wide, block_wide)
        return gi.at[pl.ds(way * 2, 2), pl.ds(first, block_wide), :]

    def i_slab(b):
        return gi.at[b, pl.ds(pl.multiple_of((y * 2 + c) * block_wide, block_wide), block_wide), :]

    def i_core(j):
        return remote(i_rows(line_y[j], 1 - c), ic1.at[j], bs.at[j], bv.at[j], to_core)

    def i_first(way):
        return remote(i_half(y2, way), ib1.at[way], bs.at[4 + way], bv.at[4 + way], to_y[way])

    def i_second(way):
        src = i_rows((yp, ym)[way], c)
        return remote(src, ib2.at[way], bs.at[6 + way], bv.at[6 + way], to_y[way])

    def i_x(hop):
        other = (p.b + hop) % X
        where = {"tensor": p.a * X + other}
        return remote(i_slab(other), ic.at[p.b], bs.at[8 + hop], bv.at[8 + p.b], where)

    def i_product():
        for b in range(X):
            gi[b] = dot(yi[...], hi[b], ((0,), (0,)))
        for j in range(4):
            i_core(j).start()

    def i_far():
        for j in range(4):
            i_core(j).wait_recv()
            ref = i_rows(line_y[j], c)
            ref[...] += ic1[j]
        for way in range(2):
            i_first(way).start()

    def i_near():
        for way in range(2):
            i_first(way).wait_recv()
            ref = i_half((yp, ym)[way], way)
            ref[...] += ib1[way]
            i_second(way).start()

    def i_own():
        for way in range(2):
            i_second(way).wait_recv()
        ref = i_rows(y, c)
        ref[...] = ref[...] + ib2[0] + ib2[1]
        for hop in range(1, X):
            i_x(hop).start()

    def i_finish():
        total = i_slab(p.b)[...]
        for hop in range(1, X):
            other = (p.b + hop) % X
            remote(i_slab(other), ic.at[other], bs.at[8 + hop], bv.at[8 + other], p.xp).wait_recv()
            total = total + ic[other]
        i_out[...] = total

    gather = [RowGather(p, yq.at[tower], n, ys.at[tower], yr.at[tower]) for tower in range(2)]
    igather = RingGather(p, yi, m, iys, iyr)

    steps = (0, 1, 4, 2, 3, 5, 6, 7)

    def advance(index):
        if index < len(steps):
            g = steps[index]
            gather[g // ZL].take_z(p.order(g % ZL))
        if 0 <= index - 2 < len(steps):
            g = steps[index - 2]
            gather[g // ZL].take_x(p.order(g % ZL))

    def item_grad_hop(hop):
        igather.take(hop)
        if hop < 4:
            igather.start(hop + 1)

    def scale_hidden():
        line = lax.broadcasted_iota(jnp.int32, (128, 128), 0)
        tiles = [jnp.zeros((128, 128), F32)] * 2
        for t in range(parts):
            for kind in range(2):
                tiles[kind] = jnp.where(line == t, scal[t, kind : kind + 1, :], tiles[kind])
        scale_of, slope_of = tiles[0].T[:n], tiles[1].T[:n]
        total = jnp.zeros((1, f), F32)
        for t in range(parts):
            here = slice(t * n, (t + 1) * n)
            value = hq[here, :].astype(F32)
            hw[here, :] = (value * slope_of[:, t : t + 1]).astype(BF16)
            total = total + jnp.sum(value * scale_of[:, t : t + 1], axis=0, keepdims=True)
        return total

    def product(tower, part_of):
        total = 0.0
        for j in (2 * part_of, 2 * part_of + 1):
            s = p.order(j)
            gather[tower].take_halves(s)
            here = pl.ds(pl.multiple_of(s * group, group), group)
            total = total + dot(yq[tower, here, :], hw[here, :], ((0,), (0,)))
        if part_of == 0:
            column = jnp.broadcast_to(along_of[tower], (128, wide)).T[:, 0:1]
            gq[tower] = column * summed_hidden - total
        else:
            gq[tower] -= total

    def resid_half(tower):
        total = summed(0, tower)
        to_owner(tower).wait_recv()
        total = total + zin[tower].astype(F32)
        value = by_tower(qa[...], count, tower).astype(F32) + total
        yq[tower, pl.ds(pl.multiple_of(p.t * n, n), n), :] = value.astype(BF16)
        return value

    mate_down(1, 0)
    mate_down(0, 0)
    combine(1, 0)
    mate_down(1, 1)
    combine(0, 0)
    mate_down(0, 1)
    send_sum(0)
    combine(1, 1)
    combine(0, 1)
    isum_hop(3)
    send_sum(1)
    q_resid = [resid_half(0)]
    advance(0)
    isum.take(4)
    own_item = ip[pl.ds(pl.multiple_of(p.z * m, m), m), :].astype(F32)
    i_resid = ia[...].astype(F32) + (own_item + land[0, 3].astype(F32) + land[1, 3].astype(F32))
    i_gain = gain_row(if_)
    i_scale = rms_scale(i_resid)
    sums[p.t, :, dq:] = jnp.sum(i_resid * i_scale * i_gain, axis=0, keepdims=True)
    q_gain = gain_row(qf)
    gain_of = [by_tower(q_gain, count, tower) for tower in range(2)]
    advance(1)
    q_resid.append(resid_half(1))
    square = sum(jnp.sum(value * value, axis=-1, keepdims=True) for value in q_resid)
    q_scale = lax.rsqrt(square / dq + EPS)
    for tower in range(2):
        part_sum = jnp.sum(q_resid[tower] * q_scale * gain_of[tower], axis=0, keepdims=True)
        sums[p.t, :, tower * wide : (tower + 1) * wide] = part_sum
    spread(sums, p.t, s1, member)
    advance(2)
    proj_copy.wait()
    gathered(sums, s1)
    advance(3)
    total = sums[0]
    for slot in range(1, parts):
        total = total + sums[slot]
    firsts = [(d % 2) * wide + (d // 2) * block_wide for d in range(count)]
    q_pooled = jnp.concatenate([total[:, at : at + block_wide] for at in firsts], axis=1) / QLEN
    i_pooled = total[:, dq:] / ILEN
    q_e = jnp.sum(dot(split_rows(q_pooled), proj[...]), axis=0, keepdims=True)
    q_norm, i_norm = unit_scale(q_e), unit_scale(i_pooled)
    hats[own, :, :di] = q_e * q_norm
    hats[own, :, di:] = i_pooled * i_norm
    spread(hats, own, s2, replica)
    advance(4)
    gathered(hats, s2)
    index = lax.broadcasted_iota(jnp.int32, (count, 2 * di), 0)
    every = jnp.zeros((count, 2 * di), F32)
    for slot in range(count):
        every = jnp.where(index == slot, hats[slot], every)
    every_query, every_items = every[:, :di], every[:, di:]
    line = lax.broadcasted_iota(jnp.int32, (count, count), 0)
    target = jnp.zeros((count, count), jnp.int32)
    for slot in range(count):
        target = jnp.where(line == slot, positive[slot], target)
    per_row, slopes = contrast(every_query, every_items, ranks[...], target)
    advance(5)
    loss[...] = jnp.sum(per_row, axis=0, keepdims=True) / count
    weights = slopes * (LOSS_SCALE / (TAU * count))
    mine = lax.broadcasted_iota(jnp.int32, (count, di), 0) == own
    q_back = jnp.sum(
        jnp.where(mine, dot(weights, every_items, precision=HIGH), 0.0), axis=0, keepdims=True
    )
    column = lax.broadcasted_iota(jnp.int32, (count, count), 1) == own
    i_back = jnp.sum(
        jnp.sum(jnp.where(column, weights, 0.0), axis=1, keepdims=True) * every_query,
        axis=0,
        keepdims=True,
    )
    advance(6)
    q_grad_e = unit_back(q_e, q_norm, q_back)
    q_up = jnp.sum(dot(split_rows(q_grad_e), proj[...], ((1,), (1,))), axis=0, keepdims=True) / QLEN
    i_up = unit_back(i_pooled, i_norm, i_back) / ILEN
    advance(7)
    along = q_gain * q_up
    along_of = [by_tower(along, count, tower) for tower in range(2)]
    inner = sum(
        jnp.sum(along_of[tower] * q_resid[tower], axis=-1, keepdims=True) for tower in range(2)
    )
    inner = inner / dq
    slope = (q_scale * q_scale * q_scale) * inner
    lane = lax.broadcasted_iota(jnp.int32, (n, 128), 1)
    columns = jnp.where(lane == 0, q_scale, jnp.where(lane == 1, slope, 0.0))
    columns = jnp.concatenate([columns, jnp.zeros((128 - n, 128), F32)], axis=0)
    scal[p.t] = columns.T[:8]
    spread(scal, p.t, s3, member)
    yi[pl.ds(pl.multiple_of(p.z * m, m), m), :] = grad_rows(i_resid, i_scale, i_gain, i_up)
    igather.start(1)
    gathered(scal, s3)
    advance(8)
    back_got(0)
    back_got(1)
    summed_hidden = scale_hidden()
    advance(9)
    item_grad_hop(1)
    product(0, 0)
    item_grad_hop(2)
    product(0, 1)
    q_start(0)
    item_grad_hop(3)
    product(1, 0)
    q_far(0)
    item_grad_hop(4)
    q_near(0)
    product(1, 1)
    q_start(1)
    i_product()
    q_far(1)
    q_own(0)
    i_far()
    q_near(1)
    i_near()
    q_own(1)
    i_own()
    q_finish(0)
    i_finish()
    q_finish(1)

    for j in range(2):
        back(j).wait_send()
        for copy in (rows.right(j), rows.left(j), rows.half_right(j), rows.half_left(j)):
            copy.wait_send()
        for q in range(2):
            for way in range(2):
                first(j, q, way).wait_send()
                second(j, q, way).wait_send()
    for q in range(2):
        to_owner(q).wait_send()
    across().wait_send()
    items.drain()
    isum.drain()
    for index in range(3):
        for kind in range(9) if index == 2 else range(5):
            w_send(index, kind).wait_send()
    for index in range(2):
        w_column(index, c).wait_send()
    for kind in range(7):
        v_send(kind).wait_send()
    for tower in range(2):
        gather[tower].drain()
        for j in range(4):
            q_core(tower, j).wait_send()
        for way in range(2):
            q_first(tower, way).wait_send()
            q_second(tower, way).wait_send()

        @pl.when(p.w != tower)
        def _():
            q_tower(tower).wait_send()

    igather.drain()
    for j in range(4):
        i_core(j).wait_send()
    for way in range(2):
        i_first(way).wait_send()
        i_second(way).wait_send()
    for hop in range(1, X):
        i_x(hop).wait_send()


def step(qa, qg, gate, up, down, ia, ig, ig_w, iu_w, id_w, qf, if_, proj, ranks, positive):
    n, dq = qa.shape
    m, di = ia.shape
    f, k = down.shape[0], id_w.shape[0]
    padded = 64 * ((f + 63) // 64)
    vmem, hbm = pl.BlockSpec(memory_space=pltpu.VMEM), pl.BlockSpec(memory_space=pl.ANY)
    smem = pl.BlockSpec(memory_space=pltpu.SMEM)
    all_i = ZR * m
    group = X * n
    parts = X * ZL
    count = ranks.shape[0]
    wide = dq // count
    dma = pltpu.SemaphoreType.DMA
    return pl.pallas_call(
        kernel,
        out_shape=(
            jax.ShapeDtypeStruct((1, 1), F32),
            jax.ShapeDtypeStruct((wide, f), F32),
            jax.ShapeDtypeStruct((wide, k), F32),
        ),
        in_specs=[vmem, vmem, hbm, hbm, hbm] + [vmem] * 7 + [hbm, vmem, smem],
        out_specs=[vmem] * 3,
        scratch_shapes=[
            pltpu.VMEM((2, 3, padded, dq), BF16),
            pltpu.VMEM(down.shape, BF16),
            pltpu.VMEM(proj.shape, BF16),
            pltpu.VMEM((2 * group, dq), BF16),
            pltpu.VMEM((2, group, dq), F32),
            pltpu.VMEM((2, group, f), F32),
            pltpu.VMEM((2, group, f), BF16),
            pltpu.VMEM((2, 2 * group, dq // 2), BF16),
            pltpu.VMEM((2, 2, 2, n // 2, dq // 2), BF16),
            pltpu.VMEM((2, 2, 2, n, dq // 2), BF16),
            pltpu.VMEM((2, n, dq // 2), BF16),
            pltpu.VMEM((2, n, dq // 2), BF16),
            pltpu.VMEM((all_i, di), BF16),
            pltpu.VMEM((3, X * k, di), BF16),
            pltpu.VMEM((all_i, di), BF16),
            pltpu.VMEM((2, 4, m, di), BF16),
            pltpu.VMEM((ZL * group, f), BF16),
            pltpu.VMEM((X, all_i, k), BF16),
            pltpu.VMEM((parts, 1, dq + di), F32),
            pltpu.VMEM((count, 1, 2 * di), F32),
            pltpu.VMEM((parts, 8, 128), F32),
            pltpu.VMEM((2, parts * n, dq // 2), BF16),
            pltpu.VMEM((ZL * group, f), BF16),
            pltpu.VMEM((all_i, di), BF16),
            pltpu.VMEM((2, dq // 2, f), F32),
            pltpu.VMEM((X, di, k), F32),
            pltpu.VMEM((2, 4, wide, f), F32),
            pltpu.VMEM((2, 2, wide // 2, f), F32),
            pltpu.VMEM((2, 2, wide, f), F32),
            pltpu.VMEM((wide, f), F32),
            pltpu.VMEM((4, X, wide, k), F32),
            pltpu.VMEM((2, 2, wide, k), F32),
            pltpu.VMEM((2, X, wide, k), F32),
            pltpu.VMEM((X, wide, k), F32),
            dma((4,)),
            dma((6, 2)),
            dma((5, 2)),
            dma((5, 2, 2)),
            dma((5, 2, 2)),
            dma((9, 3)),
            dma((9, 3)),
            dma((7,)),
            dma((7,)),
            dma((2,)),
            dma((2,)),
            dma((2, 4)),
            dma((2, 4)),
            dma((2, 4)),
            dma((2, 4)),
            dma((2,)),
            dma((2,)),
            dma((2,)),
            dma((2, 6, ZL)),
            dma((2, 5, ZL)),
            dma((2, 4)),
            dma((2, 4)),
            dma((2, 9)),
            dma((2, 9)),
            dma((12,)),
            dma((12,)),
        ],
        compiler_params=pltpu.CompilerParams(
            collective_id=0, has_side_effects=True, vmem_limit_bytes=VMEM_LIMIT
        ),
        name="towers_step",
    )(qa, qg, gate, up, down, ia, ig, ig_w, iu_w, id_w, qf, if_, proj, ranks, positive)


def body(
    q_act,
    q_norm_gain,
    q_gate,
    q_up,
    q_down,
    q_final_gain,
    projection,
    i_act,
    i_norm_gain,
    i_gate,
    i_up,
    i_down,
    i_final_gain,
    ranks,
    positive,
):
    loss, q_grad, i_grad = step(
        q_act,
        q_norm_gain,
        q_gate.T,
        q_up.T,
        q_down,
        i_act,
        i_norm_gain,
        i_gate.T,
        i_up.T,
        i_down,
        q_final_gain,
        i_final_gain,
        projection,
        ranks,
        positive,
    )
    return (loss.reshape(()), q_grad.T, i_grad.T)


def solution(mesh):
    in_specs = (
        P(("dp", "tower", "tensor"), None),
        P(),
        P(None, "tensor"),
        P(None, "tensor"),
        P("tensor", None),
        P(),
        P(),
        P(("dp", "tower", "tensor"), None),
        P(),
        P(None, ("tower", "tensor")),
        P(None, ("tower", "tensor")),
        P(("tower", "tensor"), None),
        P(),
        P(),
        P(),
    )
    out_specs = (P(), P("tensor", ("dp", "tower")), P(("tower", "tensor"), "dp"))
    return jax.shard_map(body, mesh=mesh, in_specs=in_specs, out_specs=out_specs, check_vma=False)
```

```python
import functools

import jax
import jax.numpy as jnp
from jax import lax
from jax.experimental import pallas as pl
from jax.experimental.pallas import tpu as pltpu
from jax.sharding import PartitionSpec as P

QLEN = 1536
ILEN = 512
EPS = 1e-06
TAU = 0.05
TEACH = 2.0
LOSS_SCALE = 64.0
HIGH = lax.Precision.HIGHEST
MESH = pl.DeviceIdType.MESH
F32 = jnp.float32
BF16 = jnp.bfloat16

X = 4
ZL = 4
ZR = 8
VMEM_LIMIT = 60 * 1024 * 1024


def rms_scale(values):
    return lax.rsqrt(jnp.mean(values * values, axis=-1, keepdims=True) + EPS)


def dot(left, right, dims=((1,), (0,)), precision=None):
    return lax.dot_general(
        left, right, (dims, ((), ())), preferred_element_type=F32, precision=precision
    )


def remote(src, dst, send, recv, where):
    return pltpu.make_async_remote_copy(
        src_ref=src, dst_ref=dst, send_sem=send, recv_sem=recv, device_id=where, device_id_type=MESH
    )


class Place:
    def __init__(self):
        self.t = lax.axis_index("tensor")
        self.w = lax.axis_index("tower")
        self.a = self.t // X
        self.b = self.t % X
        self.z = self.w * ZL + self.a
        self.bp = (self.b + 1) % X
        self.bm = (self.b + X - 1) % X
        self.bo = (self.b + 2) % X
        self.xp = {"tensor": self.a * X + self.bp}
        self.xm = {"tensor": self.a * X + self.bm}
        self.zp = self.ring(1)
        self.zm = self.ring(ZR - 1)

    def ring(self, step):
        z = (self.z + step) % ZR
        return {"tower": z // ZL, "tensor": (z % ZL) * X + self.b}

    def column(self, row):
        return {"tensor": row * X + self.b}

    def order(self, j):
        near = jnp.minimum(self.a, ZL - 1 - self.a)
        swapped = jnp.where(j == 0, 1, jnp.where(j == 1, 0, j))
        row = jnp.where(near == 1, swapped, j)
        return jnp.where(self.a >= 2, ZL - 1 - row, row)


def rows_of(ref, first, count, unit):
    return ref.at[pl.ds(pl.multiple_of(first, unit), count), :]


class RowGather:
    def __init__(self, place, buf, rows, send, recv):
        self.p, self.buf, self.n, self.send, self.recv = place, buf, rows, send, recv

    def block(self, s, b):
        return rows_of(self.buf, (s * X + b) * self.n, self.n, self.n)

    def half(self, s, b, h):
        n = self.n // 2
        return rows_of(self.buf, (s * X + b) * self.n + h * n, n, n)

    def up(self, s):
        ref = self.block(s, self.p.b)
        where = self.p.column(jnp.minimum(self.p.a + 1, ZL - 1))
        return remote(ref, ref, self.send.at[0, s], self.recv.at[0, s], where)

    def down(self, s):
        ref = self.block(s, self.p.b)
        where = self.p.column(jnp.maximum(self.p.a - 1, 0))
        return remote(ref, ref, self.send.at[1, s], self.recv.at[0, s], where)

    def right(self, s):
        ref = self.block(s, self.p.b)
        return remote(ref, ref, self.send.at[2, s], self.recv.at[1, s], self.p.xp)

    def left(self, s):
        ref = self.block(s, self.p.b)
        return remote(ref, ref, self.send.at[3, s], self.recv.at[2, s], self.p.xm)

    def half_right(self, s):
        ref = self.half(s, self.p.bm, 0)
        return remote(ref, ref, self.send.at[4, s], self.recv.at[3, s], self.p.xp)

    def half_left(self, s):
        ref = self.half(s, self.p.bp, 1)
        return remote(ref, ref, self.send.at[5, s], self.recv.at[4, s], self.p.xm)

    def goes_up(self, s):
        return (s <= self.p.a) & (self.p.a < ZL - 1)

    def goes_down(self, s):
        return (s >= self.p.a) & (self.p.a > 0)

    def take_z(self, s):
        @pl.when(s != self.p.a)
        def _():
            self.up(s).wait_recv()

        @pl.when(self.goes_up(s))
        def _():
            self.up(s).start()

        @pl.when(self.goes_down(s))
        def _():
            self.down(s).start()

        self.right(s).start()
        self.left(s).start()

    def take_x(self, s):
        ref = self.block(s, self.p.bm)
        remote(ref, ref, self.send.at[2, s], self.recv.at[1, s], self.p.xm).wait_recv()
        self.half_right(s).start()
        ref = self.block(s, self.p.bp)
        remote(ref, ref, self.send.at[3, s], self.recv.at[2, s], self.p.xp).wait_recv()
        self.half_left(s).start()

    def take_halves(self, s):
        ref = self.half(s, self.p.bo, 0)
        remote(ref, ref, self.send.at[4, s], self.recv.at[3, s], self.p.xm).wait_recv()
        ref = self.half(s, self.p.bo, 1)
        remote(ref, ref, self.send.at[5, s], self.recv.at[4, s], self.p.xp).wait_recv()

    def drain(self):
        def each(s, _):
            @pl.when(self.goes_up(s))
            def _():
                self.up(s).wait_send()

            @pl.when(self.goes_down(s))
            def _():
                self.down(s).wait_send()

            self.right(s).wait_send()
            self.left(s).wait_send()
            self.half_right(s).wait_send()
            self.half_left(s).wait_send()
            return 0

        lax.fori_loop(0, ZL, each, 0)


class RingGather:
    def __init__(self, place, buf, rows, send, recv):
        self.p, self.buf, self.n, self.send, self.recv = place, buf, rows, send, recv

    def ref(self, z, hop, upward):
        z = (z + 2 * ZR) % ZR
        if hop < 4:
            return rows_of(self.buf, z * self.n, self.n, self.n)
        n = self.n // 2
        return rows_of(self.buf, z * self.n + (0 if upward else n), n, n)

    def copies(self, hop):
        up = self.ref(self.p.z - hop + 1, hop, True)
        down = self.ref(self.p.z + hop - 1, hop, False)
        return (
            remote(up, up, self.send.at[0, hop - 1], self.recv.at[0, hop - 1], self.p.zp),
            remote(down, down, self.send.at[1, hop - 1], self.recv.at[1, hop - 1], self.p.zm),
        )

    def start(self, hop):
        for copy in self.copies(hop):
            copy.start()

    def take(self, hop):
        up = self.ref(self.p.z - hop, hop, True)
        down = self.ref(self.p.z + hop, hop, False)
        remote(up, up, self.send.at[0, hop - 1], self.recv.at[0, hop - 1], self.p.zm).wait_recv()
        remote(down, down, self.send.at[1, hop - 1], self.recv.at[1, hop - 1], self.p.zp).wait_recv()

    def drain(self):
        for hop in range(1, 5):
            for copy in self.copies(hop):
                copy.wait_send()


class RingSum:
    def __init__(self, place, buf, land, rows, send, recv):
        self.p, self.buf, self.land = place, buf, land
        self.n, self.send, self.recv = rows, send, recv

    def part(self, z, half):
        z = (z + 2 * ZR) % ZR
        if half is None:
            return rows_of(self.buf, z * self.n, self.n, self.n)
        n = self.n // 2
        return rows_of(self.buf, z * self.n + half * n, n, n)

    def slot(self, way, hop):
        if hop == 1:
            return self.land.at[way, 0, pl.ds(0, self.n // 2), :]
        return self.land.at[way, hop - 1]

    def copies(self, hop):
        half = (0, 1) if hop == 1 else (None, None)
        up = self.part(self.p.z + 5 - hop, half[0])
        down = self.part(self.p.z - 5 + hop, half[1])
        return (
            remote(up, self.slot(0, hop), self.send.at[0, hop - 1], self.recv.at[0, hop - 1], self.p.zp),
            remote(down, self.slot(1, hop), self.send.at[1, hop - 1], self.recv.at[1, hop - 1], self.p.zm),
        )

    def start(self, hop):
        for copy in self.copies(hop):
            copy.start()

    def take(self, hop):
        for copy in self.copies(hop):
            copy.wait_recv()

    def add(self, hop):
        half = (0, 1) if hop == 1 else (None, None)
        for way, z in ((0, self.p.z + 4 - hop), (1, self.p.z - 4 + hop)):
            ref = self.part(z, half[way])
            ref[...] = (ref[...].astype(F32) + self.slot(way, hop)[...].astype(F32)).astype(BF16)

    def drain(self):
        for hop in range(1, 5):
            for copy in self.copies(hop):
                copy.wait_send()


def gain_row(ref):
    return ref[...].astype(F32).reshape(1, -1)


def normed_rows(act, gain):
    values = act.astype(F32)
    return (values * rms_scale(values) * gain).astype(BF16)


def gated(gate_val, up_val):
    return (jax.nn.silu(gate_val) * up_val).astype(BF16)


def at_step(i, step):
    return pl.when(i == step)


def split_rows(row):
    high = row.astype(BF16).astype(F32)
    rest = row - high
    mid = rest.astype(BF16).astype(F32)
    low = rest - mid
    index = lax.broadcasted_iota(jnp.int32, (8, row.shape[1]), 0)
    out = jnp.where(index == 0, high, jnp.where(index == 1, mid, jnp.where(index == 2, low, 0.0)))
    return out.astype(BF16)


def unit_scale(vec):
    return lax.rsqrt(jnp.sum(vec * vec, axis=-1, keepdims=True) + EPS)


def unit_back(vec, scales, upstream):
    inner = jnp.sum(vec * upstream, axis=-1, keepdims=True)
    return scales * upstream - vec * (scales * scales * scales) * inner


def contrast(query_hat, item_hat, ranks, positive):
    logits = dot(query_hat, item_hat, ((1,), (1,)), HIGH) / TAU
    shifted = logits - 1.0 / TAU
    log_student = shifted - jnp.log(jnp.sum(jnp.exp(shifted), axis=1, keepdims=True))
    teach = -ranks.astype(F32) / TEACH
    log_teacher = teach - jnp.log(jnp.sum(jnp.exp(teach), axis=1, keepdims=True))
    teacher = jnp.exp(log_teacher)
    columns = lax.broadcasted_iota(jnp.int32, logits.shape, 1)
    onehot = (columns == positive).astype(F32)
    per_row = jnp.sum(
        teacher * (log_teacher - log_student) - onehot * log_student, axis=1, keepdims=True
    )
    slopes = 2.0 * jnp.exp(log_student) - onehot - teacher
    return (per_row, slopes)


def grad_rows(resid, scales, gain, upstream):
    along = gain * upstream
    inner = jnp.mean(along * resid, axis=-1, keepdims=True)
    return (scales * along - resid * (scales * scales * scales) * inner).astype(BF16)


def by_tower(values, parts, tower):
    wide = values.shape[1] // parts
    blocks = [values[:, d * wide : (d + 1) * wide] for d in range(tower, parts, 2)]
    return jnp.concatenate(blocks, axis=1)


def kernel(
    qa, qg, gate_hbm, up_hbm, down_hbm, ia, ig, ig_w, iu_w, id_w, qf, if_, proj_hbm, ranks, positive,
    loss, q_out, i_out,
    w, stage, proj, nq, part, gate_val, h2, pm, r1, r2, zs, zin, ni, wi, ip, land, hq, hi,
    sums, hats, scal, yq, hw, yi, gq, gi, qc1, qb1, qb2, qc, ic1, ib1, ib2, ic,
    loads, gs, gr, ss, sr, ws, wr, vs, vr, hs, hr, ias, iar, irs, irr,
    s1, s2, s3, ys, yr, iys, iyr, qs, qv, bs, bv,
):
    p = Place()
    n, dq = qa.shape
    m, di = ia.shape
    f, k = down_hbm.shape[0], id_w.shape[0]
    group = X * n
    h = n // 2
    parts = X * ZL
    count = hats.shape[0]
    block_wide = dq // count
    piece = w.shape[2] // 4
    wide, thin = dq // 2, dq // 4
    dp = lax.axis_index("dp")
    own = dp * 2 + p.w
    y, c = dp // 2, dp % 2
    yp, ym, y2 = (y + 1) % 4, (y + 3) % 4, (y + 2) % 4
    line_y = (y2, yp, ym, y)
    to_yp, to_ym, to_core = {"dp": yp * 2 + c}, {"dp": ym * 2 + c}, {"dp": y * 2 + 1 - c}
    to_y = (to_yp, to_ym)
    to_tower = {"tower": 1 - p.w}
    a2 = (p.a + 2) % ZL
    mate = p.a + 1 - 2 * (p.a % 2)
    to_a2, to_mate = p.column(a2), p.column(mate)

    def member(step):
        return {"tensor": (p.t + step) % parts}

    def replica(step):
        other = (own + step) % count
        return {"dp": other // 2, "tower": other % 2}

    own_weights = [
        pltpu.make_async_copy(ref, dst, loads.at[index])
        for index, (ref, dst) in enumerate(
            (
                (gate_hbm, w.at[0, 0, pl.ds(0, f), :]),
                (up_hbm, w.at[0, 1, pl.ds(0, f), :]),
                (down_hbm, stage),
            )
        )
    ]
    proj_copy = pltpu.make_async_copy(proj_hbm, proj, loads.at[3])
    for copy in own_weights:
        copy.start()
    proj_copy.start()
    barrier = pltpu.get_barrier_semaphore()

    def greet(step, _):
        pl.semaphore_signal(barrier, inc=1, device_id=member(step), device_id_type=MESH)
        pl.semaphore_signal(barrier, inc=1, device_id=replica(step), device_id_type=MESH)
        return 0

    lax.fori_loop(1, parts, greet, 0)
    for where in (p.zp, p.zm):
        pl.semaphore_signal(barrier, inc=1, device_id=where, device_id_type=MESH)
    for index in range(3):
        w[0, index, f:, :] = jnp.zeros((w.shape[2] - f, dq), BF16)
    nq[pl.ds(pl.multiple_of(p.b * n, n), n), :] = normed_rows(qa[...], gain_row(qg))
    ni[pl.ds(pl.multiple_of(p.z * m, m), m), :] = normed_rows(ia[...], gain_row(ig))
    for index, ref in enumerate((ig_w, iu_w, id_w)):
        wi[index, pl.ds(pl.multiple_of(p.b * k, k), k), :] = ref[...]
    pl.semaphore_wait(barrier, 2 * (parts - 1) + 2)

    rows = RowGather(p, nq, n, gs, gr)
    items = RingGather(p, ni, m, ias, iar)
    isum = RingSum(p, ip, land, m, irs, irr)

    def across():
        return remote(rows.block(0, p.b), rows.block(1, p.b), gs.at[0, 0], gr.at[0, 0], to_a2)

    def wpiece(which, index, line, core):
        first = pl.multiple_of(line * piece, piece)
        return w.at[which, index, pl.ds(first, piece), pl.ds(pl.multiple_of(core * wide, wide), wide)]

    def whalf(index, line, part_of):
        first = pl.multiple_of(line * piece, piece)
        column = pl.multiple_of(c * wide + part_of * thin, thin)
        return w.at[1, index, pl.ds(first, piece), pl.ds(column, thin)]

    def w_send(index, kind):
        here = wpiece(1, index, y, c)
        low, high = wpiece(1, index, ym, c), wpiece(1, index, yp, c)
        src, dst, where = (
            (wpiece(0, index, y, c), here, to_mate),
            (here, here, to_yp),
            (here, here, to_ym),
            (whalf(index, ym, 0), whalf(index, ym, 0), to_yp),
            (whalf(index, yp, 1), whalf(index, yp, 1), to_ym),
            (here, here, to_core),
            (low, low, to_core),
            (high, high, to_core),
            (wpiece(1, index, y2, c), wpiece(1, index, y2, c), to_core),
        )[kind]
        return remote(src, dst, ws.at[kind, index], wr.at[kind, index], where)

    def w_got(index, kind):
        dst = (
            wpiece(1, index, y, c),
            wpiece(1, index, ym, c),
            wpiece(1, index, yp, c),
            whalf(index, y2, 0),
            whalf(index, y2, 1),
            wpiece(1, index, y, 1 - c),
            wpiece(1, index, ym, 1 - c),
            wpiece(1, index, yp, 1 - c),
            wpiece(1, index, y2, 1 - c),
        )[kind]
        remote(dst, dst, ws.at[kind, index], wr.at[kind, index], to_core).wait_recv()

    def w_near(index):
        w_got(index, 0)
        for kind in (1, 2, 5) if index == 2 else (1, 2):
            w_send(index, kind).start()

    def w_ring(index):
        w_got(index, 1)
        w_send(index, 3).start()
        w_got(index, 2)
        w_send(index, 4).start()
        if index == 2:
            w_send(index, 6).start()
            w_send(index, 7).start()

    def w_far(index):
        w_got(index, 3)
        w_got(index, 4)
        if index == 2:
            w_send(index, 8).start()
        else:
            w_column(index, c).start()

    def w_column(index, core):
        ref = w.at[1, index, :, pl.ds(pl.multiple_of(core * wide, wide), wide)]
        return remote(ref, ref, ws.at[8, index], wr.at[8, index], to_core)

    def w_done(index):
        if index < 2:
            w_column(index, 1 - c).wait_recv()
        else:
            for kind in (5, 6, 7, 8):
                w_got(index, kind)

    def vpiece(b, core):
        column = pl.multiple_of(core * (di // 2), di // 2)
        return wi.at[:, pl.ds(pl.multiple_of(b * k, k), k), pl.ds(column, di // 2)]

    def vhalf(b, part_of):
        first = pl.multiple_of(b * k + part_of * (k // 2), k // 2)
        column = pl.multiple_of(c * (di // 2), di // 2)
        return wi.at[:, pl.ds(first, k // 2), pl.ds(column, di // 2)]

    def v_send(kind):
        ref, where = (
            (vpiece(p.b, c), p.xp),
            (vpiece(p.b, c), p.xm),
            (vhalf(p.bm, 0), p.xp),
            (vhalf(p.bp, 1), p.xm),
            (vpiece(p.bm, c), to_core),
            (vpiece(p.bp, c), to_core),
            (vpiece(p.bo, c), to_core),
        )[kind]
        return remote(ref, ref, vs.at[kind], vr.at[kind], where)

    def v_got(kind):
        ref = (
            vpiece(p.bm, c),
            vpiece(p.bp, c),
            vhalf(p.bo, 0),
            vhalf(p.bo, 1),
            vpiece(p.bm, 1 - c),
            vpiece(p.bp, 1 - c),
            vpiece(p.bo, 1 - c),
        )[kind]
        remote(ref, ref, vs.at[kind], vr.at[kind], to_core).wait_recv()

    def block(j, q, b):
        return rows_of(pm.at[q], (j * X + b) * n, n, n)

    def half(j, q, b, part_of):
        return rows_of(pm.at[q], (j * X + b) * n + part_of * h, h, h)

    def first(j, q, way):
        src = half(j, q, p.bo, way)
        where = (p.xp, p.xm)[way]
        return remote(src, r1.at[way, j, q], ss.at[way, j, q], sr.at[way, j, q], where)

    def second(j, q, way):
        src = block(j, q, (p.bp, p.bm)[way])
        where = (p.xp, p.xm)[way]
        return remote(src, r2.at[way, j, q], ss.at[2 + way, j, q], sr.at[2 + way, j, q], where)

    def to_owner(q):
        return remote(zs.at[q], zin.at[q], ss.at[4, 0, q], sr.at[4, 0, q], to_a2)

    def back(j, b):
        dst = rows_of(hq, ((p.a, a2)[j] * X + b) * n, n, n)
        src = h2.at[j, pl.ds(b * n, n), :]
        return remote(src, dst, hs.at[j, b], hr.at[j, b], to_mate)

    def back_got(j):
        other = (mate, (mate + 2) % ZL)[j]
        for b in range(X):
            dst = rows_of(hq, (other * X + b) * n, n, n)
            remote(dst, dst, hs.at[j, b], hr.at[j, b], to_mate).wait_recv()

    def rows_in(j):
        return nq[j * group : (j + 1) * group, :]

    def own_units(j):
        left = rows_in(j)
        value = gated(
            dot(left, w[0, 0, :f, :], ((1,), (1,))), dot(left, w[0, 1, :f, :], ((1,), (1,)))
        )
        hq[pl.ds(pl.multiple_of((p.a, a2)[j] * group, group), group), :] = value
        part[j] = dot(value, w[0, 2, :f, :])

    def mate_gate(j):
        gate_val[j] = dot(rows_in(j), w[1, 0, :f, :], ((1,), (1,)))

    def mate_up(j):
        h2[j] = gated(gate_val[j], dot(rows_in(j), w[1, 1, :f, :], ((1,), (1,))))
        if j == 1:
            for b in range(X):
                back(1, b).start()

    def mate_down(j, q):
        columns = slice(q * wide, (q + 1) * wide)
        total = part[j, :, columns] + dot(h2[j], w[1, 2, :f, columns])
        pm[q, j * group : (j + 1) * group, :] = total.astype(BF16)
        first(j, q, 0).start()
        first(j, q, 1).start()

    def combine(j, q):
        for way in range(2):
            first(j, q, way).wait_recv()
            ref = half(j, q, (p.bp, p.bm)[way], way)
            ref[...] = (ref[...].astype(F32) + r1[way, j, q].astype(F32)).astype(BF16)
            second(j, q, way).start()

    def summed(j, q):
        second(j, q, 0).wait_recv()
        second(j, q, 1).wait_recv()
        total = block(j, q, p.b)[...].astype(F32)
        return total + r2[0, j, q].astype(F32) + r2[1, j, q].astype(F32)

    def send_sum(q):
        zs[q] = summed(1, q).astype(BF16)
        to_owner(q).start()

    def item_hop(hop):
        items.take(hop)
        if hop < 4:
            items.start(hop + 1)

    def isum_hop(hop):
        isum.take(hop)
        isum.add(hop)
        isum.start(hop + 1)

    def item_product():
        left = ni[...]
        partial = 0.0
        for b in range(X):
            here = slice(b * k, (b + 1) * k)
            value = gated(
                dot(left, wi[0, here, :], ((1,), (1,))), dot(left, wi[1, here, :], ((1,), (1,)))
            )
            hi[b] = value
            partial = partial + dot(value, wi[2, here, :])
        ip[...] = partial.astype(BF16)
        isum.start(1)

    rows.right(0).start()
    rows.left(0).start()
    items.start(1)
    own_weights[0].wait()
    w_send(0, 0).start()
    across().start()
    v_send(0).start()
    v_send(1).start()
    own_weights[1].wait()
    own_weights[2].wait()
    for first_row in range(0, f, 112):
        chunk = stage[first_row : first_row + 112, :]
        for tower in range(2):
            columns = slice(tower * wide, (tower + 1) * wide)
            w[0, 2, first_row : first_row + 112, columns] = by_tower(chunk, count, tower)
    rows.take_x(0)
    item_hop(1)
    w_near(0)
    w_send(1, 0).start()
    rows.take_halves(0)
    own_units(0)
    remote(rows.block(0, p.b), rows.block(1, p.b), gs.at[0, 0], gr.at[0, 0], to_a2).wait_recv()
    rows.right(1).start()
    rows.left(1).start()
    item_hop(2)
    w_ring(0)
    w_near(1)
    w_send(2, 0).start()
    for kind in range(2):
        v_got(kind)
        v_send(2 + kind).start()
        v_send(4 + kind).start()
    item_hop(3)
    w_far(0)
    rows.take_x(1)
    v_got(2)
    v_got(3)
    v_send(6).start()
    w_ring(1)
    item_hop(4)
    for kind in (4, 5, 6):
        v_got(kind)
    w_near(2)
    item_product()
    w_far(1)
    w_done(0)
    mate_gate(0)
    rows.take_halves(1)
    mate_gate(1)
    isum_hop(1)
    w_ring(2)
    own_units(1)
    w_done(1)
    mate_up(1)
    isum_hop(2)
    w_far(2)
    mate_up(0)
    w_done(2)
    def spread(buf, mine, sems, partner):
        def each(hop, _):
            remote(buf.at[mine], buf.at[mine], sems.at[0], sems.at[1], partner(hop)).start()
            return 0

        lax.fori_loop(1, buf.shape[0], each, 0)

    def gathered(buf, sems):
        ref = buf.at[pl.ds(0, buf.shape[0] - 1)]
        remote(ref, ref, sems.at[0], sems.at[1], member(1)).wait()

    def q_rows(tower, line_of, core):
        return rows_of(gq.at[tower], (line_of * 2 + core) * block_wide, block_wide, block_wide)

    def q_half(tower, line_of, way):
        first = (line_of * 2 + c) * block_wide + way * (block_wide // 2)
        return rows_of(gq.at[tower], first, block_wide // 2, block_wide // 2)

    def q_core(tower, j):
        src = q_rows(tower, line_y[j], 1 - c)
        return remote(src, qc1.at[tower, j], qs.at[tower, j], qv.at[tower, j], to_core)

    def q_first(tower, way):
        src, dst = q_half(tower, y2, way), qb1.at[tower, way]
        return remote(src, dst, qs.at[tower, 4 + way], qv.at[tower, 4 + way], to_y[way])

    def q_second(tower, way):
        src, dst = q_rows(tower, (yp, ym)[way], c), qb2.at[tower, way]
        return remote(src, dst, qs.at[tower, 6 + way], qv.at[tower, 6 + way], to_y[way])

    def q_tower(tower):
        return remote(q_rows(tower, y, c), qc, qs.at[tower, 8], qv.at[tower, 8], to_tower)

    def q_start(tower):
        for j in range(4):
            q_core(tower, j).start()

    def q_far(tower):
        q_core(tower, 0).wait_recv()
        ref = q_rows(tower, y2, c)
        ref[...] += qc1[tower, 0]
        for way in range(2):
            q_first(tower, way).start()

    def q_near(tower):
        for way in range(2):
            q_core(tower, 1 + way).wait_recv()
            ref = q_rows(tower, (yp, ym)[way], c)
            ref[...] += qc1[tower, 1 + way]
            q_first(tower, way).wait_recv()
            ref = q_half(tower, (yp, ym)[way], way)
            ref[...] += qb1[tower, way]
            q_second(tower, way).start()

    def q_own(tower):
        q_core(tower, 3).wait_recv()
        for way in range(2):
            q_second(tower, way).wait_recv()
        ref = q_rows(tower, y, c)
        ref[...] = ref[...] + qc1[tower, 3] + qb2[tower, 0] + qb2[tower, 1]

        @pl.when(p.w != tower)
        def _():
            q_tower(tower).start()

    def q_finish(tower):
        @pl.when(p.w == tower)
        def _():
            q_tower(tower).wait_recv()
            q_out[...] = q_rows(tower, y, c)[...] + qc[...]

    def i_rows(line_of, core):
        first = pl.multiple_of((line_of * 2 + core) * block_wide, block_wide)
        return gi.at[:, pl.ds(first, block_wide), :]

    def i_half(line_of, way):
        first = pl.multiple_of((line_of * 2 + c) * block_wide, block_wide)
        return gi.at[pl.ds(way * 2, 2), pl.ds(first, block_wide), :]

    def i_slab(b):
        return gi.at[b, pl.ds(pl.multiple_of((y * 2 + c) * block_wide, block_wide), block_wide), :]

    def i_core(j):
        return remote(i_rows(line_y[j], 1 - c), ic1.at[j], bs.at[j], bv.at[j], to_core)

    def i_first(way):
        return remote(i_half(y2, way), ib1.at[way], bs.at[4 + way], bv.at[4 + way], to_y[way])

    def i_second(way):
        src = i_rows((yp, ym)[way], c)
        return remote(src, ib2.at[way], bs.at[6 + way], bv.at[6 + way], to_y[way])

    def i_x(hop):
        other = (p.b + hop) % X
        where = {"tensor": p.a * X + other}
        return remote(i_slab(other), ic.at[p.b], bs.at[8 + hop], bv.at[8 + p.b], where)

    def i_product():
        for b in range(X):
            gi[b] = dot(yi[...], hi[b], ((0,), (0,)))
        for j in range(4):
            i_core(j).start()

    def i_far():
        for j in range(4):
            i_core(j).wait_recv()
            ref = i_rows(line_y[j], c)
            ref[...] += ic1[j]
        for way in range(2):
            i_first(way).start()

    def i_near():
        for way in range(2):
            i_first(way).wait_recv()
            ref = i_half((yp, ym)[way], way)
            ref[...] += ib1[way]
            i_second(way).start()

    def i_own():
        for way in range(2):
            i_second(way).wait_recv()
        ref = i_rows(y, c)
        ref[...] = ref[...] + ib2[0] + ib2[1]
        for hop in range(1, X):
            i_x(hop).start()

    def i_finish():
        total = i_slab(p.b)[...]
        for hop in range(1, X):
            other = (p.b + hop) % X
            remote(i_slab(other), ic.at[other], bs.at[8 + hop], bv.at[8 + other], p.xp).wait_recv()
            total = total + ic[other]
        i_out[...] = total

    gather = [RowGather(p, yq.at[tower], n, ys.at[tower], yr.at[tower]) for tower in range(2)]
    igather = RingGather(p, yi, m, iys, iyr)

    steps = (0, 1, 4, 2, 5, 3, 6, 7)

    def advance(index):
        if index < len(steps):
            g = steps[index]
            gather[g // ZL].take_z(p.order(g % ZL))
        if 0 <= index - 2 < len(steps):
            g = steps[index - 2]
            gather[g // ZL].take_x(p.order(g % ZL))

    def item_grad_hop(hop):
        igather.take(hop)
        if hop < 4:
            igather.start(hop + 1)

    def scale_hidden():
        line = lax.broadcasted_iota(jnp.int32, (128, 128), 0)
        tiles = [jnp.zeros((128, 128), F32)] * 2
        for t in range(parts):
            for kind in range(2):
                tiles[kind] = jnp.where(line == t, scal[t, kind : kind + 1, :], tiles[kind])
        scale_of, slope_of = tiles[0].T[:n], tiles[1].T[:n]
        total = jnp.zeros((1, f), F32)
        for t in range(parts):
            here = slice(t * n, (t + 1) * n)
            value = hq[here, :].astype(F32)
            hw[here, :] = (value * slope_of[:, t : t + 1]).astype(BF16)
            total = total + jnp.sum(value * scale_of[:, t : t + 1], axis=0, keepdims=True)
        return total

    def product(tower, part_of):
        total = 0.0
        for j in (2 * part_of, 2 * part_of + 1):
            s = p.order(j)
            gather[tower].take_halves(s)
            here = pl.ds(pl.multiple_of(s * group, group), group)
            total = total + dot(yq[tower, here, :], hw[here, :], ((0,), (0,)))
        if part_of == 0:
            column = jnp.broadcast_to(along_of[tower], (128, wide)).T[:, 0:1]
            gq[tower] = column * summed_hidden - total
        else:
            gq[tower] -= total

    def resid_half(tower):
        total = summed(0, tower)
        to_owner(tower).wait_recv()
        total = total + zin[tower].astype(F32)
        value = by_tower(qa[...], count, tower).astype(F32) + total
        yq[tower, pl.ds(pl.multiple_of(p.t * n, n), n), :] = value.astype(BF16)
        return value

    mate_down(1, 0)
    mate_down(0, 0)
    combine(1, 0)
    mate_down(1, 1)
    combine(0, 0)
    mate_down(0, 1)
    send_sum(0)
    combine(1, 1)
    combine(0, 1)
    isum_hop(3)
    send_sum(1)
    q_resid = [resid_half(0)]
    advance(0)
    back(0, 0).start()
    isum.take(4)
    own_item = ip[pl.ds(pl.multiple_of(p.z * m, m), m), :].astype(F32)
    i_resid = ia[...].astype(F32) + (own_item + land[0, 3].astype(F32) + land[1, 3].astype(F32))
    i_gain = gain_row(if_)
    i_scale = rms_scale(i_resid)
    sums[p.t, :, dq:] = jnp.sum(i_resid * i_scale * i_gain, axis=0, keepdims=True)
    q_gain = gain_row(qf)
    gain_of = [by_tower(q_gain, count, tower) for tower in range(2)]
    advance(1)
    q_resid.append(resid_half(1))
    square = sum(jnp.sum(value * value, axis=-1, keepdims=True) for value in q_resid)
    q_scale = lax.rsqrt(square / dq + EPS)
    for tower in range(2):
        part_sum = jnp.sum(q_resid[tower] * q_scale * gain_of[tower], axis=0, keepdims=True)
        sums[p.t, :, tower * wide : (tower + 1) * wide] = part_sum
    spread(sums, p.t, s1, member)
    advance(2)
    back(0, 1).start()
    proj_copy.wait()
    gathered(sums, s1)
    total = sums[0]
    for slot in range(1, parts):
        total = total + sums[slot]
    firsts = [(d % 2) * wide + (d // 2) * block_wide for d in range(count)]
    q_pooled = jnp.concatenate([total[:, at : at + block_wide] for at in firsts], axis=1) / QLEN
    i_pooled = total[:, dq:] / ILEN
    q_e = jnp.sum(dot(split_rows(q_pooled), proj[...]), axis=0, keepdims=True)
    q_norm, i_norm = unit_scale(q_e), unit_scale(i_pooled)
    hats[own, :, :di] = q_e * q_norm
    hats[own, :, di:] = i_pooled * i_norm
    spread(hats, own, s2, replica)
    advance(3)
    back(0, 2).start()
    gathered(hats, s2)
    index = lax.broadcasted_iota(jnp.int32, (count, 2 * di), 0)
    every = jnp.zeros((count, 2 * di), F32)
    for slot in range(count):
        every = jnp.where(index == slot, hats[slot], every)
    every_query, every_items = every[:, :di], every[:, di:]
    line = lax.broadcasted_iota(jnp.int32, (count, count), 0)
    target = jnp.zeros((count, count), jnp.int32)
    for slot in range(count):
        target = jnp.where(line == slot, positive[slot], target)
    per_row, slopes = contrast(every_query, every_items, ranks[...], target)
    loss[...] = jnp.sum(per_row, axis=0, keepdims=True) / count
    weights = slopes * (LOSS_SCALE / (TAU * count))
    advance(4)
    back(0, 3).start()
    mine = lax.broadcasted_iota(jnp.int32, (count, di), 0) == own
    q_back = jnp.sum(
        jnp.where(mine, dot(weights, every_items, precision=HIGH), 0.0), axis=0, keepdims=True
    )
    column = lax.broadcasted_iota(jnp.int32, (count, count), 1) == own
    i_back = jnp.sum(
        jnp.sum(jnp.where(column, weights, 0.0), axis=1, keepdims=True) * every_query,
        axis=0,
        keepdims=True,
    )
    advance(5)
    q_grad_e = unit_back(q_e, q_norm, q_back)
    q_up = jnp.sum(dot(split_rows(q_grad_e), proj[...], ((1,), (1,))), axis=0, keepdims=True) / QLEN
    i_up = unit_back(i_pooled, i_norm, i_back) / ILEN
    along = q_gain * q_up
    along_of = [by_tower(along, count, tower) for tower in range(2)]
    inner = sum(
        jnp.sum(along_of[tower] * q_resid[tower], axis=-1, keepdims=True) for tower in range(2)
    )
    inner = inner / dq
    slope = (q_scale * q_scale * q_scale) * inner
    lane = lax.broadcasted_iota(jnp.int32, (n, 128), 1)
    columns = jnp.where(lane == 0, q_scale, jnp.where(lane == 1, slope, 0.0))
    columns = jnp.concatenate([columns, jnp.zeros((128 - n, 128), F32)], axis=0)
    scal[p.t] = columns.T[:8]
    spread(scal, p.t, s3, member)
    yi[pl.ds(pl.multiple_of(p.z * m, m), m), :] = grad_rows(i_resid, i_scale, i_gain, i_up)
    igather.start(1)
    advance(6)
    gathered(scal, s3)
    back_got(0)
    back_got(1)
    summed_hidden = scale_hidden()
    advance(7)
    item_grad_hop(1)
    product(0, 0)
    advance(8)
    item_grad_hop(2)
    product(0, 1)
    q_start(0)
    advance(9)
    item_grad_hop(3)
    q_far(0)
    product(1, 0)
    item_grad_hop(4)
    q_near(0)
    product(1, 1)
    q_start(1)
    i_product()
    q_far(1)
    q_own(0)
    i_far()
    q_near(1)
    i_near()
    q_own(1)
    i_own()
    q_finish(0)
    i_finish()
    q_finish(1)

    for j in range(2):
        for b in range(X):
            back(j, b).wait_send()
        for copy in (rows.right(j), rows.left(j), rows.half_right(j), rows.half_left(j)):
            copy.wait_send()
        for q in range(2):
            for way in range(2):
                first(j, q, way).wait_send()
                second(j, q, way).wait_send()
    for q in range(2):
        to_owner(q).wait_send()
    across().wait_send()
    items.drain()
    isum.drain()
    for index in range(3):
        for kind in range(9) if index == 2 else range(5):
            w_send(index, kind).wait_send()
    for index in range(2):
        w_column(index, c).wait_send()
    for kind in range(7):
        v_send(kind).wait_send()
    for tower in range(2):
        gather[tower].drain()
        for j in range(4):
            q_core(tower, j).wait_send()
        for way in range(2):
            q_first(tower, way).wait_send()
            q_second(tower, way).wait_send()

        @pl.when(p.w != tower)
        def _():
            q_tower(tower).wait_send()

    igather.drain()
    for j in range(4):
        i_core(j).wait_send()
    for way in range(2):
        i_first(way).wait_send()
        i_second(way).wait_send()
    for hop in range(1, X):
        i_x(hop).wait_send()


def step(qa, qg, gate, up, down, ia, ig, ig_w, iu_w, id_w, qf, if_, proj, ranks, positive):
    n, dq = qa.shape
    m, di = ia.shape
    f, k = down.shape[0], id_w.shape[0]
    padded = 64 * ((f + 63) // 64)
    vmem, hbm = pl.BlockSpec(memory_space=pltpu.VMEM), pl.BlockSpec(memory_space=pl.ANY)
    smem = pl.BlockSpec(memory_space=pltpu.SMEM)
    all_i = ZR * m
    group = X * n
    parts = X * ZL
    count = ranks.shape[0]
    wide = dq // count
    dma = pltpu.SemaphoreType.DMA
    return pl.pallas_call(
        kernel,
        out_shape=(
            jax.ShapeDtypeStruct((1, 1), F32),
            jax.ShapeDtypeStruct((wide, f), F32),
            jax.ShapeDtypeStruct((wide, k), F32),
        ),
        in_specs=[vmem, vmem, hbm, hbm, hbm] + [vmem] * 7 + [hbm, vmem, smem],
        out_specs=[vmem] * 3,
        scratch_shapes=[
            pltpu.VMEM((2, 3, padded, dq), BF16),
            pltpu.VMEM(down.shape, BF16),
            pltpu.VMEM(proj.shape, BF16),
            pltpu.VMEM((2 * group, dq), BF16),
            pltpu.VMEM((2, group, dq), F32),
            pltpu.VMEM((2, group, f), F32),
            pltpu.VMEM((2, group, f), BF16),
            pltpu.VMEM((2, 2 * group, dq // 2), BF16),
            pltpu.VMEM((2, 2, 2, n // 2, dq // 2), BF16),
            pltpu.VMEM((2, 2, 2, n, dq // 2), BF16),
            pltpu.VMEM((2, n, dq // 2), BF16),
            pltpu.VMEM((2, n, dq // 2), BF16),
            pltpu.VMEM((all_i, di), BF16),
            pltpu.VMEM((3, X * k, di), BF16),
            pltpu.VMEM((all_i, di), BF16),
            pltpu.VMEM((2, 4, m, di), BF16),
            pltpu.VMEM((ZL * group, f), BF16),
            pltpu.VMEM((X, all_i, k), BF16),
            pltpu.VMEM((parts, 1, dq + di), F32),
            pltpu.VMEM((count, 1, 2 * di), F32),
            pltpu.VMEM((parts, 8, 128), F32),
            pltpu.VMEM((2, parts * n, dq // 2), BF16),
            pltpu.VMEM((ZL * group, f), BF16),
            pltpu.VMEM((all_i, di), BF16),
            pltpu.VMEM((2, dq // 2, f), F32),
            pltpu.VMEM((X, di, k), F32),
            pltpu.VMEM((2, 4, wide, f), F32),
            pltpu.VMEM((2, 2, wide // 2, f), F32),
            pltpu.VMEM((2, 2, wide, f), F32),
            pltpu.VMEM((wide, f), F32),
            pltpu.VMEM((4, X, wide, k), F32),
            pltpu.VMEM((2, 2, wide, k), F32),
            pltpu.VMEM((2, X, wide, k), F32),
            pltpu.VMEM((X, wide, k), F32),
            dma((4,)),
            dma((6, 2)),
            dma((5, 2)),
            dma((5, 2, 2)),
            dma((5, 2, 2)),
            dma((9, 3)),
            dma((9, 3)),
            dma((7,)),
            dma((7,)),
            dma((2, X)),
            dma((2, X)),
            dma((2, 4)),
            dma((2, 4)),
            dma((2, 4)),
            dma((2, 4)),
            dma((2,)),
            dma((2,)),
            dma((2,)),
            dma((2, 6, ZL)),
            dma((2, 5, ZL)),
            dma((2, 4)),
            dma((2, 4)),
            dma((2, 9)),
            dma((2, 9)),
            dma((12,)),
            dma((12,)),
        ],
        compiler_params=pltpu.CompilerParams(
            collective_id=0, has_side_effects=True, vmem_limit_bytes=VMEM_LIMIT
        ),
        name="towers_step",
    )(qa, qg, gate, up, down, ia, ig, ig_w, iu_w, id_w, qf, if_, proj, ranks, positive)


def body(
    q_act,
    q_norm_gain,
    q_gate,
    q_up,
    q_down,
    q_final_gain,
    projection,
    i_act,
    i_norm_gain,
    i_gate,
    i_up,
    i_down,
    i_final_gain,
    ranks,
    positive,
):
    loss, q_grad, i_grad = step(
        q_act,
        q_norm_gain,
        q_gate.T,
        q_up.T,
        q_down,
        i_act,
        i_norm_gain,
        i_gate.T,
        i_up.T,
        i_down,
        q_final_gain,
        i_final_gain,
        projection,
        ranks,
        positive,
    )
    return (loss.reshape(()), q_grad.T, i_grad.T)


def solution(mesh):
    in_specs = (
        P(("dp", "tower", "tensor"), None),
        P(),
        P(None, "tensor"),
        P(None, "tensor"),
        P("tensor", None),
        P(),
        P(),
        P(("dp", "tower", "tensor"), None),
        P(),
        P(None, ("tower", "tensor")),
        P(None, ("tower", "tensor")),
        P(("tower", "tensor"), None),
        P(),
        P(),
        P(),
    )
    out_specs = (P(), P("tensor", ("dp", "tower")), P(("tower", "tensor"), "dp"))
    return jax.shard_map(body, mesh=mesh, in_specs=in_specs, out_specs=out_specs, check_vma=False)
```

```python
import functools

import jax
import jax.numpy as jnp
from jax import lax
from jax.experimental import pallas as pl
from jax.experimental.pallas import tpu as pltpu
from jax.sharding import PartitionSpec as P

QLEN = 1536
ILEN = 512
EPS = 1e-06
TAU = 0.05
TEACH = 2.0
LOSS_SCALE = 64.0
HIGH = lax.Precision.HIGHEST
MESH = pl.DeviceIdType.MESH
F32 = jnp.float32
BF16 = jnp.bfloat16

X = 4
ZL = 4
ZR = 8
VMEM_LIMIT = 60 * 1024 * 1024


def rms_scale(values):
    return lax.rsqrt(jnp.mean(values * values, axis=-1, keepdims=True) + EPS)


def dot(left, right, dims=((1,), (0,)), precision=None):
    return lax.dot_general(
        left, right, (dims, ((), ())), preferred_element_type=F32, precision=precision
    )


def remote(src, dst, send, recv, where):
    return pltpu.make_async_remote_copy(
        src_ref=src, dst_ref=dst, send_sem=send, recv_sem=recv, device_id=where, device_id_type=MESH
    )


class Place:
    def __init__(self):
        self.t = lax.axis_index("tensor")
        self.w = lax.axis_index("tower")
        self.a = self.t // X
        self.b = self.t % X
        self.z = self.w * ZL + self.a
        self.bp = (self.b + 1) % X
        self.bm = (self.b + X - 1) % X
        self.bo = (self.b + 2) % X
        self.xp = {"tensor": self.a * X + self.bp}
        self.xm = {"tensor": self.a * X + self.bm}
        self.zp = self.ring(1)
        self.zm = self.ring(ZR - 1)

    def ring(self, step):
        z = (self.z + step) % ZR
        return {"tower": z // ZL, "tensor": (z % ZL) * X + self.b}

    def column(self, row):
        return {"tensor": row * X + self.b}

    def order(self, j):
        near = jnp.minimum(self.a, ZL - 1 - self.a)
        swapped = jnp.where(j == 0, 1, jnp.where(j == 1, 0, j))
        row = jnp.where(near == 1, swapped, j)
        return jnp.where(self.a >= 2, ZL - 1 - row, row)


def rows_of(ref, first, count, unit):
    return ref.at[pl.ds(pl.multiple_of(first, unit), count), :]


class RowGather:
    def __init__(self, place, buf, rows, send, recv):
        self.p, self.buf, self.n, self.send, self.recv = place, buf, rows, send, recv

    def block(self, s, b):
        return rows_of(self.buf, (s * X + b) * self.n, self.n, self.n)

    def half(self, s, b, h):
        n = self.n // 2
        return rows_of(self.buf, (s * X + b) * self.n + h * n, n, n)

    def up(self, s):
        ref = self.block(s, self.p.b)
        where = self.p.column(jnp.minimum(self.p.a + 1, ZL - 1))
        return remote(ref, ref, self.send.at[0, s], self.recv.at[0, s], where)

    def down(self, s):
        ref = self.block(s, self.p.b)
        where = self.p.column(jnp.maximum(self.p.a - 1, 0))
        return remote(ref, ref, self.send.at[1, s], self.recv.at[0, s], where)

    def right(self, s):
        ref = self.block(s, self.p.b)
        return remote(ref, ref, self.send.at[2, s], self.recv.at[1, s], self.p.xp)

    def left(self, s):
        ref = self.block(s, self.p.b)
        return remote(ref, ref, self.send.at[3, s], self.recv.at[2, s], self.p.xm)

    def half_right(self, s):
        ref = self.half(s, self.p.bm, 0)
        return remote(ref, ref, self.send.at[4, s], self.recv.at[3, s], self.p.xp)

    def half_left(self, s):
        ref = self.half(s, self.p.bp, 1)
        return remote(ref, ref, self.send.at[5, s], self.recv.at[4, s], self.p.xm)

    def goes_up(self, s):
        return (s <= self.p.a) & (self.p.a < ZL - 1)

    def goes_down(self, s):
        return (s >= self.p.a) & (self.p.a > 0)

    def take_z(self, s):
        @pl.when(s != self.p.a)
        def _():
            self.up(s).wait_recv()

        @pl.when(self.goes_up(s))
        def _():
            self.up(s).start()

        @pl.when(self.goes_down(s))
        def _():
            self.down(s).start()

        self.right(s).start()
        self.left(s).start()

    def take_x(self, s):
        ref = self.block(s, self.p.bm)
        remote(ref, ref, self.send.at[2, s], self.recv.at[1, s], self.p.xm).wait_recv()
        self.half_right(s).start()
        ref = self.block(s, self.p.bp)
        remote(ref, ref, self.send.at[3, s], self.recv.at[2, s], self.p.xp).wait_recv()
        self.half_left(s).start()

    def take_halves(self, s):
        ref = self.half(s, self.p.bo, 0)
        remote(ref, ref, self.send.at[4, s], self.recv.at[3, s], self.p.xm).wait_recv()
        ref = self.half(s, self.p.bo, 1)
        remote(ref, ref, self.send.at[5, s], self.recv.at[4, s], self.p.xp).wait_recv()

    def drain(self):
        def each(s, _):
            @pl.when(self.goes_up(s))
            def _():
                self.up(s).wait_send()

            @pl.when(self.goes_down(s))
            def _():
                self.down(s).wait_send()

            self.right(s).wait_send()
            self.left(s).wait_send()
            self.half_right(s).wait_send()
            self.half_left(s).wait_send()
            return 0

        lax.fori_loop(0, ZL, each, 0)


class RingGather:
    def __init__(self, place, buf, rows, send, recv):
        self.p, self.buf, self.n, self.send, self.recv = place, buf, rows, send, recv

    def ref(self, z, hop, upward):
        z = (z + 2 * ZR) % ZR
        if hop < 4:
            return rows_of(self.buf, z * self.n, self.n, self.n)
        n = self.n // 2
        return rows_of(self.buf, z * self.n + (0 if upward else n), n, n)

    def copies(self, hop):
        up = self.ref(self.p.z - hop + 1, hop, True)
        down = self.ref(self.p.z + hop - 1, hop, False)
        return (
            remote(up, up, self.send.at[0, hop - 1], self.recv.at[0, hop - 1], self.p.zp),
            remote(down, down, self.send.at[1, hop - 1], self.recv.at[1, hop - 1], self.p.zm),
        )

    def start(self, hop):
        for copy in self.copies(hop):
            copy.start()

    def take(self, hop):
        up = self.ref(self.p.z - hop, hop, True)
        down = self.ref(self.p.z + hop, hop, False)
        remote(up, up, self.send.at[0, hop - 1], self.recv.at[0, hop - 1], self.p.zm).wait_recv()
        remote(down, down, self.send.at[1, hop - 1], self.recv.at[1, hop - 1], self.p.zp).wait_recv()

    def drain(self):
        for hop in range(1, 5):
            for copy in self.copies(hop):
                copy.wait_send()


class RingSum:
    def __init__(self, place, buf, land, rows, send, recv):
        self.p, self.buf, self.land = place, buf, land
        self.n, self.send, self.recv = rows, send, recv

    def part(self, z, half):
        z = (z + 2 * ZR) % ZR
        if half is None:
            return rows_of(self.buf, z * self.n, self.n, self.n)
        n = self.n // 2
        return rows_of(self.buf, z * self.n + half * n, n, n)

    def slot(self, way, hop):
        if hop == 1:
            return self.land.at[way, 0, pl.ds(0, self.n // 2), :]
        return self.land.at[way, hop - 1]

    def copies(self, hop):
        half = (0, 1) if hop == 1 else (None, None)
        up = self.part(self.p.z + 5 - hop, half[0])
        down = self.part(self.p.z - 5 + hop, half[1])
        return (
            remote(up, self.slot(0, hop), self.send.at[0, hop - 1], self.recv.at[0, hop - 1], self.p.zp),
            remote(down, self.slot(1, hop), self.send.at[1, hop - 1], self.recv.at[1, hop - 1], self.p.zm),
        )

    def start(self, hop):
        for copy in self.copies(hop):
            copy.start()

    def take(self, hop):
        for copy in self.copies(hop):
            copy.wait_recv()

    def add(self, hop):
        half = (0, 1) if hop == 1 else (None, None)
        for way, z in ((0, self.p.z + 4 - hop), (1, self.p.z - 4 + hop)):
            ref = self.part(z, half[way])
            ref[...] = (ref[...].astype(F32) + self.slot(way, hop)[...].astype(F32)).astype(BF16)

    def drain(self):
        for hop in range(1, 5):
            for copy in self.copies(hop):
                copy.wait_send()


def gain_row(ref):
    return ref[...].astype(F32).reshape(1, -1)


def normed_rows(act, gain):
    values = act.astype(F32)
    return (values * rms_scale(values) * gain).astype(BF16)


def gated(gate_val, up_val):
    return (jax.nn.silu(gate_val) * up_val).astype(BF16)


def at_step(i, step):
    return pl.when(i == step)


def split_rows(row):
    high = row.astype(BF16).astype(F32)
    rest = row - high
    mid = rest.astype(BF16).astype(F32)
    low = rest - mid
    index = lax.broadcasted_iota(jnp.int32, (8, row.shape[1]), 0)
    out = jnp.where(index == 0, high, jnp.where(index == 1, mid, jnp.where(index == 2, low, 0.0)))
    return out.astype(BF16)


def unit_scale(vec):
    return lax.rsqrt(jnp.sum(vec * vec, axis=-1, keepdims=True) + EPS)


def unit_back(vec, scales, upstream):
    inner = jnp.sum(vec * upstream, axis=-1, keepdims=True)
    return scales * upstream - vec * (scales * scales * scales) * inner


def contrast(query_hat, item_hat, ranks, positive):
    logits = dot(query_hat, item_hat, ((1,), (1,)), HIGH) / TAU
    shifted = logits - 1.0 / TAU
    log_student = shifted - jnp.log(jnp.sum(jnp.exp(shifted), axis=1, keepdims=True))
    teach = -ranks.astype(F32) / TEACH
    log_teacher = teach - jnp.log(jnp.sum(jnp.exp(teach), axis=1, keepdims=True))
    teacher = jnp.exp(log_teacher)
    columns = lax.broadcasted_iota(jnp.int32, logits.shape, 1)
    onehot = (columns == positive).astype(F32)
    per_row = jnp.sum(
        teacher * (log_teacher - log_student) - onehot * log_student, axis=1, keepdims=True
    )
    slopes = 2.0 * jnp.exp(log_student) - onehot - teacher
    return (per_row, slopes)


def grad_rows(resid, scales, gain, upstream):
    along = gain * upstream
    inner = jnp.mean(along * resid, axis=-1, keepdims=True)
    return (scales * along - resid * (scales * scales * scales) * inner).astype(BF16)


def by_tower(values, parts, tower):
    wide = values.shape[1] // parts
    blocks = [values[:, d * wide : (d + 1) * wide] for d in range(tower, parts, 2)]
    return jnp.concatenate(blocks, axis=1)


def kernel(
    qa, qg, gate_hbm, up_hbm, down_hbm, ia, ig, ig_w, iu_w, id_w, qf, if_, proj_hbm, ranks, positive,
    loss, q_out, i_out,
    w, stage, proj, proj_t, nq, part, gate_val, h2, pm, r1, r2, zs, zin, ni, wi, ip, land, hq, hi,
    sums, hats, scal, yq, hw, yi, gq, gi, qc1, qb1, qb2, qc, ic1, ib1, ib2, ic,
    loads, gs, gr, ss, sr, ws, wr, vs, vr, hs, hr, ias, iar, irs, irr,
    s1, s2, s3, ys, yr, iys, iyr, qs, qv, bs, bv,
):
    p = Place()
    n, dq = qa.shape
    m, di = ia.shape
    f, k = down_hbm.shape[0], id_w.shape[0]
    group = X * n
    h = n // 2
    parts = X * ZL
    count = hats.shape[0]
    block_wide = dq // count
    piece = w.shape[2] // 4
    wide, thin = dq // 2, dq // 4
    dp = lax.axis_index("dp")
    own = dp * 2 + p.w
    y, c = dp // 2, dp % 2
    yp, ym, y2 = (y + 1) % 4, (y + 3) % 4, (y + 2) % 4
    line_y = (y2, yp, ym, y)
    to_yp, to_ym, to_core = {"dp": yp * 2 + c}, {"dp": ym * 2 + c}, {"dp": y * 2 + 1 - c}
    to_y = (to_yp, to_ym)
    to_tower = {"tower": 1 - p.w}
    a2 = (p.a + 2) % ZL
    mate = p.a + 1 - 2 * (p.a % 2)
    to_a2, to_mate = p.column(a2), p.column(mate)

    def member(step):
        return {"tensor": (p.t + step) % parts}

    def replica(step):
        other = (own + step) % count
        return {"dp": other // 2, "tower": other % 2}

    own_weights = [
        pltpu.make_async_copy(ref, dst, loads.at[index])
        for index, (ref, dst) in enumerate(
            (
                (gate_hbm, w.at[0, 0, pl.ds(0, f), :]),
                (up_hbm, w.at[0, 1, pl.ds(0, f), :]),
                (down_hbm, stage),
            )
        )
    ]
    proj_copy = pltpu.make_async_copy(proj_hbm, proj, loads.at[3])
    for copy in own_weights:
        copy.start()
    proj_copy.start()
    barrier = pltpu.get_barrier_semaphore()

    def greet(step, _):
        pl.semaphore_signal(barrier, inc=1, device_id=member(step), device_id_type=MESH)
        pl.semaphore_signal(barrier, inc=1, device_id=replica(step), device_id_type=MESH)
        return 0

    lax.fori_loop(1, parts, greet, 0)
    for where in (p.zp, p.zm):
        pl.semaphore_signal(barrier, inc=1, device_id=where, device_id_type=MESH)
    for index in range(3):
        w[0, index, f:, :] = jnp.zeros((w.shape[2] - f, dq), BF16)
    nq[pl.ds(pl.multiple_of(p.b * n, n), n), :] = normed_rows(qa[...], gain_row(qg))
    ni[pl.ds(pl.multiple_of(p.z * m, m), m), :] = normed_rows(ia[...], gain_row(ig))
    for index, ref in enumerate((ig_w, iu_w, id_w)):
        wi[index, pl.ds(pl.multiple_of(p.b * k, k), k), :] = ref[...]
    pl.semaphore_wait(barrier, 2 * (parts - 1) + 2)

    rows = RowGather(p, nq, n, gs, gr)
    items = RingGather(p, ni, m, ias, iar)
    isum = RingSum(p, ip, land, m, irs, irr)

    def across():
        return remote(rows.block(0, p.b), rows.block(1, p.b), gs.at[0, 0], gr.at[0, 0], to_a2)

    def wpiece(which, index, line, core):
        first = pl.multiple_of(line * piece, piece)
        return w.at[which, index, pl.ds(first, piece), pl.ds(pl.multiple_of(core * wide, wide), wide)]

    def whalf(index, line, part_of):
        first = pl.multiple_of(line * piece, piece)
        column = pl.multiple_of(c * wide + part_of * thin, thin)
        return w.at[1, index, pl.ds(first, piece), pl.ds(column, thin)]

    def w_send(index, kind):
        here = wpiece(1, index, y, c)
        low, high = wpiece(1, index, ym, c), wpiece(1, index, yp, c)
        src, dst, where = (
            (wpiece(0, index, y, c), here, to_mate),
            (here, here, to_yp),
            (here, here, to_ym),
            (whalf(index, ym, 0), whalf(index, ym, 0), to_yp),
            (whalf(index, yp, 1), whalf(index, yp, 1), to_ym),
            (here, here, to_core),
            (low, low, to_core),
            (high, high, to_core),
            (wpiece(1, index, y2, c), wpiece(1, index, y2, c), to_core),
        )[kind]
        return remote(src, dst, ws.at[kind, index], wr.at[kind, index], where)

    def w_got(index, kind):
        dst = (
            wpiece(1, index, y, c),
            wpiece(1, index, ym, c),
            wpiece(1, index, yp, c),
            whalf(index, y2, 0),
            whalf(index, y2, 1),
            wpiece(1, index, y, 1 - c),
            wpiece(1, index, ym, 1 - c),
            wpiece(1, index, yp, 1 - c),
            wpiece(1, index, y2, 1 - c),
        )[kind]
        remote(dst, dst, ws.at[kind, index], wr.at[kind, index], to_core).wait_recv()

    def w_near(index):
        w_got(index, 0)
        for kind in (1, 2, 5) if index == 2 else (1, 2):
            w_send(index, kind).start()

    def w_ring(index):
        w_got(index, 1)
        w_send(index, 3).start()
        w_got(index, 2)
        w_send(index, 4).start()
        if index == 2:
            w_send(index, 6).start()
            w_send(index, 7).start()

    def w_far(index):
        w_got(index, 3)
        w_got(index, 4)
        if index == 2:
            w_send(index, 8).start()
        else:
            w_column(index, c).start()

    def w_column(index, core):
        ref = w.at[1, index, :, pl.ds(pl.multiple_of(core * wide, wide), wide)]
        return remote(ref, ref, ws.at[8, index], wr.at[8, index], to_core)

    def w_done(index):
        if index < 2:
            w_column(index, 1 - c).wait_recv()
        else:
            for kind in (5, 6, 7, 8):
                w_got(index, kind)

    def vpiece(b, core):
        column = pl.multiple_of(core * (di // 2), di // 2)
        return wi.at[:, pl.ds(pl.multiple_of(b * k, k), k), pl.ds(column, di // 2)]

    def vhalf(b, part_of):
        first = pl.multiple_of(b * k + part_of * (k // 2), k // 2)
        column = pl.multiple_of(c * (di // 2), di // 2)
        return wi.at[:, pl.ds(first, k // 2), pl.ds(column, di // 2)]

    def v_send(kind):
        ref, where = (
            (vpiece(p.b, c), p.xp),
            (vpiece(p.b, c), p.xm),
            (vhalf(p.bm, 0), p.xp),
            (vhalf(p.bp, 1), p.xm),
            (vpiece(p.bm, c), to_core),
            (vpiece(p.bp, c), to_core),
            (vpiece(p.bo, c), to_core),
        )[kind]
        return remote(ref, ref, vs.at[kind], vr.at[kind], where)

    def v_got(kind):
        ref = (
            vpiece(p.bm, c),
            vpiece(p.bp, c),
            vhalf(p.bo, 0),
            vhalf(p.bo, 1),
            vpiece(p.bm, 1 - c),
            vpiece(p.bp, 1 - c),
            vpiece(p.bo, 1 - c),
        )[kind]
        remote(ref, ref, vs.at[kind], vr.at[kind], to_core).wait_recv()

    def block(j, q, b):
        return rows_of(pm.at[q], (j * X + b) * n, n, n)

    def half(j, q, b, part_of):
        return rows_of(pm.at[q], (j * X + b) * n + part_of * h, h, h)

    def first(j, q, way):
        src = half(j, q, p.bo, way)
        where = (p.xp, p.xm)[way]
        return remote(src, r1.at[way, j, q], ss.at[way, j, q], sr.at[way, j, q], where)

    def second(j, q, way):
        src = block(j, q, (p.bp, p.bm)[way])
        where = (p.xp, p.xm)[way]
        return remote(src, r2.at[way, j, q], ss.at[2 + way, j, q], sr.at[2 + way, j, q], where)

    def to_owner(q):
        return remote(zs.at[q], zin.at[q], ss.at[4, 0, q], sr.at[4, 0, q], to_a2)

    def back(j, b):
        dst = rows_of(hq, ((p.a, a2)[j] * X + b) * n, n, n)
        src = h2.at[j, pl.ds(b * n, n), :]
        return remote(src, dst, hs.at[j, b], hr.at[j, b], to_mate)

    def back_got(j):
        other = (mate, (mate + 2) % ZL)[j]
        for b in range(X):
            dst = rows_of(hq, (other * X + b) * n, n, n)
            remote(dst, dst, hs.at[j, b], hr.at[j, b], to_mate).wait_recv()

    def rows_in(j):
        return nq[j * group : (j + 1) * group, :]

    def own_units(j):
        left = rows_in(j)
        value = gated(
            dot(left, w[0, 0, :f, :], ((1,), (1,))), dot(left, w[0, 1, :f, :], ((1,), (1,)))
        )
        hq[pl.ds(pl.multiple_of((p.a, a2)[j] * group, group), group), :] = value
        part[j] = dot(value, w[0, 2, :f, :])

    def mate_gate(j):
        gate_val[j] = dot(rows_in(j), w[1, 0, :f, :], ((1,), (1,)))

    def mate_up(j):
        h2[j] = gated(gate_val[j], dot(rows_in(j), w[1, 1, :f, :], ((1,), (1,))))
        if j == 1:
            for b in range(X):
                back(1, b).start()

    def mate_down(j, q):
        columns = slice(q * wide, (q + 1) * wide)
        total = part[j, :, columns] + dot(h2[j], w[1, 2, :f, columns])
        pm[q, j * group : (j + 1) * group, :] = total.astype(BF16)
        first(j, q, 0).start()
        first(j, q, 1).start()

    def combine(j, q):
        for way in range(2):
            first(j, q, way).wait_recv()
            ref = half(j, q, (p.bp, p.bm)[way], way)
            ref[...] = (ref[...].astype(F32) + r1[way, j, q].astype(F32)).astype(BF16)
            second(j, q, way).start()

    def summed(j, q):
        second(j, q, 0).wait_recv()
        second(j, q, 1).wait_recv()
        total = block(j, q, p.b)[...].astype(F32)
        return total + r2[0, j, q].astype(F32) + r2[1, j, q].astype(F32)

    def send_sum(q):
        zs[q] = summed(1, q).astype(BF16)
        to_owner(q).start()

    def item_hop(hop):
        items.take(hop)
        if hop < 4:
            items.start(hop + 1)

    def isum_hop(hop):
        isum.take(hop)
        isum.add(hop)
        isum.start(hop + 1)

    def item_product():
        left = ni[...]
        partial = 0.0
        for b in range(X):
            here = slice(b * k, (b + 1) * k)
            value = gated(
                dot(left, wi[0, here, :], ((1,), (1,))), dot(left, wi[1, here, :], ((1,), (1,)))
            )
            hi[b] = value
            partial = partial + dot(value, wi[2, here, :])
        ip[...] = partial.astype(BF16)
        isum.start(1)

    rows.right(0).start()
    rows.left(0).start()
    items.start(1)
    own_weights[0].wait()
    w_send(0, 0).start()
    across().start()
    own_weights[1].wait()
    own_weights[2].wait()
    for first_row in range(0, f, 112):
        chunk = stage[first_row : first_row + 112, :]
        for tower in range(2):
            columns = slice(tower * wide, (tower + 1) * wide)
            w[0, 2, first_row : first_row + 112, columns] = by_tower(chunk, count, tower)
    w_near(0)
    w_send(1, 0).start()
    rows.take_x(0)
    item_hop(1)
    v_send(0).start()
    v_send(1).start()
    rows.take_halves(0)
    own_units(0)
    item_hop(2)
    w_ring(0)
    w_near(1)
    w_send(2, 0).start()
    remote(rows.block(0, p.b), rows.block(1, p.b), gs.at[0, 0], gr.at[0, 0], to_a2).wait_recv()
    rows.right(1).start()
    rows.left(1).start()
    item_hop(3)
    w_far(0)
    for kind in range(2):
        v_got(kind)
        v_send(2 + kind).start()
        v_send(4 + kind).start()
    item_hop(4)
    w_ring(1)
    w_near(2)
    w_done(0)
    mate_gate(0)
    v_got(2)
    v_got(3)
    v_send(6).start()
    w_far(1)
    for kind in (4, 5, 6):
        v_got(kind)
    item_product()
    rows.take_x(1)
    w_done(1)
    mate_up(0)
    w_ring(2)
    isum_hop(1)
    proj_copy.wait()
    proj_t[...] = proj[...].T
    rows.take_halves(1)
    own_units(1)
    isum_hop(2)
    w_far(2)
    mate_gate(1)
    mate_up(1)
    w_done(2)
    def spread(buf, mine, sems, partner):
        def each(hop, _):
            remote(buf.at[mine], buf.at[mine], sems.at[0], sems.at[1], partner(hop)).start()
            return 0

        lax.fori_loop(1, buf.shape[0], each, 0)

    def gathered(buf, sems):
        ref = buf.at[pl.ds(0, buf.shape[0] - 1)]
        remote(ref, ref, sems.at[0], sems.at[1], member(1)).wait()

    def q_rows(tower, line_of, core):
        return rows_of(gq.at[tower], (line_of * 2 + core) * block_wide, block_wide, block_wide)

    def q_half(tower, line_of, way):
        first = (line_of * 2 + c) * block_wide + way * (block_wide // 2)
        return rows_of(gq.at[tower], first, block_wide // 2, block_wide // 2)

    def q_core(tower, j):
        src = q_rows(tower, line_y[j], 1 - c)
        return remote(src, qc1.at[tower, j], qs.at[tower, j], qv.at[tower, j], to_core)

    def q_first(tower, way):
        src, dst = q_half(tower, y2, way), qb1.at[tower, way]
        return remote(src, dst, qs.at[tower, 4 + way], qv.at[tower, 4 + way], to_y[way])

    def q_second(tower, way):
        src, dst = q_rows(tower, (yp, ym)[way], c), qb2.at[tower, way]
        return remote(src, dst, qs.at[tower, 6 + way], qv.at[tower, 6 + way], to_y[way])

    def q_tower(tower):
        return remote(q_rows(tower, y, c), qc, qs.at[tower, 8], qv.at[tower, 8], to_tower)

    def q_start(tower):
        for j in range(4):
            q_core(tower, j).start()

    def q_far(tower):
        q_core(tower, 0).wait_recv()
        ref = q_rows(tower, y2, c)
        ref[...] += qc1[tower, 0]
        for way in range(2):
            q_first(tower, way).start()

    def q_near(tower):
        for way in range(2):
            q_core(tower, 1 + way).wait_recv()
            ref = q_rows(tower, (yp, ym)[way], c)
            ref[...] += qc1[tower, 1 + way]
            q_first(tower, way).wait_recv()
            ref = q_half(tower, (yp, ym)[way], way)
            ref[...] += qb1[tower, way]
            q_second(tower, way).start()

    def q_own(tower):
        q_core(tower, 3).wait_recv()
        for way in range(2):
            q_second(tower, way).wait_recv()
        ref = q_rows(tower, y, c)
        ref[...] = ref[...] + qc1[tower, 3] + qb2[tower, 0] + qb2[tower, 1]

        @pl.when(p.w != tower)
        def _():
            q_tower(tower).start()

    def q_finish(tower):
        @pl.when(p.w == tower)
        def _():
            q_tower(tower).wait_recv()
            q_out[...] = q_rows(tower, y, c)[...] + qc[...]

    def i_rows(line_of, core):
        first = pl.multiple_of((line_of * 2 + core) * block_wide, block_wide)
        return gi.at[:, pl.ds(first, block_wide), :]

    def i_half(line_of, way):
        first = pl.multiple_of((line_of * 2 + c) * block_wide, block_wide)
        return gi.at[pl.ds(way * 2, 2), pl.ds(first, block_wide), :]

    def i_slab(b):
        return gi.at[b, pl.ds(pl.multiple_of((y * 2 + c) * block_wide, block_wide), block_wide), :]

    def i_core(j):
        return remote(i_rows(line_y[j], 1 - c), ic1.at[j], bs.at[j], bv.at[j], to_core)

    def i_first(way):
        return remote(i_half(y2, way), ib1.at[way], bs.at[4 + way], bv.at[4 + way], to_y[way])

    def i_second(way):
        src = i_rows((yp, ym)[way], c)
        return remote(src, ib2.at[way], bs.at[6 + way], bv.at[6 + way], to_y[way])

    def i_x(hop):
        other = (p.b + hop) % X
        where = {"tensor": p.a * X + other}
        return remote(i_slab(other), ic.at[p.b], bs.at[8 + hop], bv.at[8 + p.b], where)

    def i_product():
        for b in range(X):
            gi[b] = dot(yi[...], hi[b], ((0,), (0,)))
        for j in range(4):
            i_core(j).start()

    def i_far():
        for j in range(4):
            i_core(j).wait_recv()
            ref = i_rows(line_y[j], c)
            ref[...] += ic1[j]
        for way in range(2):
            i_first(way).start()

    def i_near():
        for way in range(2):
            i_first(way).wait_recv()
            ref = i_half((yp, ym)[way], way)
            ref[...] += ib1[way]
            i_second(way).start()

    def i_own():
        for way in range(2):
            i_second(way).wait_recv()
        ref = i_rows(y, c)
        ref[...] = ref[...] + ib2[0] + ib2[1]
        for hop in range(1, X):
            i_x(hop).start()

    def i_finish():
        total = i_slab(p.b)[...]
        for hop in range(1, X):
            other = (p.b + hop) % X
            remote(i_slab(other), ic.at[other], bs.at[8 + hop], bv.at[8 + other], p.xp).wait_recv()
            total = total + ic[other]
        i_out[...] = total

    gather = [RowGather(p, yq.at[tower], n, ys.at[tower], yr.at[tower]) for tower in range(2)]
    igather = RingGather(p, yi, m, iys, iyr)

    steps = (0, 1, 4, 2, 5, 3, 6, 7)

    def advance(index):
        if index < len(steps):
            g = steps[index]
            gather[g // ZL].take_z(p.order(g % ZL))
        if 0 <= index - 2 < len(steps):
            g = steps[index - 2]
            gather[g // ZL].take_x(p.order(g % ZL))

    def item_grad_hop(hop):
        igather.take(hop)
        if hop < 4:
            igather.start(hop + 1)

    def scale_hidden():
        line = lax.broadcasted_iota(jnp.int32, (128, 128), 0)
        tiles = [jnp.zeros((128, 128), F32)] * 2
        for t in range(parts):
            for kind in range(2):
                tiles[kind] = jnp.where(line == t, scal[t, kind : kind + 1, :], tiles[kind])
        scale_of, slope_of = tiles[0].T[:n], tiles[1].T[:n]
        total = jnp.zeros((1, f), F32)
        for t in range(parts):
            here = slice(t * n, (t + 1) * n)
            value = hq[here, :].astype(F32)
            hw[here, :] = (value * slope_of[:, t : t + 1]).astype(BF16)
            total = total + jnp.sum(value * scale_of[:, t : t + 1], axis=0, keepdims=True)
        return total

    def product(tower, part_of):
        total = 0.0
        for j in (2 * part_of, 2 * part_of + 1):
            s = p.order(j)
            gather[tower].take_halves(s)
            here = pl.ds(pl.multiple_of(s * group, group), group)
            total = total + dot(yq[tower, here, :], hw[here, :], ((0,), (0,)))
        if part_of == 0:
            column = jnp.broadcast_to(along_of[tower], (128, wide)).T[:, 0:1]
            gq[tower] = column * summed_hidden - total
        else:
            gq[tower] -= total

    def resid_half(tower):
        total = summed(0, tower)
        to_owner(tower).wait_recv()
        total = total + zin[tower].astype(F32)
        value = by_tower(qa[...], count, tower).astype(F32) + total
        yq[tower, pl.ds(pl.multiple_of(p.t * n, n), n), :] = value.astype(BF16)
        return value

    mate_down(1, 0)
    mate_down(0, 0)
    combine(1, 0)
    mate_down(1, 1)
    combine(0, 0)
    mate_down(0, 1)
    send_sum(0)
    combine(1, 1)
    combine(0, 1)
    isum_hop(3)
    send_sum(1)
    q_resid = [resid_half(0)]
    advance(0)
    back(0, 0).start()
    isum.take(4)
    own_item = ip[pl.ds(pl.multiple_of(p.z * m, m), m), :].astype(F32)
    i_resid = ia[...].astype(F32) + (own_item + land[0, 3].astype(F32) + land[1, 3].astype(F32))
    i_gain = gain_row(if_)
    i_scale = rms_scale(i_resid)
    sums[p.t, :, dq:] = jnp.sum(i_resid * i_scale * i_gain, axis=0, keepdims=True)
    q_gain = gain_row(qf)
    gain_of = [by_tower(q_gain, count, tower) for tower in range(2)]
    advance(1)
    q_resid.append(resid_half(1))
    square = sum(jnp.sum(value * value, axis=-1, keepdims=True) for value in q_resid)
    q_scale = lax.rsqrt(square / dq + EPS)
    for tower in range(2):
        part_sum = jnp.sum(q_resid[tower] * q_scale * gain_of[tower], axis=0, keepdims=True)
        sums[p.t, :, tower * wide : (tower + 1) * wide] = part_sum
    spread(sums, p.t, s1, member)
    advance(2)
    back(0, 1).start()
    gathered(sums, s1)
    total = sums[0]
    for slot in range(1, parts):
        total = total + sums[slot]
    firsts = [(d % 2) * wide + (d // 2) * block_wide for d in range(count)]
    q_pooled = jnp.concatenate([total[:, at : at + block_wide] for at in firsts], axis=1) / QLEN
    i_pooled = total[:, dq:] / ILEN
    q_e = jnp.sum(dot(split_rows(q_pooled), proj[...]), axis=0, keepdims=True)
    q_norm, i_norm = unit_scale(q_e), unit_scale(i_pooled)
    hats[own, :, :di] = q_e * q_norm
    hats[own, :, di:] = i_pooled * i_norm
    spread(hats, own, s2, replica)
    advance(3)
    back(0, 2).start()
    gathered(hats, s2)
    index = lax.broadcasted_iota(jnp.int32, (count, 2 * di), 0)
    every = jnp.zeros((count, 2 * di), F32)
    for slot in range(count):
        every = jnp.where(index == slot, hats[slot], every)
    every_query, every_items = every[:, :di], every[:, di:]
    line = lax.broadcasted_iota(jnp.int32, (count, count), 0)
    target = jnp.zeros((count, count), jnp.int32)
    for slot in range(count):
        target = jnp.where(line == slot, positive[slot], target)
    per_row, slopes = contrast(every_query, every_items, ranks[...], target)
    loss[...] = jnp.sum(per_row, axis=0, keepdims=True) / count
    weights = slopes * (LOSS_SCALE / (TAU * count))
    advance(4)
    back(0, 3).start()
    mine = lax.broadcasted_iota(jnp.int32, (count, di), 0) == own
    q_back = jnp.sum(
        jnp.where(mine, dot(weights, every_items, precision=HIGH), 0.0), axis=0, keepdims=True
    )
    column = lax.broadcasted_iota(jnp.int32, (count, count), 1) == own
    i_back = jnp.sum(
        jnp.sum(jnp.where(column, weights, 0.0), axis=1, keepdims=True) * every_query,
        axis=0,
        keepdims=True,
    )
    advance(5)
    q_grad_e = unit_back(q_e, q_norm, q_back)
    q_up = jnp.sum(dot(split_rows(q_grad_e), proj_t[...]), axis=0, keepdims=True) / QLEN
    i_up = unit_back(i_pooled, i_norm, i_back) / ILEN
    along = q_gain * q_up
    along_of = [by_tower(along, count, tower) for tower in range(2)]
    inner = sum(
        jnp.sum(along_of[tower] * q_resid[tower], axis=-1, keepdims=True) for tower in range(2)
    )
    inner = inner / dq
    slope = (q_scale * q_scale * q_scale) * inner
    lane = lax.broadcasted_iota(jnp.int32, (n, 128), 1)
    columns = jnp.where(lane == 0, q_scale, jnp.where(lane == 1, slope, 0.0))
    columns = jnp.concatenate([columns, jnp.zeros((128 - n, 128), F32)], axis=0)
    scal[p.t] = columns.T[:8]
    spread(scal, p.t, s3, member)
    yi[pl.ds(pl.multiple_of(p.z * m, m), m), :] = grad_rows(i_resid, i_scale, i_gain, i_up)
    igather.start(1)
    advance(6)
    gathered(scal, s3)
    back_got(0)
    back_got(1)
    summed_hidden = scale_hidden()
    advance(7)
    item_grad_hop(1)
    product(0, 0)
    advance(8)
    item_grad_hop(2)
    product(0, 1)
    q_start(0)
    advance(9)
    item_grad_hop(3)
    q_far(0)
    product(1, 0)
    item_grad_hop(4)
    q_near(0)
    i_product()
    product(1, 1)
    q_start(1)
    q_far(1)
    q_own(0)
    i_far()
    q_near(1)
    i_near()
    q_own(1)
    i_own()
    q_finish(0)
    i_finish()
    q_finish(1)

    for j in range(2):
        for b in range(X):
            back(j, b).wait_send()
        for copy in (rows.right(j), rows.left(j), rows.half_right(j), rows.half_left(j)):
            copy.wait_send()
        for q in range(2):
            for way in range(2):
                first(j, q, way).wait_send()
                second(j, q, way).wait_send()
    for q in range(2):
        to_owner(q).wait_send()
    across().wait_send()
    items.drain()
    isum.drain()
    for index in range(3):
        for kind in range(9) if index == 2 else range(5):
            w_send(index, kind).wait_send()
    for index in range(2):
        w_column(index, c).wait_send()
    for kind in range(7):
        v_send(kind).wait_send()
    for tower in range(2):
        gather[tower].drain()
        for j in range(4):
            q_core(tower, j).wait_send()
        for way in range(2):
            q_first(tower, way).wait_send()
            q_second(tower, way).wait_send()

        @pl.when(p.w != tower)
        def _():
            q_tower(tower).wait_send()

    igather.drain()
    for j in range(4):
        i_core(j).wait_send()
    for way in range(2):
        i_first(way).wait_send()
        i_second(way).wait_send()
    for hop in range(1, X):
        i_x(hop).wait_send()


def step(qa, qg, gate, up, down, ia, ig, ig_w, iu_w, id_w, qf, if_, proj, ranks, positive):
    n, dq = qa.shape
    m, di = ia.shape
    f, k = down.shape[0], id_w.shape[0]
    padded = 64 * ((f + 63) // 64)
    vmem, hbm = pl.BlockSpec(memory_space=pltpu.VMEM), pl.BlockSpec(memory_space=pl.ANY)
    smem = pl.BlockSpec(memory_space=pltpu.SMEM)
    all_i = ZR * m
    group = X * n
    parts = X * ZL
    count = ranks.shape[0]
    wide = dq // count
    dma = pltpu.SemaphoreType.DMA
    return pl.pallas_call(
        kernel,
        out_shape=(
            jax.ShapeDtypeStruct((1, 1), F32),
            jax.ShapeDtypeStruct((wide, f), F32),
            jax.ShapeDtypeStruct((wide, k), F32),
        ),
        in_specs=[vmem, vmem, hbm, hbm, hbm] + [vmem] * 7 + [hbm, vmem, smem],
        out_specs=[vmem] * 3,
        scratch_shapes=[
            pltpu.VMEM((2, 3, padded, dq), BF16),
            pltpu.VMEM(down.shape, BF16),
            pltpu.VMEM(proj.shape, BF16),
            pltpu.VMEM((proj.shape[1], proj.shape[0]), BF16),
            pltpu.VMEM((2 * group, dq), BF16),
            pltpu.VMEM((2, group, dq), F32),
            pltpu.VMEM((2, group, f), F32),
            pltpu.VMEM((2, group, f), BF16),
            pltpu.VMEM((2, 2 * group, dq // 2), BF16),
            pltpu.VMEM((2, 2, 2, n // 2, dq // 2), BF16),
            pltpu.VMEM((2, 2, 2, n, dq // 2), BF16),
            pltpu.VMEM((2, n, dq // 2), BF16),
            pltpu.VMEM((2, n, dq // 2), BF16),
            pltpu.VMEM((all_i, di), BF16),
            pltpu.VMEM((3, X * k, di), BF16),
            pltpu.VMEM((all_i, di), BF16),
            pltpu.VMEM((2, 4, m, di), BF16),
            pltpu.VMEM((ZL * group, f), BF16),
            pltpu.VMEM((X, all_i, k), BF16),
            pltpu.VMEM((parts, 1, dq + di), F32),
            pltpu.VMEM((count, 1, 2 * di), F32),
            pltpu.VMEM((parts, 8, 128), F32),
            pltpu.VMEM((2, parts * n, dq // 2), BF16),
            pltpu.VMEM((ZL * group, f), BF16),
            pltpu.VMEM((all_i, di), BF16),
            pltpu.VMEM((2, dq // 2, f), F32),
            pltpu.VMEM((X, di, k), F32),
            pltpu.VMEM((2, 4, wide, f), F32),
            pltpu.VMEM((2, 2, wide // 2, f), F32),
            pltpu.VMEM((2, 2, wide, f), F32),
            pltpu.VMEM((wide, f), F32),
            pltpu.VMEM((4, X, wide, k), F32),
            pltpu.VMEM((2, 2, wide, k), F32),
            pltpu.VMEM((2, X, wide, k), F32),
            pltpu.VMEM((X, wide, k), F32),
            dma((4,)),
            dma((6, 2)),
            dma((5, 2)),
            dma((5, 2, 2)),
            dma((5, 2, 2)),
            dma((9, 3)),
            dma((9, 3)),
            dma((7,)),
            dma((7,)),
            dma((2, X)),
            dma((2, X)),
            dma((2, 4)),
            dma((2, 4)),
            dma((2, 4)),
            dma((2, 4)),
            dma((2,)),
            dma((2,)),
            dma((2,)),
            dma((2, 6, ZL)),
            dma((2, 5, ZL)),
            dma((2, 4)),
            dma((2, 4)),
            dma((2, 9)),
            dma((2, 9)),
            dma((12,)),
            dma((12,)),
        ],
        compiler_params=pltpu.CompilerParams(
            collective_id=0, has_side_effects=True, vmem_limit_bytes=VMEM_LIMIT
        ),
        name="towers_step",
    )(qa, qg, gate, up, down, ia, ig, ig_w, iu_w, id_w, qf, if_, proj, ranks, positive)


def body(
    q_act,
    q_norm_gain,
    q_gate,
    q_up,
    q_down,
    q_final_gain,
    projection,
    i_act,
    i_norm_gain,
    i_gate,
    i_up,
    i_down,
    i_final_gain,
    ranks,
    positive,
):
    loss, q_grad, i_grad = step(
        q_act,
        q_norm_gain,
        q_gate.T,
        q_up.T,
        q_down,
        i_act,
        i_norm_gain,
        i_gate.T,
        i_up.T,
        i_down,
        q_final_gain,
        i_final_gain,
        projection,
        ranks,
        positive,
    )
    return (loss.reshape(()), q_grad.T, i_grad.T)


def solution(mesh):
    in_specs = (
        P(("dp", "tower", "tensor"), None),
        P(),
        P(None, "tensor"),
        P(None, "tensor"),
        P("tensor", None),
        P(),
        P(),
        P(("dp", "tower", "tensor"), None),
        P(),
        P(None, ("tower", "tensor")),
        P(None, ("tower", "tensor")),
        P(("tower", "tensor"), None),
        P(),
        P(),
        P(),
    )
    out_specs = (P(), P("tensor", ("dp", "tower")), P(("tower", "tensor"), "dp"))
    return jax.shard_map(body, mesh=mesh, in_specs=in_specs, out_specs=out_specs, check_vma=False)
```

```python
import functools

import jax
import jax.numpy as jnp
from jax import lax
from jax.experimental import pallas as pl
from jax.experimental.pallas import tpu as pltpu
from jax.sharding import PartitionSpec as P

QLEN = 1536
ILEN = 512
EPS = 1e-06
TAU = 0.05
TEACH = 2.0
LOSS_SCALE = 64.0
HIGH = lax.Precision.HIGHEST
MESH = pl.DeviceIdType.MESH
F32 = jnp.float32
BF16 = jnp.bfloat16

X = 4
ZL = 4
ZR = 8
VMEM_LIMIT = 60 * 1024 * 1024


def rms_scale(values):
    return lax.rsqrt(jnp.mean(values * values, axis=-1, keepdims=True) + EPS)


def dot(left, right, dims=((1,), (0,)), precision=None):
    return lax.dot_general(
        left, right, (dims, ((), ())), preferred_element_type=F32, precision=precision
    )


def remote(src, dst, send, recv, where):
    return pltpu.make_async_remote_copy(
        src_ref=src, dst_ref=dst, send_sem=send, recv_sem=recv, device_id=where, device_id_type=MESH
    )


class Place:
    def __init__(self):
        self.t = lax.axis_index("tensor")
        self.w = lax.axis_index("tower")
        self.a = self.t // X
        self.b = self.t % X
        self.z = self.w * ZL + self.a
        self.bp = (self.b + 1) % X
        self.bm = (self.b + X - 1) % X
        self.bo = (self.b + 2) % X
        self.xp = {"tensor": self.a * X + self.bp}
        self.xm = {"tensor": self.a * X + self.bm}
        self.zp = self.ring(1)
        self.zm = self.ring(ZR - 1)

    def ring(self, step):
        z = (self.z + step) % ZR
        return {"tower": z // ZL, "tensor": (z % ZL) * X + self.b}

    def column(self, row):
        return {"tensor": row * X + self.b}

    def order(self, j):
        near = jnp.minimum(self.a, ZL - 1 - self.a)
        swapped = jnp.where(j == 0, 1, jnp.where(j == 1, 0, j))
        row = jnp.where(near == 1, swapped, j)
        return jnp.where(self.a >= 2, ZL - 1 - row, row)


def rows_of(ref, first, count, unit):
    return ref.at[pl.ds(pl.multiple_of(first, unit), count), :]


class RowGather:
    def __init__(self, place, buf, rows, send, recv):
        self.p, self.buf, self.n, self.send, self.recv = place, buf, rows, send, recv

    def block(self, s, b):
        return rows_of(self.buf, (s * X + b) * self.n, self.n, self.n)

    def half(self, s, b, h):
        n = self.n // 2
        return rows_of(self.buf, (s * X + b) * self.n + h * n, n, n)

    def up(self, s):
        ref = self.block(s, self.p.b)
        where = self.p.column(jnp.minimum(self.p.a + 1, ZL - 1))
        return remote(ref, ref, self.send.at[0, s], self.recv.at[0, s], where)

    def down(self, s):
        ref = self.block(s, self.p.b)
        where = self.p.column(jnp.maximum(self.p.a - 1, 0))
        return remote(ref, ref, self.send.at[1, s], self.recv.at[0, s], where)

    def right(self, s):
        ref = self.block(s, self.p.b)
        return remote(ref, ref, self.send.at[2, s], self.recv.at[1, s], self.p.xp)

    def left(self, s):
        ref = self.block(s, self.p.b)
        return remote(ref, ref, self.send.at[3, s], self.recv.at[2, s], self.p.xm)

    def half_right(self, s):
        ref = self.half(s, self.p.bm, 0)
        return remote(ref, ref, self.send.at[4, s], self.recv.at[3, s], self.p.xp)

    def half_left(self, s):
        ref = self.half(s, self.p.bp, 1)
        return remote(ref, ref, self.send.at[5, s], self.recv.at[4, s], self.p.xm)

    def goes_up(self, s):
        return (s <= self.p.a) & (self.p.a < ZL - 1)

    def goes_down(self, s):
        return (s >= self.p.a) & (self.p.a > 0)

    def take_z(self, s):
        @pl.when(s != self.p.a)
        def _():
            self.up(s).wait_recv()

        @pl.when(self.goes_up(s))
        def _():
            self.up(s).start()

        @pl.when(self.goes_down(s))
        def _():
            self.down(s).start()

        self.right(s).start()
        self.left(s).start()

    def take_x(self, s):
        ref = self.block(s, self.p.bm)
        remote(ref, ref, self.send.at[2, s], self.recv.at[1, s], self.p.xm).wait_recv()
        self.half_right(s).start()
        ref = self.block(s, self.p.bp)
        remote(ref, ref, self.send.at[3, s], self.recv.at[2, s], self.p.xp).wait_recv()
        self.half_left(s).start()

    def take_halves(self, s):
        ref = self.half(s, self.p.bo, 0)
        remote(ref, ref, self.send.at[4, s], self.recv.at[3, s], self.p.xm).wait_recv()
        ref = self.half(s, self.p.bo, 1)
        remote(ref, ref, self.send.at[5, s], self.recv.at[4, s], self.p.xp).wait_recv()

    def drain(self):
        def each(s, _):
            @pl.when(self.goes_up(s))
            def _():
                self.up(s).wait_send()

            @pl.when(self.goes_down(s))
            def _():
                self.down(s).wait_send()

            self.right(s).wait_send()
            self.left(s).wait_send()
            self.half_right(s).wait_send()
            self.half_left(s).wait_send()
            return 0

        lax.fori_loop(0, ZL, each, 0)


class RingGather:
    def __init__(self, place, buf, rows, send, recv):
        self.p, self.buf, self.n, self.send, self.recv = place, buf, rows, send, recv

    def ref(self, z, hop, upward):
        z = (z + 2 * ZR) % ZR
        if hop < 4:
            return rows_of(self.buf, z * self.n, self.n, self.n)
        n = self.n // 2
        return rows_of(self.buf, z * self.n + (0 if upward else n), n, n)

    def copies(self, hop):
        up = self.ref(self.p.z - hop + 1, hop, True)
        down = self.ref(self.p.z + hop - 1, hop, False)
        return (
            remote(up, up, self.send.at[0, hop - 1], self.recv.at[0, hop - 1], self.p.zp),
            remote(down, down, self.send.at[1, hop - 1], self.recv.at[1, hop - 1], self.p.zm),
        )

    def start(self, hop):
        for copy in self.copies(hop):
            copy.start()

    def take(self, hop):
        up = self.ref(self.p.z - hop, hop, True)
        down = self.ref(self.p.z + hop, hop, False)
        remote(up, up, self.send.at[0, hop - 1], self.recv.at[0, hop - 1], self.p.zm).wait_recv()
        remote(down, down, self.send.at[1, hop - 1], self.recv.at[1, hop - 1], self.p.zp).wait_recv()

    def drain(self):
        for hop in range(1, 5):
            for copy in self.copies(hop):
                copy.wait_send()


class RingSum:
    def __init__(self, place, buf, land, rows, send, recv):
        self.p, self.buf, self.land = place, buf, land
        self.n, self.send, self.recv = rows, send, recv

    def part(self, z, half):
        z = (z + 2 * ZR) % ZR
        if half is None:
            return rows_of(self.buf, z * self.n, self.n, self.n)
        n = self.n // 2
        return rows_of(self.buf, z * self.n + half * n, n, n)

    def slot(self, way, hop):
        if hop == 1:
            return self.land.at[way, 0, pl.ds(0, self.n // 2), :]
        return self.land.at[way, hop - 1]

    def copies(self, hop):
        half = (0, 1) if hop == 1 else (None, None)
        up = self.part(self.p.z + 5 - hop, half[0])
        down = self.part(self.p.z - 5 + hop, half[1])
        return (
            remote(up, self.slot(0, hop), self.send.at[0, hop - 1], self.recv.at[0, hop - 1], self.p.zp),
            remote(down, self.slot(1, hop), self.send.at[1, hop - 1], self.recv.at[1, hop - 1], self.p.zm),
        )

    def start(self, hop):
        for copy in self.copies(hop):
            copy.start()

    def take(self, hop):
        for copy in self.copies(hop):
            copy.wait_recv()

    def add(self, hop):
        half = (0, 1) if hop == 1 else (None, None)
        for way, z in ((0, self.p.z + 4 - hop), (1, self.p.z - 4 + hop)):
            ref = self.part(z, half[way])
            ref[...] = (ref[...].astype(F32) + self.slot(way, hop)[...].astype(F32)).astype(BF16)

    def drain(self):
        for hop in range(1, 5):
            for copy in self.copies(hop):
                copy.wait_send()


def gain_row(ref):
    return ref[...].astype(F32).reshape(1, -1)


def normed_rows(act, gain):
    values = act.astype(F32)
    return (values * rms_scale(values) * gain).astype(BF16)


def gated(gate_val, up_val):
    return (jax.nn.silu(gate_val) * up_val).astype(BF16)


def at_step(i, step):
    return pl.when(i == step)


def split_rows(row):
    high = row.astype(BF16).astype(F32)
    rest = row - high
    mid = rest.astype(BF16).astype(F32)
    low = rest - mid
    index = lax.broadcasted_iota(jnp.int32, (8, row.shape[1]), 0)
    out = jnp.where(index == 0, high, jnp.where(index == 1, mid, jnp.where(index == 2, low, 0.0)))
    return out.astype(BF16)


def unit_scale(vec):
    return lax.rsqrt(jnp.sum(vec * vec, axis=-1, keepdims=True) + EPS)


def unit_back(vec, scales, upstream):
    inner = jnp.sum(vec * upstream, axis=-1, keepdims=True)
    return scales * upstream - vec * (scales * scales * scales) * inner


def contrast(query_hat, item_hat, ranks, positive):
    logits = dot(query_hat, item_hat, ((1,), (1,)), HIGH) / TAU
    shifted = logits - 1.0 / TAU
    log_student = shifted - jnp.log(jnp.sum(jnp.exp(shifted), axis=1, keepdims=True))
    teach = -ranks.astype(F32) / TEACH
    log_teacher = teach - jnp.log(jnp.sum(jnp.exp(teach), axis=1, keepdims=True))
    teacher = jnp.exp(log_teacher)
    columns = lax.broadcasted_iota(jnp.int32, logits.shape, 1)
    onehot = (columns == positive).astype(F32)
    per_row = jnp.sum(
        teacher * (log_teacher - log_student) - onehot * log_student, axis=1, keepdims=True
    )
    slopes = 2.0 * jnp.exp(log_student) - onehot - teacher
    return (per_row, slopes)


def grad_rows(resid, scales, gain, upstream):
    along = gain * upstream
    inner = jnp.mean(along * resid, axis=-1, keepdims=True)
    return (scales * along - resid * (scales * scales * scales) * inner).astype(BF16)


def by_tower(values, parts, tower):
    wide = values.shape[1] // parts
    blocks = [values[:, d * wide : (d + 1) * wide] for d in range(tower, parts, 2)]
    return jnp.concatenate(blocks, axis=1)


def kernel(
    qa, qg, gate_hbm, up_hbm, down_hbm, ia, ig, ig_w, iu_w, id_w, qf, if_, proj_hbm, ranks, positive,
    loss, q_out, i_out,
    w, stage, proj, proj_t, nq, part, gate_val, h2, pm, r1, r2, zs, zin, ni, wi, ip, land, hq, hi,
    sums, hats, scal, yq, hw, yi, gq, gi, qc1, qb1, qb2, qc, ic1, ib1, ib2, ic,
    loads, gs, gr, ss, sr, ws, wr, vs, vr, hs, hr, ias, iar, irs, irr,
    s1, s2, s3, ys, yr, iys, iyr, qs, qv, bs, bv,
):
    p = Place()
    n, dq = qa.shape
    m, di = ia.shape
    f, k = down_hbm.shape[0], id_w.shape[0]
    group = X * n
    h = n // 2
    parts = X * ZL
    count = hats.shape[0]
    block_wide = dq // count
    piece = w.shape[2] // 4
    wide, thin = dq // 2, dq // 4
    dp = lax.axis_index("dp")
    own = dp * 2 + p.w
    y, c = dp // 2, dp % 2
    yp, ym, y2 = (y + 1) % 4, (y + 3) % 4, (y + 2) % 4
    line_y = (y2, yp, ym, y)
    to_yp, to_ym, to_core = {"dp": yp * 2 + c}, {"dp": ym * 2 + c}, {"dp": y * 2 + 1 - c}
    to_y = (to_yp, to_ym)
    to_tower = {"tower": 1 - p.w}
    a2 = (p.a + 2) % ZL
    mate = p.a + 1 - 2 * (p.a % 2)
    to_a2, to_mate = p.column(a2), p.column(mate)

    def member(step):
        return {"tensor": (p.t + step) % parts}

    def replica(step):
        other = (own + step) % count
        return {"dp": other // 2, "tower": other % 2}

    own_weights = [
        pltpu.make_async_copy(ref, dst, loads.at[index])
        for index, (ref, dst) in enumerate(
            (
                (gate_hbm, w.at[0, 0, pl.ds(0, f), :]),
                (up_hbm, w.at[0, 1, pl.ds(0, f), :]),
                (down_hbm, stage),
            )
        )
    ]
    proj_copy = pltpu.make_async_copy(proj_hbm, proj, loads.at[3])
    for copy in own_weights:
        copy.start()
    proj_copy.start()
    barrier = pltpu.get_barrier_semaphore()

    def greet(step, _):
        pl.semaphore_signal(barrier, inc=1, device_id=member(step), device_id_type=MESH)
        pl.semaphore_signal(barrier, inc=1, device_id=replica(step), device_id_type=MESH)
        return 0

    lax.fori_loop(1, parts, greet, 0)
    for where in (p.zp, p.zm):
        pl.semaphore_signal(barrier, inc=1, device_id=where, device_id_type=MESH)
    for index in range(3):
        w[0, index, f:, :] = jnp.zeros((w.shape[2] - f, dq), BF16)
    nq[pl.ds(pl.multiple_of(p.b * n, n), n), :] = normed_rows(qa[...], gain_row(qg))
    ni[pl.ds(pl.multiple_of(p.z * m, m), m), :] = normed_rows(ia[...], gain_row(ig))
    for index, ref in enumerate((ig_w, iu_w, id_w)):
        wi[index, pl.ds(pl.multiple_of(p.b * k, k), k), :] = ref[...]
    pl.semaphore_wait(barrier, 2 * (parts - 1) + 2)

    rows = RowGather(p, nq, n, gs, gr)
    items = RingGather(p, ni, m, ias, iar)
    isum = RingSum(p, ip, land, m, irs, irr)

    def across():
        return remote(rows.block(0, p.b), rows.block(1, p.b), gs.at[0, 0], gr.at[0, 0], to_a2)

    def wpiece(which, index, line, core):
        first = pl.multiple_of(line * piece, piece)
        return w.at[which, index, pl.ds(first, piece), pl.ds(pl.multiple_of(core * wide, wide), wide)]

    def whalf(index, line, part_of):
        first = pl.multiple_of(line * piece, piece)
        column = pl.multiple_of(c * wide + part_of * thin, thin)
        return w.at[1, index, pl.ds(first, piece), pl.ds(column, thin)]

    def w_send(index, kind):
        here = wpiece(1, index, y, c)
        low, high = wpiece(1, index, ym, c), wpiece(1, index, yp, c)
        src, dst, where = (
            (wpiece(0, index, y, c), here, to_mate),
            (here, here, to_yp),
            (here, here, to_ym),
            (whalf(index, ym, 0), whalf(index, ym, 0), to_yp),
            (whalf(index, yp, 1), whalf(index, yp, 1), to_ym),
            (here, here, to_core),
            (low, low, to_core),
            (high, high, to_core),
            (wpiece(1, index, y2, c), wpiece(1, index, y2, c), to_core),
        )[kind]
        return remote(src, dst, ws.at[kind, index], wr.at[kind, index], where)

    def w_got(index, kind):
        dst = (
            wpiece(1, index, y, c),
            wpiece(1, index, ym, c),
            wpiece(1, index, yp, c),
            whalf(index, y2, 0),
            whalf(index, y2, 1),
            wpiece(1, index, y, 1 - c),
            wpiece(1, index, ym, 1 - c),
            wpiece(1, index, yp, 1 - c),
            wpiece(1, index, y2, 1 - c),
        )[kind]
        remote(dst, dst, ws.at[kind, index], wr.at[kind, index], to_core).wait_recv()

    def w_near(index):
        w_got(index, 0)
        for kind in (1, 2, 5) if index == 2 else (1, 2):
            w_send(index, kind).start()

    def w_ring(index):
        w_got(index, 1)
        w_send(index, 3).start()
        w_got(index, 2)
        w_send(index, 4).start()
        if index == 2:
            w_send(index, 6).start()
            w_send(index, 7).start()

    def w_far(index):
        w_got(index, 3)
        w_got(index, 4)
        if index == 2:
            w_send(index, 8).start()
        else:
            w_column(index, c).start()

    def w_column(index, core):
        ref = w.at[1, index, :, pl.ds(pl.multiple_of(core * wide, wide), wide)]
        return remote(ref, ref, ws.at[8, index], wr.at[8, index], to_core)

    def w_done(index):
        if index < 2:
            w_column(index, 1 - c).wait_recv()
        else:
            for kind in (5, 6, 7, 8):
                w_got(index, kind)

    def vpiece(b, core):
        column = pl.multiple_of(core * (di // 2), di // 2)
        return wi.at[:, pl.ds(pl.multiple_of(b * k, k), k), pl.ds(column, di // 2)]

    def vhalf(b, part_of):
        first = pl.multiple_of(b * k + part_of * (k // 2), k // 2)
        column = pl.multiple_of(c * (di // 2), di // 2)
        return wi.at[:, pl.ds(first, k // 2), pl.ds(column, di // 2)]

    def v_send(kind):
        ref, where = (
            (vpiece(p.b, c), p.xp),
            (vpiece(p.b, c), p.xm),
            (vhalf(p.bm, 0), p.xp),
            (vhalf(p.bp, 1), p.xm),
            (vpiece(p.bm, c), to_core),
            (vpiece(p.bp, c), to_core),
            (vpiece(p.bo, c), to_core),
        )[kind]
        return remote(ref, ref, vs.at[kind], vr.at[kind], where)

    def v_got(kind):
        ref = (
            vpiece(p.bm, c),
            vpiece(p.bp, c),
            vhalf(p.bo, 0),
            vhalf(p.bo, 1),
            vpiece(p.bm, 1 - c),
            vpiece(p.bp, 1 - c),
            vpiece(p.bo, 1 - c),
        )[kind]
        remote(ref, ref, vs.at[kind], vr.at[kind], to_core).wait_recv()

    def block(j, q, b):
        return rows_of(pm.at[q], (j * X + b) * n, n, n)

    def half(j, q, b, part_of):
        return rows_of(pm.at[q], (j * X + b) * n + part_of * h, h, h)

    def first(j, q, way):
        src = half(j, q, p.bo, way)
        where = (p.xp, p.xm)[way]
        return remote(src, r1.at[way, j, q], ss.at[way, j, q], sr.at[way, j, q], where)

    def second(j, q, way):
        src = block(j, q, (p.bp, p.bm)[way])
        where = (p.xp, p.xm)[way]
        return remote(src, r2.at[way, j, q], ss.at[2 + way, j, q], sr.at[2 + way, j, q], where)

    def to_owner(q):
        return remote(zs.at[q], zin.at[q], ss.at[4, 0, q], sr.at[4, 0, q], to_a2)

    def back(j, b):
        dst = rows_of(hq, ((p.a, a2)[j] * X + b) * n, n, n)
        src = h2.at[j, pl.ds(b * n, n), :]
        return remote(src, dst, hs.at[j, b], hr.at[j, b], to_mate)

    def back_got(j):
        other = (mate, (mate + 2) % ZL)[j]
        for b in range(X):
            dst = rows_of(hq, (other * X + b) * n, n, n)
            remote(dst, dst, hs.at[j, b], hr.at[j, b], to_mate).wait_recv()

    def rows_in(j):
        return nq[j * group : (j + 1) * group, :]

    def own_units(j):
        left = rows_in(j)
        value = gated(
            dot(left, w[0, 0, :f, :], ((1,), (1,))), dot(left, w[0, 1, :f, :], ((1,), (1,)))
        )
        hq[pl.ds(pl.multiple_of((p.a, a2)[j] * group, group), group), :] = value
        part[j] = dot(value, w[0, 2, :f, :])

    def mate_gate(j):
        gate_val[j] = dot(rows_in(j), w[1, 0, :f, :], ((1,), (1,)))

    def mate_up(j):
        h2[j] = gated(gate_val[j], dot(rows_in(j), w[1, 1, :f, :], ((1,), (1,))))
        if j == 1:
            for b in range(X):
                back(1, b).start()

    def mate_down(j, q):
        columns = slice(q * wide, (q + 1) * wide)
        total = part[j, :, columns] + dot(h2[j], w[1, 2, :f, columns])
        pm[q, j * group : (j + 1) * group, :] = total.astype(BF16)
        first(j, q, 0).start()
        first(j, q, 1).start()

    def combine(j, q):
        for way in range(2):
            first(j, q, way).wait_recv()
            ref = half(j, q, (p.bp, p.bm)[way], way)
            ref[...] = (ref[...].astype(F32) + r1[way, j, q].astype(F32)).astype(BF16)
            second(j, q, way).start()

    def summed(j, q):
        second(j, q, 0).wait_recv()
        second(j, q, 1).wait_recv()
        total = block(j, q, p.b)[...].astype(F32)
        return total + r2[0, j, q].astype(F32) + r2[1, j, q].astype(F32)

    def send_sum(q):
        zs[q] = summed(1, q).astype(BF16)
        to_owner(q).start()

    def item_hop(hop):
        items.take(hop)
        if hop < 4:
            items.start(hop + 1)

    def isum_hop(hop):
        isum.take(hop)
        isum.add(hop)
        isum.start(hop + 1)

    def item_product():
        left = ni[...]
        partial = 0.0
        for b in range(X):
            here = slice(b * k, (b + 1) * k)
            value = gated(
                dot(left, wi[0, here, :], ((1,), (1,))), dot(left, wi[1, here, :], ((1,), (1,)))
            )
            hi[b] = value
            partial = partial + dot(value, wi[2, here, :])
        ip[...] = partial.astype(BF16)
        isum.start(1)

    rows.right(0).start()
    rows.left(0).start()
    items.start(1)
    own_weights[0].wait()
    w_send(0, 0).start()
    across().start()
    own_weights[1].wait()
    own_weights[2].wait()
    for first_row in range(0, f, 112):
        chunk = stage[first_row : first_row + 112, :]
        for tower in range(2):
            columns = slice(tower * wide, (tower + 1) * wide)
            w[0, 2, first_row : first_row + 112, columns] = by_tower(chunk, count, tower)
    w_near(0)
    w_send(1, 0).start()
    rows.take_x(0)
    item_hop(1)
    v_send(0).start()
    v_send(1).start()
    rows.take_halves(0)
    own_units(0)
    item_hop(2)
    w_ring(0)
    w_near(1)
    w_send(2, 0).start()
    remote(rows.block(0, p.b), rows.block(1, p.b), gs.at[0, 0], gr.at[0, 0], to_a2).wait_recv()
    rows.right(1).start()
    rows.left(1).start()
    item_hop(3)
    w_far(0)
    for kind in range(2):
        v_got(kind)
        v_send(2 + kind).start()
        v_send(4 + kind).start()
    item_hop(4)
    w_ring(1)
    w_near(2)
    w_done(0)
    mate_gate(0)
    v_got(2)
    v_got(3)
    v_send(6).start()
    w_far(1)
    for kind in (4, 5, 6):
        v_got(kind)
    item_product()
    rows.take_x(1)
    w_done(1)
    mate_up(0)
    w_ring(2)
    isum_hop(1)
    proj_copy.wait()
    proj_t[...] = proj[...].T
    rows.take_halves(1)
    own_units(1)
    isum_hop(2)
    w_far(2)
    mate_gate(1)
    mate_up(1)
    w_done(2)
    def spread(buf, mine, sems, partner):
        def each(hop, _):
            remote(buf.at[mine], buf.at[mine], sems.at[0], sems.at[1], partner(hop)).start()
            return 0

        lax.fori_loop(1, buf.shape[0], each, 0)

    def gathered(buf, sems):
        ref = buf.at[pl.ds(0, buf.shape[0] - 1)]
        remote(ref, ref, sems.at[0], sems.at[1], member(1)).wait()

    def q_rows(tower, line_of, core):
        return rows_of(gq.at[tower], (line_of * 2 + core) * block_wide, block_wide, block_wide)

    def q_half(tower, line_of, way):
        first = (line_of * 2 + c) * block_wide + way * (block_wide // 2)
        return rows_of(gq.at[tower], first, block_wide // 2, block_wide // 2)

    def q_core(tower, j):
        src = q_rows(tower, line_y[j], 1 - c)
        return remote(src, qc1.at[tower, j], qs.at[tower, j], qv.at[tower, j], to_core)

    def q_first(tower, way):
        src, dst = q_half(tower, y2, way), qb1.at[tower, way]
        return remote(src, dst, qs.at[tower, 4 + way], qv.at[tower, 4 + way], to_y[way])

    def q_second(tower, way):
        src, dst = q_rows(tower, (yp, ym)[way], c), qb2.at[tower, way]
        return remote(src, dst, qs.at[tower, 6 + way], qv.at[tower, 6 + way], to_y[way])

    def q_tower(tower):
        return remote(q_rows(tower, y, c), qc, qs.at[tower, 8], qv.at[tower, 8], to_tower)

    def q_start(tower):
        for j in range(4):
            q_core(tower, j).start()

    def q_far(tower):
        q_core(tower, 0).wait_recv()
        ref = q_rows(tower, y2, c)
        ref[...] += qc1[tower, 0]
        for way in range(2):
            q_first(tower, way).start()

    def q_near(tower):
        for way in range(2):
            q_core(tower, 1 + way).wait_recv()
            ref = q_rows(tower, (yp, ym)[way], c)
            ref[...] += qc1[tower, 1 + way]
            q_first(tower, way).wait_recv()
            ref = q_half(tower, (yp, ym)[way], way)
            ref[...] += qb1[tower, way]
            q_second(tower, way).start()

    def q_own(tower):
        q_core(tower, 3).wait_recv()
        for way in range(2):
            q_second(tower, way).wait_recv()
        ref = q_rows(tower, y, c)
        ref[...] = ref[...] + qc1[tower, 3] + qb2[tower, 0] + qb2[tower, 1]

        @pl.when(p.w != tower)
        def _():
            q_tower(tower).start()

    def q_finish(tower):
        @pl.when(p.w == tower)
        def _():
            q_tower(tower).wait_recv()
            q_out[...] = q_rows(tower, y, c)[...] + qc[...]

    def i_rows(line_of, core):
        first = pl.multiple_of((line_of * 2 + core) * block_wide, block_wide)
        return gi.at[:, pl.ds(first, block_wide), :]

    def i_half(line_of, way):
        first = pl.multiple_of((line_of * 2 + c) * block_wide, block_wide)
        return gi.at[pl.ds(way * 2, 2), pl.ds(first, block_wide), :]

    def i_slab(b):
        return gi.at[b, pl.ds(pl.multiple_of((y * 2 + c) * block_wide, block_wide), block_wide), :]

    def i_core(j):
        return remote(i_rows(line_y[j], 1 - c), ic1.at[j], bs.at[j], bv.at[j], to_core)

    def i_first(way):
        return remote(i_half(y2, way), ib1.at[way], bs.at[4 + way], bv.at[4 + way], to_y[way])

    def i_second(way):
        src = i_rows((yp, ym)[way], c)
        return remote(src, ib2.at[way], bs.at[6 + way], bv.at[6 + way], to_y[way])

    def i_x(hop):
        other = (p.b + hop) % X
        where = {"tensor": p.a * X + other}
        return remote(i_slab(other), ic.at[p.b], bs.at[8 + hop], bv.at[8 + p.b], where)

    def i_product():
        for b in range(X):
            gi[b] = dot(yi[...], hi[b], ((0,), (0,)))
        for j in range(4):
            i_core(j).start()

    def i_far():
        for j in range(4):
            i_core(j).wait_recv()
            ref = i_rows(line_y[j], c)
            ref[...] += ic1[j]
        for way in range(2):
            i_first(way).start()

    def i_near():
        for way in range(2):
            i_first(way).wait_recv()
            ref = i_half((yp, ym)[way], way)
            ref[...] += ib1[way]
            i_second(way).start()

    def i_own():
        for way in range(2):
            i_second(way).wait_recv()
        ref = i_rows(y, c)
        ref[...] = ref[...] + ib2[0] + ib2[1]
        for hop in range(1, X):
            i_x(hop).start()

    def i_finish():
        total = i_slab(p.b)[...]
        for hop in range(1, X):
            other = (p.b + hop) % X
            remote(i_slab(other), ic.at[other], bs.at[8 + hop], bv.at[8 + other], p.xp).wait_recv()
            total = total + ic[other]
        i_out[...] = total

    gather = [RowGather(p, yq.at[tower], n, ys.at[tower], yr.at[tower]) for tower in range(2)]
    igather = RingGather(p, yi, m, iys, iyr)

    steps = (0, 1, 4, 2, 5, 3, 6, 7)

    def advance(index):
        if index < len(steps):
            g = steps[index]
            gather[g // ZL].take_z(p.order(g % ZL))
        if 0 <= index - 2 < len(steps):
            g = steps[index - 2]
            gather[g // ZL].take_x(p.order(g % ZL))

    def item_grad_hop(hop):
        igather.take(hop)
        if hop < 4:
            igather.start(hop + 1)

    def scale_hidden():
        line = lax.broadcasted_iota(jnp.int32, (128, 128), 0)
        tiles = [jnp.zeros((128, 128), F32)] * 2
        for t in range(parts):
            for kind in range(2):
                tiles[kind] = jnp.where(line == t, scal[t, kind : kind + 1, :], tiles[kind])
        scale_of, slope_of = tiles[0].T[:n], tiles[1].T[:n]
        total = jnp.zeros((1, f), F32)
        for t in range(parts):
            here = slice(t * n, (t + 1) * n)
            value = hq[here, :].astype(F32)
            hw[here, :] = (value * slope_of[:, t : t + 1]).astype(BF16)
            total = total + jnp.sum(value * scale_of[:, t : t + 1], axis=0, keepdims=True)
        return total

    def product(tower, part_of):
        total = 0.0
        for j in (2 * part_of, 2 * part_of + 1):
            s = p.order(j)
            gather[tower].take_halves(s)
            here = pl.ds(pl.multiple_of(s * group, group), group)
            total = total + dot(yq[tower, here, :], hw[here, :], ((0,), (0,)))
        if part_of == 0:
            column = jnp.broadcast_to(along_of[tower], (128, wide)).T[:, 0:1]
            gq[tower] = column * summed_hidden - total
        else:
            gq[tower] -= total

    def resid_half(tower):
        total = summed(0, tower)
        to_owner(tower).wait_recv()
        total = total + zin[tower].astype(F32)
        value = by_tower(qa[...], count, tower).astype(F32) + total
        yq[tower, pl.ds(pl.multiple_of(p.t * n, n), n), :] = value.astype(BF16)
        return value

    mate_down(1, 0)
    mate_down(0, 0)
    combine(1, 0)
    mate_down(1, 1)
    combine(0, 0)
    mate_down(0, 1)
    send_sum(0)
    combine(1, 1)
    combine(0, 1)
    isum_hop(3)
    send_sum(1)
    q_resid = [resid_half(0)]
    advance(0)
    back(0, 0).start()
    isum.take(4)
    own_item = ip[pl.ds(pl.multiple_of(p.z * m, m), m), :].astype(F32)
    i_resid = ia[...].astype(F32) + (own_item + land[0, 3].astype(F32) + land[1, 3].astype(F32))
    i_gain = gain_row(if_)
    i_scale = rms_scale(i_resid)
    sums[p.t, :, dq:] = jnp.sum(i_resid * i_scale * i_gain, axis=0, keepdims=True)
    q_gain = gain_row(qf)
    gain_of = [by_tower(q_gain, count, tower) for tower in range(2)]
    advance(1)
    q_resid.append(resid_half(1))
    square = sum(jnp.sum(value * value, axis=-1, keepdims=True) for value in q_resid)
    q_scale = lax.rsqrt(square / dq + EPS)
    for tower in range(2):
        part_sum = jnp.sum(q_resid[tower] * q_scale * gain_of[tower], axis=0, keepdims=True)
        sums[p.t, :, tower * wide : (tower + 1) * wide] = part_sum
    spread(sums, p.t, s1, member)
    advance(2)
    back(0, 1).start()
    gathered(sums, s1)
    total = sums[0]
    for slot in range(1, parts):
        total = total + sums[slot]
    firsts = [(d % 2) * wide + (d // 2) * block_wide for d in range(count)]
    q_pooled = jnp.concatenate([total[:, at : at + block_wide] for at in firsts], axis=1) / QLEN
    i_pooled = total[:, dq:] / ILEN
    q_e = jnp.sum(dot(split_rows(q_pooled), proj[...]), axis=0, keepdims=True)
    q_norm, i_norm = unit_scale(q_e), unit_scale(i_pooled)
    hats[own, :, :di] = q_e * q_norm
    hats[own, :, di:] = i_pooled * i_norm
    spread(hats, own, s2, replica)
    advance(3)
    back(0, 2).start()
    gathered(hats, s2)
    index = lax.broadcasted_iota(jnp.int32, (count, 2 * di), 0)
    every = jnp.zeros((count, 2 * di), F32)
    for slot in range(count):
        every = jnp.where(index == slot, hats[slot], every)
    every_query, every_items = every[:, :di], every[:, di:]
    line = lax.broadcasted_iota(jnp.int32, (count, count), 0)
    target = jnp.zeros((count, count), jnp.int32)
    for slot in range(count):
        target = jnp.where(line == slot, positive[slot], target)
    per_row, slopes = contrast(every_query, every_items, ranks[...], target)
    loss[...] = jnp.sum(per_row, axis=0, keepdims=True) / count
    weights = slopes * (LOSS_SCALE / (TAU * count))
    advance(4)
    back(0, 3).start()
    mine = lax.broadcasted_iota(jnp.int32, (count, di), 0) == own
    q_back = jnp.sum(
        jnp.where(mine, dot(weights, every_items, precision=HIGH), 0.0), axis=0, keepdims=True
    )
    column = lax.broadcasted_iota(jnp.int32, (count, count), 1) == own
    i_back = jnp.sum(
        jnp.sum(jnp.where(column, weights, 0.0), axis=1, keepdims=True) * every_query,
        axis=0,
        keepdims=True,
    )
    advance(5)
    q_grad_e = unit_back(q_e, q_norm, q_back)
    q_up = jnp.sum(dot(split_rows(q_grad_e), proj_t[...]), axis=0, keepdims=True) / QLEN
    i_up = unit_back(i_pooled, i_norm, i_back) / ILEN
    along = q_gain * q_up
    along_of = [by_tower(along, count, tower) for tower in range(2)]
    inner = sum(
        jnp.sum(along_of[tower] * q_resid[tower], axis=-1, keepdims=True) for tower in range(2)
    )
    inner = inner / dq
    slope = (q_scale * q_scale * q_scale) * inner
    lane = lax.broadcasted_iota(jnp.int32, (n, 128), 1)
    columns = jnp.where(lane == 0, q_scale, jnp.where(lane == 1, slope, 0.0))
    columns = jnp.concatenate([columns, jnp.zeros((128 - n, 128), F32)], axis=0)
    scal[p.t] = columns.T[:8]
    spread(scal, p.t, s3, member)
    yi[pl.ds(pl.multiple_of(p.z * m, m), m), :] = grad_rows(i_resid, i_scale, i_gain, i_up)
    igather.start(1)
    advance(6)
    gathered(scal, s3)
    back_got(0)
    back_got(1)
    summed_hidden = scale_hidden()
    advance(7)
    item_grad_hop(1)
    product(0, 0)
    advance(8)
    item_grad_hop(2)
    product(0, 1)
    q_start(0)
    advance(9)
    item_grad_hop(3)
    q_far(0)
    product(1, 0)
    item_grad_hop(4)
    q_near(0)
    i_product()
    product(1, 1)
    q_start(1)
    q_far(1)
    for j in range(2):
        for b in range(X):
            back(j, b).wait_send()
        for copy in (rows.right(j), rows.left(j), rows.half_right(j), rows.half_left(j)):
            copy.wait_send()
        for q in range(2):
            for way in range(2):
                first(j, q, way).wait_send()
                second(j, q, way).wait_send()
    for q in range(2):
        to_owner(q).wait_send()
    across().wait_send()
    items.drain()
    isum.drain()
    q_own(0)
    i_far()
    q_near(1)
    for index in range(3):
        for kind in range(9) if index == 2 else range(5):
            w_send(index, kind).wait_send()
    for index in range(2):
        w_column(index, c).wait_send()
    for kind in range(7):
        v_send(kind).wait_send()
    i_near()
    gather[0].drain()
    gather[1].drain()
    igather.drain()
    q_own(1)
    i_own()
    q_finish(0)
    for tower in range(2):
        for j in range(4):
            q_core(tower, j).wait_send()
        for way in range(2):
            q_first(tower, way).wait_send()
            q_second(tower, way).wait_send()
    for j in range(4):
        i_core(j).wait_send()
    for way in range(2):
        i_first(way).wait_send()
        i_second(way).wait_send()
    i_finish()
    q_finish(1)
    for hop in range(1, X):
        i_x(hop).wait_send()
    for tower in range(2):

        @pl.when(p.w != tower)
        def _():
            q_tower(tower).wait_send()


def step(qa, qg, gate, up, down, ia, ig, ig_w, iu_w, id_w, qf, if_, proj, ranks, positive):
    n, dq = qa.shape
    m, di = ia.shape
    f, k = down.shape[0], id_w.shape[0]
    padded = 64 * ((f + 63) // 64)
    vmem, hbm = pl.BlockSpec(memory_space=pltpu.VMEM), pl.BlockSpec(memory_space=pl.ANY)
    smem = pl.BlockSpec(memory_space=pltpu.SMEM)
    all_i = ZR * m
    group = X * n
    parts = X * ZL
    count = ranks.shape[0]
    wide = dq // count
    dma = pltpu.SemaphoreType.DMA
    return pl.pallas_call(
        kernel,
        out_shape=(
            jax.ShapeDtypeStruct((1, 1), F32),
            jax.ShapeDtypeStruct((wide, f), F32),
            jax.ShapeDtypeStruct((wide, k), F32),
        ),
        in_specs=[vmem, vmem, hbm, hbm, hbm] + [vmem] * 7 + [hbm, vmem, smem],
        out_specs=[vmem] * 3,
        scratch_shapes=[
            pltpu.VMEM((2, 3, padded, dq), BF16),
            pltpu.VMEM(down.shape, BF16),
            pltpu.VMEM(proj.shape, BF16),
            pltpu.VMEM((proj.shape[1], proj.shape[0]), BF16),
            pltpu.VMEM((2 * group, dq), BF16),
            pltpu.VMEM((2, group, dq), F32),
            pltpu.VMEM((2, group, f), F32),
            pltpu.VMEM((2, group, f), BF16),
            pltpu.VMEM((2, 2 * group, dq // 2), BF16),
            pltpu.VMEM((2, 2, 2, n // 2, dq // 2), BF16),
            pltpu.VMEM((2, 2, 2, n, dq // 2), BF16),
            pltpu.VMEM((2, n, dq // 2), BF16),
            pltpu.VMEM((2, n, dq // 2), BF16),
            pltpu.VMEM((all_i, di), BF16),
            pltpu.VMEM((3, X * k, di), BF16),
            pltpu.VMEM((all_i, di), BF16),
            pltpu.VMEM((2, 4, m, di), BF16),
            pltpu.VMEM((ZL * group, f), BF16),
            pltpu.VMEM((X, all_i, k), BF16),
            pltpu.VMEM((parts, 1, dq + di), F32),
            pltpu.VMEM((count, 1, 2 * di), F32),
            pltpu.VMEM((parts, 8, 128), F32),
            pltpu.VMEM((2, parts * n, dq // 2), BF16),
            pltpu.VMEM((ZL * group, f), BF16),
            pltpu.VMEM((all_i, di), BF16),
            pltpu.VMEM((2, dq // 2, f), F32),
            pltpu.VMEM((X, di, k), F32),
            pltpu.VMEM((2, 4, wide, f), F32),
            pltpu.VMEM((2, 2, wide // 2, f), F32),
            pltpu.VMEM((2, 2, wide, f), F32),
            pltpu.VMEM((wide, f), F32),
            pltpu.VMEM((4, X, wide, k), F32),
            pltpu.VMEM((2, 2, wide, k), F32),
            pltpu.VMEM((2, X, wide, k), F32),
            pltpu.VMEM((X, wide, k), F32),
            dma((4,)),
            dma((6, 2)),
            dma((5, 2)),
            dma((5, 2, 2)),
            dma((5, 2, 2)),
            dma((9, 3)),
            dma((9, 3)),
            dma((7,)),
            dma((7,)),
            dma((2, X)),
            dma((2, X)),
            dma((2, 4)),
            dma((2, 4)),
            dma((2, 4)),
            dma((2, 4)),
            dma((2,)),
            dma((2,)),
            dma((2,)),
            dma((2, 6, ZL)),
            dma((2, 5, ZL)),
            dma((2, 4)),
            dma((2, 4)),
            dma((2, 9)),
            dma((2, 9)),
            dma((12,)),
            dma((12,)),
        ],
        compiler_params=pltpu.CompilerParams(
            collective_id=0, has_side_effects=True, vmem_limit_bytes=VMEM_LIMIT
        ),
        name="towers_step",
    )(qa, qg, gate, up, down, ia, ig, ig_w, iu_w, id_w, qf, if_, proj, ranks, positive)


def body(
    q_act,
    q_norm_gain,
    q_gate,
    q_up,
    q_down,
    q_final_gain,
    projection,
    i_act,
    i_norm_gain,
    i_gate,
    i_up,
    i_down,
    i_final_gain,
    ranks,
    positive,
):
    loss, q_grad, i_grad = step(
        q_act,
        q_norm_gain,
        q_gate.T,
        q_up.T,
        q_down,
        i_act,
        i_norm_gain,
        i_gate.T,
        i_up.T,
        i_down,
        q_final_gain,
        i_final_gain,
        projection,
        ranks,
        positive,
    )
    return (loss.reshape(()), q_grad.T, i_grad.T)


def solution(mesh):
    in_specs = (
        P(("dp", "tower", "tensor"), None),
        P(),
        P(None, "tensor"),
        P(None, "tensor"),
        P("tensor", None),
        P(),
        P(),
        P(("dp", "tower", "tensor"), None),
        P(),
        P(None, ("tower", "tensor")),
        P(None, ("tower", "tensor")),
        P(("tower", "tensor"), None),
        P(),
        P(),
        P(),
    )
    out_specs = (P(), P("tensor", ("dp", "tower")), P(("tower", "tensor"), "dp"))
    return jax.shard_map(body, mesh=mesh, in_specs=in_specs, out_specs=out_specs, check_vma=False)
```

```python
import functools

import jax
import jax.numpy as jnp
from jax import lax
from jax.experimental import pallas as pl
from jax.experimental.pallas import tpu as pltpu
from jax.sharding import PartitionSpec as P

QLEN = 1536
ILEN = 512
EPS = 1e-06
TAU = 0.05
TEACH = 2.0
LOSS_SCALE = 64.0
HIGH = lax.Precision.HIGHEST
MESH = pl.DeviceIdType.MESH
F32 = jnp.float32
BF16 = jnp.bfloat16

X = 4
ZL = 4
ZR = 8
VMEM_LIMIT = 60 * 1024 * 1024


def rms_scale(values):
    return lax.rsqrt(jnp.mean(values * values, axis=-1, keepdims=True) + EPS)


def dot(left, right, dims=((1,), (0,)), precision=None):
    return lax.dot_general(
        left, right, (dims, ((), ())), preferred_element_type=F32, precision=precision
    )


def remote(src, dst, send, recv, where):
    return pltpu.make_async_remote_copy(
        src_ref=src, dst_ref=dst, send_sem=send, recv_sem=recv, device_id=where, device_id_type=MESH
    )


class Place:
    def __init__(self):
        self.t = lax.axis_index("tensor")
        self.w = lax.axis_index("tower")
        self.a = self.t // X
        self.b = self.t % X
        self.z = self.w * ZL + self.a
        self.bp = (self.b + 1) % X
        self.bm = (self.b + X - 1) % X
        self.bo = (self.b + 2) % X
        self.xp = {"tensor": self.a * X + self.bp}
        self.xm = {"tensor": self.a * X + self.bm}
        self.zp = self.ring(1)
        self.zm = self.ring(ZR - 1)

    def ring(self, step):
        z = (self.z + step) % ZR
        return {"tower": z // ZL, "tensor": (z % ZL) * X + self.b}

    def column(self, row):
        return {"tensor": row * X + self.b}

    def order(self, j):
        near = jnp.minimum(self.a, ZL - 1 - self.a)
        swapped = jnp.where(j == 0, 1, jnp.where(j == 1, 0, j))
        row = jnp.where(near == 1, swapped, j)
        return jnp.where(self.a >= 2, ZL - 1 - row, row)


def rows_of(ref, first, count, unit):
    return ref.at[pl.ds(pl.multiple_of(first, unit), count), :]


class RowGather:
    def __init__(self, place, buf, rows, send, recv):
        self.p, self.buf, self.n, self.send, self.recv = place, buf, rows, send, recv

    def block(self, s, b):
        return rows_of(self.buf, (s * X + b) * self.n, self.n, self.n)

    def half(self, s, b, h):
        n = self.n // 2
        return rows_of(self.buf, (s * X + b) * self.n + h * n, n, n)

    def up(self, s):
        ref = self.block(s, self.p.b)
        where = self.p.column(jnp.minimum(self.p.a + 1, ZL - 1))
        return remote(ref, ref, self.send.at[0, s], self.recv.at[0, s], where)

    def down(self, s):
        ref = self.block(s, self.p.b)
        where = self.p.column(jnp.maximum(self.p.a - 1, 0))
        return remote(ref, ref, self.send.at[1, s], self.recv.at[0, s], where)

    def right(self, s):
        ref = self.block(s, self.p.b)
        return remote(ref, ref, self.send.at[2, s], self.recv.at[1, s], self.p.xp)

    def left(self, s):
        ref = self.block(s, self.p.b)
        return remote(ref, ref, self.send.at[3, s], self.recv.at[2, s], self.p.xm)

    def half_right(self, s):
        ref = self.half(s, self.p.bm, 0)
        return remote(ref, ref, self.send.at[4, s], self.recv.at[3, s], self.p.xp)

    def half_left(self, s):
        ref = self.half(s, self.p.bp, 1)
        return remote(ref, ref, self.send.at[5, s], self.recv.at[4, s], self.p.xm)

    def goes_up(self, s):
        return (s <= self.p.a) & (self.p.a < ZL - 1)

    def goes_down(self, s):
        return (s >= self.p.a) & (self.p.a > 0)

    def take_z(self, s):
        @pl.when(s != self.p.a)
        def _():
            self.up(s).wait_recv()

        @pl.when(self.goes_up(s))
        def _():
            self.up(s).start()

        @pl.when(self.goes_down(s))
        def _():
            self.down(s).start()

        self.right(s).start()
        self.left(s).start()

    def take_x(self, s):
        ref = self.block(s, self.p.bm)
        remote(ref, ref, self.send.at[2, s], self.recv.at[1, s], self.p.xm).wait_recv()
        self.half_right(s).start()
        ref = self.block(s, self.p.bp)
        remote(ref, ref, self.send.at[3, s], self.recv.at[2, s], self.p.xp).wait_recv()
        self.half_left(s).start()

    def take_halves(self, s):
        ref = self.half(s, self.p.bo, 0)
        remote(ref, ref, self.send.at[4, s], self.recv.at[3, s], self.p.xm).wait_recv()
        ref = self.half(s, self.p.bo, 1)
        remote(ref, ref, self.send.at[5, s], self.recv.at[4, s], self.p.xp).wait_recv()

    def drain(self):
        def each(s, _):
            @pl.when(self.goes_up(s))
            def _():
                self.up(s).wait_send()

            @pl.when(self.goes_down(s))
            def _():
                self.down(s).wait_send()

            self.right(s).wait_send()
            self.left(s).wait_send()
            self.half_right(s).wait_send()
            self.half_left(s).wait_send()
            return 0

        lax.fori_loop(0, ZL, each, 0)


class RingGather:
    def __init__(self, place, buf, rows, send, recv):
        self.p, self.buf, self.n, self.send, self.recv = place, buf, rows, send, recv

    def ref(self, z, hop, upward):
        z = (z + 2 * ZR) % ZR
        if hop < 4:
            return rows_of(self.buf, z * self.n, self.n, self.n)
        n = self.n // 2
        return rows_of(self.buf, z * self.n + (0 if upward else n), n, n)

    def copies(self, hop):
        up = self.ref(self.p.z - hop + 1, hop, True)
        down = self.ref(self.p.z + hop - 1, hop, False)
        return (
            remote(up, up, self.send.at[0, hop - 1], self.recv.at[0, hop - 1], self.p.zp),
            remote(down, down, self.send.at[1, hop - 1], self.recv.at[1, hop - 1], self.p.zm),
        )

    def start(self, hop):
        for copy in self.copies(hop):
            copy.start()

    def take(self, hop):
        up = self.ref(self.p.z - hop, hop, True)
        down = self.ref(self.p.z + hop, hop, False)
        remote(up, up, self.send.at[0, hop - 1], self.recv.at[0, hop - 1], self.p.zm).wait_recv()
        remote(down, down, self.send.at[1, hop - 1], self.recv.at[1, hop - 1], self.p.zp).wait_recv()

    def drain(self):
        for hop in range(1, 5):
            for copy in self.copies(hop):
                copy.wait_send()


class RingSum:
    def __init__(self, place, buf, land, rows, send, recv):
        self.p, self.buf, self.land = place, buf, land
        self.n, self.send, self.recv = rows, send, recv

    def part(self, z, half):
        z = (z + 2 * ZR) % ZR
        if half is None:
            return rows_of(self.buf, z * self.n, self.n, self.n)
        n = self.n // 2
        return rows_of(self.buf, z * self.n + half * n, n, n)

    def slot(self, way, hop):
        if hop == 1:
            return self.land.at[way, 0, pl.ds(0, self.n // 2), :]
        return self.land.at[way, hop - 1]

    def copies(self, hop):
        half = (0, 1) if hop == 1 else (None, None)
        up = self.part(self.p.z + 5 - hop, half[0])
        down = self.part(self.p.z - 5 + hop, half[1])
        return (
            remote(up, self.slot(0, hop), self.send.at[0, hop - 1], self.recv.at[0, hop - 1], self.p.zp),
            remote(down, self.slot(1, hop), self.send.at[1, hop - 1], self.recv.at[1, hop - 1], self.p.zm),
        )

    def start(self, hop):
        for copy in self.copies(hop):
            copy.start()

    def take(self, hop):
        for copy in self.copies(hop):
            copy.wait_recv()

    def add(self, hop):
        half = (0, 1) if hop == 1 else (None, None)
        for way, z in ((0, self.p.z + 4 - hop), (1, self.p.z - 4 + hop)):
            ref = self.part(z, half[way])
            ref[...] = (ref[...].astype(F32) + self.slot(way, hop)[...].astype(F32)).astype(BF16)

    def drain(self):
        for hop in range(1, 5):
            for copy in self.copies(hop):
                copy.wait_send()


def gain_row(ref):
    return ref[...].astype(F32).reshape(1, -1)


def normed_rows(act, gain):
    values = act.astype(F32)
    return (values * rms_scale(values) * gain).astype(BF16)


def gated(gate_val, up_val):
    return (jax.nn.silu(gate_val) * up_val).astype(BF16)


def at_step(i, step):
    return pl.when(i == step)


def split_rows(row):
    high = row.astype(BF16).astype(F32)
    rest = row - high
    mid = rest.astype(BF16).astype(F32)
    low = rest - mid
    index = lax.broadcasted_iota(jnp.int32, (8, row.shape[1]), 0)
    out = jnp.where(index == 0, high, jnp.where(index == 1, mid, jnp.where(index == 2, low, 0.0)))
    return out.astype(BF16)


def unit_scale(vec):
    return lax.rsqrt(jnp.sum(vec * vec, axis=-1, keepdims=True) + EPS)


def unit_back(vec, scales, upstream):
    inner = jnp.sum(vec * upstream, axis=-1, keepdims=True)
    return scales * upstream - vec * (scales * scales * scales) * inner


def contrast(query_hat, item_hat, ranks, positive):
    logits = dot(query_hat, item_hat, ((1,), (1,)), HIGH) / TAU
    shifted = logits - 1.0 / TAU
    log_student = shifted - jnp.log(jnp.sum(jnp.exp(shifted), axis=1, keepdims=True))
    teach = -ranks.astype(F32) / TEACH
    log_teacher = teach - jnp.log(jnp.sum(jnp.exp(teach), axis=1, keepdims=True))
    teacher = jnp.exp(log_teacher)
    columns = lax.broadcasted_iota(jnp.int32, logits.shape, 1)
    onehot = (columns == positive).astype(F32)
    per_row = jnp.sum(
        teacher * (log_teacher - log_student) - onehot * log_student, axis=1, keepdims=True
    )
    slopes = 2.0 * jnp.exp(log_student) - onehot - teacher
    return (per_row, slopes)


def grad_rows(resid, scales, gain, upstream):
    along = gain * upstream
    inner = jnp.mean(along * resid, axis=-1, keepdims=True)
    return (scales * along - resid * (scales * scales * scales) * inner).astype(BF16)


def by_tower(values, parts, tower):
    wide = values.shape[1] // parts
    blocks = [values[:, d * wide : (d + 1) * wide] for d in range(tower, parts, 2)]
    return jnp.concatenate(blocks, axis=1)


def kernel(
    qa, qg, gate_hbm, up_hbm, down_hbm, ia, ig, ig_w, iu_w, id_w, qf, if_, proj_hbm, ranks, positive,
    loss, q_out, i_out,
    w, stage, proj, proj_t, nq, part, gate_val, h2, pm, r1, r2, zs, zin, ni, wi, ip, land, hq, hi,
    sums, hats, scal, yq, hw, yi, gq, gi, qc1, qb1, qb2, qc, ic1, ib1, ib2, ic,
    loads, gs, gr, ss, sr, ws, wr, vs, vr, hs, hr, ias, iar, irs, irr,
    s1, s2, s3, ys, yr, iys, iyr, qs, qv, bs, bv,
):
    p = Place()
    n, dq = qa.shape
    m, di = ia.shape
    f, k = down_hbm.shape[0], id_w.shape[0]
    group = X * n
    h = n // 2
    parts = X * ZL
    count = hats.shape[0]
    block_wide = dq // count
    piece = w.shape[2] // 4
    wide, thin = dq // 2, dq // 4
    dp = lax.axis_index("dp")
    own = dp * 2 + p.w
    y, c = dp // 2, dp % 2
    yp, ym, y2 = (y + 1) % 4, (y + 3) % 4, (y + 2) % 4
    line_y = (y2, yp, ym, y)
    to_yp, to_ym, to_core = {"dp": yp * 2 + c}, {"dp": ym * 2 + c}, {"dp": y * 2 + 1 - c}
    to_y = (to_yp, to_ym)
    to_tower = {"tower": 1 - p.w}
    a2 = (p.a + 2) % ZL
    mate = p.a + 1 - 2 * (p.a % 2)
    to_a2, to_mate = p.column(a2), p.column(mate)

    def member(step):
        return {"tensor": (p.t + step) % parts}

    def replica(step):
        other = (own + step) % count
        return {"dp": other // 2, "tower": other % 2}

    own_weights = [
        pltpu.make_async_copy(ref, dst, loads.at[index])
        for index, (ref, dst) in enumerate(
            (
                (gate_hbm, w.at[0, 0, pl.ds(0, f), :]),
                (up_hbm, w.at[0, 1, pl.ds(0, f), :]),
                (down_hbm, stage),
            )
        )
    ]
    proj_copy = pltpu.make_async_copy(proj_hbm, proj, loads.at[3])
    for copy in own_weights:
        copy.start()
    proj_copy.start()
    barrier = pltpu.get_barrier_semaphore()

    def greet(step, _):
        pl.semaphore_signal(barrier, inc=1, device_id=member(step), device_id_type=MESH)
        pl.semaphore_signal(barrier, inc=1, device_id=replica(step), device_id_type=MESH)
        return 0

    lax.fori_loop(1, parts, greet, 0)
    for where in (p.zp, p.zm):
        pl.semaphore_signal(barrier, inc=1, device_id=where, device_id_type=MESH)
    for index in range(3):
        w[0, index, f:, :] = jnp.zeros((w.shape[2] - f, dq), BF16)
    nq[pl.ds(pl.multiple_of(p.b * n, n), n), :] = normed_rows(qa[...], gain_row(qg))
    ni[pl.ds(pl.multiple_of(p.z * m, m), m), :] = normed_rows(ia[...], gain_row(ig))
    for index, ref in enumerate((ig_w, iu_w, id_w)):
        wi[index, pl.ds(pl.multiple_of(p.b * k, k), k), :] = ref[...]
    pl.semaphore_wait(barrier, 2 * (parts - 1) + 2)

    rows = RowGather(p, nq, n, gs, gr)
    items = RingGather(p, ni, m, ias, iar)
    isum = RingSum(p, ip, land, m, irs, irr)

    def across():
        return remote(rows.block(0, p.b), rows.block(1, p.b), gs.at[0, 0], gr.at[0, 0], to_a2)

    def wpiece(which, index, line, core):
        first = pl.multiple_of(line * piece, piece)
        return w.at[which, index, pl.ds(first, piece), pl.ds(pl.multiple_of(core * wide, wide), wide)]

    def whalf(index, line, part_of):
        first = pl.multiple_of(line * piece, piece)
        column = pl.multiple_of(c * wide + part_of * thin, thin)
        return w.at[1, index, pl.ds(first, piece), pl.ds(column, thin)]

    def w_send(index, kind):
        here = wpiece(1, index, y, c)
        low, high = wpiece(1, index, ym, c), wpiece(1, index, yp, c)
        src, dst, where = (
            (wpiece(0, index, y, c), here, to_mate),
            (here, here, to_yp),
            (here, here, to_ym),
            (whalf(index, ym, 0), whalf(index, ym, 0), to_yp),
            (whalf(index, yp, 1), whalf(index, yp, 1), to_ym),
            (here, here, to_core),
            (low, low, to_core),
            (high, high, to_core),
            (wpiece(1, index, y2, c), wpiece(1, index, y2, c), to_core),
        )[kind]
        return remote(src, dst, ws.at[kind, index], wr.at[kind, index], where)

    def w_got(index, kind):
        dst = (
            wpiece(1, index, y, c),
            wpiece(1, index, ym, c),
            wpiece(1, index, yp, c),
            whalf(index, y2, 0),
            whalf(index, y2, 1),
            wpiece(1, index, y, 1 - c),
            wpiece(1, index, ym, 1 - c),
            wpiece(1, index, yp, 1 - c),
            wpiece(1, index, y2, 1 - c),
        )[kind]
        remote(dst, dst, ws.at[kind, index], wr.at[kind, index], to_core).wait_recv()

    def w_near(index):
        w_got(index, 0)
        for kind in (1, 2, 5) if index == 2 else (1, 2):
            w_send(index, kind).start()

    def w_ring(index):
        w_got(index, 1)
        w_send(index, 3).start()
        w_got(index, 2)
        w_send(index, 4).start()
        if index == 2:
            w_send(index, 6).start()
            w_send(index, 7).start()

    def w_far(index):
        w_got(index, 3)
        w_got(index, 4)
        if index == 2:
            w_send(index, 8).start()
        else:
            w_column(index, c).start()

    def w_column(index, core):
        ref = w.at[1, index, :, pl.ds(pl.multiple_of(core * wide, wide), wide)]
        return remote(ref, ref, ws.at[8, index], wr.at[8, index], to_core)

    def w_done(index):
        if index < 2:
            w_column(index, 1 - c).wait_recv()
        else:
            for kind in (5, 6, 7, 8):
                w_got(index, kind)

    def vpiece(b, core):
        column = pl.multiple_of(core * (di // 2), di // 2)
        return wi.at[:, pl.ds(pl.multiple_of(b * k, k), k), pl.ds(column, di // 2)]

    def vhalf(b, part_of):
        first = pl.multiple_of(b * k + part_of * (k // 2), k // 2)
        column = pl.multiple_of(c * (di // 2), di // 2)
        return wi.at[:, pl.ds(first, k // 2), pl.ds(column, di // 2)]

    def v_send(kind):
        ref, where = (
            (vpiece(p.b, c), p.xp),
            (vpiece(p.b, c), p.xm),
            (vhalf(p.bm, 0), p.xp),
            (vhalf(p.bp, 1), p.xm),
            (vpiece(p.bm, c), to_core),
            (vpiece(p.bp, c), to_core),
            (vpiece(p.bo, c), to_core),
        )[kind]
        return remote(ref, ref, vs.at[kind], vr.at[kind], where)

    def v_got(kind):
        ref = (
            vpiece(p.bm, c),
            vpiece(p.bp, c),
            vhalf(p.bo, 0),
            vhalf(p.bo, 1),
            vpiece(p.bm, 1 - c),
            vpiece(p.bp, 1 - c),
            vpiece(p.bo, 1 - c),
        )[kind]
        remote(ref, ref, vs.at[kind], vr.at[kind], to_core).wait_recv()

    def block(j, q, b):
        return rows_of(pm.at[q], (j * X + b) * n, n, n)

    def half(j, q, b, part_of):
        return rows_of(pm.at[q], (j * X + b) * n + part_of * h, h, h)

    def first(j, q, way):
        src = half(j, q, p.bo, way)
        where = (p.xp, p.xm)[way]
        return remote(src, r1.at[way, j, q], ss.at[way, j, q], sr.at[way, j, q], where)

    def second(j, q, way):
        src = block(j, q, (p.bp, p.bm)[way])
        where = (p.xp, p.xm)[way]
        return remote(src, r2.at[way, j, q], ss.at[2 + way, j, q], sr.at[2 + way, j, q], where)

    def to_owner(q):
        return remote(zs.at[q], zin.at[q], ss.at[4, 0, q], sr.at[4, 0, q], to_a2)

    def back(j, b):
        dst = rows_of(hq, ((p.a, a2)[j] * X + b) * n, n, n)
        src = h2.at[j, pl.ds(b * n, n), :]
        return remote(src, dst, hs.at[j, b], hr.at[j, b], to_mate)

    def back_got(j):
        other = (mate, (mate + 2) % ZL)[j]
        for b in range(X):
            dst = rows_of(hq, (other * X + b) * n, n, n)
            remote(dst, dst, hs.at[j, b], hr.at[j, b], to_mate).wait_recv()

    def rows_in(j):
        return nq[j * group : (j + 1) * group, :]

    def own_units(j):
        left = rows_in(j)
        value = gated(
            dot(left, w[0, 0, :f, :], ((1,), (1,))), dot(left, w[0, 1, :f, :], ((1,), (1,)))
        )
        hq[pl.ds(pl.multiple_of((p.a, a2)[j] * group, group), group), :] = value
        part[j] = dot(value, w[0, 2, :f, :])

    def mate_gate(j):
        gate_val[j] = dot(rows_in(j), w[1, 0, :f, :], ((1,), (1,)))

    def mate_up(j):
        h2[j] = gated(gate_val[j], dot(rows_in(j), w[1, 1, :f, :], ((1,), (1,))))
        if j == 1:
            for b in range(X):
                back(1, b).start()

    def mate_down(j, q):
        columns = slice(q * wide, (q + 1) * wide)
        total = part[j, :, columns] + dot(h2[j], w[1, 2, :f, columns])
        pm[q, j * group : (j + 1) * group, :] = total.astype(BF16)
        first(j, q, 0).start()
        first(j, q, 1).start()

    def combine(j, q):
        for way in range(2):
            first(j, q, way).wait_recv()
            ref = half(j, q, (p.bp, p.bm)[way], way)
            ref[...] = (ref[...].astype(F32) + r1[way, j, q].astype(F32)).astype(BF16)
            second(j, q, way).start()

    def summed(j, q):
        second(j, q, 0).wait_recv()
        second(j, q, 1).wait_recv()
        total = block(j, q, p.b)[...].astype(F32)
        return total + r2[0, j, q].astype(F32) + r2[1, j, q].astype(F32)

    def send_sum(q):
        zs[q] = summed(1, q).astype(BF16)
        to_owner(q).start()

    def item_hop(hop):
        items.take(hop)
        if hop < 4:
            items.start(hop + 1)

    def isum_hop(hop):
        isum.take(hop)
        isum.add(hop)
        isum.start(hop + 1)

    def item_product():
        left = ni[...]
        partial = 0.0
        for b in range(X):
            here = slice(b * k, (b + 1) * k)
            value = gated(
                dot(left, wi[0, here, :], ((1,), (1,))), dot(left, wi[1, here, :], ((1,), (1,)))
            )
            hi[b] = value
            partial = partial + dot(value, wi[2, here, :])
        ip[...] = partial.astype(BF16)
        isum.start(1)

    rows.right(0).start()
    rows.left(0).start()
    items.start(1)
    own_weights[0].wait()
    w_send(0, 0).start()
    across().start()
    own_weights[1].wait()
    own_weights[2].wait()
    for first_row in range(0, f, 112):
        chunk = stage[first_row : first_row + 112, :]
        for tower in range(2):
            columns = slice(tower * wide, (tower + 1) * wide)
            w[0, 2, first_row : first_row + 112, columns] = by_tower(chunk, count, tower)
    w_near(0)
    w_send(1, 0).start()
    rows.take_x(0)
    item_hop(1)
    v_send(0).start()
    v_send(1).start()
    w_send(2, 0).start()
    rows.take_halves(0)
    own_units(0)
    item_hop(2)
    w_ring(0)
    w_near(1)
    remote(rows.block(0, p.b), rows.block(1, p.b), gs.at[0, 0], gr.at[0, 0], to_a2).wait_recv()
    rows.right(1).start()
    rows.left(1).start()
    item_hop(3)
    w_far(0)
    for kind in range(2):
        v_got(kind)
        v_send(2 + kind).start()
        v_send(4 + kind).start()
    item_hop(4)
    w_ring(1)
    w_near(2)
    w_done(0)
    mate_gate(0)
    v_got(2)
    v_got(3)
    v_send(6).start()
    w_far(1)
    for kind in (4, 5, 6):
        v_got(kind)
    item_product()
    rows.take_x(1)
    w_done(1)
    mate_up(0)
    w_ring(2)
    isum_hop(1)
    proj_copy.wait()
    proj_t[...] = proj[...].T
    rows.take_halves(1)
    own_units(1)
    isum_hop(2)
    w_far(2)
    mate_gate(1)
    mate_up(1)
    w_done(2)
    def spread(buf, mine, sems, partner):
        def each(hop, _):
            remote(buf.at[mine], buf.at[mine], sems.at[0], sems.at[1], partner(hop)).start()
            return 0

        lax.fori_loop(1, buf.shape[0], each, 0)

    def gathered(buf, sems):
        ref = buf.at[pl.ds(0, buf.shape[0] - 1)]
        remote(ref, ref, sems.at[0], sems.at[1], member(1)).wait()

    def q_rows(tower, line_of, core):
        return rows_of(gq.at[tower], (line_of * 2 + core) * block_wide, block_wide, block_wide)

    def q_half(tower, line_of, way):
        first = (line_of * 2 + c) * block_wide + way * (block_wide // 2)
        return rows_of(gq.at[tower], first, block_wide // 2, block_wide // 2)

    def q_core(tower, j):
        src = q_rows(tower, line_y[j], 1 - c)
        return remote(src, qc1.at[tower, j], qs.at[tower, j], qv.at[tower, j], to_core)

    def q_first(tower, way):
        src, dst = q_half(tower, y2, way), qb1.at[tower, way]
        return remote(src, dst, qs.at[tower, 4 + way], qv.at[tower, 4 + way], to_y[way])

    def q_second(tower, way):
        src, dst = q_rows(tower, (yp, ym)[way], c), qb2.at[tower, way]
        return remote(src, dst, qs.at[tower, 6 + way], qv.at[tower, 6 + way], to_y[way])

    def q_tower(tower):
        return remote(q_rows(tower, y, c), qc, qs.at[tower, 8], qv.at[tower, 8], to_tower)

    def q_start(tower):
        for j in range(4):
            q_core(tower, j).start()

    def q_far(tower):
        q_core(tower, 0).wait_recv()
        ref = q_rows(tower, y2, c)
        ref[...] += qc1[tower, 0]
        for way in range(2):
            q_first(tower, way).start()

    def q_near(tower):
        for way in range(2):
            q_core(tower, 1 + way).wait_recv()
            ref = q_rows(tower, (yp, ym)[way], c)
            ref[...] += qc1[tower, 1 + way]
            q_first(tower, way).wait_recv()
            ref = q_half(tower, (yp, ym)[way], way)
            ref[...] += qb1[tower, way]
            q_second(tower, way).start()

    def q_own(tower):
        q_core(tower, 3).wait_recv()
        for way in range(2):
            q_second(tower, way).wait_recv()
        ref = q_rows(tower, y, c)
        ref[...] = ref[...] + qc1[tower, 3] + qb2[tower, 0] + qb2[tower, 1]

        @pl.when(p.w != tower)
        def _():
            q_tower(tower).start()

    def q_finish(tower):
        @pl.when(p.w == tower)
        def _():
            q_tower(tower).wait_recv()
            q_out[...] = q_rows(tower, y, c)[...] + qc[...]

    def i_rows(line_of, core):
        first = pl.multiple_of((line_of * 2 + core) * block_wide, block_wide)
        return gi.at[:, pl.ds(first, block_wide), :]

    def i_half(line_of, way):
        first = pl.multiple_of((line_of * 2 + c) * block_wide, block_wide)
        return gi.at[pl.ds(way * 2, 2), pl.ds(first, block_wide), :]

    def i_slab(b):
        return gi.at[b, pl.ds(pl.multiple_of((y * 2 + c) * block_wide, block_wide), block_wide), :]

    def i_core(j):
        return remote(i_rows(line_y[j], 1 - c), ic1.at[j], bs.at[j], bv.at[j], to_core)

    def i_first(way):
        return remote(i_half(y2, way), ib1.at[way], bs.at[4 + way], bv.at[4 + way], to_y[way])

    def i_second(way):
        src = i_rows((yp, ym)[way], c)
        return remote(src, ib2.at[way], bs.at[6 + way], bv.at[6 + way], to_y[way])

    def i_x(hop):
        other = (p.b + hop) % X
        where = {"tensor": p.a * X + other}
        return remote(i_slab(other), ic.at[p.b], bs.at[8 + hop], bv.at[8 + p.b], where)

    def i_product():
        for b in range(X):
            gi[b] = dot(yi[...], hi[b], ((0,), (0,)))
        for j in range(4):
            i_core(j).start()

    def i_far():
        for j in range(4):
            i_core(j).wait_recv()
            ref = i_rows(line_y[j], c)
            ref[...] += ic1[j]
        for way in range(2):
            i_first(way).start()

    def i_near():
        for way in range(2):
            i_first(way).wait_recv()
            ref = i_half((yp, ym)[way], way)
            ref[...] += ib1[way]
            i_second(way).start()

    def i_own():
        for way in range(2):
            i_second(way).wait_recv()
        ref = i_rows(y, c)
        ref[...] = ref[...] + ib2[0] + ib2[1]
        for hop in range(1, X):
            i_x(hop).start()

    def i_finish():
        total = i_slab(p.b)[...]
        for hop in range(1, X):
            other = (p.b + hop) % X
            remote(i_slab(other), ic.at[other], bs.at[8 + hop], bv.at[8 + other], p.xp).wait_recv()
            total = total + ic[other]
        i_out[...] = total

    gather = [RowGather(p, yq.at[tower], n, ys.at[tower], yr.at[tower]) for tower in range(2)]
    igather = RingGather(p, yi, m, iys, iyr)

    steps = (0, 1, 4, 2, 5, 3, 6, 7)

    def advance(index):
        if index < len(steps):
            g = steps[index]
            gather[g // ZL].take_z(p.order(g % ZL))
        if 0 <= index - 2 < len(steps):
            g = steps[index - 2]
            gather[g // ZL].take_x(p.order(g % ZL))

    def item_grad_hop(hop):
        igather.take(hop)
        if hop < 4:
            igather.start(hop + 1)

    def scale_hidden():
        line = lax.broadcasted_iota(jnp.int32, (128, 128), 0)
        tiles = [jnp.zeros((128, 128), F32)] * 2
        for t in range(parts):
            for kind in range(2):
                tiles[kind] = jnp.where(line == t, scal[t, kind : kind + 1, :], tiles[kind])
        scale_of, slope_of = tiles[0].T[:n], tiles[1].T[:n]
        total = jnp.zeros((1, f), F32)
        for t in range(parts):
            here = slice(t * n, (t + 1) * n)
            value = hq[here, :].astype(F32)
            hw[here, :] = (value * slope_of[:, t : t + 1]).astype(BF16)
            total = total + jnp.sum(value * scale_of[:, t : t + 1], axis=0, keepdims=True)
        return total

    def product(tower, part_of):
        total = 0.0
        for j in (2 * part_of, 2 * part_of + 1):
            s = p.order(j)
            gather[tower].take_halves(s)
            here = pl.ds(pl.multiple_of(s * group, group), group)
            total = total + dot(yq[tower, here, :], hw[here, :], ((0,), (0,)))
        if part_of == 0:
            column = jnp.broadcast_to(along_of[tower], (128, wide)).T[:, 0:1]
            gq[tower] = column * summed_hidden - total
        else:
            gq[tower] -= total

    def resid_half(tower):
        total = summed(0, tower)
        to_owner(tower).wait_recv()
        total = total + zin[tower].astype(F32)
        value = by_tower(qa[...], count, tower).astype(F32) + total
        yq[tower, pl.ds(pl.multiple_of(p.t * n, n), n), :] = value.astype(BF16)
        return value

    mate_down(1, 0)
    mate_down(0, 0)
    combine(1, 0)
    mate_down(1, 1)
    combine(0, 0)
    mate_down(0, 1)
    send_sum(0)
    combine(1, 1)
    combine(0, 1)
    isum_hop(3)
    send_sum(1)
    q_resid = [resid_half(0)]
    advance(0)
    back(0, 0).start()
    isum.take(4)
    own_item = ip[pl.ds(pl.multiple_of(p.z * m, m), m), :].astype(F32)
    i_resid = ia[...].astype(F32) + (own_item + land[0, 3].astype(F32) + land[1, 3].astype(F32))
    i_gain = gain_row(if_)
    i_scale = rms_scale(i_resid)
    sums[p.t, :, dq:] = jnp.sum(i_resid * i_scale * i_gain, axis=0, keepdims=True)
    q_gain = gain_row(qf)
    gain_of = [by_tower(q_gain, count, tower) for tower in range(2)]
    advance(1)
    q_resid.append(resid_half(1))
    square = sum(jnp.sum(value * value, axis=-1, keepdims=True) for value in q_resid)
    q_scale = lax.rsqrt(square / dq + EPS)
    for tower in range(2):
        part_sum = jnp.sum(q_resid[tower] * q_scale * gain_of[tower], axis=0, keepdims=True)
        sums[p.t, :, tower * wide : (tower + 1) * wide] = part_sum
    spread(sums, p.t, s1, member)
    advance(2)
    back(0, 1).start()
    gathered(sums, s1)
    total = sums[0]
    for slot in range(1, parts):
        total = total + sums[slot]
    firsts = [(d % 2) * wide + (d // 2) * block_wide for d in range(count)]
    q_pooled = jnp.concatenate([total[:, at : at + block_wide] for at in firsts], axis=1) / QLEN
    i_pooled = total[:, dq:] / ILEN
    q_e = jnp.sum(dot(split_rows(q_pooled), proj[...]), axis=0, keepdims=True)
    q_norm, i_norm = unit_scale(q_e), unit_scale(i_pooled)
    hats[own, :, :di] = q_e * q_norm
    hats[own, :, di:] = i_pooled * i_norm
    spread(hats, own, s2, replica)
    advance(3)
    back(0, 2).start()
    gathered(hats, s2)
    index = lax.broadcasted_iota(jnp.int32, (count, 2 * di), 0)
    every = jnp.zeros((count, 2 * di), F32)
    for slot in range(count):
        every = jnp.where(index == slot, hats[slot], every)
    every_query, every_items = every[:, :di], every[:, di:]
    line = lax.broadcasted_iota(jnp.int32, (count, count), 0)
    target = jnp.zeros((count, count), jnp.int32)
    for slot in range(count):
        target = jnp.where(line == slot, positive[slot], target)
    per_row, slopes = contrast(every_query, every_items, ranks[...], target)
    loss[...] = jnp.sum(per_row, axis=0, keepdims=True) / count
    weights = slopes * (LOSS_SCALE / (TAU * count))
    advance(4)
    back(0, 3).start()
    mine = lax.broadcasted_iota(jnp.int32, (count, di), 0) == own
    q_back = jnp.sum(
        jnp.where(mine, dot(weights, every_items, precision=HIGH), 0.0), axis=0, keepdims=True
    )
    column = lax.broadcasted_iota(jnp.int32, (count, count), 1) == own
    i_back = jnp.sum(
        jnp.sum(jnp.where(column, weights, 0.0), axis=1, keepdims=True) * every_query,
        axis=0,
        keepdims=True,
    )
    advance(5)
    q_grad_e = unit_back(q_e, q_norm, q_back)
    q_up = jnp.sum(dot(split_rows(q_grad_e), proj_t[...]), axis=0, keepdims=True) / QLEN
    i_up = unit_back(i_pooled, i_norm, i_back) / ILEN
    along = q_gain * q_up
    along_of = [by_tower(along, count, tower) for tower in range(2)]
    inner = sum(
        jnp.sum(along_of[tower] * q_resid[tower], axis=-1, keepdims=True) for tower in range(2)
    )
    inner = inner / dq
    slope = (q_scale * q_scale * q_scale) * inner
    lane = lax.broadcasted_iota(jnp.int32, (n, 128), 1)
    columns = jnp.where(lane == 0, q_scale, jnp.where(lane == 1, slope, 0.0))
    columns = jnp.concatenate([columns, jnp.zeros((128 - n, 128), F32)], axis=0)
    scal[p.t] = columns.T[:8]
    spread(scal, p.t, s3, member)
    yi[pl.ds(pl.multiple_of(p.z * m, m), m), :] = grad_rows(i_resid, i_scale, i_gain, i_up)
    igather.start(1)
    advance(6)
    gathered(scal, s3)
    back_got(0)
    back_got(1)
    summed_hidden = scale_hidden()
    advance(7)
    item_grad_hop(1)
    product(0, 0)
    advance(8)
    item_grad_hop(2)
    product(0, 1)
    q_start(0)
    advance(9)
    item_grad_hop(3)
    q_far(0)
    product(1, 0)
    item_grad_hop(4)
    q_near(0)
    i_product()
    product(1, 1)
    q_start(1)
    q_far(1)
    for j in range(2):
        for b in range(X):
            back(j, b).wait_send()
        for copy in (rows.right(j), rows.left(j), rows.half_right(j), rows.half_left(j)):
            copy.wait_send()
        for q in range(2):
            for way in range(2):
                first(j, q, way).wait_send()
                second(j, q, way).wait_send()
    for q in range(2):
        to_owner(q).wait_send()
    across().wait_send()
    items.drain()
    isum.drain()
    q_own(0)
    i_far()
    q_near(1)
    for index in range(3):
        for kind in range(9) if index == 2 else range(5):
            w_send(index, kind).wait_send()
    for index in range(2):
        w_column(index, c).wait_send()
    for kind in range(7):
        v_send(kind).wait_send()
    i_near()
    gather[0].drain()
    gather[1].drain()
    igather.drain()
    q_own(1)
    i_own()
    q_finish(0)
    for tower in range(2):
        for j in range(4):
            q_core(tower, j).wait_send()
        for way in range(2):
            q_first(tower, way).wait_send()
            q_second(tower, way).wait_send()
    for j in range(4):
        i_core(j).wait_send()
    for way in range(2):
        i_first(way).wait_send()
        i_second(way).wait_send()
    i_finish()
    q_finish(1)
    for hop in range(1, X):
        i_x(hop).wait_send()
    for tower in range(2):

        @pl.when(p.w != tower)
        def _():
            q_tower(tower).wait_send()


def step(qa, qg, gate, up, down, ia, ig, ig_w, iu_w, id_w, qf, if_, proj, ranks, positive):
    n, dq = qa.shape
    m, di = ia.shape
    f, k = down.shape[0], id_w.shape[0]
    padded = 64 * ((f + 63) // 64)
    vmem, hbm = pl.BlockSpec(memory_space=pltpu.VMEM), pl.BlockSpec(memory_space=pl.ANY)
    smem = pl.BlockSpec(memory_space=pltpu.SMEM)
    all_i = ZR * m
    group = X * n
    parts = X * ZL
    count = ranks.shape[0]
    wide = dq // count
    dma = pltpu.SemaphoreType.DMA
    return pl.pallas_call(
        kernel,
        out_shape=(
            jax.ShapeDtypeStruct((1, 1), F32),
            jax.ShapeDtypeStruct((wide, f), F32),
            jax.ShapeDtypeStruct((wide, k), F32),
        ),
        in_specs=[vmem, vmem, hbm, hbm, hbm] + [vmem] * 7 + [hbm, vmem, smem],
        out_specs=[vmem] * 3,
        scratch_shapes=[
            pltpu.VMEM((2, 3, padded, dq), BF16),
            pltpu.VMEM(down.shape, BF16),
            pltpu.VMEM(proj.shape, BF16),
            pltpu.VMEM((proj.shape[1], proj.shape[0]), BF16),
            pltpu.VMEM((2 * group, dq), BF16),
            pltpu.VMEM((2, group, dq), F32),
            pltpu.VMEM((2, group, f), F32),
            pltpu.VMEM((2, group, f), BF16),
            pltpu.VMEM((2, 2 * group, dq // 2), BF16),
            pltpu.VMEM((2, 2, 2, n // 2, dq // 2), BF16),
            pltpu.VMEM((2, 2, 2, n, dq // 2), BF16),
            pltpu.VMEM((2, n, dq // 2), BF16),
            pltpu.VMEM((2, n, dq // 2), BF16),
            pltpu.VMEM((all_i, di), BF16),
            pltpu.VMEM((3, X * k, di), BF16),
            pltpu.VMEM((all_i, di), BF16),
            pltpu.VMEM((2, 4, m, di), BF16),
            pltpu.VMEM((ZL * group, f), BF16),
            pltpu.VMEM((X, all_i, k), BF16),
            pltpu.VMEM((parts, 1, dq + di), F32),
            pltpu.VMEM((count, 1, 2 * di), F32),
            pltpu.VMEM((parts, 8, 128), F32),
            pltpu.VMEM((2, parts * n, dq // 2), BF16),
            pltpu.VMEM((ZL * group, f), BF16),
            pltpu.VMEM((all_i, di), BF16),
            pltpu.VMEM((2, dq // 2, f), F32),
            pltpu.VMEM((X, di, k), F32),
            pltpu.VMEM((2, 4, wide, f), F32),
            pltpu.VMEM((2, 2, wide // 2, f), F32),
            pltpu.VMEM((2, 2, wide, f), F32),
            pltpu.VMEM((wide, f), F32),
            pltpu.VMEM((4, X, wide, k), F32),
            pltpu.VMEM((2, 2, wide, k), F32),
            pltpu.VMEM((2, X, wide, k), F32),
            pltpu.VMEM((X, wide, k), F32),
            dma((4,)),
            dma((6, 2)),
            dma((5, 2)),
            dma((5, 2, 2)),
            dma((5, 2, 2)),
            dma((9, 3)),
            dma((9, 3)),
            dma((7,)),
            dma((7,)),
            dma((2, X)),
            dma((2, X)),
            dma((2, 4)),
            dma((2, 4)),
            dma((2, 4)),
            dma((2, 4)),
            dma((2,)),
            dma((2,)),
            dma((2,)),
            dma((2, 6, ZL)),
            dma((2, 5, ZL)),
            dma((2, 4)),
            dma((2, 4)),
            dma((2, 9)),
            dma((2, 9)),
            dma((12,)),
            dma((12,)),
        ],
        compiler_params=pltpu.CompilerParams(
            collective_id=0, has_side_effects=True, vmem_limit_bytes=VMEM_LIMIT
        ),
        name="towers_step",
    )(qa, qg, gate, up, down, ia, ig, ig_w, iu_w, id_w, qf, if_, proj, ranks, positive)


def body(
    q_act,
    q_norm_gain,
    q_gate,
    q_up,
    q_down,
    q_final_gain,
    projection,
    i_act,
    i_norm_gain,
    i_gate,
    i_up,
    i_down,
    i_final_gain,
    ranks,
    positive,
):
    loss, q_grad, i_grad = step(
        q_act,
        q_norm_gain,
        q_gate.T,
        q_up.T,
        q_down,
        i_act,
        i_norm_gain,
        i_gate.T,
        i_up.T,
        i_down,
        q_final_gain,
        i_final_gain,
        projection,
        ranks,
        positive,
    )
    return (loss.reshape(()), q_grad.T, i_grad.T)


def solution(mesh):
    in_specs = (
        P(("dp", "tower", "tensor"), None),
        P(),
        P(None, "tensor"),
        P(None, "tensor"),
        P("tensor", None),
        P(),
        P(),
        P(("dp", "tower", "tensor"), None),
        P(),
        P(None, ("tower", "tensor")),
        P(None, ("tower", "tensor")),
        P(("tower", "tensor"), None),
        P(),
        P(),
        P(),
    )
    out_specs = (P(), P("tensor", ("dp", "tower")), P(("tower", "tensor"), "dp"))
    return jax.shard_map(body, mesh=mesh, in_specs=in_specs, out_specs=out_specs, check_vma=False)
```
